32 devices in a mesh: dp: 8 (over z, x), fsdp: 4 (over y, core).
Axes of the slice: x: 2, y: 2, z: 4, core: 2. Of those that a mesh axis runs over, the one named last changes fastest.
Arguments:
- embed_table: float32 [768, 32128], P(('dp', 'fsdp')), may hold values from -6 to 6
- square_weights: float32 [5, 768, 768], P(None, 'dp', 'fsdp'), may hold values from -0.21875 to 0.21875
- expand_weight: float32 [768, 3072], P('dp', 'fsdp'), may hold values from -0.21875 to 0.21875
- reduce_weight: float32 [3072, 768], P('dp', 'fsdp'), may hold values from -0.109375 to 0.109375
- norm_gains: float32 [3, 768], P(None, ('dp', 'fsdp')), as said below
- position_bias: float32 [32, 12], replicated, may hold values from -6 to 6
- log_scale: float32 [1], replicated, may hold values from 3 to 3.4
- table_moment: float32 [768, 32128], P(('dp', 'fsdp')), may hold values from -3.8146973e-06 to 3.8146973e-06
- table_second: float32 [768, 32128], P(('dp', 'fsdp')), may hold values from 9.275199e-15 to 3.7100795e-14
- square_moment: float32 [5, 768, 768], P(None, 'dp', 'fsdp'), may hold values from -6.1035156e-05 to 6.1035156e-05
- square_second: float32 [5, 768, 768], P(None, 'dp', 'fsdp'), may hold values from 3.8646664e-12 to 6.183466e-11
- expand_moment: float32 [768, 3072], P('dp', 'fsdp'), may hold values from -6.1035156e-05 to 6.1035156e-05
- expand_second: float32 [768, 3072], P('dp', 'fsdp'), may hold values from 3.8646664e-12 to 6.183466e-11
- reduce_moment: float32 [3072, 768], P('dp', 'fsdp'), may hold values from -6.1035156e-05 to 6.1035156e-05
- reduce_second: float32 [3072, 768], P('dp', 'fsdp'), may hold values from 3.8646664e-12 to 6.183466e-11
- gains_moment: float32 [3, 768], P(None, ('dp', 'fsdp')), may hold values from -0.00030517578 to 0.00030517578
- gains_second: float32 [3, 768], P(None, ('dp', 'fsdp')), may hold values from 9.661665e-11 to 1.5458664e-09
- position_moment: float32 [32, 12], replicated, may hold values from -0.00030517578 to 0.00030517578
- position_second: float32 [32, 12], replicated, may hold values from 9.6616656e-12 to 1.5458665e-10
- scale_moment: float32 [1], replicated, may hold values from -0.00030517578 to 0.00030517578
- scale_second: float32 [1], replicated, may hold values from 9.661665e-11 to 1.5458664e-09
- query_tokens: int32 [128, 64], P(('dp', 'fsdp')), may hold values from 0 to 32127
- answer_tokens: int32 [128, 128], P(('dp', 'fsdp')), may hold values from 0 to 32127
- query_length: int32 [128], P(('dp', 'fsdp')), may hold values from 1 to 64, as said below
- answer_length: int32 [128], P(('dp', 'fsdp')), may hold values from 1 to 128, as said below
- premise_tokens: int32 [64, 64], P(('dp', 'fsdp')), may hold values from 0 to 32127
- hypothesis_tokens: int32 [64, 64], P(('dp', 'fsdp')), may hold values from 0 to 32127
- hard_negative: int32 [64], P(('dp', 'fsdp')), may hold values from 0 to 63
Outputs:
- moment_table: float32 [768, 32128], P(('dp', 'fsdp'))
- second_table: float32 [768, 32128], P(('dp', 'fsdp'))
- updated_table: float32 [768, 32128], P(('dp', 'fsdp'))
- moment_square: float32 [5, 768, 768], P(None, 'dp', 'fsdp')
- second_square: float32 [5, 768, 768], P(None, 'dp', 'fsdp')
- updated_square: float32 [5, 768, 768], P(None, 'dp', 'fsdp')
- moment_expand: float32 [768, 3072], P('dp', 'fsdp')
- second_expand: float32 [768, 3072], P('dp', 'fsdp')
- updated_expand: float32 [768, 3072], P('dp', 'fsdp')
- moment_reduce: float32 [3072, 768], P('dp', 'fsdp')
- second_reduce: float32 [3072, 768], P('dp', 'fsdp')
- updated_reduce: float32 [3072, 768], P('dp', 'fsdp')
- moment_gains: float32 [3, 768], P(None, ('dp', 'fsdp'))
- second_gains: float32 [3, 768], P(None, ('dp', 'fsdp'))
- updated_gains: float32 [3, 768], P(None, ('dp', 'fsdp'))
- moment_position: float32 [32, 12], replicated
- second_position: float32 [32, 12], replicated
- updated_position: float32 [32, 12], replicated
- moment_scale: float32 [1], replicated
- second_scale: float32 [1], replicated
- updated_scale: float32 [1], replicated
- losses: float32 [2], replicated
- gradient_norm: float32 [], replicated
The draws below stay inside these ranges and needn't reach their ends.
Inputs may be any that keep to these rules, and one draw needn't show every extreme that they name: `query_length`: each query has 1 to 64 tokens; some query has all 64. `answer_length`: each answer has 1 to 128 tokens; some answer has all 128. `norm_gains`: gains positive.
All inputs are finite; a program needn't handle non-finite values.
Results may differ from the reference program's by a relative error of at most 0.013.
Values may be sent and summed in bfloat16 or wider, within the bound.
A program may use at most 576 MiB of HBM per device.

```python
import math
import jax
import jax.numpy as jnp
import numpy as np
from jax import lax

D = 768
HEADS = 12
HEAD = 64
FF = 3072
V = 32128
BUCKETS = 32
MAXDIST = 128
LQ = 64
LA = 128
LN = 64
QA_DEV = 4
NLI_DEV = 2
STEP = 10
QA_PAIRS = 128
NLI_PAIRS = 64
DEVICES = 32


def draw_norm_gains(key, part):
    key = jax.random.fold_in(key, 13)
    ratio = 3.0
    places = jnp.arange(D, dtype=jnp.float32) / D
    rising = jnp.exp(jnp.log(ratio) * (places - 0.5))
    jitter = jax.random.uniform(key, (3, D), jnp.float32, 0.8, 1.25)
    return rising[None, :] * jitter


def rising_lengths(key, count, longest):
    first_key, second_key = jax.random.split(key)
    places = jnp.arange(count, dtype=jnp.int32)
    upper = 1 + (longest - 1) * (count + 2 * places) // (3 * count)
    upper = jnp.minimum(upper, longest)
    lengths = jax.random.randint(first_key, (count,), 1, upper + 1)
    chosen = jax.random.randint(second_key, (), 0, count)
    return jnp.where(places == chosen, longest, lengths).astype(jnp.int32)


def draw_query_length(key, part):
    key = jax.random.fold_in(key, 11)
    return rising_lengths(key, QA_PAIRS, LQ)


def draw_answer_length(key, part):
    key = jax.random.fold_in(key, 12)
    return rising_lengths(key, QA_PAIRS, LA)


def banded_ids(key, count, length, per_device):
    band_key, wide_key, other_key, pick_key = jax.random.split(key, 4)
    band_width = max(1, V // DEVICES)
    owner = jnp.arange(count, dtype=jnp.int32) // per_device
    band_start = jnp.minimum(owner * band_width, V - band_width)
    inside = band_start[:, None] + jax.random.randint(band_key, (count, length), 0, band_width)
    first_wide = jax.random.randint(wide_key, (count, length), 0, V)
    second_wide = jax.random.randint(other_key, (count, length), 0, V)
    spread_ids = jnp.minimum(first_wide, second_wide)
    pick = jax.random.randint(pick_key, (count, length), 0, 2)
    return jnp.where(pick == 0, inside, spread_ids).astype(jnp.int32)


def draw_query_tokens(key, part):
    key = jax.random.fold_in(key, 21)
    return banded_ids(key, QA_PAIRS, LQ, QA_DEV)


def draw_answer_tokens(key, part):
    key = jax.random.fold_in(key, 22)
    return banded_ids(key, QA_PAIRS, LA, QA_DEV)


def draw_premise_tokens(key, part):
    key = jax.random.fold_in(key, 23)
    return banded_ids(key, NLI_PAIRS, LN, NLI_DEV)


def draw_hypothesis_tokens(key, part):
    key = jax.random.fold_in(key, 24)
    return banded_ids(key, NLI_PAIRS, LN, NLI_DEV)


def place_ends(array, key, least, top_value):
    extent = array.shape
    spot = [jax.random.randint(jax.random.fold_in(key, axis), (), 0, extent[axis]) for axis in range(len(extent))]
    array = array.at[tuple(spot)].set(least)
    longest = extent.index(max(extent))
    spot[longest] = (spot[longest] + 1) % extent[longest]
    return array.at[tuple(spot)].set(top_value)


def levels(stream_key, dims, cuts, low, largest):
    def one(position, shards_of):
        draws = jax.random.uniform(jax.random.fold_in(jax.random.fold_in(stream_key, 6), position), (shards_of,), jnp.float32, low / len(cuts), largest / len(cuts))
        return jnp.repeat(jnp.exp(draws), dims[position] // shards_of).reshape((-1,) + (1,) * (len(dims) - position - 1))

    factor_of = one(*cuts[0])
    for cut in cuts[1:]:
        factor_of = factor_of * one(*cut)
    return factor_of


def normal_values(rng, shape, width, limit, pieces=(), held_as=jnp.bfloat16):
    values = jax.random.normal(rng, shape, jnp.float32) * width
    if len(pieces) > 0:
        values = levels(rng, shape, pieces, -0.22, 0.18) * values
    return jnp.clip(values, min=-limit, max=limit).astype(held_as)


def setup_inputs(seed: int = 0) -> dict:
    streams_of = jax.random.split(jax.random.key(seed), 29)
    return {
        "embed_table": normal_values(streams_of[0], (D, V), 1.0, 6.0, ((0, 32),), jnp.float32),
        "square_weights": normal_values(streams_of[1], (5, D, D), D ** -0.5, 0.21875, ((1, 8), (2, 4)), jnp.float32),
        "expand_weight": normal_values(streams_of[2], (D, FF), D ** -0.5, 0.21875, ((0, 8), (1, 4)), jnp.float32),
        "reduce_weight": normal_values(streams_of[3], (FF, D), FF ** -0.5, 0.109375, ((0, 8), (1, 4)), jnp.float32),
        "norm_gains": draw_norm_gains(jax.random.fold_in(streams_of[28], 71), 0),
        "position_bias": normal_values(streams_of[5], (BUCKETS, HEADS), 1.0, 6.0, (), jnp.float32),
        "log_scale": jnp.clip(jax.random.uniform(streams_of[6], (1,), jnp.float32, 3.0, 3.4), 3.0, 3.4),
        "table_moment": normal_values(streams_of[7], (D, V), (0.004 / (V*D + 5*D*D + 2*D*FF + 3*D) ** 0.5), 3.814697265625e-06, ((0, 32),), jnp.float32),
        "table_second": jnp.clip(jnp.exp(math.log(3.7100795254995517e-14) - 1.3862944 * jax.random.uniform(streams_of[8], (D, V), jnp.float32) ** levels(streams_of[8], (D, V), ((0, 32),), -0.2, 0.2)), 9.275198813748879e-15, 3.7100795254995517e-14),
        "square_moment": normal_values(streams_of[9], (5, D, D), (0.0556 / (V*D + 5*D*D + 2*D*FF + 3*D) ** 0.5), 6.103515625e-05, ((1, 8), (2, 4)), jnp.float32),
        "square_second": jnp.clip(jnp.exp(math.log(6.183466239040314e-11) - 2.7725887 * jax.random.uniform(streams_of[10], (5, D, D), jnp.float32) ** levels(streams_of[10], (5, D, D), ((1, 8), (2, 4)), -0.2, 0.2)), 3.864666399400196e-12, 6.183466239040314e-11),
        "expand_moment": normal_values(streams_of[11], (D, FF), (0.0556 / (V*D + 5*D*D + 2*D*FF + 3*D) ** 0.5), 6.103515625e-05, ((0, 8), (1, 4)), jnp.float32),
        "expand_second": jnp.clip(jnp.exp(math.log(6.183466239040314e-11) - 2.7725887 * jax.random.uniform(streams_of[12], (D, FF), jnp.float32) ** levels(streams_of[12], (D, FF), ((0, 8), (1, 4)), -0.2, 0.2)), 3.864666399400196e-12, 6.183466239040314e-11),
        "reduce_moment": normal_values(streams_of[13], (FF, D), (0.0556 / (V*D + 5*D*D + 2*D*FF + 3*D) ** 0.5), 6.103515625e-05, ((0, 8), (1, 4)), jnp.float32),
        "reduce_second": jnp.clip(jnp.exp(math.log(6.183466239040314e-11) - 2.7725887 * jax.random.uniform(streams_of[14], (FF, D), jnp.float32) ** levels(streams_of[14], (FF, D), ((0, 8), (1, 4)), -0.2, 0.2)), 3.864666399400196e-12, 6.183466239040314e-11),
        "gains_moment": normal_values(streams_of[15], (3, D), (0.278 / (V*D + 5*D*D + 2*D*FF + 3*D) ** 0.5), 0.00030517578, ((1, 32),), jnp.float32),
        "gains_second": jnp.clip(jnp.exp(math.log(1.5458664348599882e-09) - 2.7725887 * jax.random.uniform(streams_of[16], (3, D), jnp.float32) ** levels(streams_of[16], (3, D), ((1, 32),), -0.2, 0.2)), 9.661665217874926e-11, 1.5458664348599882e-09),
        "position_moment": normal_values(streams_of[17], (BUCKETS, HEADS), (0.278 / (V*D + 5*D*D + 2*D*FF + 3*D) ** 0.5), 0.00030517578, (), jnp.float32),
        "position_second": jnp.clip(jnp.exp(jax.random.uniform(streams_of[18], (BUCKETS, HEADS), jnp.float32, math.log(9.661665564819621e-12), math.log(1.5458664903711394e-10))), 9.661665564819621e-12, 1.5458664903711394e-10),
        "scale_moment": normal_values(streams_of[19], (1,), (0.278 / (V*D + 5*D*D + 2*D*FF + 3*D) ** 0.5), 0.00030517578, (), jnp.float32),
        "scale_second": jnp.clip(jnp.exp(jax.random.uniform(streams_of[20], (1,), jnp.float32, math.log(9.661665217874926e-11), math.log(1.5458664348599882e-09))), 9.661665217874926e-11, 1.5458664348599882e-09),
        "query_tokens": draw_query_tokens(jax.random.fold_in(streams_of[28], 71), 0),
        "answer_tokens": draw_answer_tokens(jax.random.fold_in(streams_of[28], 71), 0),
        "query_length": draw_query_length(jax.random.fold_in(streams_of[28], 71), 0),
        "answer_length": draw_answer_length(jax.random.fold_in(streams_of[28], 71), 0),
        "premise_tokens": draw_premise_tokens(jax.random.fold_in(streams_of[28], 71), 0),
        "hypothesis_tokens": draw_hypothesis_tokens(jax.random.fold_in(streams_of[28], 71), 0),
        "hard_negative": place_ends(jax.random.randint(streams_of[27], (NLI_PAIRS,), 0, NLI_PAIRS), jax.random.fold_in(streams_of[27], 1), 0, NLI_PAIRS - 1).astype(jnp.int32),
    }


@jax.custom_vjp
def low(v):
    return lax.optimization_barrier(v.astype(jnp.bfloat16)).astype(jnp.float32)

@jax.custom_vjp
def low_back(v):
    return v

def low_keep(v):
    return (low(v), None)

def low_pass(kept, grad):
    return (grad,)

def back_keep(v):
    return (v, None)

def back_low(kept, grad):
    return (low(grad),)
low.defvjp(low_keep, low_pass)
low_back.defvjp(back_keep, back_low)
HIGHEST = lax.Precision.HIGHEST
NORM_EPS = 1e-06
LEARN_RATE = 0.03
TABLE_RATE = 0.4
SMALL_RATE = 0.5
BETA_ONE = 0.9
BETA_TWO = 0.999
ADAM_EPS = 1e-08
WEIGHT_DECAY = 0.01
CLIP_NORM = 0.5

def bucket_table(length):
    places = np.arange(length)
    offset = places[None, :] - places[:, None]
    half_count = BUCKETS // 2
    exact_count = half_count // 2
    upper = (offset > 0).astype(np.int64) * half_count
    distance = np.abs(offset)
    far_bucket = exact_count + (np.log(np.maximum(distance, 1) / exact_count) / np.log(MAXDIST / exact_count) * (half_count - exact_count)).astype(np.int64)
    far_bucket = np.minimum(far_bucket, half_count - 1)
    return (upper + np.where(distance < exact_count, distance, far_bucket)).astype(np.int32)

def rms_norm(values, gain):
    return values * lax.rsqrt(lax.optimization_barrier(jnp.mean(values * values, axis=-1, keepdims=True)) + NORM_EPS) * gain

def project(values, weight):
    return jnp.einsum('...d,df->...f', values, weight, precision=HIGHEST)

def encode(tokens, lengths, weights, length):
    embed_low, square_low, expand_low, reduce_low, gain_low, position_bias = weights
    batch_rows = tokens.shape[0]
    key_mask = jnp.arange(length)[None, :] < lengths[:, None]
    start_rows = jnp.take(embed_low, tokens, axis=0)
    normed_one = low(rms_norm(start_rows, gain_low[0]))

    def heads_of(weight):
        return low(low_back(project(normed_one, weight))).reshape(batch_rows, length, HEADS, HEAD)
    queries = heads_of(square_low[0])
    keys_here = heads_of(square_low[1])
    values_here = heads_of(square_low[2])
    bias_table = jnp.transpose(position_bias[bucket_table(length)], (2, 0, 1))
    scores = low_back(jnp.einsum('bqhe,bkhe->bhqk', queries, keys_here, precision=HIGHEST) * HEAD ** (-0.5) + bias_table[None])
    scores = jnp.where(key_mask[:, None, None, :], scores, -1e+30)
    attend = low(jax.nn.softmax(scores, axis=-1))
    mixed_heads = low(low_back(jnp.einsum('bhqk,bkhe->bqhe', attend, values_here, precision=HIGHEST))).reshape(batch_rows, length, D)
    middle = start_rows + low_back(project(mixed_heads, square_low[3]))
    normed_two = low(rms_norm(middle, gain_low[1]))
    hidden_pre = low_back(project(normed_two, expand_low))
    ending = middle + low_back(project(low(jax.nn.gelu(hidden_pre)), reduce_low))
    output = rms_norm(ending, gain_low[2])
    pooled = low(lax.optimization_barrier(jnp.sum(jnp.where(key_mask[:, :, None], output, 0.0), axis=1)) / lengths[:, None].astype(jnp.float32))
    projected = low_back(project(pooled, square_low[4]))
    return projected * lax.rsqrt(lax.optimization_barrier(jnp.sum(projected * projected, axis=-1, keepdims=True)) + NORM_EPS)

def encode_all(tokens, lengths, weights, length):
    total_rows = tokens.shape[0]
    block_rows = math.gcd(total_rows, max(1, 4096 // length))

    def one_block(block_pair):
        return encode(block_pair[0], block_pair[1], weights, length)
    result = lax.map(jax.checkpoint(one_block), (tokens.reshape(-1, block_rows, length), lengths.reshape(-1, block_rows)))
    return result.reshape(total_rows, D)

def contrast(left, right, scale, extra):
    sims = low_back(jnp.dot(low(left), low(right).T, precision=HIGHEST))
    logits = scale * sims
    spread = jax.nn.logsumexp(logits, axis=1, b=1.0 + extra)
    return jnp.sum(spread - jnp.diagonal(logits))

def adam_update(weight, moment, second, grad, factor, rate):
    clipped = grad * factor
    moment_new = BETA_ONE * moment + (1 - BETA_ONE) * clipped
    second_new = BETA_TWO * second + (1 - BETA_TWO) * clipped * clipped
    moment_hat = moment_new / (1 - BETA_ONE ** STEP)
    second_hat = second_new / (1 - BETA_TWO ** STEP)
    updated = weight - rate * (moment_hat / (jnp.sqrt(second_hat) + ADAM_EPS) + WEIGHT_DECAY * weight)
    return (moment_new, second_new, updated)

def reference(embed_table, square_weights, expand_weight, reduce_weight, norm_gains, position_bias, log_scale, table_moment, table_second, square_moment, square_second, expand_moment, expand_second, reduce_moment, reduce_second, gains_moment, gains_second, position_moment, position_second, scale_moment, scale_second, query_tokens, answer_tokens, query_length, answer_length, premise_tokens, hypothesis_tokens, hard_negative):
    full_length = jnp.full((NLI_PAIRS,), LN, jnp.int32)
    negatives = (jnp.arange(NLI_PAIRS)[None, :] == hard_negative[:, None]).astype(jnp.float32)
    no_extra = jnp.zeros((QA_PAIRS, QA_PAIRS), jnp.float32)

    def objective(params):
        table_val, square_val, expand_val, reduce_val, gain_val, position_val, scale_val = params
        weights = (low(table_val).T, low(square_val), low(expand_val), low(reduce_val), low(gain_val), position_val)
        queries = encode_all(query_tokens, query_length, weights, LQ)
        answers = encode_all(answer_tokens, answer_length, weights, LA)
        premises = encode_all(premise_tokens, full_length, weights, LN)
        hypotheses = encode_all(hypothesis_tokens, full_length, weights, LN)
        scale = jnp.exp(scale_val[0])
        first_loss = contrast(queries, answers, scale, no_extra)
        second_loss = contrast(premises, hypotheses, scale, negatives)
        return (first_loss + second_loss, jnp.stack([first_loss, second_loss]))
    params = (embed_table, square_weights, expand_weight, reduce_weight, norm_gains, position_bias, log_scale)
    total_loss, pull_back, losses = jax.vjp(objective, params, has_aux=True)
    grads = pull_back(jnp.ones_like(total_loss))[0]
    square_sum = sum((jnp.sum(grad * grad) for grad in grads))
    gradient_norm = jnp.sqrt(square_sum)
    factor = jnp.minimum(1.0, CLIP_NORM / gradient_norm)
    table_out = adam_update(embed_table, table_moment, table_second, grads[0], factor, TABLE_RATE)
    square_out = adam_update(square_weights, square_moment, square_second, grads[1], factor, LEARN_RATE)
    expand_out = adam_update(expand_weight, expand_moment, expand_second, grads[2], factor, LEARN_RATE)
    reduce_out = adam_update(reduce_weight, reduce_moment, reduce_second, grads[3], factor, LEARN_RATE)
    gains_out = adam_update(norm_gains, gains_moment, gains_second, grads[4], factor, SMALL_RATE)
    position_out = adam_update(position_bias, position_moment, position_second, grads[5], factor, SMALL_RATE)
    scale_out = adam_update(log_scale, scale_moment, scale_second, grads[6], factor, SMALL_RATE)
    return (table_out[0], table_out[1], table_out[2], square_out[0], square_out[1], square_out[2], expand_out[0], expand_out[1], expand_out[2], reduce_out[0], reduce_out[1], reduce_out[2], gains_out[0], gains_out[1], gains_out[2], position_out[0], position_out[1], position_out[2], scale_out[0], scale_out[1], scale_out[2], losses, gradient_norm)
```

```python
import functools

import jax
import jax.numpy as jnp
import numpy as np
from jax import lax
from jax.experimental import pallas as pl
from jax.experimental.pallas import tpu as pltpu
from jax.sharding import PartitionSpec as P

D = 768
HEADS = 12
HEAD = 64
BUCKETS = 32
MAXDIST = 128
STEP = 10


HIGHEST = lax.Precision.HIGHEST
NORM_EPS = 1e-06
LEARN_RATE = 0.03
TABLE_RATE = 0.4
SMALL_RATE = 0.5
BETA_ONE = 0.9
BETA_TWO = 0.999
ADAM_EPS = 1e-08
WEIGHT_DECAY = 0.01
CLIP_NORM = 0.5


def bucket_table(length):
    places = np.arange(length)
    offset = places[None, :] - places[:, None]
    half_count = BUCKETS // 2
    exact_count = half_count // 2
    upper = (offset > 0).astype(np.int64) * half_count
    distance = np.abs(offset)
    far_bucket = exact_count + (
        np.log(np.maximum(distance, 1) / exact_count)
        / np.log(MAXDIST / exact_count)
        * (half_count - exact_count)
    ).astype(np.int64)
    far_bucket = np.minimum(far_bucket, half_count - 1)
    return (upper + np.where(distance < exact_count, distance, far_bucket)).astype(np.int32)


def bucket_onehot(length):
    flat_table = bucket_table(length).reshape(-1)
    return jnp.asarray((flat_table[:, None] == np.arange(BUCKETS)[None, :]).astype(np.float32))


def product(left, right):
    return jnp.dot(left, right, preferred_element_type=jnp.float32)


def product_left(left, right):
    return lax.dot_general(
        left, right, (((0,), (0,)), ((), ())), preferred_element_type=jnp.float32
    )


def product_right(left, right):
    return lax.dot_general(
        left, right, (((1,), (1,)), ((), ())), preferred_element_type=jnp.float32
    )


def norm_scale(values):
    return lax.rsqrt(jnp.mean(values * values, axis=-1, keepdims=True) + NORM_EPS)


def norm_back(values, scale, gain, grad):
    weighted = grad * gain
    inner = jnp.mean(weighted * values, axis=-1, keepdims=True)
    return (scale * weighted - values * scale**3 * inner, jnp.sum(grad * values * scale, axis=0))


def attention_bias(position_bias, length):
    onehot = bucket_onehot(length)
    flat_bias = jnp.dot(onehot, position_bias, precision=HIGHEST)
    return (jnp.transpose(flat_bias.reshape(length, length, HEADS), (2, 0, 1)), onehot)


def attention_scores(queries, keys_here, bias_table, key_mask):
    scores = (
        jnp.einsum("bqhe,bkhe->bhqk", queries, keys_here, preferred_element_type=jnp.float32)
        * HEAD ** (-0.5)
        + bias_table[None]
    )
    return jnp.where(key_mask[:, None, None, :], scores, -1e30)


def layer_forward(start_rows, key_mask, layer, length):
    square_low, expand_low, reduce_low, gain_rows, position_bias = layer
    head_shape = (key_mask.shape[0], length, HEADS, HEAD)
    scale_one = norm_scale(start_rows)
    normed_one = (start_rows * scale_one * gain_rows[0]).astype(jnp.bfloat16)
    queries = product(normed_one, square_low[0]).astype(jnp.bfloat16)
    keys_here = product(normed_one, square_low[1]).astype(jnp.bfloat16)
    values_here = product(normed_one, square_low[2]).astype(jnp.bfloat16)
    bias_table, onehot = attention_bias(position_bias, length)
    scores = attention_scores(
        queries.reshape(head_shape), keys_here.reshape(head_shape), bias_table, key_mask
    )
    row_top = jnp.max(scores, axis=-1, keepdims=True)
    raised = jnp.exp(scores - row_top)
    row_total = jnp.sum(raised, axis=-1, keepdims=True)
    log_total = row_top + jnp.log(row_total)
    attend = (raised / row_total).astype(jnp.bfloat16)
    mixed_heads = (
        jnp.einsum(
            "bhqk,bkhe->bqhe",
            attend,
            values_here.reshape(head_shape),
            preferred_element_type=jnp.float32,
        )
        .reshape(-1, D)
        .astype(jnp.bfloat16)
    )
    middle = start_rows + product(mixed_heads, square_low[3])
    scale_two = norm_scale(middle)
    normed_two = (middle * scale_two * gain_rows[1]).astype(jnp.bfloat16)
    hidden_pre = product(normed_two, expand_low)
    hidden_act = jax.nn.gelu(hidden_pre).astype(jnp.bfloat16)
    ending = middle + product(hidden_act, reduce_low)
    scale_three = norm_scale(ending)
    output = ending * scale_three * gain_rows[2]
    stored = (
        start_rows,
        scale_one,
        normed_one,
        queries,
        keys_here,
        values_here,
        log_total,
        mixed_heads,
        middle,
        scale_two,
        normed_two,
        hidden_pre,
        hidden_act,
        ending,
        scale_three,
    )
    return (output, stored)


def layer_backward(grad_out, key_mask, layer, stored, length):
    square_low, expand_low, reduce_low, gain_rows, position_bias = layer
    (
        start_rows,
        scale_one,
        normed_one,
        queries,
        keys_here,
        values_here,
        log_total,
        mixed_heads,
        middle,
        scale_two,
        normed_two,
        hidden_pre,
        hidden_act,
        ending,
        scale_three,
    ) = stored
    head_shape = (key_mask.shape[0], length, HEADS, HEAD)
    grad_end, gain_three = norm_back(ending, scale_three, gain_rows[2], grad_out)
    grad_end_low = grad_end.astype(jnp.bfloat16)
    grad_reduce = product_left(hidden_act, grad_end_low)
    grad_act = product_right(grad_end_low, reduce_low)
    grad_pre = jax.vjp(jax.nn.gelu, hidden_pre)[1](grad_act)[0].astype(jnp.bfloat16)
    grad_expand = product_left(normed_two, grad_pre)
    grad_normed_two = product_right(grad_pre, expand_low)
    grad_mid_norm, gain_two = norm_back(middle, scale_two, gain_rows[1], grad_normed_two)
    grad_middle = grad_end + grad_mid_norm
    grad_mid_low = grad_middle.astype(jnp.bfloat16)
    grad_output_proj = product_left(mixed_heads, grad_mid_low)
    grad_mixed = product_right(grad_mid_low, square_low[3]).astype(jnp.bfloat16).reshape(head_shape)
    bias_table, onehot = attention_bias(position_bias, length)
    query_heads = queries.reshape(head_shape)
    key_heads = keys_here.reshape(head_shape)
    value_heads = values_here.reshape(head_shape)
    scores = attention_scores(query_heads, key_heads, bias_table, key_mask)
    attend_full = jnp.exp(scores - log_total)
    attend = attend_full.astype(jnp.bfloat16)
    grad_attend = jnp.einsum(
        "bqhe,bkhe->bhqk", grad_mixed, value_heads, preferred_element_type=jnp.float32
    )
    grad_values = (
        jnp.einsum("bhqk,bqhe->bkhe", attend, grad_mixed, preferred_element_type=jnp.float32)
        .astype(jnp.bfloat16)
        .reshape(-1, D)
    )
    grad_scores = attend_full * (
        grad_attend - jnp.sum(grad_attend * attend_full, axis=-1, keepdims=True)
    )
    grad_scores_low = grad_scores.astype(jnp.bfloat16)
    grad_queries = (
        (
            jnp.einsum(
                "bhqk,bkhe->bqhe", grad_scores_low, key_heads, preferred_element_type=jnp.float32
            )
            * HEAD ** (-0.5)
        )
        .astype(jnp.bfloat16)
        .reshape(-1, D)
    )
    grad_keys = (
        (
            jnp.einsum(
                "bhqk,bqhe->bkhe", grad_scores_low, query_heads, preferred_element_type=jnp.float32
            )
            * HEAD ** (-0.5)
        )
        .astype(jnp.bfloat16)
        .reshape(-1, D)
    )
    summed_scores = jnp.sum(grad_scores_low.astype(jnp.float32), axis=0).reshape(
        HEADS, length * length
    )
    grad_position = lax.dot_general(
        onehot, summed_scores, (((0,), (1,)), ((), ())), precision=HIGHEST
    )
    grad_normed_one = (
        product_right(grad_queries, square_low[0])
        + product_right(grad_keys, square_low[1])
        + product_right(grad_values, square_low[2])
    )
    grad_start_norm, gain_one = norm_back(start_rows, scale_one, gain_rows[0], grad_normed_one)
    grad_start = grad_middle + grad_start_norm
    grad_squares = jnp.stack(
        [
            product_left(normed_one, grad_queries),
            product_left(normed_one, grad_keys),
            product_left(normed_one, grad_values),
            grad_output_proj,
        ]
    )
    return (
        grad_start,
        (
            grad_squares,
            grad_expand,
            grad_reduce,
            jnp.stack([gain_one, gain_two, gain_three]),
            grad_position,
        ),
    )


def contrast_local(left_low, right_low, scale, extra, target):
    sims = product_right(left_low, right_low)
    logits = scale * sims
    row_top = jnp.max(logits, axis=1, keepdims=True)
    raised = (1.0 + extra) * jnp.exp(logits - row_top)
    row_total = jnp.sum(raised, axis=1, keepdims=True)
    spread = row_top[:, 0] + jnp.log(row_total[:, 0])
    target_hit = jnp.arange(right_low.shape[0])[None, :] == target[:, None]
    loss_sum = jnp.sum(spread - jnp.sum(jnp.where(target_hit, logits, 0.0), axis=1))
    grad_logits = raised / row_total - target_hit.astype(jnp.float32)
    grad_scale = jnp.sum(grad_logits * sims)
    grad_sims = (scale * grad_logits).astype(jnp.bfloat16)
    return (loss_sum, grad_scale, product(grad_sims, right_low), product_left(grad_sims, left_low))


def pool_rows(output, key_mask, lengths, length):
    shaped = output.reshape(key_mask.shape[0], length, D)
    return jnp.sum(jnp.where(key_mask[:, :, None], shaped, 0.0), axis=1) / lengths[:, None].astype(
        jnp.float32
    )


def spread_rows(grad_rows, key_mask, lengths):
    spread = jnp.where(key_mask[:, :, None], grad_rows[:, None, :], 0.0) / lengths[
        :, None, None
    ].astype(jnp.float32)
    return spread.reshape(-1, D)


def adam_update(weight, moment, second, grad, factor, rate):
    clipped = grad * factor
    moment_new = BETA_ONE * moment + (1 - BETA_ONE) * clipped
    second_new = BETA_TWO * second + (1 - BETA_TWO) * clipped * clipped
    moment_hat = moment_new / (1 - BETA_ONE**STEP)
    second_hat = second_new / (1 - BETA_TWO**STEP)
    updated = weight - rate * (
        moment_hat / (jnp.sqrt(second_hat) + ADAM_EPS) + WEIGHT_DECAY * weight
    )
    return (moment_new, second_new, updated)


LANES = 128
GROUPS = 4
SLOT = LANES // GROUPS
VMEM_CAP = 48 * 1024 * 1024

def fold_rows(vocab):
    per = -(-vocab // GROUPS)
    return -(-per // LANES) * LANES

def up8(n):
    return -(-n // 8) * 8

def eye():
    r = lax.broadcasted_iota(jnp.int32, (LANES, LANES), 0)
    c = lax.broadcasted_iota(jnp.int32, (LANES, LANES), 1)
    return (r == c).astype(jnp.float32).astype(jnp.bfloat16)

def lookup_kernel(fold, row_ref, group_ref, table_ref, out_ref, turned, rows):
    feats, vocab = table_ref.shape
    tokens = rows.shape[0]
    @pl.when(pl.program_id(0) == 0)
    def _():
        pad = jnp.zeros((SLOT - feats, LANES), jnp.float32)
        def build(b, _):
            parts = []
            for j in range(GROUPS):
                start = jnp.minimum(j * fold + b * LANES, vocab - LANES)
                start = pl.multiple_of(start, LANES)
                parts += [table_ref[:, pl.ds(start, LANES)], pad]
            tile = jnp.concatenate(parts, axis=0)
            turned[pl.ds(pl.multiple_of(b * LANES, LANES), LANES), :] = tile.T
            return 0
        lax.fori_loop(0, fold // LANES, build, 0)
        turned[pl.ds(fold, 8), :] = jnp.zeros((8, LANES), jnp.float32)
    UN = 32
    def fetch(b, _):
        for k in range(UN):
            t = b * UN + k
            rows[pl.ds(t, 1), :] = turned[pl.ds(row_ref[0, 0, t], 1), :]
        return 0
    lax.fori_loop(0, tokens // UN, fetch, 0)
    wide = lax.dot_general(eye(), rows[...].astype(jnp.bfloat16), (((1,), (1,)), ((), ())), preferred_element_type=jnp.float32)
    group = group_ref[0]
    total = jnp.where(group == 0, wide[:SLOT], 0.0)
    for j in range(1, GROUPS):
        total = total + jnp.where(group == j, wide[j * SLOT:(j + 1) * SLOT], 0.0)
    half = tokens // 2
    out_ref[0] = jnp.concatenate([total[:feats, :half], total[:feats, half:]], axis=0).astype(jnp.bfloat16)

def lookup(table, rows_idx, groups_idx):
    feats, vocab = table.shape
    n, tokens = rows_idx.shape[0], rows_idx.shape[2]
    fold = fold_rows(vocab)
    return pl.pallas_call(
        functools.partial(lookup_kernel, fold),
        grid=(n,),
        out_shape=jax.ShapeDtypeStruct((n, 2 * feats, tokens // 2), jnp.bfloat16),
        in_specs=[
            pl.BlockSpec((1, 1, tokens), lambda s: (s, 0, 0), memory_space=pltpu.SMEM),
            pl.BlockSpec((1, 1, tokens), lambda s: (s, 0, 0)),
            pl.BlockSpec((feats, vocab), lambda s: (0, 0)),
        ],
        out_specs=pl.BlockSpec((1, 2 * feats, tokens // 2), lambda s: (s, 0, 0)),
        scratch_shapes=[pltpu.VMEM((fold + 8, LANES), jnp.float32), pltpu.VMEM((tokens, LANES), jnp.float32)],
        compiler_params=pltpu.CompilerParams(vmem_limit_bytes=VMEM_CAP),
        name="lookup",
    )(rows_idx, groups_idx, table)

def scatter_kernel(fold, row_ref, group_ref, grad_ref, out_ref, total, rows):
    feats, vocab = out_ref.shape
    tokens = rows.shape[0]
    step = pl.program_id(0)
    @pl.when(step == 0)
    def _():
        def clear(b, _):
            total[pl.ds(pl.multiple_of(b * LANES, LANES), LANES), :] = jnp.zeros((LANES, LANES), jnp.float32)
            return 0
        lax.fori_loop(0, fold // LANES, clear, 0)
        total[pl.ds(fold, 8), :] = jnp.zeros((8, LANES), jnp.float32)
    block = grad_ref[0].astype(jnp.float32)
    flat = jnp.concatenate([block[:feats], block[feats:]], axis=1)
    group = group_ref[0]
    pad = jnp.zeros((SLOT - feats, tokens), jnp.float32)
    parts = []
    for j in range(GROUPS):
        parts += [jnp.where(group == j, flat, 0.0), pad]
    spread = jnp.concatenate(parts, axis=0).astype(jnp.bfloat16)
    rows[...] = lax.dot_general(spread, eye(), (((0,), (0,)), ((), ())), preferred_element_type=jnp.float32)
    LN = 16
    stride = tokens // LN
    def add(i, _):
        at = [row_ref[0, 0, i + stride * k] for k in range(LN)]
        new = [total[pl.ds(at[k], 1), :] + rows[pl.ds(i + stride * k, 1), :] for k in range(LN)]
        for k in range(LN):
            total[pl.ds(at[k], 1), :] = new[k]
        return 0
    lax.fori_loop(0, stride, add, 0, unroll=2)
    @pl.when(step == pl.num_programs(0) - 1)
    def _():
        whole = (vocab - (GROUPS - 1) * fold) // LANES
        def turn(b, _):
            tile = total[pl.ds(pl.multiple_of(b * LANES, LANES), LANES), :].T
            for j in range(GROUPS):
                out_ref[:, pl.ds(pl.multiple_of(j * fold + b * LANES, LANES), LANES)] = tile[j * SLOT:j * SLOT + feats]
            return 0
        lax.fori_loop(0, whole, turn, 0)
        for b in range(whole, fold // LANES):
            tile = total[pl.ds(b * LANES, LANES), :].T
            for j in range(GROUPS - 1):
                out_ref[:, pl.ds(j * fold + b * LANES, LANES)] = tile[j * SLOT:j * SLOT + feats]

def scatter(grads, rows_idx, groups_idx, vocab):
    n, tokens = rows_idx.shape[0], rows_idx.shape[2]
    feats = grads.shape[1] // 2
    fold = fold_rows(vocab)
    return pl.pallas_call(
        functools.partial(scatter_kernel, fold),
        grid=(n,),
        out_shape=jax.ShapeDtypeStruct((feats, vocab), jnp.float32),
        in_specs=[
            pl.BlockSpec((1, 1, tokens), lambda s: (s, 0, 0), memory_space=pltpu.SMEM),
            pl.BlockSpec((1, 1, tokens), lambda s: (s, 0, 0)),
            pl.BlockSpec((1, 2 * feats, tokens // 2), lambda s: (s, 0, 0)),
        ],
        out_specs=pl.BlockSpec((feats, vocab), lambda s: (0, 0)),
        scratch_shapes=[pltpu.VMEM((fold + 8, LANES), jnp.float32), pltpu.VMEM((tokens, LANES), jnp.float32)],
        compiler_params=pltpu.CompilerParams(vmem_limit_bytes=VMEM_CAP),
        name="scatter",
    )(rows_idx, groups_idx, grads)

def token_keys(tokens, fold):
    count = tokens.shape[0]
    key = (tokens % fold) * GROUPS + tokens // fold
    places = jnp.arange(count, dtype=jnp.int32)
    same_before = (key[:, None] == key[None, :]) & (places[:, None] < places[None, :])
    first = ~jnp.any(same_before, axis=0)
    rank = jnp.sum(((key[None, :] < key[:, None]) & first[None, :]).astype(jnp.int32), axis=1)
    hit = rank[:, None] == places[None, :]
    packed = GROUPS * fold + jnp.sum(jnp.where(hit & first[:, None], key[:, None] - GROUPS * fold, 0), axis=0)
    return packed, hit.astype(jnp.bfloat16)


MESH = pl.DeviceIdType.MESH


def exchange_kernel(same, src, dst, send_sem, recv_sem, own_sem):
    rows, cols = lax.axis_size("dp"), lax.axis_size("fsdp")
    count = rows * cols
    me = lax.axis_index("dp") * cols + lax.axis_index("fsdp")
    barrier = pltpu.get_barrier_semaphore()

    def device(k):
        to = lax.rem(me + k, count)
        return (to // cols, lax.rem(to, cols))

    def greet(k, carry):
        pl.semaphore_signal(barrier, inc=1, device_id=device(k), device_id_type=MESH)
        return carry

    def copy(k):
        to = lax.rem(me + k, count)
        return pltpu.make_async_remote_copy(
            src_ref=src.at[0 if same else to],
            dst_ref=dst.at[me],
            send_sem=send_sem.at[k],
            recv_sem=recv_sem.at[k],
            device_id=device(k),
            device_id_type=MESH,
        )

    def start(k, carry):
        copy(k).start()
        return carry

    def end(k, carry):
        copy(k).wait()
        return carry

    lax.fori_loop(1, count, greet, 0)
    own = pltpu.make_async_copy(src.at[0 if same else me], dst.at[me], own_sem)
    own.start()
    pl.semaphore_wait(barrier, count - 1)
    lax.fori_loop(1, count, start, 0)
    own.wait()
    lax.fori_loop(1, count, end, 0)


def exchange(blocks, same, call_id, name):
    count = lax.axis_size("dp") * lax.axis_size("fsdp")
    return pl.pallas_call(
        functools.partial(exchange_kernel, same),
        out_shape=jax.ShapeDtypeStruct((count,) + blocks.shape[1:], blocks.dtype),
        in_specs=[pl.BlockSpec(memory_space=pl.ANY)],
        out_specs=pl.BlockSpec(memory_space=pl.ANY),
        scratch_shapes=[
            pltpu.SemaphoreType.DMA((count,)),
            pltpu.SemaphoreType.DMA((count,)),
            pltpu.SemaphoreType.DMA,
        ],
        compiler_params=pltpu.CompilerParams(collective_id=call_id, has_side_effects=True),
        name=name,
    )(blocks)


def shards(
    embed_table,
    square_weights,
    expand_weight,
    reduce_weight,
    norm_gains,
    position_bias,
    log_scale,
    table_moment,
    table_second,
    square_moment,
    square_second,
    expand_moment,
    expand_second,
    reduce_moment,
    reduce_second,
    gains_moment,
    gains_second,
    position_moment,
    position_second,
    scale_moment,
    scale_second,
    query_tokens,
    answer_tokens,
    query_length,
    answer_length,
    premise_tokens,
    hypothesis_tokens,
    hard_negative,
):
    both = ("dp", "fsdp")
    count = lax.axis_size("dp") * lax.axis_size("fsdp")
    feats, vocab_size = embed_table.shape
    feats_pad = up8(feats)
    fold = fold_rows(vocab_size)
    query_rows = query_tokens.shape[0]
    nli_rows = premise_tokens.shape[0]
    short_length = query_tokens.shape[1]
    long_length = answer_tokens.shape[1]
    short_tokens = jnp.concatenate([query_tokens, premise_tokens, hypothesis_tokens], axis=0)
    short_lengths = jnp.concatenate(
        [query_length, jnp.full((2 * nli_rows,), short_length, jnp.int32)]
    )
    all_tokens = jnp.concatenate([short_tokens.reshape(-1), answer_tokens.reshape(-1)])
    token_count = all_tokens.shape[0]
    packed, hit = token_keys(all_tokens, fold)
    packed_all = exchange(packed.reshape(1, -1, LANES), True, 0, "share_keys")
    packed_all = packed_all.reshape(count, 1, token_count)
    row_all, group_all = packed_all >> 2, packed_all & 3

    def gather_layer():
        def whole(weight, row_axis):
            low = weight.astype(jnp.bfloat16)
            parts = lax.all_gather(low, both, axis=0, tiled=False)
            dp, fsdp = lax.axis_size("dp"), lax.axis_size("fsdp")
            parts = parts.reshape((dp, fsdp) + low.shape)
            lead = tuple(range(2, 2 + row_axis))
            order = lead + (0, 2 + row_axis, 1, 3 + row_axis)
            shape = low.shape[:row_axis] + (dp * low.shape[row_axis], fsdp * low.shape[row_axis + 1])
            return parts.transpose(order).reshape(shape)

        gains = exchange(jnp.pad(norm_gains, ((0, 5), (0, LANES - feats)))[None], True, 1, "share_gains")
        gains = gains[:, :3, :feats].transpose(1, 0, 2).reshape(3, D)
        return (
            whole(square_weights, 1),
            whole(expand_weight, 0),
            whole(reduce_weight, 0),
            gains.astype(jnp.bfloat16).astype(jnp.float32),
            position_bias,
        )

    layer = gather_layer()
    table_low = embed_table.astype(jnp.bfloat16).astype(jnp.float32)
    if feats_pad > feats:
        table_low = jnp.pad(table_low, ((0, feats_pad - feats), (0, 0)))
    found = exchange(lookup(table_low, row_all, group_all), False, 2, "send_features")
    half = token_count // 2
    found = found.reshape(count, 2, feats_pad, half)[:, :, :feats]
    found = found.transpose(0, 2, 1, 3).reshape(D, token_count)
    embedded = product_right(hit, found)
    split_at = short_tokens.shape[0] * short_length
    short_mask = jnp.arange(short_length)[None, :] < short_lengths[:, None]
    long_mask = jnp.arange(long_length)[None, :] < answer_length[:, None]
    short_out, short_stored = layer_forward(embedded[:split_at], short_mask, layer, short_length)
    long_out, long_stored = layer_forward(embedded[split_at:], long_mask, layer, long_length)
    pooled = jnp.concatenate(
        [
            pool_rows(short_out, short_mask, short_lengths, short_length),
            pool_rows(long_out, long_mask, answer_length, long_length),
        ],
        axis=0,
    )
    pooled_low = pooled.astype(jnp.bfloat16)
    projected = product(pooled_low, layer[0][4])
    inverse = lax.rsqrt(jnp.sum(projected * projected, axis=-1, keepdims=True) + NORM_EPS)
    embeds = projected * inverse
    embeds_low = embeds.astype(jnp.bfloat16)
    hypo_start = query_rows + nli_rows
    answer_start = query_rows + 2 * nli_rows
    seq_count = answer_start + query_rows
    seq_pad = -(-seq_count // 16) * 16
    gathered = exchange(
        jnp.pad(embeds_low, ((0, seq_pad - seq_count), (0, 0)))[None], True, 3, "share_embeds"
    )
    negative_all = exchange(
        jnp.pad(hard_negative, (0, 8 * LANES - nli_rows)).reshape(1, 8, LANES), True, 4, "share_negatives"
    ).reshape(count, -1)[:, :nli_rows].reshape(-1)
    queries_all = gathered[:, :query_rows].reshape(-1, D)
    premises_all = gathered[:, query_rows:hypo_start].reshape(-1, D)
    hypotheses_all = gathered[:, hypo_start:answer_start].reshape(-1, D)
    answers_all = gathered[:, answer_start:seq_count].reshape(-1, D)
    scale = jnp.exp(log_scale[0])
    position = lax.axis_index(both)

    def contrast(left, right, extra, own):
        sims = product_right(left, right)
        logits = scale * sims
        row_top = jnp.max(logits, axis=1, keepdims=True)
        raised = (1.0 + extra) * jnp.exp(logits - row_top)
        row_total = jnp.sum(raised, axis=1, keepdims=True)
        spread = row_top[:, 0] + jnp.log(row_total[:, 0])
        target_hit = jnp.eye(left.shape[0], dtype=jnp.float32)
        loss_sum = jnp.sum(spread - jnp.sum(target_hit * logits, axis=1))
        grad_logits = raised / row_total - target_hit
        grad_scale = jnp.sum(grad_logits * sims)
        grad_sims = (scale * grad_logits).astype(jnp.bfloat16)
        mine_left = lax.dynamic_slice_in_dim(grad_sims, position * own, own, 0)
        mine_right = lax.dynamic_slice_in_dim(grad_sims, position * own, own, 1)
        return (loss_sum, grad_scale, product(mine_left, right), product_left(mine_right, left))

    first_loss, first_dscale, grad_queries, grad_answers = contrast(
        queries_all, answers_all, 0.0, query_rows
    )
    negatives = (jnp.arange(hypotheses_all.shape[0])[None, :] == negative_all[:, None]).astype(
        jnp.float32
    )
    second_loss, second_dscale, grad_premises, grad_hypotheses = contrast(
        premises_all, hypotheses_all, negatives, nli_rows
    )
    grad_embeds = jnp.concatenate(
        [grad_queries, grad_premises, grad_hypotheses, grad_answers], axis=0
    )
    grad_projected = (
        inverse * (grad_embeds - embeds * jnp.sum(grad_embeds * embeds, axis=-1, keepdims=True))
    ).astype(jnp.bfloat16)
    grad_proj_weight = product_left(pooled_low, grad_projected)
    grad_pooled = product_right(grad_projected, layer[0][4])
    short_rows = short_tokens.shape[0]
    grad_short_start, short_grads = layer_backward(
        spread_rows(grad_pooled[:short_rows], short_mask, short_lengths),
        short_mask,
        layer,
        short_stored,
        short_length,
    )
    grad_long_start, long_grads = layer_backward(
        spread_rows(grad_pooled[short_rows:], long_mask, answer_length),
        long_mask,
        layer,
        long_stored,
        long_length,
    )
    grad_squares = jnp.concatenate([short_grads[0] + long_grads[0], grad_proj_weight[None]], axis=0)
    grad_expand = short_grads[1] + long_grads[1]
    grad_reduce = short_grads[2] + long_grads[2]
    grad_gains = short_grads[3] + long_grads[3]
    grad_position = short_grads[4] + long_grads[4]
    grad_scale = ((first_dscale + second_dscale) * scale).reshape(1)
    grad_tokens = jnp.concatenate([grad_short_start, grad_long_start], axis=0)
    merged = product_left(grad_tokens.astype(jnp.bfloat16), hit).astype(jnp.bfloat16)
    merged = merged.reshape(count, feats, 2, half).transpose(0, 2, 1, 3)
    if feats_pad > feats:
        merged = jnp.pad(merged, ((0, 0), (0, 0), (0, feats_pad - feats), (0, 0)))
    returned = exchange(merged.reshape(count, 2 * feats_pad, half), False, 5, "send_gradients")
    grad_table = scatter(returned, row_all, group_all, vocab_size)[:feats]
    squares_part = lax.psum_scatter(grad_squares, "dp", scatter_dimension=1, tiled=True)
    reduced = (
        lax.psum_scatter(squares_part, "fsdp", scatter_dimension=2, tiled=True),
        lax.psum_scatter(
            lax.psum_scatter(grad_expand, "dp", scatter_dimension=0, tiled=True),
            "fsdp", scatter_dimension=1, tiled=True),
        lax.psum_scatter(
            lax.psum_scatter(grad_reduce, "dp", scatter_dimension=0, tiled=True),
            "fsdp", scatter_dimension=1, tiled=True),
    )
    local_square = (
        jnp.sum(reduced[0] * reduced[0])
        + jnp.sum(reduced[1] * reduced[1])
        + jnp.sum(reduced[2] * reduced[2])
        + jnp.sum(grad_table * grad_table)
    )
    small = jnp.concatenate([grad_gains.reshape(-1), grad_position.reshape(-1), local_square.reshape(1)])
    small_rows = -(-small.shape[0] // (8 * LANES)) * 8
    small = jnp.pad(small, (0, small_rows * LANES - small.shape[0])).reshape(1, small_rows, LANES)
    summed = jnp.sum(exchange(small, True, 6, "share_small"), axis=0).reshape(-1)
    gains_total = summed[: 3 * D].reshape(3, D)
    position_total = summed[3 * D : 3 * D + BUCKETS * HEADS].reshape(BUCKETS, HEADS)
    square_total = summed[3 * D + BUCKETS * HEADS]
    scale_total = grad_scale
    losses = jnp.stack([first_loss, second_loss])
    grad_gain_shard = lax.dynamic_slice_in_dim(gains_total, position * feats, feats, 1)
    gradient_norm = jnp.sqrt(
        square_total
        + jnp.sum(gains_total * gains_total)
        + jnp.sum(position_total * position_total)
        + jnp.sum(scale_total * scale_total)
    )
    factor = jnp.minimum(1.0, CLIP_NORM / gradient_norm)
    table_out = adam_update(embed_table, table_moment, table_second, grad_table, factor, TABLE_RATE)
    square_out = adam_update(
        square_weights, square_moment, square_second, reduced[0], factor, LEARN_RATE
    )
    expand_out = adam_update(
        expand_weight, expand_moment, expand_second, reduced[1], factor, LEARN_RATE
    )
    reduce_out = adam_update(
        reduce_weight, reduce_moment, reduce_second, reduced[2], factor, LEARN_RATE
    )
    gains_out = adam_update(
        norm_gains, gains_moment, gains_second, grad_gain_shard, factor, SMALL_RATE
    )
    position_out = adam_update(
        position_bias, position_moment, position_second, position_total, factor, SMALL_RATE
    )
    scale_out = adam_update(log_scale, scale_moment, scale_second, scale_total, factor, SMALL_RATE)
    return (
        *table_out,
        *square_out,
        *expand_out,
        *reduce_out,
        *gains_out,
        *position_out,
        *scale_out,
        losses,
        gradient_norm,
    )


def solution(mesh):
    return jax.shard_map(
        shards,
        mesh=mesh,
        in_specs=(
            P(("dp", "fsdp"), None),
            P(None, "dp", "fsdp"),
            P("dp", "fsdp"),
            P("dp", "fsdp"),
            P(None, ("dp", "fsdp")),
            P(),
            P(),
            P(("dp", "fsdp"), None),
            P(("dp", "fsdp"), None),
            P(None, "dp", "fsdp"),
            P(None, "dp", "fsdp"),
            P("dp", "fsdp"),
            P("dp", "fsdp"),
            P("dp", "fsdp"),
            P("dp", "fsdp"),
            P(None, ("dp", "fsdp")),
            P(None, ("dp", "fsdp")),
            P(),
            P(),
            P(),
            P(),
            P(("dp", "fsdp"), None),
            P(("dp", "fsdp"), None),
            P(("dp", "fsdp")),
            P(("dp", "fsdp")),
            P(("dp", "fsdp"), None),
            P(("dp", "fsdp"), None),
            P(("dp", "fsdp")),
        ),
        out_specs=(
            P(("dp", "fsdp"), None),
            P(("dp", "fsdp"), None),
            P(("dp", "fsdp"), None),
            P(None, "dp", "fsdp"),
            P(None, "dp", "fsdp"),
            P(None, "dp", "fsdp"),
            P("dp", "fsdp"),
            P("dp", "fsdp"),
            P("dp", "fsdp"),
            P("dp", "fsdp"),
            P("dp", "fsdp"),
            P("dp", "fsdp"),
            P(None, ("dp", "fsdp")),
            P(None, ("dp", "fsdp")),
            P(None, ("dp", "fsdp")),
            P(),
            P(),
            P(),
            P(),
            P(),
            P(),
            P(),
            P(),
        ),
        check_vma=False,
    )
```

```python
import functools

import jax
import jax.numpy as jnp
import numpy as np
from jax import lax
from jax.experimental import pallas as pl
from jax.experimental.pallas import tpu as pltpu
from jax.sharding import PartitionSpec as P

D = 768
HEADS = 12
HEAD = 64
BUCKETS = 32
MAXDIST = 128
STEP = 10


HIGHEST = lax.Precision.HIGHEST
NORM_EPS = 1e-06
LEARN_RATE = 0.03
TABLE_RATE = 0.4
SMALL_RATE = 0.5
BETA_ONE = 0.9
BETA_TWO = 0.999
ADAM_EPS = 1e-08
WEIGHT_DECAY = 0.01
CLIP_NORM = 0.5


def bucket_table(length):
    places = np.arange(length)
    offset = places[None, :] - places[:, None]
    half_count = BUCKETS // 2
    exact_count = half_count // 2
    upper = (offset > 0).astype(np.int64) * half_count
    distance = np.abs(offset)
    far_bucket = exact_count + (
        np.log(np.maximum(distance, 1) / exact_count)
        / np.log(MAXDIST / exact_count)
        * (half_count - exact_count)
    ).astype(np.int64)
    far_bucket = np.minimum(far_bucket, half_count - 1)
    return (upper + np.where(distance < exact_count, distance, far_bucket)).astype(np.int32)


def bucket_onehot(length):
    flat_table = bucket_table(length).reshape(-1)
    return jnp.asarray((flat_table[:, None] == np.arange(BUCKETS)[None, :]).astype(np.float32))


def product(left, right):
    return jnp.dot(left, right, preferred_element_type=jnp.float32)


def product_left(left, right):
    return lax.dot_general(
        left, right, (((0,), (0,)), ((), ())), preferred_element_type=jnp.float32
    )


def product_right(left, right):
    return lax.dot_general(
        left, right, (((1,), (1,)), ((), ())), preferred_element_type=jnp.float32
    )


def attention_bias(position_bias, length):
    onehot = bucket_onehot(length)
    flat_bias = jnp.dot(onehot, position_bias, precision=HIGHEST)
    return (jnp.transpose(flat_bias.reshape(length, length, HEADS), (2, 0, 1)), onehot)


def adam_update(weight, moment, second, grad, factor, rate):
    clipped = grad * factor
    moment_new = BETA_ONE * moment + (1 - BETA_ONE) * clipped
    second_new = BETA_TWO * second + (1 - BETA_TWO) * clipped * clipped
    moment_hat = moment_new / (1 - BETA_ONE**STEP)
    second_hat = second_new / (1 - BETA_TWO**STEP)
    updated = weight - rate * (
        moment_hat / (jnp.sqrt(second_hat) + ADAM_EPS) + WEIGHT_DECAY * weight
    )
    return (moment_new, second_new, updated)


LANES = 128
GROUPS = 4
SLOT = LANES // GROUPS
VMEM_CAP = 56 * 1024 * 1024

def fold_rows(vocab):
    per = -(-vocab // GROUPS)
    return -(-per // LANES) * LANES

def up8(n):
    return -(-n // 8) * 8

def eye():
    r = lax.broadcasted_iota(jnp.int32, (LANES, LANES), 0)
    c = lax.broadcasted_iota(jnp.int32, (LANES, LANES), 1)
    return (r == c).astype(jnp.float32).astype(jnp.bfloat16)

def lookup_kernel(fold, row_ref, group_ref, table_ref, out_ref, turned, rows):
    feats, vocab = table_ref.shape
    tokens = rows.shape[0]
    @pl.when(pl.program_id(0) == 0)
    def _():
        pad = jnp.zeros((SLOT - feats, LANES), jnp.float32)
        def build(b, _):
            parts = []
            for j in range(GROUPS):
                start = jnp.minimum(j * fold + b * LANES, vocab - LANES)
                start = pl.multiple_of(start, LANES)
                parts += [table_ref[:, pl.ds(start, LANES)], pad]
            tile = jnp.concatenate(parts, axis=0)
            turned[pl.ds(pl.multiple_of(b * LANES, LANES), LANES), :] = tile.T
            return 0
        lax.fori_loop(0, fold // LANES, build, 0)
        turned[pl.ds(fold, 8), :] = jnp.zeros((8, LANES), jnp.float32)
    UN = 32
    def fetch(b, _):
        for k in range(UN):
            t = b * UN + k
            rows[pl.ds(t, 1), :] = turned[pl.ds(row_ref[0, 0, t], 1), :]
        return 0
    lax.fori_loop(0, tokens // UN, fetch, 0)
    wide = lax.dot_general(eye(), rows[...].astype(jnp.bfloat16), (((1,), (1,)), ((), ())), preferred_element_type=jnp.float32)
    group = group_ref[0]
    total = jnp.where(group == 0, wide[:SLOT], 0.0)
    for j in range(1, GROUPS):
        total = total + jnp.where(group == j, wide[j * SLOT:(j + 1) * SLOT], 0.0)
    half = tokens // 2
    out_ref[0] = jnp.concatenate([total[:feats, :half], total[:feats, half:]], axis=0).astype(jnp.bfloat16)

def lookup(table, rows_idx, groups_idx):
    feats, vocab = table.shape
    n, tokens = rows_idx.shape[0], rows_idx.shape[2]
    fold = fold_rows(vocab)
    return pl.pallas_call(
        functools.partial(lookup_kernel, fold),
        grid=(n,),
        out_shape=jax.ShapeDtypeStruct((n, 2 * feats, tokens // 2), jnp.bfloat16),
        in_specs=[
            pl.BlockSpec((1, 1, tokens), lambda s: (s, 0, 0), memory_space=pltpu.SMEM),
            pl.BlockSpec((1, 1, tokens), lambda s: (s, 0, 0)),
            pl.BlockSpec((feats, vocab), lambda s: (0, 0)),
        ],
        out_specs=pl.BlockSpec((1, 2 * feats, tokens // 2), lambda s: (s, 0, 0)),
        scratch_shapes=[pltpu.VMEM((fold + 8, LANES), jnp.float32), pltpu.VMEM((tokens, LANES), jnp.float32)],
        compiler_params=pltpu.CompilerParams(vmem_limit_bytes=VMEM_CAP),
        name="lookup",
    )(rows_idx, groups_idx, table)

def scatter_kernel(fold, row_ref, group_ref, grad_ref, out_ref, total, rows):
    feats, vocab = out_ref.shape
    tokens = rows.shape[0]
    step = pl.program_id(0)
    @pl.when(step == 0)
    def _():
        def clear(b, _):
            total[pl.ds(pl.multiple_of(b * LANES, LANES), LANES), :] = jnp.zeros((LANES, LANES), jnp.float32)
            return 0
        lax.fori_loop(0, fold // LANES, clear, 0)
        total[pl.ds(fold, 8), :] = jnp.zeros((8, LANES), jnp.float32)
    block = grad_ref[0].astype(jnp.float32)
    flat = jnp.concatenate([block[:feats], block[feats:]], axis=1)
    group = group_ref[0]
    pad = jnp.zeros((SLOT - feats, tokens), jnp.float32)
    parts = []
    for j in range(GROUPS):
        parts += [jnp.where(group == j, flat, 0.0), pad]
    spread = jnp.concatenate(parts, axis=0).astype(jnp.bfloat16)
    rows[...] = lax.dot_general(spread, eye(), (((0,), (0,)), ((), ())), preferred_element_type=jnp.float32)
    LN = 16
    stride = tokens // LN
    def add(i, _):
        at = [row_ref[0, 0, i + stride * k] for k in range(LN)]
        new = [total[pl.ds(at[k], 1), :] + rows[pl.ds(i + stride * k, 1), :] for k in range(LN)]
        for k in range(LN):
            total[pl.ds(at[k], 1), :] = new[k]
        return 0
    lax.fori_loop(0, stride, add, 0, unroll=2)
    @pl.when(step == pl.num_programs(0) - 1)
    def _():
        whole = (vocab - (GROUPS - 1) * fold) // LANES
        def turn(b, _):
            tile = total[pl.ds(pl.multiple_of(b * LANES, LANES), LANES), :].T
            for j in range(GROUPS):
                out_ref[:, pl.ds(pl.multiple_of(j * fold + b * LANES, LANES), LANES)] = tile[j * SLOT:j * SLOT + feats]
            return 0
        lax.fori_loop(0, whole, turn, 0)
        for b in range(whole, fold // LANES):
            tile = total[pl.ds(b * LANES, LANES), :].T
            for j in range(GROUPS - 1):
                out_ref[:, pl.ds(j * fold + b * LANES, LANES)] = tile[j * SLOT:j * SLOT + feats]

def scatter(grads, rows_idx, groups_idx, vocab):
    n, tokens = rows_idx.shape[0], rows_idx.shape[2]
    feats = grads.shape[1] // 2
    fold = fold_rows(vocab)
    return pl.pallas_call(
        functools.partial(scatter_kernel, fold),
        grid=(n,),
        out_shape=jax.ShapeDtypeStruct((feats, vocab), jnp.float32),
        in_specs=[
            pl.BlockSpec((1, 1, tokens), lambda s: (s, 0, 0), memory_space=pltpu.SMEM),
            pl.BlockSpec((1, 1, tokens), lambda s: (s, 0, 0)),
            pl.BlockSpec((1, 2 * feats, tokens // 2), lambda s: (s, 0, 0)),
        ],
        out_specs=pl.BlockSpec((feats, vocab), lambda s: (0, 0)),
        scratch_shapes=[pltpu.VMEM((fold + 8, LANES), jnp.float32), pltpu.VMEM((tokens, LANES), jnp.float32)],
        compiler_params=pltpu.CompilerParams(vmem_limit_bytes=VMEM_CAP),
        name="scatter",
    )(rows_idx, groups_idx, grads)

def token_keys(tokens, fold):
    count = tokens.shape[0]
    key = (tokens % fold) * GROUPS + tokens // fold
    places = jnp.arange(count, dtype=jnp.int32)
    same_before = (key[:, None] == key[None, :]) & (places[:, None] < places[None, :])
    first = ~jnp.any(same_before, axis=0)
    rank = jnp.sum(((key[None, :] < key[:, None]) & first[None, :]).astype(jnp.int32), axis=1)
    hit = (rank[:, None] == places[None, :]) & first[:, None]
    packed = GROUPS * fold + jnp.sum(jnp.where(hit, key[:, None] - GROUPS * fold, 0), axis=0)
    return packed, rank


MESH = pl.DeviceIdType.MESH


def exchange_kernel(same, src, dst, send_sem, recv_sem, own_sem):
    rows, cols = lax.axis_size("dp"), lax.axis_size("fsdp")
    count = rows * cols
    me = lax.axis_index("dp") * cols + lax.axis_index("fsdp")
    barrier = pltpu.get_barrier_semaphore()

    def device(k):
        to = lax.rem(me + k, count)
        return (to // cols, lax.rem(to, cols))

    def greet(k, carry):
        pl.semaphore_signal(barrier, inc=1, device_id=device(k), device_id_type=MESH)
        return carry

    def copy(k):
        to = lax.rem(me + k, count)
        return pltpu.make_async_remote_copy(
            src_ref=src.at[0 if same else to],
            dst_ref=dst.at[me],
            send_sem=send_sem.at[k],
            recv_sem=recv_sem.at[k],
            device_id=device(k),
            device_id_type=MESH,
        )

    def start(k, carry):
        copy(k).start()
        return carry

    def end(k, carry):
        copy(k).wait()
        return carry

    lax.fori_loop(1, count, greet, 0)
    own = pltpu.make_async_copy(src.at[0 if same else me], dst.at[me], own_sem)
    own.start()
    pl.semaphore_wait(barrier, count - 1)
    lax.fori_loop(1, count, start, 0)
    own.wait()
    lax.fori_loop(1, count, end, 0)


def exchange(blocks, same, call_id, name):
    count = lax.axis_size("dp") * lax.axis_size("fsdp")
    return pl.pallas_call(
        functools.partial(exchange_kernel, same),
        out_shape=jax.ShapeDtypeStruct((count,) + blocks.shape[1:], blocks.dtype),
        in_specs=[pl.BlockSpec(memory_space=pl.ANY)],
        out_specs=pl.BlockSpec(memory_space=pl.ANY),
        scratch_shapes=[
            pltpu.SemaphoreType.DMA((count,)),
            pltpu.SemaphoreType.DMA((count,)),
            pltpu.SemaphoreType.DMA,
        ],
        compiler_params=pltpu.CompilerParams(collective_id=call_id, has_side_effects=True),
        name=name,
    )(blocks)


SQUARE, EXPAND, REDUCE = range(3)
KINDS = 3
STEPS = (5, 6, 4)
FIRST = (3, 3, 2)


def spot(refs, kind, z, x, y, core):
    dp = z * 2 + x
    column = y * 2 + core
    if kind == SQUARE:
        return refs[kind].at[
            :,
            pl.ds(pl.multiple_of(dp * 96 + core * 48, 16), 48),
            pl.ds(pl.multiple_of(y * 384, 128), 384),
        ]
    if kind == EXPAND:
        return refs[kind].at[
            pl.ds(pl.multiple_of(dp * 96, 16), 96), pl.ds(pl.multiple_of(column * 768, 128), 768)
        ]
    return refs[kind].at[
        pl.ds(pl.multiple_of(column * 192, 16), 192), pl.ds(pl.multiple_of(dp * 384, 128), 384)
    ]


def spot_part(refs, kind, z, x, y, core, part):
    dp = z * 2 + x
    column = y * 2 + core
    if kind == SQUARE:
        return refs[kind].at[
            pl.ds(0, 3) if part == 0 else pl.ds(3, 2),
            pl.ds(pl.multiple_of(dp * 96 + core * 48, 16), 48),
            pl.ds(pl.multiple_of(y * 384, 128), 384),
        ]
    if kind == EXPAND:
        return refs[kind].at[
            pl.ds(pl.multiple_of(dp * 96 + part * 48, 16), 48),
            pl.ds(pl.multiple_of(column * 768, 128), 768),
        ]
    return refs[kind].at[
        pl.ds(pl.multiple_of(column * 192 + part * 96, 16), 96),
        pl.ds(pl.multiple_of(dp * 384, 128), 384),
    ]


def block_part(ref, kind, part):
    if kind == SQUARE:
        return ref.at[pl.ds(0, 3) if part == 0 else pl.ds(3, 2)]
    half = 48 if kind == EXPAND else 96
    return ref.at[pl.ds(part * half, half)]


def block_step(ref, kind, k):
    if kind == SQUARE:
        return ref.at[k]
    rows = 16 if kind == EXPAND else 48
    return ref.at[pl.ds(pl.multiple_of(k * rows, 16), rows)]


BLOCKS = ((5, 48, 384), (96, 768), (192, 384))


def place():
    dp, fsdp = lax.axis_index("dp"), lax.axis_index("fsdp")
    return dp // 2, lax.rem(dp, 2), fsdp // 2, lax.rem(fsdp, 2)


def device_at(z, x, y, core):
    return (z * 2 + x, y * 2 + core)


def greet_neighbours(depth):
    z, x, y, core = place()
    barrier = pltpu.get_barrier_semaphore()

    def hello(target):
        pl.semaphore_signal(barrier, inc=1, device_id=target, device_id_type=MESH)

    hello(device_at(z, x, y, 1 - core))
    hello(device_at(z, 1 - x, y, core))
    hello(device_at(z, x, 1 - y, core))

    @pl.when(z > 0)
    def _():
        hello(device_at(z - 1, x, y, core))

    @pl.when(z < depth - 1)
    def _():
        hello(device_at(z + 1, x, y, core))

    above = jnp.where(z < depth - 1, 1, 0)
    below = jnp.where(z > 0, 1, 0)
    pl.semaphore_wait(barrier, 3 + above + below)


def remote(src, dst, send_sem, recv_sem, target):
    return pltpu.make_async_remote_copy(
        src_ref=src, dst_ref=dst, send_sem=send_sem, recv_sem=recv_sem,
        device_id=target, device_id_type=MESH)


def gather_kernel(depth, *refs):
    mine, outs = refs[:KINDS], refs[KINDS : 2 * KINDS]
    theirs, own = refs[2 * KINDS : 2 * KINDS + 2]
    pair_send, pair_recv, own_sem, send, got, sib_send, sib_got, diag_got = refs[2 * KINDS + 2 :]
    z, x, y, core = place()
    sibling = device_at(z, x, y, 1 - core)
    x_next, y_next = device_at(z, 1 - x, y, core), device_at(z, x, 1 - y, core)
    greet_neighbours(depth)
    pair = remote(mine[SQUARE].at[1 - core], theirs, pair_send, pair_recv, sibling)
    pair.start()

    def number(z_at, x_at, y_at):
        return (z_at * 2 + x_at) * 2 + y_at

    def to(way, a, z_at, x_at, y_at, target, part=None, src=None):
        k = number(z_at, x_at, y_at)
        if part is None:
            spot_at, recv = spot(outs, a, z_at, x_at, y_at, core), got.at[a, k]
        else:
            spot_at = spot_part(outs, a, z_at, x_at, y_at, core, part)
            recv = diag_got.at[a, z_at, part]
        return remote(spot_at if src is None else src, spot_at, send.at[way, a, k], recv, target)

    def to_sibling(a, z_at, x_at, y_at, src=None):
        spot_at = spot(outs, a, z_at, x_at, y_at, core)
        k = number(z_at, x_at, y_at)
        return remote(spot_at if src is None else src, spot_at, sib_send.at[a, k], sib_got.at[a, k], sibling)

    def from_sibling(a, z_at, x_at, y_at):
        spot_at = spot(outs, a, z_at, x_at, y_at, 1 - core)
        k = number(z_at, x_at, y_at)
        return remote(spot_at, spot_at, sib_send.at[a, k], sib_got.at[a, k], sibling)

    UP, DOWN, ACROSS_X, ACROSS_Y = range(4)
    sources = [own, mine[EXPAND], mine[REDUCE]]
    for a in (EXPAND, REDUCE, SQUARE):
        if a == SQUARE:
            row = lax.broadcasted_iota(jnp.int32, (192, 384), 0)
            col = lax.broadcasted_iota(jnp.int32, (192, 384), 1)
            here = (row + core * 192 == col).astype(jnp.float32).astype(jnp.bfloat16)
            there = (row + (1 - core) * 192 == col).astype(jnp.float32).astype(jnp.bfloat16)
            pair.wait_recv()
            for k in range(5):
                block = jnp.dot(mine[a][core, k], here, preferred_element_type=jnp.float32) + jnp.dot(
                    theirs[k], there, preferred_element_type=jnp.float32
                )
                own[k] = block.astype(jnp.bfloat16)
        pltpu.make_async_copy(sources[a], spot(outs, a, z, x, y, core), own_sem.at[a]).start()

        @pl.when(z < depth - 1)
        def _():
            to(UP, a, z, x, y, device_at(z + 1, x, y, core), src=sources[a]).start()

        @pl.when(z > 0)
        def _():
            to(DOWN, a, z, x, y, device_at(z - 1, x, y, core), src=sources[a]).start()

        to(ACROSS_X, a, z, x, y, x_next, src=sources[a]).start()
        to(ACROSS_Y, a, z, x, y, y_next, src=sources[a]).start()
        to_sibling(a, z, x, y, src=sources[a]).start()

    def sides(step, act):
        if step == 0:
            act(z)
            return
        for sign in (1, -1):
            z_at = z + sign * step

            @pl.when((z_at >= 0) & (z_at < depth))
            def _():
                act(z_at)

    def first(step):
        def act(z_at):
            for a in range(KINDS):
                to(UP, a, z_at, x, y, sibling).wait_recv()

                @pl.when((z_at < z) & (z < depth - 1))
                def _():
                    to(UP, a, z_at, x, y, device_at(z + 1, x, y, core)).start()

                @pl.when((z_at > z) & (z > 0))
                def _():
                    to(DOWN, a, z_at, x, y, device_at(z - 1, x, y, core)).start()

                to(ACROSS_X, a, z_at, x, y, x_next).start()
                to(ACROSS_Y, a, z_at, x, y, y_next).start()
                to_sibling(a, z_at, x, y).start()

        sides(step, act)

    def second(step):
        def act(z_at):
            for a in range(KINDS):
                to(UP, a, z_at, 1 - x, y, sibling).wait_recv()
                to(ACROSS_Y, a, z_at, 1 - x, y, y_next, 0).start()
                to_sibling(a, z_at, 1 - x, y).start()
                to(UP, a, z_at, x, 1 - y, sibling).wait_recv()
                to(ACROSS_X, a, z_at, x, 1 - y, x_next, 1).start()
                to_sibling(a, z_at, x, 1 - y).start()

        sides(step, act)

    def third(step):
        def act(z_at):
            for a in range(KINDS):
                for part in range(2):
                    to(UP, a, z_at, 1 - x, 1 - y, sibling, part).wait_recv()
                to_sibling(a, z_at, 1 - x, 1 - y).start()

        sides(step, act)

    for step in range(1, depth + 2):
        if step < depth:
            first(step)
        if 0 <= step - 1 < depth:
            second(step - 1)
        if 0 <= step - 2 < depth:
            third(step - 2)

    pair.wait_send()
    for a in range(KINDS):
        pltpu.make_async_copy(sources[a], spot(outs, a, z, x, y, core), own_sem.at[a]).wait()

    def finish(z_at, carry):
        for a in range(KINDS):

            @pl.when((z_at <= z) & (z < depth - 1))
            def _():
                to(UP, a, z_at, x, y, x_next).wait_send()

            @pl.when((z_at >= z) & (z > 0))
            def _():
                to(DOWN, a, z_at, x, y, x_next).wait_send()

            to(ACROSS_X, a, z_at, x, y, x_next).wait_send()
            to(ACROSS_Y, a, z_at, x, y, y_next).wait_send()
            to(ACROSS_Y, a, z_at, 1 - x, y, y_next, 0).wait_send()
            to(ACROSS_X, a, z_at, x, 1 - y, x_next, 1).wait_send()
            for x_at in range(2):
                for y_at in range(2):
                    to_sibling(a, z_at, x_at, y_at).wait_send()
                    from_sibling(a, z_at, x_at, y_at).wait_recv()
        return carry

    lax.fori_loop(0, depth, finish, 0)


def gather_blocks(square, expand, reduce_turned, call_id):
    depth = lax.axis_size("dp") // 2
    count = 4 * depth
    return pl.pallas_call(
        functools.partial(gather_kernel, depth),
        out_shape=[
            jax.ShapeDtypeStruct((5, 768, 768), jnp.bfloat16),
            jax.ShapeDtypeStruct((768, 3072), jnp.bfloat16),
            jax.ShapeDtypeStruct((768, 3072), jnp.bfloat16),
        ],
        in_specs=[pl.BlockSpec(memory_space=pltpu.VMEM)] * KINDS,
        out_specs=[pl.BlockSpec(memory_space=pltpu.VMEM)] * KINDS,
        scratch_shapes=[
            pltpu.VMEM((5, 48, 192), jnp.bfloat16),
            pltpu.VMEM((5, 48, 384), jnp.bfloat16),
            pltpu.SemaphoreType.DMA,
            pltpu.SemaphoreType.DMA,
            pltpu.SemaphoreType.DMA((KINDS,)),
            pltpu.SemaphoreType.DMA((4, KINDS, count)),
            pltpu.SemaphoreType.DMA((KINDS, count)),
            pltpu.SemaphoreType.DMA((KINDS, count)),
            pltpu.SemaphoreType.DMA((KINDS, count)),
            pltpu.SemaphoreType.DMA((KINDS, depth, 2)),
        ],
        compiler_params=pltpu.CompilerParams(
            collective_id=call_id, has_side_effects=True, vmem_limit_bytes=VMEM_CAP
        ),
        name="gather_layer",
    )(square, expand, reduce_turned)


def reduce_kernel(depth, *refs):
    count = KINDS
    grads, outs = refs[:count], refs[count : 2 * count]
    work, paired, step_one, from_x, from_y, from_z = [
        refs[(2 + k) * count : (3 + k) * count] for k in range(6)
    ]
    spare = refs[8 * count]
    load_sem, pair_send, pair_got, send, one_got, x_got, y_got, z_got, end_send, end_got = refs[8 * count + 1 :]
    z, x, y, core = place()
    sibling = device_at(z, x, y, 1 - core)
    x_next, y_next = device_at(z, 1 - x, y, core), device_at(z, x, 1 - y, core)
    greet_neighbours(depth)

    def index(z_at, x_at):
        return z_at * 2 + x_at

    def load(a, z_at, x_at, y_at):
        i = index(z_at, x_at)
        return pltpu.make_async_copy(
            spot(grads, a, z_at, x_at, y_at, core), work[a].at[i, y_at], load_sem.at[a, i, y_at]
        )

    def pair(a, z_at, x_at, y_at):
        i = index(z_at, x_at)
        return remote(
            spot(grads, a, z_at, x_at, y_at, 1 - core),
            paired[a].at[i, y_at],
            pair_send.at[a, i, y_at],
            pair_got.at[a, i, y_at],
            sibling,
        )

    rounds = list(range(depth - 1, -1, -1))

    def sides(step, act):
        if step == 0:
            act(z)
            return
        for sign in (1, -1):
            z_at = z + sign * step

            @pl.when((z_at >= 0) & (z_at < depth))
            def _():
                act(z_at)

    for x_at, y_at in ((1 - x, 1 - y), (1 - x, y), (x, 1 - y), (x, y)):
        for step in rounds:

            def begin(z_at):
                for a in range(count):
                    load(a, z_at, x_at, y_at).start()
                    pair(a, z_at, x_at, y_at).start()

            sides(step, begin)

    def ready(a, z_at, x_at, y_at):
        load(a, z_at, x_at, y_at).wait()
        pair(a, z_at, x_at, y_at).wait_recv()

    def total(a, z_at, x_at, y_at, first, last, extra=()):
        i = index(z_at, x_at)

        def add(k, carry):
            here = block_step(work[a].at[i, y_at], a, k)
            value = here[...].astype(jnp.float32)
            value = value + block_step(paired[a].at[i, y_at], a, k)[...].astype(jnp.float32)
            for buffer in extra:
                value = value + block_step(buffer, a, k)[...].astype(jnp.float32)
            here[...] = value.astype(jnp.bfloat16)
            return carry

        lax.fori_loop(first, last, add, 0)

    def diag_copy(a, z_at, part):
        return remote(
            block_part(work[a].at[index(z_at, 1 - x), 1 - y], a, part),
            block_part(step_one[a].at[z_at], a, part),
            send.at[part, a, z_at],
            one_got.at[a, part, z_at],
            y_next if part == 0 else x_next,
        )

    def diag(z_at):
        for a in range(count):
            ready(a, z_at, 1 - x, 1 - y)
            total(a, z_at, 1 - x, 1 - y, 0, STEPS[a])
            for part in range(2):
                diag_copy(a, z_at, part).start()

    def x_copy(a, z_at):
        return remote(work[a].at[index(z_at, 1 - x), y], from_x[a].at[z_at], send.at[2, a, z_at], x_got.at[a, z_at], x_next)

    def y_copy(a, z_at):
        return remote(work[a].at[index(z_at, x), 1 - y], from_y[a].at[z_at], send.at[3, a, z_at], y_got.at[a, z_at], y_next)

    def columns(z_at):
        for a in range(count):
            middle, last = FIRST[a], STEPS[a]
            ready(a, z_at, 1 - x, y)
            diag_copy(a, z_at, 0).wait_recv()
            total(a, z_at, 1 - x, y, 0, middle, [step_one[a].at[z_at]])
            total(a, z_at, 1 - x, y, middle, last)
            x_copy(a, z_at).start()
            ready(a, z_at, x, 1 - y)
            diag_copy(a, z_at, 1).wait_recv()
            total(a, z_at, x, 1 - y, 0, middle)
            total(a, z_at, x, 1 - y, middle, last, [step_one[a].at[z_at]])
            y_copy(a, z_at).start()

    def z_copy(a, z_at, side):
        target = device_at(z + 1, x, y, core) if side == 0 else device_at(z - 1, x, y, core)
        return remote(work[a].at[index(z_at, x), y], from_z[a].at[side, z_at], send.at[4, a, z_at], z_got.at[a, side, z_at], target)

    def line(step):
        def act(z_at):
            for a in range(count):
                ready(a, z_at, x, y)
                x_copy(a, z_at).wait_recv()
                y_copy(a, z_at).wait_recv()
                across = [from_x[a].at[z_at], from_y[a].at[z_at]]
                if step > 0:
                    upward = z_at > z
                    before = (upward & (z > 0)) | (jnp.logical_not(upward) & (z < depth - 1))
                    side = jnp.where(upward, 0, 1)

                    @pl.when(before)
                    def _():
                        remote(
                            work[a].at[index(z_at, x), y],
                            from_z[a].at[side, z_at],
                            send.at[4, a, z_at],
                            z_got.at[a, side, z_at],
                            sibling,
                        ).wait_recv()
                        total(a, z_at, x, y, 0, STEPS[a], across + [from_z[a].at[side, z_at]])

                    @pl.when(jnp.logical_not(before))
                    def _():
                        total(a, z_at, x, y, 0, STEPS[a], across)

                    @pl.when(upward)
                    def _():
                        z_copy(a, z_at, 0).start()

                    @pl.when(jnp.logical_not(upward))
                    def _():
                        z_copy(a, z_at, 1).start()
                else:
                    for side in range(2):
                        present = (z > 0) if side == 0 else (z < depth - 1)

                        @pl.when(present)
                        def _():
                            z_copy(a, z, side).wait_recv()

                        @pl.when(jnp.logical_not(present))
                        def _():
                            from_z[a][side, z] = jnp.zeros(BLOCKS[a], jnp.bfloat16)

                    def finish(k, carry):
                        i = index(z, x)
                        value = block_step(work[a].at[i, y], a, k)[...].astype(jnp.float32)
                        for buffer in [paired[a].at[i, y]] + across + [from_z[a].at[0, z], from_z[a].at[1, z]]:
                            value = value + block_step(buffer, a, k)[...].astype(jnp.float32)
                        if a == SQUARE:
                            low, high = value[:, :192], pltpu.roll(value, 192, 1)[:, :192]
                            outs[a][core, k] = jnp.where(core == 0, low, high)
                            spare[k] = jnp.where(core == 0, high, low)
                        else:
                            block_step(outs[a], a, k)[...] = value
                        return carry

                    lax.fori_loop(0, STEPS[a], finish, 0)
                    if a == SQUARE:
                        end_copy().start()

        sides(step, act)

    def end_copy():
        return remote(spare, outs[SQUARE].at[core], end_send, end_got, sibling)

    for k in range(depth + 2):
        if k < depth:
            sides(rounds[k], diag)
        if 0 <= k - 1 < depth:
            sides(rounds[k - 1], columns)
        if 0 <= k - 2 < depth:
            line(rounds[k - 2])

    def finish_all(z_at, carry):
        for a in range(count):
            for x_at in range(2):
                for y_at in range(2):
                    pair(a, z_at, x_at, y_at).wait_send()
            for part in range(2):
                diag_copy(a, z_at, part).wait_send()
            x_copy(a, z_at).wait_send()
            y_copy(a, z_at).wait_send()

            @pl.when(z_at != z)
            def _():
                z_copy(a, z_at, 0).wait_send()
        return carry

    lax.fori_loop(0, depth, finish_all, 0)
    end_copy().wait_send()
    remote(spare, outs[SQUARE].at[1 - core], end_send, end_got, sibling).wait_recv()


def reduce_blocks(square, expand, reduce_turned, call_id):
    depth = lax.axis_size("dp") // 2

    def buffers(*lead):
        return [pltpu.VMEM(lead + block, jnp.bfloat16) for block in BLOCKS]

    return pl.pallas_call(
        functools.partial(reduce_kernel, depth),
        out_shape=[
            jax.ShapeDtypeStruct((2, 5, 48, 192), jnp.float32),
            jax.ShapeDtypeStruct((96, 768), jnp.float32),
            jax.ShapeDtypeStruct((192, 384), jnp.float32),
        ],
        in_specs=[pl.BlockSpec(memory_space=pl.ANY)] * KINDS,
        out_specs=[pl.BlockSpec(memory_space=pltpu.VMEM)] * KINDS,
        scratch_shapes=buffers(2 * depth, 2)
        + buffers(2 * depth, 2)
        + buffers(depth)
        + buffers(depth)
        + buffers(depth)
        + buffers(2, depth)
        + [
            pltpu.VMEM((5, 48, 192), jnp.float32),
            pltpu.SemaphoreType.DMA((KINDS, 2 * depth, 2)),
            pltpu.SemaphoreType.DMA((KINDS, 2 * depth, 2)),
            pltpu.SemaphoreType.DMA((KINDS, 2 * depth, 2)),
            pltpu.SemaphoreType.DMA((5, KINDS, depth)),
            pltpu.SemaphoreType.DMA((KINDS, 2, depth)),
            pltpu.SemaphoreType.DMA((KINDS, depth)),
            pltpu.SemaphoreType.DMA((KINDS, depth)),
            pltpu.SemaphoreType.DMA((KINDS, 2, depth)),
            pltpu.SemaphoreType.DMA,
            pltpu.SemaphoreType.DMA,
        ],
        compiler_params=pltpu.CompilerParams(
            collective_id=call_id, has_side_effects=True, vmem_limit_bytes=VMEM_CAP
        ),
        name="reduce_layer",
    )(square, expand, reduce_turned)


TILE = 128
PAIRS = HEADS // 2
GELU_IN = (2.0 / np.pi) ** 0.5


def dot_nn(left, right):
    return jnp.dot(left, right, preferred_element_type=jnp.float32)


def dot_nt(left, right):
    return lax.dot_general(left, right, (((1,), (1,)), ((), ())), preferred_element_type=jnp.float32)


def dot_tn(left, right):
    return lax.dot_general(left, right, (((0,), (0,)), ((), ())), preferred_element_type=jnp.float32)


def rows_at(index, size):
    return pl.ds(pl.multiple_of(index * size, size), size)


def split_heads(block):
    low = lax.broadcasted_iota(jnp.int32, block.shape, 1) < HEAD
    wide = block.astype(jnp.float32)
    first = jnp.where(low, wide, 0.0).astype(jnp.bfloat16)
    second = jnp.where(low, 0.0, wide).astype(jnp.bfloat16)
    return jnp.concatenate([first, second], axis=0)


def join_heads(stacked):
    return jnp.concatenate([stacked[:TILE], stacked[TILE:]], axis=1)


def pair_probs(query, keys_here, bias, mask):
    scores = dot_nt(split_heads(query), keys_here) * HEAD ** (-0.5) + bias
    scores = scores + mask
    raised = jnp.exp(scores - jnp.max(scores, axis=1, keepdims=True))
    return raised / jnp.sum(raised, axis=1, keepdims=True)


def pair_bias(bias_ref, pair):
    return jnp.concatenate([bias_ref[2 * pair], bias_ref[2 * pair + 1]], axis=0)


def tile_mask(mask_ref, tile):
    mask = mask_ref[tile]
    return jnp.concatenate([mask, mask], axis=0)


def hot_rows(rank_ref, rows, tokens):
    place = lax.broadcasted_iota(jnp.int32, (rows.size, tokens), 1)
    return (rank_ref[rows, :1] == place).astype(jnp.float32).astype(jnp.bfloat16)


def norm_rows(values, gain):
    scale = lax.rsqrt(jnp.mean(values * values, axis=1, keepdims=True) + NORM_EPS)
    return values * scale * gain


def gelu_parts(pre):
    inner = GELU_IN * (pre + 0.044715 * pre * pre * pre)
    return jnp.tanh(inner)


def forward_kernel(
    found_ref, rank_ref, square_ref, expand_ref, reduce_ref, gains_ref, bias_ref, mask_ref, pool_ref, length_ref,
    start_ref, query_ref, key_ref, value_ref, mixed_ref, middle_ref, ending_ref, low_ref, pooled_ref, embed_ref,
    inverse_ref, normed, pooled_sum,
):
    tokens = start_ref.shape[0]
    big = 512

    def begin(r, carry):
        rows = rows_at(r, 256)
        start = dot_nt(hot_rows(rank_ref, rows, tokens), found_ref[...])
        start_ref[rows, :] = start.astype(jnp.bfloat16)
        normed[rows, :] = norm_rows(start, gains_ref[0:1]).astype(jnp.bfloat16)
        return carry

    lax.fori_loop(0, tokens // 256, begin, 0)
    for k, target in enumerate((query_ref, key_ref, value_ref)):

        def project(r, carry):
            rows = rows_at(r, big)
            target[rows, :] = dot_nn(normed[rows, :], square_ref[k]).astype(jnp.bfloat16)
            return carry

        lax.fori_loop(0, tokens // big, project, 0)

    def attend(t, carry):
        rows = rows_at(t, TILE)
        mask = tile_mask(mask_ref, t)
        for pair in range(PAIRS):
            lanes = pl.ds(pair * TILE, TILE)
            probs = pair_probs(query_ref[rows, lanes], key_ref[rows, lanes], pair_bias(bias_ref, pair), mask)
            mixed = dot_nn(join_heads(probs).astype(jnp.bfloat16), split_heads(value_ref[rows, lanes]))
            mixed_ref[rows, lanes] = mixed.astype(jnp.bfloat16)
        return carry

    lax.fori_loop(0, tokens // TILE, attend, 0)

    def merge(r, carry):
        rows = rows_at(r, big)
        middle = start_ref[rows, :].astype(jnp.float32) + dot_nn(mixed_ref[rows, :], square_ref[3])
        middle_ref[rows, :] = middle
        ending_ref[rows, :] = middle
        normed[rows, :] = norm_rows(middle, gains_ref[1:2]).astype(jnp.bfloat16)
        return carry

    lax.fori_loop(0, tokens // big, merge, 0)
    wide = expand_ref.shape[1]

    def feed(c, carry):
        lanes = rows_at(c, D)

        def rows_of(r, inner):
            rows = rows_at(r, big)
            pre = dot_nn(normed[rows, :], expand_ref[:, lanes])
            act = (0.5 * pre * (1.0 + gelu_parts(pre))).astype(jnp.bfloat16)
            ending_ref[rows, :] += dot_nt(act, reduce_ref[:, lanes])
            return inner

        return lax.fori_loop(0, tokens // big, rows_of, carry)

    lax.fori_loop(0, wide // D, feed, 0)
    pooled_sum[...] = jnp.zeros_like(pooled_sum)

    def pool(r, carry):
        rows = rows_at(r, 256)
        output = norm_rows(ending_ref[rows, :], gains_ref[2:3])
        pooled_sum[...] += jnp.dot(
            pool_ref[:, rows], output, precision=HIGHEST, preferred_element_type=jnp.float32
        )
        return carry

    lax.fori_loop(0, tokens // 256, pool, 0)
    pooled = (pooled_sum[...] / length_ref[:, :1]).astype(jnp.bfloat16)
    pooled_ref[...] = pooled
    projected = dot_nn(pooled, square_ref[4])
    inverse = lax.rsqrt(jnp.sum(projected * projected, axis=1, keepdims=True) + NORM_EPS)
    embeds = projected * inverse
    embed_ref[...] = embeds
    low_ref[...] = embeds.astype(jnp.bfloat16)
    inverse_ref[...] = jnp.broadcast_to(inverse, inverse_ref.shape)


def run_forward(found, rank, square, expand, reduce_turned, gains, bias, mask, pool, lengths):
    tokens = found.shape[1]
    seqs = pool.shape[0]
    low = jnp.bfloat16
    flat = jax.ShapeDtypeStruct((tokens, D), low)
    full = jax.ShapeDtypeStruct((tokens, D), jnp.float32)
    return pl.pallas_call(
        forward_kernel,
        out_shape=[
            flat, flat, flat, flat, flat, full, full,
            jax.ShapeDtypeStruct((seqs, D), low),
            jax.ShapeDtypeStruct((seqs, D), low),
            jax.ShapeDtypeStruct((seqs, D), jnp.float32),
            jax.ShapeDtypeStruct((seqs, LANES), jnp.float32),
        ],
        scratch_shapes=[pltpu.VMEM((tokens, D), low), pltpu.VMEM((seqs, D), jnp.float32)],
        compiler_params=pltpu.CompilerParams(vmem_limit_bytes=VMEM_CAP),
        name="layer_forward",
    )(found, rank, square, expand, reduce_turned, gains, bias, mask, pool, lengths)


def norm_back_rows(values, gain, grad):
    scale = lax.rsqrt(jnp.mean(values * values, axis=1, keepdims=True) + NORM_EPS)
    weighted = grad * gain
    inner = jnp.mean(weighted * values, axis=1, keepdims=True)
    through = scale * weighted - values * (scale * scale * scale * inner)
    return through, jnp.sum(grad * values * scale, axis=0, keepdims=True)


def feed_back_kernel(
    grad_embed_ref, embed_ref, inverse_ref, pool_ref, length_ref, last_ref, middle_ref, ending_ref, expand_ref,
    reduce_ref, gains_ref,
    grad_expand_ref, grad_reduce_ref, grad_middle_ref, grad_low_ref, grad_proj_ref, grad_gains_ref,
    normed, normed_turned, end_low, end_turned, back,
):
    tokens = middle_ref.shape[0]
    embeds, grads = embed_ref[...], grad_embed_ref[...]
    grad_proj = inverse_ref[:, :1] * (grads - embeds * jnp.sum(grads * embeds, axis=1, keepdims=True))
    grad_proj = grad_proj.astype(jnp.bfloat16)
    grad_proj_ref[...] = grad_proj
    grad_pooled = dot_nt(grad_proj, last_ref[0]) / length_ref[:, :1]
    grad_gains_ref[...] = jnp.zeros_like(grad_gains_ref)

    def begin(r, carry):
        rows = rows_at(r, 256)
        grad_out = lax.dot_general(
            pool_ref[:, rows], grad_pooled, (((0,), (0,)), ((), ())), precision=HIGHEST,
            preferred_element_type=jnp.float32,
        )
        through, gain = norm_back_rows(ending_ref[rows, :], gains_ref[2:3], grad_out)
        grad_gains_ref[2:3] += gain
        grad_middle_ref[rows, :] = through
        end_low[rows, :] = through.astype(jnp.bfloat16)
        end_turned[:, rows] = through.T.astype(jnp.bfloat16)
        middle_normed = norm_rows(middle_ref[rows, :], gains_ref[1:2])
        normed[rows, :] = middle_normed.astype(jnp.bfloat16)
        normed_turned[:, rows] = middle_normed.T.astype(jnp.bfloat16)
        return carry

    lax.fori_loop(0, tokens // 256, begin, 0)
    back[...] = jnp.zeros_like(back)
    wide = expand_ref.shape[1]
    step = 384

    def feed(c, carry):
        lanes = rows_at(c, step)
        pre = dot_nn(normed[...], expand_ref[:, lanes])
        grad_act = dot_nn(end_low[...], reduce_ref[:, lanes])
        turn = gelu_parts(pre)
        act = (0.5 * pre * (1.0 + turn)).astype(jnp.bfloat16)
        slope = 0.5 * (1.0 + turn) + 0.5 * pre * (1.0 - turn * turn) * GELU_IN * (1.0 + 3.0 * 0.044715 * pre * pre)
        grad_pre = (grad_act * slope).astype(jnp.bfloat16)
        grad_reduce_ref[:, lanes] = dot_nn(end_turned[...], act).astype(jnp.bfloat16)
        grad_expand_ref[:, lanes] = dot_nn(normed_turned[...], grad_pre).astype(jnp.bfloat16)
        back[...] += dot_nt(grad_pre, expand_ref[:, lanes])
        return carry

    lax.fori_loop(0, wide // step, feed, 0)

    def end(r, carry):
        rows = rows_at(r, 256)
        through, gain = norm_back_rows(middle_ref[rows, :], gains_ref[1:2], back[rows, :])
        grad_gains_ref[1:2] += gain
        grad_middle = grad_middle_ref[rows, :] + through
        grad_middle_ref[rows, :] = grad_middle
        grad_low_ref[rows, :] = grad_middle.astype(jnp.bfloat16)
        return carry

    lax.fori_loop(0, tokens // 256, end, 0)


def run_feed_back(grad_embed, embeds, inverse, pool, lengths, square, middle, ending, expand, reduce_turned, gains):
    tokens = middle.shape[0]
    seqs = pool.shape[0]
    low = jnp.bfloat16
    whole = pl.BlockSpec(memory_space=pltpu.VMEM)
    return pl.pallas_call(
        feed_back_kernel,
        grid=(1,),
        out_shape=[
            jax.ShapeDtypeStruct(expand.shape, low),
            jax.ShapeDtypeStruct(reduce_turned.shape, low),
            jax.ShapeDtypeStruct((tokens, D), jnp.float32),
            jax.ShapeDtypeStruct((tokens, D), low),
            jax.ShapeDtypeStruct((seqs, D), low),
            jax.ShapeDtypeStruct((8, D), jnp.float32),
        ],
        in_specs=[whole] * 5
        + [pl.BlockSpec((1, D, D), lambda i: (4, 0, 0))]
        + [whole] * 5,
        out_specs=[whole] * 6,
        scratch_shapes=[
            pltpu.VMEM((tokens, D), low),
            pltpu.VMEM((D, tokens), low),
            pltpu.VMEM((tokens, D), low),
            pltpu.VMEM((D, tokens), low),
            pltpu.VMEM((tokens, D), jnp.float32),
        ],
        compiler_params=pltpu.CompilerParams(vmem_limit_bytes=VMEM_CAP),
        name="feed_backward",
    )(grad_embed, embeds, inverse, pool, lengths, square, middle, ending, expand, reduce_turned, gains)


def attend_back_kernel(
    grad_middle_ref, grad_low_ref, grad_proj_ref, pooled_ref, start_ref, query_ref, key_ref, value_ref, mixed_ref,
    square_ref, gains_ref, bias_ref, mask_ref, rank_ref,
    grad_square_ref, grad_score_ref, grad_gain_ref, send_ref,
    grad_mixed, turned, grad_query, grad_key, grad_value, start_low,
):
    tokens = start_ref.shape[0]
    big = 512
    grad_square_ref[4] = dot_tn(pooled_ref[...], grad_proj_ref[...]).astype(jnp.bfloat16)

    def begin(r, carry):
        rows = rows_at(r, big)
        grad_mixed[rows, :] = dot_nt(grad_low_ref[rows, :], square_ref[3]).astype(jnp.bfloat16)
        turned[:, rows] = mixed_ref[rows, :].astype(jnp.float32).T.astype(jnp.bfloat16)
        return carry

    lax.fori_loop(0, tokens // big, begin, 0)

    def outer(target, right_ref):
        def part(r, carry):
            rows = rows_at(r, 384)
            grad_square_ref[target, rows, :] = dot_nn(turned[rows, :], right_ref[...]).astype(jnp.bfloat16)
            return carry

        lax.fori_loop(0, D // 384, part, 0)

    outer(3, grad_low_ref)
    grad_score_ref[...] = jnp.zeros_like(grad_score_ref)

    def attend(t, carry):
        rows = rows_at(t, TILE)
        mask = tile_mask(mask_ref, t)
        for pair in range(PAIRS):
            lanes = pl.ds(pair * TILE, TILE)
            query, keys_here = query_ref[rows, lanes], key_ref[rows, lanes]
            probs = pair_probs(query, keys_here, pair_bias(bias_ref, pair), mask)
            grads = split_heads(grad_mixed[rows, lanes])
            grad_probs = dot_nt(grads, value_ref[rows, lanes])
            grad_value[rows, lanes] = dot_tn(probs.astype(jnp.bfloat16), grads).astype(jnp.bfloat16)
            inner = jnp.sum(grad_probs * probs, axis=1, keepdims=True)
            grad_scores = (probs * (grad_probs - inner)).astype(jnp.bfloat16)
            kept = grad_scores.astype(jnp.float32)
            grad_score_ref[2 * pair] += kept[:TILE]
            grad_score_ref[2 * pair + 1] += kept[TILE:]
            grad_query[rows, lanes] = (
                dot_nn(join_heads(grad_scores), split_heads(keys_here)) * HEAD ** (-0.5)
            ).astype(jnp.bfloat16)
            grad_key[rows, lanes] = (dot_tn(grad_scores, split_heads(query)) * HEAD ** (-0.5)).astype(jnp.bfloat16)
        return carry

    lax.fori_loop(0, tokens // TILE, attend, 0)

    def renorm(r, carry):
        rows = rows_at(r, 256)
        normed = norm_rows(start_ref[rows, :].astype(jnp.float32), gains_ref[0:1])
        turned[:, rows] = normed.T.astype(jnp.bfloat16)
        return carry

    lax.fori_loop(0, tokens // 256, renorm, 0)
    outer(0, grad_query)
    outer(1, grad_key)
    outer(2, grad_value)
    grad_gain_ref[...] = jnp.zeros_like(grad_gain_ref)

    def end(r, carry):
        rows = rows_at(r, 256)
        grad_normed = (
            dot_nt(grad_query[rows, :], square_ref[0])
            + dot_nt(grad_key[rows, :], square_ref[1])
            + dot_nt(grad_value[rows, :], square_ref[2])
        )
        through, gain = norm_back_rows(start_ref[rows, :].astype(jnp.float32), gains_ref[0:1], grad_normed)
        grad_gain_ref[0:1] += gain
        turned[:, rows] = (grad_middle_ref[rows, :] + through).T.astype(jnp.bfloat16)
        return carry

    lax.fori_loop(0, tokens // 256, end, 0)

    def hot(r, carry):
        rows = rows_at(r, 256)
        start_low[rows, :] = hot_rows(rank_ref, rows, tokens)
        return carry

    lax.fori_loop(0, tokens // 256, hot, 0)

    def gather_rows(r, carry):
        rows = rows_at(r, 384)
        send_ref[rows, :] = dot_nn(turned[rows, :], start_low[...]).astype(jnp.bfloat16)
        return carry

    lax.fori_loop(0, D // 384, gather_rows, 0)


def run_attend_back(
    grad_middle, grad_low, grad_proj, pooled, start, queries, keys_here, values_here, mixed, square, gains, bias,
    mask, rank,
):
    tokens = start.shape[0]
    low = jnp.bfloat16
    return pl.pallas_call(
        attend_back_kernel,
        out_shape=[
            jax.ShapeDtypeStruct((5, D, D), low),
            jax.ShapeDtypeStruct((HEADS, TILE, TILE), jnp.float32),
            jax.ShapeDtypeStruct((8, D), jnp.float32),
            jax.ShapeDtypeStruct((D, tokens), low),
        ],
        scratch_shapes=[
            pltpu.VMEM((tokens, D), low),
            pltpu.VMEM((D, tokens), low),
            pltpu.VMEM((tokens, D), low),
            pltpu.VMEM((tokens, D), low),
            pltpu.VMEM((tokens, D), low),
            pltpu.VMEM((tokens, tokens), low),
        ],
        compiler_params=pltpu.CompilerParams(vmem_limit_bytes=VMEM_CAP),
        name="attend_backward",
    )(
        grad_middle, grad_low, grad_proj, pooled, start, queries, keys_here, values_here, mixed, square, gains, bias,
        mask, rank,
    )


def shards(
    embed_table,
    square_weights,
    expand_weight,
    reduce_weight,
    norm_gains,
    position_bias,
    log_scale,
    table_moment,
    table_second,
    square_moment,
    square_second,
    expand_moment,
    expand_second,
    reduce_moment,
    reduce_second,
    gains_moment,
    gains_second,
    position_moment,
    position_second,
    scale_moment,
    scale_second,
    query_tokens,
    answer_tokens,
    query_length,
    answer_length,
    premise_tokens,
    hypothesis_tokens,
    hard_negative,
):
    both = ("dp", "fsdp")
    dp_size, fsdp_size = lax.axis_size("dp"), lax.axis_size("fsdp")
    count = dp_size * fsdp_size
    direct = dp_size == 8 and fsdp_size == 4
    position = lax.axis_index(both)
    feats, vocab_size = embed_table.shape
    feats_pad = up8(feats)
    fold = fold_rows(vocab_size)
    query_rows = query_tokens.shape[0]
    nli_rows = premise_tokens.shape[0]
    short_length = query_tokens.shape[1]
    long_length = answer_tokens.shape[1]
    short_tokens = jnp.concatenate([query_tokens, premise_tokens, hypothesis_tokens], axis=0)
    lengths = jnp.concatenate(
        [query_length, jnp.full((2 * nli_rows,), short_length, jnp.int32), answer_length]
    )
    all_tokens = jnp.concatenate([short_tokens.reshape(-1), answer_tokens.reshape(-1)])
    token_count = all_tokens.shape[0]
    hypo_start = query_rows + nli_rows
    answer_start = query_rows + 2 * nli_rows
    seq_count = answer_start + query_rows
    seq_pad = -(-seq_count // 16) * 16
    split_at = short_tokens.shape[0] * short_length

    packed, rank = token_keys(all_tokens, fold)
    start_info = jnp.concatenate(
        [
            packed.reshape(-1, LANES).astype(jnp.float32),
            jnp.pad(hard_negative, (0, LANES - nli_rows)).reshape(1, LANES).astype(jnp.float32),
            jnp.pad(norm_gains, ((0, 7 - 3), (0, LANES - feats))),
        ],
        axis=0,
    )
    key_rows = token_count // LANES
    info_all = exchange(start_info[None], True, 0, "share_start")
    packed_all = info_all[:, :key_rows].astype(jnp.int32).reshape(count, 1, token_count)
    negative_all = info_all[:, key_rows, :nli_rows].astype(jnp.int32).reshape(-1)
    gains = info_all[:, key_rows + 1 : key_rows + 4, :feats].transpose(1, 0, 2).reshape(3, D)
    gains = jnp.pad(gains.astype(jnp.bfloat16).astype(jnp.float32), ((0, 5), (0, 0)))
    row_all, group_all = packed_all >> 2, packed_all & 3

    square_low = square_weights.astype(jnp.bfloat16)
    expand_low = expand_weight.astype(jnp.bfloat16)
    reduce_low = reduce_weight.astype(jnp.bfloat16).T
    if direct:
        square_pieces = square_low.reshape(5, 2, 48, 192).transpose(1, 0, 2, 3)
        square_all, expand_all, reduce_all = gather_blocks(square_pieces, expand_low, reduce_low, 1)
    else:

        def whole(piece, row_name, column_name):
            axis = piece.ndim - 2
            wide = lax.all_gather(piece, column_name, axis=axis + 1, tiled=True)
            return lax.all_gather(wide, row_name, axis=axis, tiled=True)

        square_all = whole(square_low, "dp", "fsdp")
        expand_all = whole(expand_low, "dp", "fsdp")
        reduce_all = whole(reduce_low, "fsdp", "dp")

    table_low = embed_table.astype(jnp.bfloat16).astype(jnp.float32)
    if feats_pad > feats:
        table_low = jnp.pad(table_low, ((0, feats_pad - feats), (0, 0)))
    found = exchange(lookup(table_low, row_all, group_all), False, 2, "send_features")
    half = token_count // 2
    found = found.reshape(count, 2, feats_pad, half)[:, :, :feats]
    found = found.transpose(0, 2, 1, 3).reshape(D, token_count)

    sequence = np.concatenate(
        [
            np.repeat(np.arange(answer_start), short_length),
            answer_start + np.repeat(np.arange(query_rows), long_length),
        ]
    )
    inside = np.concatenate(
        [
            np.tile(np.arange(short_length), answer_start),
            np.tile(np.arange(long_length), query_rows),
        ]
    )
    lengths_pad = jnp.pad(lengths, (0, seq_pad - seq_count), constant_values=1)
    pool = (sequence[None, :] == np.arange(seq_pad)[:, None]) & (inside[None, :] < lengths_pad[:, None])
    token_ok = jnp.any(pool, axis=0).reshape(-1, 1, TILE)
    sequence_tiles = sequence.reshape(-1, TILE)
    together = sequence_tiles[:, :, None] == sequence_tiles[:, None, :]
    mask = jnp.where(together & token_ok, 0.0, -1e30).astype(jnp.float32)
    pool = pool.astype(jnp.float32)
    length_rows = jnp.broadcast_to(lengths_pad.astype(jnp.float32)[:, None], (seq_pad, LANES))
    rank_rows = jnp.broadcast_to(rank[:, None], (token_count, LANES))
    bias, onehot = attention_bias(position_bias, TILE)

    (start, queries, keys_here, values_here, mixed, middle, ending, embeds_low, pooled, embeds, inverse) = run_forward(
        found, rank_rows, square_all, expand_all, reduce_all, gains, bias, mask, pool, length_rows
    )
    gathered = exchange(embeds_low[None], True, 3, "share_embeds")
    queries_all = gathered[:, :query_rows].reshape(-1, D)
    premises_all = gathered[:, query_rows:hypo_start].reshape(-1, D)
    hypotheses_all = gathered[:, hypo_start:answer_start].reshape(-1, D)
    answers_all = gathered[:, answer_start:seq_count].reshape(-1, D)
    scale = jnp.exp(log_scale[0])

    def contrast(left, right, extra, own):
        sims = product_right(left, right)
        logits = scale * sims
        row_top = jnp.max(logits, axis=1, keepdims=True)
        raised = (1.0 + extra) * jnp.exp(logits - row_top)
        row_total = jnp.sum(raised, axis=1, keepdims=True)
        spread = row_top[:, 0] + jnp.log(row_total[:, 0])
        target_hit = jnp.eye(left.shape[0], dtype=jnp.float32)
        loss_sum = jnp.sum(spread - jnp.sum(target_hit * logits, axis=1))
        grad_logits = raised / row_total - target_hit
        grad_scale = jnp.sum(grad_logits * sims)
        grad_sims = (scale * grad_logits).astype(jnp.bfloat16)
        mine_left = lax.dynamic_slice_in_dim(grad_sims, position * own, own, 0)
        mine_right = lax.dynamic_slice_in_dim(grad_sims, position * own, own, 1)
        return (loss_sum, grad_scale, product(mine_left, right), product_left(mine_right, left))

    first_loss, first_dscale, grad_queries, grad_answers = contrast(
        queries_all, answers_all, 0.0, query_rows
    )
    negatives = (jnp.arange(hypotheses_all.shape[0])[None, :] == negative_all[:, None]).astype(
        jnp.float32
    )
    second_loss, second_dscale, grad_premises, grad_hypotheses = contrast(
        premises_all, hypotheses_all, negatives, nli_rows
    )
    grad_embeds = jnp.concatenate(
        [
            grad_queries,
            grad_premises,
            grad_hypotheses,
            grad_answers,
            jnp.zeros((seq_pad - seq_count, D), jnp.float32),
        ],
        axis=0,
    )
    (grad_expand, grad_reduce, grad_middle, grad_middle_low, grad_proj, late_gains) = run_feed_back(
        grad_embeds, embeds, inverse, pool, length_rows, square_all, middle, ending, expand_all, reduce_all, gains
    )
    (grad_square, grad_scores, first_gain, merged) = run_attend_back(
        grad_middle, grad_middle_low, grad_proj, pooled, start, queries, keys_here, values_here, mixed, square_all,
        gains, bias, mask, rank_rows
    )
    grad_gains = jnp.concatenate([first_gain[:1], late_gains[1:3]], axis=0)
    grad_position = lax.dot_general(
        onehot, grad_scores.reshape(HEADS, TILE * TILE), (((0,), (1,)), ((), ())), precision=HIGHEST
    )
    grad_scale = ((first_dscale + second_dscale) * scale).reshape(1)
    merged = merged.reshape(count, feats, 2, half).transpose(0, 2, 1, 3)
    if feats_pad > feats:
        merged = jnp.pad(merged, ((0, 0), (0, 0), (0, feats_pad - feats), (0, 0)))
    returned = exchange(merged.reshape(count, 2 * feats_pad, half), False, 4, "send_gradients")
    grad_table = scatter(returned, row_all, group_all, vocab_size)[:feats]
    if direct:
        square_sum, expand_sum, reduce_sum = reduce_blocks(grad_square, grad_expand, grad_reduce, 5)
        square_sum = square_sum.transpose(1, 0, 2, 3).reshape(5, 96, 192)
    else:

        def shard(gradient, row_name, column_name):
            axis = gradient.ndim - 2
            part = lax.psum_scatter(
                gradient.astype(jnp.float32), row_name, scatter_dimension=axis, tiled=True
            )
            return lax.psum_scatter(part, column_name, scatter_dimension=axis + 1, tiled=True)

        square_sum = shard(grad_square, "dp", "fsdp")
        expand_sum = shard(grad_expand, "dp", "fsdp")
        reduce_sum = shard(grad_reduce, "fsdp", "dp")
    reduced = (square_sum, expand_sum, reduce_sum.T)
    local_square = (
        jnp.sum(reduced[0] * reduced[0])
        + jnp.sum(reduced[1] * reduced[1])
        + jnp.sum(reduce_sum * reduce_sum)
        + jnp.sum(grad_table * grad_table)
    )
    small = jnp.concatenate([grad_gains.reshape(-1), grad_position.reshape(-1), local_square.reshape(1)])
    small_rows = -(-small.shape[0] // (8 * LANES)) * 8
    small = jnp.pad(small, (0, small_rows * LANES - small.shape[0])).reshape(1, small_rows, LANES)
    summed = jnp.sum(exchange(small, True, 6, "share_small"), axis=0).reshape(-1)
    gains_total = summed[: 3 * D].reshape(3, D)
    position_total = summed[3 * D : 3 * D + BUCKETS * HEADS].reshape(BUCKETS, HEADS)
    square_total = summed[3 * D + BUCKETS * HEADS]
    scale_total = grad_scale
    losses = jnp.stack([first_loss, second_loss])
    grad_gain_shard = lax.dynamic_slice_in_dim(gains_total, position * feats, feats, 1)
    gradient_norm = jnp.sqrt(
        square_total
        + jnp.sum(gains_total * gains_total)
        + jnp.sum(position_total * position_total)
        + jnp.sum(scale_total * scale_total)
    )
    factor = jnp.minimum(1.0, CLIP_NORM / gradient_norm)
    table_out = adam_update(embed_table, table_moment, table_second, grad_table, factor, TABLE_RATE)
    square_out = adam_update(
        square_weights, square_moment, square_second, reduced[0], factor, LEARN_RATE
    )
    expand_out = adam_update(
        expand_weight, expand_moment, expand_second, reduced[1], factor, LEARN_RATE
    )
    reduce_out = adam_update(
        reduce_weight, reduce_moment, reduce_second, reduced[2], factor, LEARN_RATE
    )
    gains_out = adam_update(
        norm_gains, gains_moment, gains_second, grad_gain_shard, factor, SMALL_RATE
    )
    position_out = adam_update(
        position_bias, position_moment, position_second, position_total, factor, SMALL_RATE
    )
    scale_out = adam_update(log_scale, scale_moment, scale_second, scale_total, factor, SMALL_RATE)
    return (
        *table_out,
        *square_out,
        *expand_out,
        *reduce_out,
        *gains_out,
        *position_out,
        *scale_out,
        losses,
        gradient_norm,
    )


def solution(mesh):
    return jax.shard_map(
        shards,
        mesh=mesh,
        in_specs=(
            P(("dp", "fsdp"), None),
            P(None, "dp", "fsdp"),
            P("dp", "fsdp"),
            P("dp", "fsdp"),
            P(None, ("dp", "fsdp")),
            P(),
            P(),
            P(("dp", "fsdp"), None),
            P(("dp", "fsdp"), None),
            P(None, "dp", "fsdp"),
            P(None, "dp", "fsdp"),
            P("dp", "fsdp"),
            P("dp", "fsdp"),
            P("dp", "fsdp"),
            P("dp", "fsdp"),
            P(None, ("dp", "fsdp")),
            P(None, ("dp", "fsdp")),
            P(),
            P(),
            P(),
            P(),
            P(("dp", "fsdp"), None),
            P(("dp", "fsdp"), None),
            P(("dp", "fsdp")),
            P(("dp", "fsdp")),
            P(("dp", "fsdp"), None),
            P(("dp", "fsdp"), None),
            P(("dp", "fsdp")),
        ),
        out_specs=(
            P(("dp", "fsdp"), None),
            P(("dp", "fsdp"), None),
            P(("dp", "fsdp"), None),
            P(None, "dp", "fsdp"),
            P(None, "dp", "fsdp"),
            P(None, "dp", "fsdp"),
            P("dp", "fsdp"),
            P("dp", "fsdp"),
            P("dp", "fsdp"),
            P("dp", "fsdp"),
            P("dp", "fsdp"),
            P("dp", "fsdp"),
            P(None, ("dp", "fsdp")),
            P(None, ("dp", "fsdp")),
            P(None, ("dp", "fsdp")),
            P(),
            P(),
            P(),
            P(),
            P(),
            P(),
            P(),
            P(),
        ),
        check_vma=False,
    )
```

```python
import functools

import jax
import jax.numpy as jnp
import numpy as np
from jax import lax
from jax.experimental import pallas as pl
from jax.experimental.pallas import tpu as pltpu
from jax.sharding import PartitionSpec as P

D = 768
HEADS = 12
HEAD = 64
BUCKETS = 32
MAXDIST = 128
STEP = 10


HIGHEST = lax.Precision.HIGHEST
NORM_EPS = 1e-06
LEARN_RATE = 0.03
TABLE_RATE = 0.4
SMALL_RATE = 0.5
BETA_ONE = 0.9
BETA_TWO = 0.999
ADAM_EPS = 1e-08
WEIGHT_DECAY = 0.01
CLIP_NORM = 0.5


def bucket_table(length):
    places = np.arange(length)
    offset = places[None, :] - places[:, None]
    half_count = BUCKETS // 2
    exact_count = half_count // 2
    upper = (offset > 0).astype(np.int64) * half_count
    distance = np.abs(offset)
    far_bucket = exact_count + (
        np.log(np.maximum(distance, 1) / exact_count)
        / np.log(MAXDIST / exact_count)
        * (half_count - exact_count)
    ).astype(np.int64)
    far_bucket = np.minimum(far_bucket, half_count - 1)
    return (upper + np.where(distance < exact_count, distance, far_bucket)).astype(np.int32)


def bucket_onehot(length):
    flat_table = bucket_table(length).reshape(-1)
    return jnp.asarray((flat_table[:, None] == np.arange(BUCKETS)[None, :]).astype(np.float32))


def product(left, right):
    return jnp.dot(left, right, preferred_element_type=jnp.float32)


def product_left(left, right):
    return lax.dot_general(
        left, right, (((0,), (0,)), ((), ())), preferred_element_type=jnp.float32
    )


def product_right(left, right):
    return lax.dot_general(
        left, right, (((1,), (1,)), ((), ())), preferred_element_type=jnp.float32
    )


def attention_bias(position_bias, length):
    onehot = bucket_onehot(length)
    flat_bias = jnp.dot(onehot, position_bias, precision=HIGHEST)
    return (jnp.transpose(flat_bias.reshape(length, length, HEADS), (2, 0, 1)), onehot)


def adam_update(weight, moment, second, grad, factor, rate):
    clipped = grad * factor
    moment_new = BETA_ONE * moment + (1 - BETA_ONE) * clipped
    second_new = BETA_TWO * second + (1 - BETA_TWO) * clipped * clipped
    moment_hat = moment_new / (1 - BETA_ONE**STEP)
    second_hat = second_new / (1 - BETA_TWO**STEP)
    updated = weight - rate * (
        moment_hat / (jnp.sqrt(second_hat) + ADAM_EPS) + WEIGHT_DECAY * weight
    )
    return (moment_new, second_new, updated)


LANES = 128
GROUPS = 4
SLOT = LANES // GROUPS
VMEM_CAP = 56 * 1024 * 1024

def fold_rows(vocab):
    per = -(-vocab // GROUPS)
    return -(-per // LANES) * LANES

def up8(n):
    return -(-n // 8) * 8

def eye():
    r = lax.broadcasted_iota(jnp.int32, (LANES, LANES), 0)
    c = lax.broadcasted_iota(jnp.int32, (LANES, LANES), 1)
    return (r == c).astype(jnp.float32).astype(jnp.bfloat16)

def turn_table(fold, table_ref, turned):
    feats, vocab = table_ref.shape
    pad = jnp.zeros((SLOT - feats, LANES), jnp.float32)

    def build(b, carry):
        parts = []
        for j in range(GROUPS):
            start = jnp.minimum(j * fold + b * LANES, vocab - LANES)
            start = pl.multiple_of(start, LANES)
            parts += [table_ref[:, pl.ds(start, LANES)], pad]
        tile = jnp.concatenate(parts, axis=0)
        turned[pl.ds(pl.multiple_of(b * LANES, LANES), LANES), :] = tile.T
        return carry

    lax.fori_loop(0, fold // LANES, build, 0)
    turned[pl.ds(fold, 8), :] = jnp.zeros((8, LANES), jnp.float32)


def look_up(row_ref, group_ref, source, turned, rows, feats):
    tokens = rows.shape[0]
    batch = 32

    def fetch(b, carry):
        for k in range(batch):
            t = b * batch + k
            rows[pl.ds(t, 1), :] = turned[pl.ds(row_ref[source, t], 1), :]
        return carry

    lax.fori_loop(0, tokens // batch, fetch, 0)
    wide = dot_nt(eye(), rows[...].astype(jnp.bfloat16))
    group = group_ref[source]
    total = jnp.where(group == 0, wide[:SLOT], 0.0)
    for j in range(1, GROUPS):
        total = total + jnp.where(group == j, wide[j * SLOT : (j + 1) * SLOT], 0.0)
    half = tokens // 2
    return jnp.concatenate([total[:feats, :half], total[:feats, half:]], axis=0).astype(jnp.bfloat16)


def lookup_kernel(fold, row_ref, group_ref, table_ref, out_ref, turned, rows):
    @pl.when(pl.program_id(0) == 0)
    def _():
        turn_table(fold, table_ref, turned)

    out_ref[0] = look_up(row_ref, group_ref, 0, turned, rows, table_ref.shape[0])


def lookup(table, rows_idx, groups_idx):
    feats, vocab = table.shape
    n, tokens = rows_idx.shape[0], rows_idx.shape[2]
    fold = fold_rows(vocab)
    return pl.pallas_call(
        functools.partial(lookup_kernel, fold),
        grid=(n,),
        out_shape=jax.ShapeDtypeStruct((n, 2 * feats, tokens // 2), jnp.bfloat16),
        in_specs=[
            pl.BlockSpec((None, 1, tokens), lambda s: (s, 0, 0), memory_space=pltpu.SMEM),
            pl.BlockSpec((1, 1, tokens), lambda s: (s, 0, 0)),
            pl.BlockSpec((feats, vocab), lambda s: (0, 0)),
        ],
        out_specs=pl.BlockSpec((1, 2 * feats, tokens // 2), lambda s: (s, 0, 0)),
        scratch_shapes=[pltpu.VMEM((fold + 8, LANES), jnp.float32), pltpu.VMEM((tokens, LANES), jnp.float32)],
        compiler_params=pltpu.CompilerParams(vmem_limit_bytes=VMEM_CAP),
        name="lookup",
    )(rows_idx, groups_idx, table)

def scatter_kernel(fold, row_ref, group_ref, grad_ref, out_ref, total, rows):
    feats, vocab = out_ref.shape
    tokens = rows.shape[0]
    step = pl.program_id(0)
    @pl.when(step == 0)
    def _():
        def clear(b, _):
            total[pl.ds(pl.multiple_of(b * LANES, LANES), LANES), :] = jnp.zeros((LANES, LANES), jnp.float32)
            return 0
        lax.fori_loop(0, fold // LANES, clear, 0)
        total[pl.ds(fold, 8), :] = jnp.zeros((8, LANES), jnp.float32)
    block = grad_ref[0].astype(jnp.float32)
    flat = jnp.concatenate([block[:feats], block[feats:]], axis=1)
    group = group_ref[0]
    pad = jnp.zeros((SLOT - feats, tokens), jnp.float32)
    parts = []
    for j in range(GROUPS):
        parts += [jnp.where(group == j, flat, 0.0), pad]
    spread = jnp.concatenate(parts, axis=0).astype(jnp.bfloat16)
    rows[...] = lax.dot_general(spread, eye(), (((0,), (0,)), ((), ())), preferred_element_type=jnp.float32)
    LN = 16
    stride = tokens // LN
    def add(i, _):
        at = [row_ref[0, 0, i + stride * k] for k in range(LN)]
        new = [total[pl.ds(at[k], 1), :] + rows[pl.ds(i + stride * k, 1), :] for k in range(LN)]
        for k in range(LN):
            total[pl.ds(at[k], 1), :] = new[k]
        return 0
    lax.fori_loop(0, stride, add, 0, unroll=2)
    @pl.when(step == pl.num_programs(0) - 1)
    def _():
        whole = (vocab - (GROUPS - 1) * fold) // LANES
        def turn(b, _):
            tile = total[pl.ds(pl.multiple_of(b * LANES, LANES), LANES), :].T
            for j in range(GROUPS):
                out_ref[:, pl.ds(pl.multiple_of(j * fold + b * LANES, LANES), LANES)] = tile[j * SLOT:j * SLOT + feats]
            return 0
        lax.fori_loop(0, whole, turn, 0)
        for b in range(whole, fold // LANES):
            tile = total[pl.ds(b * LANES, LANES), :].T
            for j in range(GROUPS - 1):
                out_ref[:, pl.ds(j * fold + b * LANES, LANES)] = tile[j * SLOT:j * SLOT + feats]

def scatter(grads, rows_idx, groups_idx, vocab):
    n, tokens = rows_idx.shape[0], rows_idx.shape[2]
    feats = grads.shape[1] // 2
    fold = fold_rows(vocab)
    return pl.pallas_call(
        functools.partial(scatter_kernel, fold),
        grid=(n,),
        out_shape=jax.ShapeDtypeStruct((feats, vocab), jnp.float32),
        in_specs=[
            pl.BlockSpec((1, 1, tokens), lambda s: (s, 0, 0), memory_space=pltpu.SMEM),
            pl.BlockSpec((1, 1, tokens), lambda s: (s, 0, 0)),
            pl.BlockSpec((1, 2 * feats, tokens // 2), lambda s: (s, 0, 0)),
        ],
        out_specs=pl.BlockSpec((feats, vocab), lambda s: (0, 0)),
        scratch_shapes=[pltpu.VMEM((fold + 8, LANES), jnp.float32), pltpu.VMEM((tokens, LANES), jnp.float32)],
        compiler_params=pltpu.CompilerParams(vmem_limit_bytes=VMEM_CAP),
        name="scatter",
    )(rows_idx, groups_idx, grads)

def token_keys(tokens, fold):
    count = tokens.shape[0]
    key = (tokens % fold) * GROUPS + tokens // fold
    places = jnp.arange(count, dtype=jnp.int32)
    same_before = (key[:, None] == key[None, :]) & (places[:, None] < places[None, :])
    first = ~jnp.any(same_before, axis=0)
    rank = jnp.sum(((key[None, :] < key[:, None]) & first[None, :]).astype(jnp.int32), axis=1)
    hit = (rank[:, None] == places[None, :]) & first[:, None]
    packed = GROUPS * fold + jnp.sum(jnp.where(hit, key[:, None] - GROUPS * fold, 0), axis=0)
    return packed, rank


MESH = pl.DeviceIdType.MESH


def greet_all(count, cols, me):
    barrier = pltpu.get_barrier_semaphore()

    def greet(k, carry):
        to = lax.rem(me + k, count)
        pl.semaphore_signal(barrier, inc=1, device_id=(to // cols, lax.rem(to, cols)), device_id_type=MESH)
        return carry

    lax.fori_loop(1, count, greet, 0)
    pl.semaphore_wait(barrier, count - 1)


def exchange_kernel(same, src, dst, send_sem, recv_sem, own_sem):
    rows, cols = lax.axis_size("dp"), lax.axis_size("fsdp")
    count = rows * cols
    me = lax.axis_index("dp") * cols + lax.axis_index("fsdp")
    barrier = pltpu.get_barrier_semaphore()

    def device(k):
        to = lax.rem(me + k, count)
        return (to // cols, lax.rem(to, cols))

    def greet(k, carry):
        pl.semaphore_signal(barrier, inc=1, device_id=device(k), device_id_type=MESH)
        return carry

    def copy(k):
        to = lax.rem(me + k, count)
        return pltpu.make_async_remote_copy(
            src_ref=src.at[0 if same else to],
            dst_ref=dst.at[me],
            send_sem=send_sem.at[k],
            recv_sem=recv_sem.at[k],
            device_id=device(k),
            device_id_type=MESH,
        )

    def start(k, carry):
        copy(k).start()
        return carry

    def end(k, carry):
        copy(k).wait()
        return carry

    lax.fori_loop(1, count, greet, 0)
    own = pltpu.make_async_copy(src.at[0 if same else me], dst.at[me], own_sem)
    own.start()
    pl.semaphore_wait(barrier, count - 1)
    lax.fori_loop(1, count, start, 0)
    own.wait()
    lax.fori_loop(1, count, end, 0)


def exchange(blocks, same, call_id, name):
    count = lax.axis_size("dp") * lax.axis_size("fsdp")
    return pl.pallas_call(
        functools.partial(exchange_kernel, same),
        out_shape=jax.ShapeDtypeStruct((count,) + blocks.shape[1:], blocks.dtype),
        in_specs=[pl.BlockSpec(memory_space=pl.ANY)],
        out_specs=pl.BlockSpec(memory_space=pl.ANY),
        scratch_shapes=[
            pltpu.SemaphoreType.DMA((count,)),
            pltpu.SemaphoreType.DMA((count,)),
            pltpu.SemaphoreType.DMA,
        ],
        compiler_params=pltpu.CompilerParams(collective_id=call_id, has_side_effects=True),
        name=name,
    )(blocks)


SQUARE, EXPAND, REDUCE = range(3)
KINDS = 3
STEPS = (5, 6, 4)
FIRST = (3, 3, 2)


def spot(refs, kind, z, x, y, core):
    dp = z * 2 + x
    column = y * 2 + core
    if kind == SQUARE:
        return refs[kind].at[
            :,
            pl.ds(pl.multiple_of(dp * 96 + core * 48, 16), 48),
            pl.ds(pl.multiple_of(y * 384, 128), 384),
        ]
    if kind == EXPAND:
        return refs[kind].at[
            pl.ds(pl.multiple_of(dp * 96, 16), 96), pl.ds(pl.multiple_of(column * 768, 128), 768)
        ]
    return refs[kind].at[
        pl.ds(pl.multiple_of(column * 192, 16), 192), pl.ds(pl.multiple_of(dp * 384, 128), 384)
    ]


def spot_part(refs, kind, z, x, y, core, part):
    dp = z * 2 + x
    column = y * 2 + core
    if kind == SQUARE:
        return refs[kind].at[
            pl.ds(0, 3) if part == 0 else pl.ds(3, 2),
            pl.ds(pl.multiple_of(dp * 96 + core * 48, 16), 48),
            pl.ds(pl.multiple_of(y * 384, 128), 384),
        ]
    if kind == EXPAND:
        return refs[kind].at[
            pl.ds(pl.multiple_of(dp * 96 + part * 48, 16), 48),
            pl.ds(pl.multiple_of(column * 768, 128), 768),
        ]
    return refs[kind].at[
        pl.ds(pl.multiple_of(column * 192 + part * 96, 16), 96),
        pl.ds(pl.multiple_of(dp * 384, 128), 384),
    ]


def block_part(ref, kind, part):
    if kind == SQUARE:
        return ref.at[pl.ds(0, 3) if part == 0 else pl.ds(3, 2)]
    half = 48 if kind == EXPAND else 96
    return ref.at[pl.ds(part * half, half)]


def block_step(ref, kind, k):
    if kind == SQUARE:
        return ref.at[k]
    rows = 16 if kind == EXPAND else 48
    return ref.at[pl.ds(pl.multiple_of(k * rows, 16), rows)]


BLOCKS = ((5, 48, 384), (96, 768), (192, 384))


def place():
    dp, fsdp = lax.axis_index("dp"), lax.axis_index("fsdp")
    return dp // 2, lax.rem(dp, 2), fsdp // 2, lax.rem(fsdp, 2)


def device_at(z, x, y, core):
    return (z * 2 + x, y * 2 + core)


def greet_neighbours(depth):
    z, x, y, core = place()
    barrier = pltpu.get_barrier_semaphore()

    def hello(target):
        pl.semaphore_signal(barrier, inc=1, device_id=target, device_id_type=MESH)

    hello(device_at(z, x, y, 1 - core))
    hello(device_at(z, 1 - x, y, core))
    hello(device_at(z, x, 1 - y, core))

    @pl.when(z > 0)
    def _():
        hello(device_at(z - 1, x, y, core))

    @pl.when(z < depth - 1)
    def _():
        hello(device_at(z + 1, x, y, core))

    above = jnp.where(z < depth - 1, 1, 0)
    below = jnp.where(z > 0, 1, 0)
    pl.semaphore_wait(barrier, 3 + above + below)


def remote(src, dst, send_sem, recv_sem, target):
    return pltpu.make_async_remote_copy(
        src_ref=src, dst_ref=dst, send_sem=send_sem, recv_sem=recv_sem,
        device_id=target, device_id_type=MESH)


def front_kernel(fold, depth, row_ref, group_ref, table_ref, square_in, expand_in, reduce_in, *refs):
    mine = (square_in, expand_in, reduce_in)
    found, outs = refs[0], refs[1 : 1 + KINDS]
    theirs, own, turned, rows, blocks = refs[1 + KINDS : 6 + KINDS]
    (
        pair_send, pair_recv, own_sem, send, got, sib_send, sib_got, diag_got, part_send, part_got, part_own
    ) = refs[6 + KINDS :]
    dp_size, fsdp_size = lax.axis_size("dp"), lax.axis_size("fsdp")
    count = dp_size * fsdp_size
    me = lax.axis_index("dp") * fsdp_size + lax.axis_index("fsdp")
    z, x, y, core = place()
    sibling = device_at(z, x, y, 1 - core)
    x_next, y_next = device_at(z, 1 - x, y, core), device_at(z, x, 1 - y, core)
    greet_all(count, fsdp_size, me)
    pair = remote(mine[SQUARE].at[1 - core], theirs, pair_send, pair_recv, sibling)
    pair.start()

    def number(z_at, x_at, y_at):
        return (z_at * 2 + x_at) * 2 + y_at

    def to(way, a, z_at, x_at, y_at, target, part=None, src=None):
        k = number(z_at, x_at, y_at)
        if part is None:
            spot_at, recv = spot(outs, a, z_at, x_at, y_at, core), got.at[a, k]
        else:
            spot_at = spot_part(outs, a, z_at, x_at, y_at, core, part)
            recv = diag_got.at[a, z_at, part]
        return remote(spot_at if src is None else src, spot_at, send.at[way, a, k], recv, target)

    def to_sibling(a, z_at, x_at, y_at, src=None):
        spot_at = spot(outs, a, z_at, x_at, y_at, core)
        k = number(z_at, x_at, y_at)
        return remote(spot_at if src is None else src, spot_at, sib_send.at[a, k], sib_got.at[a, k], sibling)

    def from_sibling(a, z_at, x_at, y_at):
        spot_at = spot(outs, a, z_at, x_at, y_at, 1 - core)
        k = number(z_at, x_at, y_at)
        return remote(spot_at, spot_at, sib_send.at[a, k], sib_got.at[a, k], sibling)

    UP, DOWN, ACROSS_X, ACROSS_Y = range(4)
    sources = [own, mine[EXPAND], mine[REDUCE]]
    for a in (EXPAND, REDUCE, SQUARE):
        if a == SQUARE:
            row = lax.broadcasted_iota(jnp.int32, (192, 384), 0)
            col = lax.broadcasted_iota(jnp.int32, (192, 384), 1)
            here = (row + core * 192 == col).astype(jnp.float32).astype(jnp.bfloat16)
            there = (row + (1 - core) * 192 == col).astype(jnp.float32).astype(jnp.bfloat16)
            pair.wait_recv()
            for k in range(5):
                block = jnp.dot(mine[a][core, k], here, preferred_element_type=jnp.float32) + jnp.dot(
                    theirs[k], there, preferred_element_type=jnp.float32
                )
                own[k] = block.astype(jnp.bfloat16)
        pltpu.make_async_copy(sources[a], spot(outs, a, z, x, y, core), own_sem.at[a]).start()

        @pl.when(z < depth - 1)
        def _():
            to(UP, a, z, x, y, device_at(z + 1, x, y, core), src=sources[a]).start()

        @pl.when(z > 0)
        def _():
            to(DOWN, a, z, x, y, device_at(z - 1, x, y, core), src=sources[a]).start()

        to(ACROSS_X, a, z, x, y, x_next, src=sources[a]).start()
        to(ACROSS_Y, a, z, x, y, y_next, src=sources[a]).start()
        to_sibling(a, z, x, y, src=sources[a]).start()

    def sides(step, act):
        if step == 0:
            act(z)
            return
        for sign in (1, -1):
            z_at = z + sign * step

            @pl.when((z_at >= 0) & (z_at < depth))
            def _():
                act(z_at)

    def first(step):
        def act(z_at):
            for a in range(KINDS):
                to(UP, a, z_at, x, y, sibling).wait_recv()

                @pl.when((z_at < z) & (z < depth - 1))
                def _():
                    to(UP, a, z_at, x, y, device_at(z + 1, x, y, core)).start()

                @pl.when((z_at > z) & (z > 0))
                def _():
                    to(DOWN, a, z_at, x, y, device_at(z - 1, x, y, core)).start()

                to(ACROSS_X, a, z_at, x, y, x_next).start()
                to(ACROSS_Y, a, z_at, x, y, y_next).start()
                to_sibling(a, z_at, x, y).start()

        sides(step, act)

    def second(step):
        def act(z_at):
            for a in range(KINDS):
                to(UP, a, z_at, 1 - x, y, sibling).wait_recv()
                to(ACROSS_Y, a, z_at, 1 - x, y, y_next, 0).start()
                to_sibling(a, z_at, 1 - x, y).start()
                to(UP, a, z_at, x, 1 - y, sibling).wait_recv()
                to(ACROSS_X, a, z_at, x, 1 - y, x_next, 1).start()
                to_sibling(a, z_at, x, 1 - y).start()

        sides(step, act)

    def third(step):
        def act(z_at):
            for a in range(KINDS):
                for part in range(2):
                    to(UP, a, z_at, 1 - x, 1 - y, sibling, part).wait_recv()
                to_sibling(a, z_at, 1 - x, 1 - y).start()

        sides(step, act)

    turn_table(fold, table_ref, turned)

    def part_copy(k):
        target = lax.rem(me + k, count)
        return pltpu.make_async_remote_copy(
            src_ref=blocks.at[target],
            dst_ref=found.at[me],
            send_sem=part_send.at[k],
            recv_sem=part_got.at[k],
            device_id=(target // fsdp_size, lax.rem(target, fsdp_size)),
            device_id_type=MESH,
        )

    def serve(k, carry):
        target = lax.rem(me + k, count)
        blocks[target] = look_up(row_ref, group_ref, target, turned, rows, table_ref.shape[0])
        part_copy(k).start()
        return carry

    relays = []
    for step in range(1, depth + 2):
        if step < depth:
            relays.append((first, step))
        if 0 <= step - 1 < depth:
            relays.append((second, step - 1))
        if 0 <= step - 2 < depth:
            relays.append((third, step - 2))
    done = 1
    for n, (relay, step) in enumerate(relays):
        until = min(count, 1 + ((n + 1) * count) // len(relays)) if n < len(relays) - 1 else count
        lax.fori_loop(done, until, serve, 0)
        done = until
        relay(step)
    blocks[me] = look_up(row_ref, group_ref, me, turned, rows, table_ref.shape[0])
    own_part = pltpu.make_async_copy(blocks.at[me], found.at[me], part_own)
    own_part.start()

    pair.wait_send()
    for a in range(KINDS):
        pltpu.make_async_copy(sources[a], spot(outs, a, z, x, y, core), own_sem.at[a]).wait()

    def finish(z_at, carry):
        for a in range(KINDS):

            @pl.when((z_at <= z) & (z < depth - 1))
            def _():
                to(UP, a, z_at, x, y, x_next).wait_send()

            @pl.when((z_at >= z) & (z > 0))
            def _():
                to(DOWN, a, z_at, x, y, x_next).wait_send()

            to(ACROSS_X, a, z_at, x, y, x_next).wait_send()
            to(ACROSS_Y, a, z_at, x, y, y_next).wait_send()
            to(ACROSS_Y, a, z_at, 1 - x, y, y_next, 0).wait_send()
            to(ACROSS_X, a, z_at, x, 1 - y, x_next, 1).wait_send()
            for x_at in range(2):
                for y_at in range(2):
                    to_sibling(a, z_at, x_at, y_at).wait_send()
                    from_sibling(a, z_at, x_at, y_at).wait_recv()
        return carry

    lax.fori_loop(0, depth, finish, 0)
    own_part.wait()

    def end_part(k, carry):
        part_copy(k).wait()
        return carry

    lax.fori_loop(1, count, end_part, 0)


def run_front(row_all, group_all, table, square, expand, reduce_turned, call_id):
    depth = lax.axis_size("dp") // 2
    spots = 4 * depth
    count, tokens = row_all.shape
    feats, vocab = table.shape
    fold = fold_rows(vocab)
    blocks = (count, 2 * feats, tokens // 2)
    whole = pl.BlockSpec(memory_space=pltpu.VMEM)
    anywhere = pl.BlockSpec(memory_space=pl.ANY)
    return pl.pallas_call(
        functools.partial(front_kernel, fold, depth),
        out_shape=[
            jax.ShapeDtypeStruct(blocks, jnp.bfloat16),
            jax.ShapeDtypeStruct((5, 768, 768), jnp.bfloat16),
            jax.ShapeDtypeStruct((768, 3072), jnp.bfloat16),
            jax.ShapeDtypeStruct((768, 3072), jnp.bfloat16),
        ],
        in_specs=[pl.BlockSpec(memory_space=pltpu.SMEM)] + [whole] * 5,
        out_specs=[anywhere] * 4,
        scratch_shapes=[
            pltpu.VMEM((5, 48, 192), jnp.bfloat16),
            pltpu.VMEM((5, 48, 384), jnp.bfloat16),
            pltpu.VMEM((fold + 8, LANES), jnp.float32),
            pltpu.VMEM((tokens, LANES), jnp.float32),
            pltpu.VMEM(blocks, jnp.bfloat16),
            pltpu.SemaphoreType.DMA,
            pltpu.SemaphoreType.DMA,
            pltpu.SemaphoreType.DMA((KINDS,)),
            pltpu.SemaphoreType.DMA((4, KINDS, spots)),
            pltpu.SemaphoreType.DMA((KINDS, spots)),
            pltpu.SemaphoreType.DMA((KINDS, spots)),
            pltpu.SemaphoreType.DMA((KINDS, spots)),
            pltpu.SemaphoreType.DMA((KINDS, depth, 2)),
            pltpu.SemaphoreType.DMA((count,)),
            pltpu.SemaphoreType.DMA((count,)),
            pltpu.SemaphoreType.DMA,
        ],
        compiler_params=pltpu.CompilerParams(
            collective_id=call_id, has_side_effects=True, vmem_limit_bytes=VMEM_CAP
        ),
        name="front",
    )(row_all, group_all.reshape(count, 1, tokens), table, square, expand, reduce_turned)


def reduce_kernel(depth, *refs):
    count = KINDS
    grads, outs = refs[:count], refs[count : 2 * count]
    work, paired, step_one, from_x, from_y, from_z = [
        refs[(2 + k) * count : (3 + k) * count] for k in range(6)
    ]
    spare = refs[8 * count]
    load_sem, pair_send, pair_got, send, one_got, x_got, y_got, z_got, end_send, end_got = refs[8 * count + 1 :]
    z, x, y, core = place()
    sibling = device_at(z, x, y, 1 - core)
    x_next, y_next = device_at(z, 1 - x, y, core), device_at(z, x, 1 - y, core)
    greet_neighbours(depth)

    def index(z_at, x_at):
        return z_at * 2 + x_at

    def load(a, z_at, x_at, y_at):
        i = index(z_at, x_at)
        return pltpu.make_async_copy(
            spot(grads, a, z_at, x_at, y_at, core), work[a].at[i, y_at], load_sem.at[a, i, y_at]
        )

    def pair(a, z_at, x_at, y_at):
        i = index(z_at, x_at)
        return remote(
            spot(grads, a, z_at, x_at, y_at, 1 - core),
            paired[a].at[i, y_at],
            pair_send.at[a, i, y_at],
            pair_got.at[a, i, y_at],
            sibling,
        )

    rounds = list(range(depth - 1, -1, -1))

    def sides(step, act):
        if step == 0:
            act(z)
            return
        for sign in (1, -1):
            z_at = z + sign * step

            @pl.when((z_at >= 0) & (z_at < depth))
            def _():
                act(z_at)

    for x_at, y_at in ((1 - x, 1 - y), (1 - x, y), (x, 1 - y), (x, y)):
        for step in rounds:

            def begin(z_at):
                for a in range(count):
                    load(a, z_at, x_at, y_at).start()
                    pair(a, z_at, x_at, y_at).start()

            sides(step, begin)

    def ready(a, z_at, x_at, y_at):
        load(a, z_at, x_at, y_at).wait()
        pair(a, z_at, x_at, y_at).wait_recv()

    def total(a, z_at, x_at, y_at, first, last, extra=()):
        i = index(z_at, x_at)

        def add(k, carry):
            here = block_step(work[a].at[i, y_at], a, k)
            value = here[...].astype(jnp.float32)
            value = value + block_step(paired[a].at[i, y_at], a, k)[...].astype(jnp.float32)
            for buffer in extra:
                value = value + block_step(buffer, a, k)[...].astype(jnp.float32)
            here[...] = value.astype(jnp.bfloat16)
            return carry

        lax.fori_loop(first, last, add, 0)

    def diag_copy(a, z_at, part):
        return remote(
            block_part(work[a].at[index(z_at, 1 - x), 1 - y], a, part),
            block_part(step_one[a].at[z_at], a, part),
            send.at[part, a, z_at],
            one_got.at[a, part, z_at],
            y_next if part == 0 else x_next,
        )

    def diag(z_at):
        for a in range(count):
            ready(a, z_at, 1 - x, 1 - y)
            total(a, z_at, 1 - x, 1 - y, 0, STEPS[a])
            for part in range(2):
                diag_copy(a, z_at, part).start()

    def x_copy(a, z_at):
        return remote(work[a].at[index(z_at, 1 - x), y], from_x[a].at[z_at], send.at[2, a, z_at], x_got.at[a, z_at], x_next)

    def y_copy(a, z_at):
        return remote(work[a].at[index(z_at, x), 1 - y], from_y[a].at[z_at], send.at[3, a, z_at], y_got.at[a, z_at], y_next)

    def columns(z_at):
        for a in range(count):
            middle, last = FIRST[a], STEPS[a]
            ready(a, z_at, 1 - x, y)
            diag_copy(a, z_at, 0).wait_recv()
            total(a, z_at, 1 - x, y, 0, middle, [step_one[a].at[z_at]])
            total(a, z_at, 1 - x, y, middle, last)
            x_copy(a, z_at).start()
            ready(a, z_at, x, 1 - y)
            diag_copy(a, z_at, 1).wait_recv()
            total(a, z_at, x, 1 - y, 0, middle)
            total(a, z_at, x, 1 - y, middle, last, [step_one[a].at[z_at]])
            y_copy(a, z_at).start()

    def z_copy(a, z_at, side):
        target = device_at(z + 1, x, y, core) if side == 0 else device_at(z - 1, x, y, core)
        return remote(work[a].at[index(z_at, x), y], from_z[a].at[side, z_at], send.at[4, a, z_at], z_got.at[a, side, z_at], target)

    def line(step):
        def act(z_at):
            for a in range(count):
                ready(a, z_at, x, y)
                x_copy(a, z_at).wait_recv()
                y_copy(a, z_at).wait_recv()
                across = [from_x[a].at[z_at], from_y[a].at[z_at]]
                if step > 0:
                    upward = z_at > z
                    before = (upward & (z > 0)) | (jnp.logical_not(upward) & (z < depth - 1))
                    side = jnp.where(upward, 0, 1)

                    @pl.when(before)
                    def _():
                        remote(
                            work[a].at[index(z_at, x), y],
                            from_z[a].at[side, z_at],
                            send.at[4, a, z_at],
                            z_got.at[a, side, z_at],
                            sibling,
                        ).wait_recv()
                        total(a, z_at, x, y, 0, STEPS[a], across + [from_z[a].at[side, z_at]])

                    @pl.when(jnp.logical_not(before))
                    def _():
                        total(a, z_at, x, y, 0, STEPS[a], across)

                    @pl.when(upward)
                    def _():
                        z_copy(a, z_at, 0).start()

                    @pl.when(jnp.logical_not(upward))
                    def _():
                        z_copy(a, z_at, 1).start()
                else:
                    for side in range(2):
                        present = (z > 0) if side == 0 else (z < depth - 1)

                        @pl.when(present)
                        def _():
                            z_copy(a, z, side).wait_recv()

                        @pl.when(jnp.logical_not(present))
                        def _():
                            from_z[a][side, z] = jnp.zeros(BLOCKS[a], jnp.bfloat16)

                    def finish(k, carry):
                        i = index(z, x)
                        value = block_step(work[a].at[i, y], a, k)[...].astype(jnp.float32)
                        for buffer in [paired[a].at[i, y]] + across + [from_z[a].at[0, z], from_z[a].at[1, z]]:
                            value = value + block_step(buffer, a, k)[...].astype(jnp.float32)
                        if a == SQUARE:
                            low, high = value[:, :192], pltpu.roll(value, 192, 1)[:, :192]
                            outs[a][core, k] = jnp.where(core == 0, low, high)
                            spare[k] = jnp.where(core == 0, high, low)
                        else:
                            block_step(outs[a], a, k)[...] = value
                        return carry

                    lax.fori_loop(0, STEPS[a], finish, 0)
                    if a == SQUARE:
                        end_copy().start()

        sides(step, act)

    def end_copy():
        return remote(spare, outs[SQUARE].at[core], end_send, end_got, sibling)

    for k in range(depth + 2):
        if k < depth:
            sides(rounds[k], diag)
        if 0 <= k - 1 < depth:
            sides(rounds[k - 1], columns)
        if 0 <= k - 2 < depth:
            line(rounds[k - 2])

    def finish_all(z_at, carry):
        for a in range(count):
            for x_at in range(2):
                for y_at in range(2):
                    pair(a, z_at, x_at, y_at).wait_send()
            for part in range(2):
                diag_copy(a, z_at, part).wait_send()
            x_copy(a, z_at).wait_send()
            y_copy(a, z_at).wait_send()

            @pl.when(z_at != z)
            def _():
                z_copy(a, z_at, 0).wait_send()
        return carry

    lax.fori_loop(0, depth, finish_all, 0)
    end_copy().wait_send()
    remote(spare, outs[SQUARE].at[1 - core], end_send, end_got, sibling).wait_recv()


def reduce_blocks(square, expand, reduce_turned, call_id):
    depth = lax.axis_size("dp") // 2

    def buffers(*lead):
        return [pltpu.VMEM(lead + block, jnp.bfloat16) for block in BLOCKS]

    return pl.pallas_call(
        functools.partial(reduce_kernel, depth),
        out_shape=[
            jax.ShapeDtypeStruct((2, 5, 48, 192), jnp.float32),
            jax.ShapeDtypeStruct((96, 768), jnp.float32),
            jax.ShapeDtypeStruct((192, 384), jnp.float32),
        ],
        in_specs=[pl.BlockSpec(memory_space=pl.ANY)] * KINDS,
        out_specs=[pl.BlockSpec(memory_space=pltpu.VMEM)] * KINDS,
        scratch_shapes=buffers(2 * depth, 2)
        + buffers(2 * depth, 2)
        + buffers(depth)
        + buffers(depth)
        + buffers(depth)
        + buffers(2, depth)
        + [
            pltpu.VMEM((5, 48, 192), jnp.float32),
            pltpu.SemaphoreType.DMA((KINDS, 2 * depth, 2)),
            pltpu.SemaphoreType.DMA((KINDS, 2 * depth, 2)),
            pltpu.SemaphoreType.DMA((KINDS, 2 * depth, 2)),
            pltpu.SemaphoreType.DMA((5, KINDS, depth)),
            pltpu.SemaphoreType.DMA((KINDS, 2, depth)),
            pltpu.SemaphoreType.DMA((KINDS, depth)),
            pltpu.SemaphoreType.DMA((KINDS, depth)),
            pltpu.SemaphoreType.DMA((KINDS, 2, depth)),
            pltpu.SemaphoreType.DMA,
            pltpu.SemaphoreType.DMA,
        ],
        compiler_params=pltpu.CompilerParams(
            collective_id=call_id, has_side_effects=True, vmem_limit_bytes=VMEM_CAP
        ),
        name="reduce_layer",
    )(square, expand, reduce_turned)


TILE = 128
PAIRS = HEADS // 2
GELU_IN = (2.0 / np.pi) ** 0.5


def dot_nn(left, right):
    return jnp.dot(left, right, preferred_element_type=jnp.float32)


def dot_nt(left, right):
    return lax.dot_general(left, right, (((1,), (1,)), ((), ())), preferred_element_type=jnp.float32)


def dot_tn(left, right):
    return lax.dot_general(left, right, (((0,), (0,)), ((), ())), preferred_element_type=jnp.float32)


def rows_at(index, size):
    return pl.ds(pl.multiple_of(index * size, size), size)


def split_heads(block):
    low = lax.broadcasted_iota(jnp.int32, block.shape, 1) < HEAD
    wide = block.astype(jnp.float32)
    first = jnp.where(low, wide, 0.0).astype(jnp.bfloat16)
    second = jnp.where(low, 0.0, wide).astype(jnp.bfloat16)
    return jnp.concatenate([first, second], axis=0)


def join_heads(stacked):
    return jnp.concatenate([stacked[:TILE], stacked[TILE:]], axis=1)


def pair_probs(query, keys_here, bias, mask):
    scores = dot_nt(split_heads(query), keys_here) * HEAD ** (-0.5) + bias
    scores = scores + mask
    raised = jnp.exp(scores - jnp.max(scores, axis=1, keepdims=True))
    return raised / jnp.sum(raised, axis=1, keepdims=True)


def pair_bias(bias_ref, pair):
    return jnp.concatenate([bias_ref[2 * pair], bias_ref[2 * pair + 1]], axis=0)


def tile_mask(mask_ref, tile):
    mask = mask_ref[tile]
    return jnp.concatenate([mask, mask], axis=0)


def hot_rows(rank_ref, rows, tokens):
    place = lax.broadcasted_iota(jnp.int32, (rows.size, tokens), 1)
    return (rank_ref[rows, :1] == place).astype(jnp.float32).astype(jnp.bfloat16)


def norm_rows(values, gain):
    scale = lax.rsqrt(jnp.mean(values * values, axis=1, keepdims=True) + NORM_EPS)
    return values * scale * gain


def gelu_parts(pre):
    inner = GELU_IN * (pre + 0.044715 * pre * pre * pre)
    return jnp.tanh(inner)


def forward_kernel(
    found_ref, rank_ref, square_ref, expand_ref, reduce_ref, gains_ref, bias_ref, mask_ref, pool_ref, length_ref,
    start_ref, query_ref, key_ref, value_ref, mixed_ref, middle_ref, ending_ref, low_ref, pooled_ref, embed_ref,
    inverse_ref, normed, pooled_sum,
):
    tokens = start_ref.shape[0]
    big = 512

    def begin(r, carry):
        rows = rows_at(r, 256)
        start = dot_nt(hot_rows(rank_ref, rows, tokens), found_ref[...])
        start_ref[rows, :] = start.astype(jnp.bfloat16)
        normed[rows, :] = norm_rows(start, gains_ref[0:1]).astype(jnp.bfloat16)
        return carry

    lax.fori_loop(0, tokens // 256, begin, 0)
    for k, target in enumerate((query_ref, key_ref, value_ref)):

        def project(r, carry):
            rows = rows_at(r, big)
            target[rows, :] = dot_nn(normed[rows, :], square_ref[k]).astype(jnp.bfloat16)
            return carry

        lax.fori_loop(0, tokens // big, project, 0)

    def attend(t, carry):
        rows = rows_at(t, TILE)
        mask = tile_mask(mask_ref, t)
        for pair in range(PAIRS):
            lanes = pl.ds(pair * TILE, TILE)
            probs = pair_probs(query_ref[rows, lanes], key_ref[rows, lanes], pair_bias(bias_ref, pair), mask)
            mixed = dot_nn(join_heads(probs).astype(jnp.bfloat16), split_heads(value_ref[rows, lanes]))
            mixed_ref[rows, lanes] = mixed.astype(jnp.bfloat16)
        return carry

    lax.fori_loop(0, tokens // TILE, attend, 0)

    def merge(r, carry):
        rows = rows_at(r, big)
        middle = start_ref[rows, :].astype(jnp.float32) + dot_nn(mixed_ref[rows, :], square_ref[3])
        middle_ref[rows, :] = middle
        ending_ref[rows, :] = middle
        normed[rows, :] = norm_rows(middle, gains_ref[1:2]).astype(jnp.bfloat16)
        return carry

    lax.fori_loop(0, tokens // big, merge, 0)
    wide = expand_ref.shape[1]

    def feed(c, carry):
        lanes = rows_at(c, D)

        def rows_of(r, inner):
            rows = rows_at(r, big)
            pre = dot_nn(normed[rows, :], expand_ref[:, lanes])
            act = (0.5 * pre * (1.0 + gelu_parts(pre))).astype(jnp.bfloat16)
            ending_ref[rows, :] += dot_nt(act, reduce_ref[:, lanes])
            return inner

        return lax.fori_loop(0, tokens // big, rows_of, carry)

    lax.fori_loop(0, wide // D, feed, 0)
    pooled_sum[...] = jnp.zeros_like(pooled_sum)

    def pool(r, carry):
        rows = rows_at(r, 256)
        output = norm_rows(ending_ref[rows, :], gains_ref[2:3])
        pooled_sum[...] += jnp.dot(
            pool_ref[:, rows], output, precision=HIGHEST, preferred_element_type=jnp.float32
        )
        return carry

    lax.fori_loop(0, tokens // 256, pool, 0)
    pooled = (pooled_sum[...] / length_ref[:, :1]).astype(jnp.bfloat16)
    pooled_ref[...] = pooled
    projected = dot_nn(pooled, square_ref[4])
    inverse = lax.rsqrt(jnp.sum(projected * projected, axis=1, keepdims=True) + NORM_EPS)
    embeds = projected * inverse
    embed_ref[...] = embeds
    low_ref[...] = embeds.astype(jnp.bfloat16)
    inverse_ref[...] = jnp.broadcast_to(inverse, inverse_ref.shape)


def run_forward(found, rank, square, expand, reduce_turned, gains, bias, mask, pool, lengths):
    tokens = found.shape[1]
    seqs = pool.shape[0]
    low = jnp.bfloat16
    flat = jax.ShapeDtypeStruct((tokens, D), low)
    full = jax.ShapeDtypeStruct((tokens, D), jnp.float32)
    return pl.pallas_call(
        forward_kernel,
        out_shape=[
            flat, flat, flat, flat, flat, full, full,
            jax.ShapeDtypeStruct((seqs, D), low),
            jax.ShapeDtypeStruct((seqs, D), low),
            jax.ShapeDtypeStruct((seqs, D), jnp.float32),
            jax.ShapeDtypeStruct((seqs, LANES), jnp.float32),
        ],
        scratch_shapes=[pltpu.VMEM((tokens, D), low), pltpu.VMEM((seqs, D), jnp.float32)],
        compiler_params=pltpu.CompilerParams(vmem_limit_bytes=VMEM_CAP),
        name="layer_forward",
    )(found, rank, square, expand, reduce_turned, gains, bias, mask, pool, lengths)


def norm_back_rows(values, gain, grad):
    scale = lax.rsqrt(jnp.mean(values * values, axis=1, keepdims=True) + NORM_EPS)
    weighted = grad * gain
    inner = jnp.mean(weighted * values, axis=1, keepdims=True)
    through = scale * weighted - values * (scale * scale * scale * inner)
    return through, jnp.sum(grad * values * scale, axis=0, keepdims=True)


def feed_back_kernel(
    grad_embed_ref, embed_ref, inverse_ref, pool_ref, length_ref, last_ref, middle_ref, ending_ref, expand_ref,
    reduce_ref, gains_ref,
    grad_expand_ref, grad_reduce_ref, grad_middle_ref, grad_low_ref, grad_proj_ref, grad_gains_ref,
    normed, normed_turned, end_low, end_turned, back,
):
    tokens = middle_ref.shape[0]
    embeds, grads = embed_ref[...], grad_embed_ref[...]
    grad_proj = inverse_ref[:, :1] * (grads - embeds * jnp.sum(grads * embeds, axis=1, keepdims=True))
    grad_proj = grad_proj.astype(jnp.bfloat16)
    grad_proj_ref[...] = grad_proj
    grad_pooled = dot_nt(grad_proj, last_ref[0]) / length_ref[:, :1]
    grad_gains_ref[...] = jnp.zeros_like(grad_gains_ref)

    def begin(r, carry):
        rows = rows_at(r, 256)
        grad_out = lax.dot_general(
            pool_ref[:, rows], grad_pooled, (((0,), (0,)), ((), ())), precision=HIGHEST,
            preferred_element_type=jnp.float32,
        )
        through, gain = norm_back_rows(ending_ref[rows, :], gains_ref[2:3], grad_out)
        grad_gains_ref[2:3] += gain
        grad_middle_ref[rows, :] = through
        end_low[rows, :] = through.astype(jnp.bfloat16)
        end_turned[:, rows] = through.T.astype(jnp.bfloat16)
        middle_normed = norm_rows(middle_ref[rows, :], gains_ref[1:2])
        normed[rows, :] = middle_normed.astype(jnp.bfloat16)
        normed_turned[:, rows] = middle_normed.T.astype(jnp.bfloat16)
        return carry

    lax.fori_loop(0, tokens // 256, begin, 0)
    back[...] = jnp.zeros_like(back)
    wide = expand_ref.shape[1]
    step = 384

    def feed(c, carry):
        lanes = rows_at(c, step)
        pre = dot_nn(normed[...], expand_ref[:, lanes])
        grad_act = dot_nn(end_low[...], reduce_ref[:, lanes])
        turn = gelu_parts(pre)
        act = (0.5 * pre * (1.0 + turn)).astype(jnp.bfloat16)
        slope = 0.5 * (1.0 + turn) + 0.5 * pre * (1.0 - turn * turn) * GELU_IN * (1.0 + 3.0 * 0.044715 * pre * pre)
        grad_pre = (grad_act * slope).astype(jnp.bfloat16)
        grad_reduce_ref[:, lanes] = dot_nn(end_turned[...], act).astype(jnp.bfloat16)
        grad_expand_ref[:, lanes] = dot_nn(normed_turned[...], grad_pre).astype(jnp.bfloat16)
        back[...] += dot_nt(grad_pre, expand_ref[:, lanes])
        return carry

    lax.fori_loop(0, wide // step, feed, 0)

    def end(r, carry):
        rows = rows_at(r, 256)
        through, gain = norm_back_rows(middle_ref[rows, :], gains_ref[1:2], back[rows, :])
        grad_gains_ref[1:2] += gain
        grad_middle = grad_middle_ref[rows, :] + through
        grad_middle_ref[rows, :] = grad_middle
        grad_low_ref[rows, :] = grad_middle.astype(jnp.bfloat16)
        return carry

    lax.fori_loop(0, tokens // 256, end, 0)


def run_feed_back(grad_embed, embeds, inverse, pool, lengths, square, middle, ending, expand, reduce_turned, gains):
    tokens = middle.shape[0]
    seqs = pool.shape[0]
    low = jnp.bfloat16
    whole = pl.BlockSpec(memory_space=pltpu.VMEM)
    return pl.pallas_call(
        feed_back_kernel,
        grid=(1,),
        out_shape=[
            jax.ShapeDtypeStruct(expand.shape, low),
            jax.ShapeDtypeStruct(reduce_turned.shape, low),
            jax.ShapeDtypeStruct((tokens, D), jnp.float32),
            jax.ShapeDtypeStruct((tokens, D), low),
            jax.ShapeDtypeStruct((seqs, D), low),
            jax.ShapeDtypeStruct((8, D), jnp.float32),
        ],
        in_specs=[whole] * 5
        + [pl.BlockSpec((1, D, D), lambda i: (4, 0, 0))]
        + [whole] * 5,
        out_specs=[whole] * 6,
        scratch_shapes=[
            pltpu.VMEM((tokens, D), low),
            pltpu.VMEM((D, tokens), low),
            pltpu.VMEM((tokens, D), low),
            pltpu.VMEM((D, tokens), low),
            pltpu.VMEM((tokens, D), jnp.float32),
        ],
        compiler_params=pltpu.CompilerParams(vmem_limit_bytes=VMEM_CAP),
        name="feed_backward",
    )(grad_embed, embeds, inverse, pool, lengths, square, middle, ending, expand, reduce_turned, gains)


def attend_back_kernel(
    grad_middle_ref, grad_low_ref, grad_proj_ref, pooled_ref, start_ref, query_ref, key_ref, value_ref, mixed_ref,
    square_ref, gains_ref, bias_ref, mask_ref, rank_ref,
    grad_square_ref, grad_score_ref, grad_gain_ref, send_ref,
    grad_mixed, turned, grad_query, grad_key, grad_value, start_low,
):
    tokens = start_ref.shape[0]
    big = 512
    grad_square_ref[4] = dot_tn(pooled_ref[...], grad_proj_ref[...]).astype(jnp.bfloat16)

    def begin(r, carry):
        rows = rows_at(r, big)
        grad_mixed[rows, :] = dot_nt(grad_low_ref[rows, :], square_ref[3]).astype(jnp.bfloat16)
        turned[:, rows] = mixed_ref[rows, :].astype(jnp.float32).T.astype(jnp.bfloat16)
        return carry

    lax.fori_loop(0, tokens // big, begin, 0)

    def outer(target, right_ref):
        def part(r, carry):
            rows = rows_at(r, 384)
            grad_square_ref[target, rows, :] = dot_nn(turned[rows, :], right_ref[...]).astype(jnp.bfloat16)
            return carry

        lax.fori_loop(0, D // 384, part, 0)

    outer(3, grad_low_ref)
    grad_score_ref[...] = jnp.zeros_like(grad_score_ref)

    def attend(t, carry):
        rows = rows_at(t, TILE)
        mask = tile_mask(mask_ref, t)
        for pair in range(PAIRS):
            lanes = pl.ds(pair * TILE, TILE)
            query, keys_here = query_ref[rows, lanes], key_ref[rows, lanes]
            probs = pair_probs(query, keys_here, pair_bias(bias_ref, pair), mask)
            grads = split_heads(grad_mixed[rows, lanes])
            grad_probs = dot_nt(grads, value_ref[rows, lanes])
            grad_value[rows, lanes] = dot_tn(probs.astype(jnp.bfloat16), grads).astype(jnp.bfloat16)
            inner = jnp.sum(grad_probs * probs, axis=1, keepdims=True)
            grad_scores = (probs * (grad_probs - inner)).astype(jnp.bfloat16)
            kept = grad_scores.astype(jnp.float32)
            grad_score_ref[2 * pair] += kept[:TILE]
            grad_score_ref[2 * pair + 1] += kept[TILE:]
            grad_query[rows, lanes] = (
                dot_nn(join_heads(grad_scores), split_heads(keys_here)) * HEAD ** (-0.5)
            ).astype(jnp.bfloat16)
            grad_key[rows, lanes] = (dot_tn(grad_scores, split_heads(query)) * HEAD ** (-0.5)).astype(jnp.bfloat16)
        return carry

    lax.fori_loop(0, tokens // TILE, attend, 0)

    def renorm(r, carry):
        rows = rows_at(r, 256)
        normed = norm_rows(start_ref[rows, :].astype(jnp.float32), gains_ref[0:1])
        turned[:, rows] = normed.T.astype(jnp.bfloat16)
        return carry

    lax.fori_loop(0, tokens // 256, renorm, 0)
    outer(0, grad_query)
    outer(1, grad_key)
    outer(2, grad_value)
    grad_gain_ref[...] = jnp.zeros_like(grad_gain_ref)

    def end(r, carry):
        rows = rows_at(r, 256)
        grad_normed = (
            dot_nt(grad_query[rows, :], square_ref[0])
            + dot_nt(grad_key[rows, :], square_ref[1])
            + dot_nt(grad_value[rows, :], square_ref[2])
        )
        through, gain = norm_back_rows(start_ref[rows, :].astype(jnp.float32), gains_ref[0:1], grad_normed)
        grad_gain_ref[0:1] += gain
        turned[:, rows] = (grad_middle_ref[rows, :] + through).T.astype(jnp.bfloat16)
        return carry

    lax.fori_loop(0, tokens // 256, end, 0)

    def hot(r, carry):
        rows = rows_at(r, 256)
        start_low[rows, :] = hot_rows(rank_ref, rows, tokens)
        return carry

    lax.fori_loop(0, tokens // 256, hot, 0)

    def gather_rows(r, carry):
        rows = rows_at(r, 384)
        send_ref[rows, :] = dot_nn(turned[rows, :], start_low[...]).astype(jnp.bfloat16)
        return carry

    lax.fori_loop(0, D // 384, gather_rows, 0)


def run_attend_back(
    grad_middle, grad_low, grad_proj, pooled, start, queries, keys_here, values_here, mixed, square, gains, bias,
    mask, rank,
):
    tokens = start.shape[0]
    low = jnp.bfloat16
    return pl.pallas_call(
        attend_back_kernel,
        out_shape=[
            jax.ShapeDtypeStruct((5, D, D), low),
            jax.ShapeDtypeStruct((HEADS, TILE, TILE), jnp.float32),
            jax.ShapeDtypeStruct((8, D), jnp.float32),
            jax.ShapeDtypeStruct((D, tokens), low),
        ],
        scratch_shapes=[
            pltpu.VMEM((tokens, D), low),
            pltpu.VMEM((D, tokens), low),
            pltpu.VMEM((tokens, D), low),
            pltpu.VMEM((tokens, D), low),
            pltpu.VMEM((tokens, D), low),
            pltpu.VMEM((tokens, tokens), low),
        ],
        compiler_params=pltpu.CompilerParams(vmem_limit_bytes=VMEM_CAP),
        name="attend_backward",
    )(
        grad_middle, grad_low, grad_proj, pooled, start, queries, keys_here, values_here, mixed, square, gains, bias,
        mask, rank,
    )


def shards(
    embed_table,
    square_weights,
    expand_weight,
    reduce_weight,
    norm_gains,
    position_bias,
    log_scale,
    table_moment,
    table_second,
    square_moment,
    square_second,
    expand_moment,
    expand_second,
    reduce_moment,
    reduce_second,
    gains_moment,
    gains_second,
    position_moment,
    position_second,
    scale_moment,
    scale_second,
    query_tokens,
    answer_tokens,
    query_length,
    answer_length,
    premise_tokens,
    hypothesis_tokens,
    hard_negative,
):
    both = ("dp", "fsdp")
    dp_size, fsdp_size = lax.axis_size("dp"), lax.axis_size("fsdp")
    count = dp_size * fsdp_size
    direct = dp_size == 8 and fsdp_size == 4
    position = lax.axis_index(both)
    feats, vocab_size = embed_table.shape
    feats_pad = up8(feats)
    fold = fold_rows(vocab_size)
    query_rows = query_tokens.shape[0]
    nli_rows = premise_tokens.shape[0]
    short_length = query_tokens.shape[1]
    long_length = answer_tokens.shape[1]
    short_tokens = jnp.concatenate([query_tokens, premise_tokens, hypothesis_tokens], axis=0)
    lengths = jnp.concatenate(
        [query_length, jnp.full((2 * nli_rows,), short_length, jnp.int32), answer_length]
    )
    all_tokens = jnp.concatenate([short_tokens.reshape(-1), answer_tokens.reshape(-1)])
    token_count = all_tokens.shape[0]
    hypo_start = query_rows + nli_rows
    answer_start = query_rows + 2 * nli_rows
    seq_count = answer_start + query_rows
    seq_pad = -(-seq_count // 16) * 16
    split_at = short_tokens.shape[0] * short_length

    packed, rank = token_keys(all_tokens, fold)
    start_info = jnp.concatenate(
        [
            packed.reshape(-1, LANES).astype(jnp.float32),
            jnp.pad(hard_negative, (0, LANES - nli_rows)).reshape(1, LANES).astype(jnp.float32),
            jnp.pad(norm_gains, ((0, 7 - 3), (0, LANES - feats))),
        ],
        axis=0,
    )
    key_rows = token_count // LANES
    info_all = exchange(start_info[None], True, 0, "share_start")
    packed_all = info_all[:, :key_rows].astype(jnp.int32).reshape(count, 1, token_count)
    negative_all = info_all[:, key_rows, :nli_rows].astype(jnp.int32).reshape(-1)
    gains = info_all[:, key_rows + 1 : key_rows + 4, :feats].transpose(1, 0, 2).reshape(3, D)
    gains = jnp.pad(gains.astype(jnp.bfloat16).astype(jnp.float32), ((0, 5), (0, 0)))
    row_all, group_all = packed_all >> 2, packed_all & 3

    square_low = square_weights.astype(jnp.bfloat16)
    expand_low = expand_weight.astype(jnp.bfloat16)
    reduce_low = reduce_weight.astype(jnp.bfloat16).T
    table_low = embed_table.astype(jnp.bfloat16).astype(jnp.float32)
    if direct:
        square_pieces = square_low.reshape(5, 2, 48, 192).transpose(1, 0, 2, 3)
        found, square_all, expand_all, reduce_all = run_front(
            row_all[:, 0], group_all[:, 0], table_low, square_pieces, expand_low, reduce_low, 1
        )
    else:

        def whole(piece, row_name, column_name):
            axis = piece.ndim - 2
            wide = lax.all_gather(piece, column_name, axis=axis + 1, tiled=True)
            return lax.all_gather(wide, row_name, axis=axis, tiled=True)

        square_all = whole(square_low, "dp", "fsdp")
        expand_all = whole(expand_low, "dp", "fsdp")
        reduce_all = whole(reduce_low, "fsdp", "dp")
        if feats_pad > feats:
            table_low = jnp.pad(table_low, ((0, feats_pad - feats), (0, 0)))
        found = exchange(lookup(table_low, row_all, group_all), False, 2, "send_features")
    half = token_count // 2
    found = found.reshape(count, 2, feats_pad, half)[:, :, :feats]
    found = found.transpose(0, 2, 1, 3).reshape(D, token_count)

    sequence = np.concatenate(
        [
            np.repeat(np.arange(answer_start), short_length),
            answer_start + np.repeat(np.arange(query_rows), long_length),
        ]
    )
    inside = np.concatenate(
        [
            np.tile(np.arange(short_length), answer_start),
            np.tile(np.arange(long_length), query_rows),
        ]
    )
    lengths_pad = jnp.pad(lengths, (0, seq_pad - seq_count), constant_values=1)
    pool = (sequence[None, :] == np.arange(seq_pad)[:, None]) & (inside[None, :] < lengths_pad[:, None])
    token_ok = jnp.any(pool, axis=0).reshape(-1, 1, TILE)
    sequence_tiles = sequence.reshape(-1, TILE)
    together = sequence_tiles[:, :, None] == sequence_tiles[:, None, :]
    mask = jnp.where(together & token_ok, 0.0, -1e30).astype(jnp.float32)
    pool = pool.astype(jnp.float32)
    length_rows = jnp.broadcast_to(lengths_pad.astype(jnp.float32)[:, None], (seq_pad, LANES))
    rank_rows = jnp.broadcast_to(rank[:, None], (token_count, LANES))
    bias, onehot = attention_bias(position_bias, TILE)

    (start, queries, keys_here, values_here, mixed, middle, ending, embeds_low, pooled, embeds, inverse) = run_forward(
        found, rank_rows, square_all, expand_all, reduce_all, gains, bias, mask, pool, length_rows
    )
    gathered = exchange(embeds_low[None], True, 3, "share_embeds")
    queries_all = gathered[:, :query_rows].reshape(-1, D)
    premises_all = gathered[:, query_rows:hypo_start].reshape(-1, D)
    hypotheses_all = gathered[:, hypo_start:answer_start].reshape(-1, D)
    answers_all = gathered[:, answer_start:seq_count].reshape(-1, D)
    scale = jnp.exp(log_scale[0])

    def contrast(left, right, extra, own):
        sims = product_right(left, right)
        logits = scale * sims
        row_top = jnp.max(logits, axis=1, keepdims=True)
        raised = (1.0 + extra) * jnp.exp(logits - row_top)
        row_total = jnp.sum(raised, axis=1, keepdims=True)
        spread = row_top[:, 0] + jnp.log(row_total[:, 0])
        target_hit = jnp.eye(left.shape[0], dtype=jnp.float32)
        loss_sum = jnp.sum(spread - jnp.sum(target_hit * logits, axis=1))
        grad_logits = raised / row_total - target_hit
        grad_scale = jnp.sum(grad_logits * sims)
        grad_sims = (scale * grad_logits).astype(jnp.bfloat16)
        mine_left = lax.dynamic_slice_in_dim(grad_sims, position * own, own, 0)
        mine_right = lax.dynamic_slice_in_dim(grad_sims, position * own, own, 1)
        return (loss_sum, grad_scale, product(mine_left, right), product_left(mine_right, left))

    first_loss, first_dscale, grad_queries, grad_answers = contrast(
        queries_all, answers_all, 0.0, query_rows
    )
    negatives = (jnp.arange(hypotheses_all.shape[0])[None, :] == negative_all[:, None]).astype(
        jnp.float32
    )
    second_loss, second_dscale, grad_premises, grad_hypotheses = contrast(
        premises_all, hypotheses_all, negatives, nli_rows
    )
    grad_embeds = jnp.concatenate(
        [
            grad_queries,
            grad_premises,
            grad_hypotheses,
            grad_answers,
            jnp.zeros((seq_pad - seq_count, D), jnp.float32),
        ],
        axis=0,
    )
    (grad_expand, grad_reduce, grad_middle, grad_middle_low, grad_proj, late_gains) = run_feed_back(
        grad_embeds, embeds, inverse, pool, length_rows, square_all, middle, ending, expand_all, reduce_all, gains
    )
    (grad_square, grad_scores, first_gain, merged) = run_attend_back(
        grad_middle, grad_middle_low, grad_proj, pooled, start, queries, keys_here, values_here, mixed, square_all,
        gains, bias, mask, rank_rows
    )
    grad_gains = jnp.concatenate([first_gain[:1], late_gains[1:3]], axis=0)
    grad_position = lax.dot_general(
        onehot, grad_scores.reshape(HEADS, TILE * TILE), (((0,), (1,)), ((), ())), precision=HIGHEST
    )
    grad_scale = ((first_dscale + second_dscale) * scale).reshape(1)
    merged = merged.reshape(count, feats, 2, half).transpose(0, 2, 1, 3)
    if feats_pad > feats:
        merged = jnp.pad(merged, ((0, 0), (0, 0), (0, feats_pad - feats), (0, 0)))
    returned = exchange(merged.reshape(count, 2 * feats_pad, half), False, 4, "send_gradients")
    grad_table = scatter(returned, row_all, group_all, vocab_size)[:feats]
    if direct:
        square_sum, expand_sum, reduce_sum = reduce_blocks(grad_square, grad_expand, grad_reduce, 5)
        square_sum = square_sum.transpose(1, 0, 2, 3).reshape(5, 96, 192)
    else:

        def shard(gradient, row_name, column_name):
            axis = gradient.ndim - 2
            part = lax.psum_scatter(
                gradient.astype(jnp.float32), row_name, scatter_dimension=axis, tiled=True
            )
            return lax.psum_scatter(part, column_name, scatter_dimension=axis + 1, tiled=True)

        square_sum = shard(grad_square, "dp", "fsdp")
        expand_sum = shard(grad_expand, "dp", "fsdp")
        reduce_sum = shard(grad_reduce, "fsdp", "dp")
    reduced = (square_sum, expand_sum, reduce_sum.T)
    local_square = (
        jnp.sum(reduced[0] * reduced[0])
        + jnp.sum(reduced[1] * reduced[1])
        + jnp.sum(reduce_sum * reduce_sum)
        + jnp.sum(grad_table * grad_table)
    )
    small = jnp.concatenate([grad_gains.reshape(-1), grad_position.reshape(-1), local_square.reshape(1)])
    small_rows = -(-small.shape[0] // (8 * LANES)) * 8
    small = jnp.pad(small, (0, small_rows * LANES - small.shape[0])).reshape(1, small_rows, LANES)
    summed = jnp.sum(exchange(small, True, 6, "share_small"), axis=0).reshape(-1)
    gains_total = summed[: 3 * D].reshape(3, D)
    position_total = summed[3 * D : 3 * D + BUCKETS * HEADS].reshape(BUCKETS, HEADS)
    square_total = summed[3 * D + BUCKETS * HEADS]
    scale_total = grad_scale
    losses = jnp.stack([first_loss, second_loss])
    grad_gain_shard = lax.dynamic_slice_in_dim(gains_total, position * feats, feats, 1)
    gradient_norm = jnp.sqrt(
        square_total
        + jnp.sum(gains_total * gains_total)
        + jnp.sum(position_total * position_total)
        + jnp.sum(scale_total * scale_total)
    )
    factor = jnp.minimum(1.0, CLIP_NORM / gradient_norm)
    table_out = adam_update(embed_table, table_moment, table_second, grad_table, factor, TABLE_RATE)
    square_out = adam_update(
        square_weights, square_moment, square_second, reduced[0], factor, LEARN_RATE
    )
    expand_out = adam_update(
        expand_weight, expand_moment, expand_second, reduced[1], factor, LEARN_RATE
    )
    reduce_out = adam_update(
        reduce_weight, reduce_moment, reduce_second, reduced[2], factor, LEARN_RATE
    )
    gains_out = adam_update(
        norm_gains, gains_moment, gains_second, grad_gain_shard, factor, SMALL_RATE
    )
    position_out = adam_update(
        position_bias, position_moment, position_second, position_total, factor, SMALL_RATE
    )
    scale_out = adam_update(log_scale, scale_moment, scale_second, scale_total, factor, SMALL_RATE)
    return (
        *table_out,
        *square_out,
        *expand_out,
        *reduce_out,
        *gains_out,
        *position_out,
        *scale_out,
        losses,
        gradient_norm,
    )


def solution(mesh):
    return jax.shard_map(
        shards,
        mesh=mesh,
        in_specs=(
            P(("dp", "fsdp"), None),
            P(None, "dp", "fsdp"),
            P("dp", "fsdp"),
            P("dp", "fsdp"),
            P(None, ("dp", "fsdp")),
            P(),
            P(),
            P(("dp", "fsdp"), None),
            P(("dp", "fsdp"), None),
            P(None, "dp", "fsdp"),
            P(None, "dp", "fsdp"),
            P("dp", "fsdp"),
            P("dp", "fsdp"),
            P("dp", "fsdp"),
            P("dp", "fsdp"),
            P(None, ("dp", "fsdp")),
            P(None, ("dp", "fsdp")),
            P(),
            P(),
            P(),
            P(),
            P(("dp", "fsdp"), None),
            P(("dp", "fsdp"), None),
            P(("dp", "fsdp")),
            P(("dp", "fsdp")),
            P(("dp", "fsdp"), None),
            P(("dp", "fsdp"), None),
            P(("dp", "fsdp")),
        ),
        out_specs=(
            P(("dp", "fsdp"), None),
            P(("dp", "fsdp"), None),
            P(("dp", "fsdp"), None),
            P(None, "dp", "fsdp"),
            P(None, "dp", "fsdp"),
            P(None, "dp", "fsdp"),
            P("dp", "fsdp"),
            P("dp", "fsdp"),
            P("dp", "fsdp"),
            P("dp", "fsdp"),
            P("dp", "fsdp"),
            P("dp", "fsdp"),
            P(None, ("dp", "fsdp")),
            P(None, ("dp", "fsdp")),
            P(None, ("dp", "fsdp")),
            P(),
            P(),
            P(),
            P(),
            P(),
            P(),
            P(),
            P(),
        ),
        check_vma=False,
    )
```

```python
import functools

import jax
import jax.numpy as jnp
import numpy as np
from jax import lax
from jax.experimental import pallas as pl
from jax.experimental.pallas import tpu as pltpu
from jax.sharding import PartitionSpec as P

D = 768
HEADS = 12
HEAD = 64
BUCKETS = 32
MAXDIST = 128
STEP = 10


HIGHEST = lax.Precision.HIGHEST
NORM_EPS = 1e-06
LEARN_RATE = 0.03
TABLE_RATE = 0.4
SMALL_RATE = 0.5
BETA_ONE = 0.9
BETA_TWO = 0.999
ADAM_EPS = 1e-08
WEIGHT_DECAY = 0.01
CLIP_NORM = 0.5


def bucket_table(length):
    places = np.arange(length)
    offset = places[None, :] - places[:, None]
    half_count = BUCKETS // 2
    exact_count = half_count // 2
    upper = (offset > 0).astype(np.int64) * half_count
    distance = np.abs(offset)
    far_bucket = exact_count + (
        np.log(np.maximum(distance, 1) / exact_count)
        / np.log(MAXDIST / exact_count)
        * (half_count - exact_count)
    ).astype(np.int64)
    far_bucket = np.minimum(far_bucket, half_count - 1)
    return (upper + np.where(distance < exact_count, distance, far_bucket)).astype(np.int32)


def bucket_onehot(length):
    flat_table = bucket_table(length).reshape(-1)
    return jnp.asarray((flat_table[:, None] == np.arange(BUCKETS)[None, :]).astype(np.float32))


def product(left, right):
    return jnp.dot(left, right, preferred_element_type=jnp.float32)


def product_left(left, right):
    return lax.dot_general(
        left, right, (((0,), (0,)), ((), ())), preferred_element_type=jnp.float32
    )


def product_right(left, right):
    return lax.dot_general(
        left, right, (((1,), (1,)), ((), ())), preferred_element_type=jnp.float32
    )


def attention_bias(position_bias, length):
    onehot = bucket_onehot(length)
    flat_bias = jnp.dot(onehot, position_bias, precision=HIGHEST)
    return (jnp.transpose(flat_bias.reshape(length, length, HEADS), (2, 0, 1)), onehot)


def adam_update(weight, moment, second, grad, factor, rate):
    clipped = grad * factor
    moment_new = BETA_ONE * moment + (1 - BETA_ONE) * clipped
    second_new = BETA_TWO * second + (1 - BETA_TWO) * clipped * clipped
    moment_hat = moment_new / (1 - BETA_ONE**STEP)
    second_hat = second_new / (1 - BETA_TWO**STEP)
    updated = weight - rate * (
        moment_hat / (jnp.sqrt(second_hat) + ADAM_EPS) + WEIGHT_DECAY * weight
    )
    return (moment_new, second_new, updated)


LANES = 128
GROUPS = 4
SLOT = LANES // GROUPS
VMEM_CAP = 56 * 1024 * 1024

def fold_rows(vocab):
    per = -(-vocab // GROUPS)
    return -(-per // LANES) * LANES

def up8(n):
    return -(-n // 8) * 8

def eye():
    r = lax.broadcasted_iota(jnp.int32, (LANES, LANES), 0)
    c = lax.broadcasted_iota(jnp.int32, (LANES, LANES), 1)
    return (r == c).astype(jnp.float32).astype(jnp.bfloat16)

def turn_table(fold, table_ref, turned):
    feats, vocab = table_ref.shape
    pad = jnp.zeros((SLOT - feats, LANES), jnp.float32)

    def build(b, carry):
        parts = []
        for j in range(GROUPS):
            start = jnp.minimum(j * fold + b * LANES, vocab - LANES)
            start = pl.multiple_of(start, LANES)
            parts += [table_ref[:, pl.ds(start, LANES)], pad]
        tile = jnp.concatenate(parts, axis=0)
        turned[pl.ds(pl.multiple_of(b * LANES, LANES), LANES), :] = tile.T
        return carry

    lax.fori_loop(0, fold // LANES, build, 0)
    turned[pl.ds(fold, 8), :] = jnp.zeros((8, LANES), jnp.float32)


def look_up(row_ref, group_ref, source, turned, rows, feats):
    tokens = rows.shape[0]
    batch = 32

    def fetch(b, carry):
        for k in range(batch):
            t = b * batch + k
            rows[pl.ds(t, 1), :] = turned[pl.ds(row_ref[source, t], 1), :]
        return carry

    lax.fori_loop(0, tokens // batch, fetch, 0)
    wide = dot_nt(eye(), rows[...].astype(jnp.bfloat16))
    group = group_ref[source]
    total = jnp.where(group == 0, wide[:SLOT], 0.0)
    for j in range(1, GROUPS):
        total = total + jnp.where(group == j, wide[j * SLOT : (j + 1) * SLOT], 0.0)
    half = tokens // 2
    return jnp.concatenate([total[:feats, :half], total[:feats, half:]], axis=0).astype(jnp.bfloat16)


def lookup_kernel(fold, row_ref, group_ref, table_ref, out_ref, turned, rows):
    @pl.when(pl.program_id(0) == 0)
    def _():
        turn_table(fold, table_ref, turned)

    out_ref[0] = look_up(row_ref, group_ref, 0, turned, rows, table_ref.shape[0])


def lookup(table, rows_idx, groups_idx):
    feats, vocab = table.shape
    n, tokens = rows_idx.shape[0], rows_idx.shape[2]
    fold = fold_rows(vocab)
    return pl.pallas_call(
        functools.partial(lookup_kernel, fold),
        grid=(n,),
        out_shape=jax.ShapeDtypeStruct((n, 2 * feats, tokens // 2), jnp.bfloat16),
        in_specs=[
            pl.BlockSpec((None, 1, tokens), lambda s: (s, 0, 0), memory_space=pltpu.SMEM),
            pl.BlockSpec((1, 1, tokens), lambda s: (s, 0, 0)),
            pl.BlockSpec((feats, vocab), lambda s: (0, 0)),
        ],
        out_specs=pl.BlockSpec((1, 2 * feats, tokens // 2), lambda s: (s, 0, 0)),
        scratch_shapes=[pltpu.VMEM((fold + 8, LANES), jnp.float32), pltpu.VMEM((tokens, LANES), jnp.float32)],
        compiler_params=pltpu.CompilerParams(vmem_limit_bytes=VMEM_CAP),
        name="lookup",
    )(rows_idx, groups_idx, table)

def scatter_kernel(fold, row_ref, group_ref, grad_ref, out_ref, total, rows):
    feats, vocab = out_ref.shape
    tokens = rows.shape[0]
    step = pl.program_id(0)
    @pl.when(step == 0)
    def _():
        def clear(b, _):
            total[pl.ds(pl.multiple_of(b * LANES, LANES), LANES), :] = jnp.zeros((LANES, LANES), jnp.float32)
            return 0
        lax.fori_loop(0, fold // LANES, clear, 0)
        total[pl.ds(fold, 8), :] = jnp.zeros((8, LANES), jnp.float32)
    block = grad_ref[0].astype(jnp.float32)
    flat = jnp.concatenate([block[:feats], block[feats:]], axis=1)
    group = group_ref[0]
    pad = jnp.zeros((SLOT - feats, tokens), jnp.float32)
    parts = []
    for j in range(GROUPS):
        parts += [jnp.where(group == j, flat, 0.0), pad]
    spread = jnp.concatenate(parts, axis=0).astype(jnp.bfloat16)
    rows[...] = lax.dot_general(spread, eye(), (((0,), (0,)), ((), ())), preferred_element_type=jnp.float32)
    LN = 16
    stride = tokens // LN
    def add(i, _):
        at = [row_ref[0, 0, i + stride * k] for k in range(LN)]
        new = [total[pl.ds(at[k], 1), :] + rows[pl.ds(i + stride * k, 1), :] for k in range(LN)]
        for k in range(LN):
            total[pl.ds(at[k], 1), :] = new[k]
        return 0
    lax.fori_loop(0, stride, add, 0, unroll=2)
    @pl.when(step == pl.num_programs(0) - 1)
    def _():
        whole = (vocab - (GROUPS - 1) * fold) // LANES
        def turn(b, _):
            tile = total[pl.ds(pl.multiple_of(b * LANES, LANES), LANES), :].T
            for j in range(GROUPS):
                out_ref[:, pl.ds(pl.multiple_of(j * fold + b * LANES, LANES), LANES)] = tile[j * SLOT:j * SLOT + feats]
            return 0
        lax.fori_loop(0, whole, turn, 0)
        for b in range(whole, fold // LANES):
            tile = total[pl.ds(b * LANES, LANES), :].T
            for j in range(GROUPS - 1):
                out_ref[:, pl.ds(j * fold + b * LANES, LANES)] = tile[j * SLOT:j * SLOT + feats]

def scatter(grads, rows_idx, groups_idx, vocab):
    n, tokens = rows_idx.shape[0], rows_idx.shape[2]
    feats = grads.shape[1] // 2
    fold = fold_rows(vocab)
    return pl.pallas_call(
        functools.partial(scatter_kernel, fold),
        grid=(n,),
        out_shape=jax.ShapeDtypeStruct((feats, vocab), jnp.float32),
        in_specs=[
            pl.BlockSpec((1, 1, tokens), lambda s: (s, 0, 0), memory_space=pltpu.SMEM),
            pl.BlockSpec((1, 1, tokens), lambda s: (s, 0, 0)),
            pl.BlockSpec((1, 2 * feats, tokens // 2), lambda s: (s, 0, 0)),
        ],
        out_specs=pl.BlockSpec((feats, vocab), lambda s: (0, 0)),
        scratch_shapes=[pltpu.VMEM((fold + 8, LANES), jnp.float32), pltpu.VMEM((tokens, LANES), jnp.float32)],
        compiler_params=pltpu.CompilerParams(vmem_limit_bytes=VMEM_CAP),
        name="scatter",
    )(rows_idx, groups_idx, grads)

def token_keys(tokens, fold):
    count = tokens.shape[0]
    key = (tokens % fold) * GROUPS + tokens // fold
    places = jnp.arange(count, dtype=jnp.int32)
    same_before = (key[:, None] == key[None, :]) & (places[:, None] < places[None, :])
    first = ~jnp.any(same_before, axis=0)
    rank = jnp.sum(((key[None, :] < key[:, None]) & first[None, :]).astype(jnp.int32), axis=1)
    hit = (rank[:, None] == places[None, :]) & first[:, None]
    packed = GROUPS * fold + jnp.sum(jnp.where(hit, key[:, None] - GROUPS * fold, 0), axis=0)
    return packed, rank


MESH = pl.DeviceIdType.MESH


def greet_all(count, cols, me):
    barrier = pltpu.get_barrier_semaphore()

    def greet(k, carry):
        to = lax.rem(me + k, count)
        pl.semaphore_signal(barrier, inc=1, device_id=(to // cols, lax.rem(to, cols)), device_id_type=MESH)
        return carry

    lax.fori_loop(1, count, greet, 0)
    pl.semaphore_wait(barrier, count - 1)


def exchange_kernel(same, src, dst, send_sem, recv_sem, own_sem):
    rows, cols = lax.axis_size("dp"), lax.axis_size("fsdp")
    count = rows * cols
    me = lax.axis_index("dp") * cols + lax.axis_index("fsdp")
    barrier = pltpu.get_barrier_semaphore()

    def device(k):
        to = lax.rem(me + k, count)
        return (to // cols, lax.rem(to, cols))

    def greet(k, carry):
        pl.semaphore_signal(barrier, inc=1, device_id=device(k), device_id_type=MESH)
        return carry

    def copy(k):
        to = lax.rem(me + k, count)
        return pltpu.make_async_remote_copy(
            src_ref=src.at[0 if same else to],
            dst_ref=dst.at[me],
            send_sem=send_sem.at[k],
            recv_sem=recv_sem.at[k],
            device_id=device(k),
            device_id_type=MESH,
        )

    def start(k, carry):
        copy(k).start()
        return carry

    def end(k, carry):
        copy(k).wait()
        return carry

    lax.fori_loop(1, count, greet, 0)
    own = pltpu.make_async_copy(src.at[0 if same else me], dst.at[me], own_sem)
    own.start()
    pl.semaphore_wait(barrier, count - 1)
    lax.fori_loop(1, count, start, 0)
    own.wait()
    lax.fori_loop(1, count, end, 0)


def exchange(blocks, same, call_id, name):
    count = lax.axis_size("dp") * lax.axis_size("fsdp")
    return pl.pallas_call(
        functools.partial(exchange_kernel, same),
        out_shape=jax.ShapeDtypeStruct((count,) + blocks.shape[1:], blocks.dtype),
        in_specs=[pl.BlockSpec(memory_space=pl.ANY)],
        out_specs=pl.BlockSpec(memory_space=pl.ANY),
        scratch_shapes=[
            pltpu.SemaphoreType.DMA((count,)),
            pltpu.SemaphoreType.DMA((count,)),
            pltpu.SemaphoreType.DMA,
        ],
        compiler_params=pltpu.CompilerParams(collective_id=call_id, has_side_effects=True),
        name=name,
    )(blocks)


SQUARE, EXPAND, REDUCE = range(3)
KINDS = 3
STEPS = (5, 6, 4)
FIRST = (3, 3, 2)


def spot(refs, kind, z, x, y, core):
    dp = z * 2 + x
    column = y * 2 + core
    if kind == SQUARE:
        return refs[kind].at[
            :,
            pl.ds(pl.multiple_of(dp * 96 + core * 48, 16), 48),
            pl.ds(pl.multiple_of(y * 384, 128), 384),
        ]
    if kind == EXPAND:
        return refs[kind].at[
            pl.ds(pl.multiple_of(dp * 96, 16), 96), pl.ds(pl.multiple_of(column * 768, 128), 768)
        ]
    return refs[kind].at[
        pl.ds(pl.multiple_of(column * 192, 16), 192), pl.ds(pl.multiple_of(dp * 384, 128), 384)
    ]


def spot_part(refs, kind, z, x, y, core, part):
    dp = z * 2 + x
    column = y * 2 + core
    if kind == SQUARE:
        return refs[kind].at[
            pl.ds(0, 3) if part == 0 else pl.ds(3, 2),
            pl.ds(pl.multiple_of(dp * 96 + core * 48, 16), 48),
            pl.ds(pl.multiple_of(y * 384, 128), 384),
        ]
    if kind == EXPAND:
        return refs[kind].at[
            pl.ds(pl.multiple_of(dp * 96 + part * 48, 16), 48),
            pl.ds(pl.multiple_of(column * 768, 128), 768),
        ]
    return refs[kind].at[
        pl.ds(pl.multiple_of(column * 192 + part * 96, 16), 96),
        pl.ds(pl.multiple_of(dp * 384, 128), 384),
    ]


def block_part(ref, kind, part):
    if kind == SQUARE:
        return ref.at[pl.ds(0, 3) if part == 0 else pl.ds(3, 2)]
    half = 48 if kind == EXPAND else 96
    return ref.at[pl.ds(part * half, half)]


def block_step(ref, kind, k):
    if kind == SQUARE:
        return ref.at[k]
    rows = 16 if kind == EXPAND else 48
    return ref.at[pl.ds(pl.multiple_of(k * rows, 16), rows)]


BLOCKS = ((5, 48, 384), (96, 768), (192, 384))


def place():
    dp, fsdp = lax.axis_index("dp"), lax.axis_index("fsdp")
    return dp // 2, lax.rem(dp, 2), fsdp // 2, lax.rem(fsdp, 2)


def device_at(z, x, y, core):
    return (z * 2 + x, y * 2 + core)


def greet_neighbours(depth):
    z, x, y, core = place()
    barrier = pltpu.get_barrier_semaphore()

    def hello(target):
        pl.semaphore_signal(barrier, inc=1, device_id=target, device_id_type=MESH)

    hello(device_at(z, x, y, 1 - core))
    hello(device_at(z, 1 - x, y, core))
    hello(device_at(z, x, 1 - y, core))

    @pl.when(z > 0)
    def _():
        hello(device_at(z - 1, x, y, core))

    @pl.when(z < depth - 1)
    def _():
        hello(device_at(z + 1, x, y, core))

    above = jnp.where(z < depth - 1, 1, 0)
    below = jnp.where(z > 0, 1, 0)
    pl.semaphore_wait(barrier, 3 + above + below)


def remote(src, dst, send_sem, recv_sem, target):
    return pltpu.make_async_remote_copy(
        src_ref=src, dst_ref=dst, send_sem=send_sem, recv_sem=recv_sem,
        device_id=target, device_id_type=MESH)


def front_kernel(fold, depth, row_ref, group_ref, table_ref, square_in, expand_in, reduce_in, *refs):
    mine = (square_in, expand_in, reduce_in)
    found, outs = refs[0], refs[1 : 1 + KINDS]
    theirs, own, turned, rows, blocks = refs[1 + KINDS : 6 + KINDS]
    (
        pair_send, pair_recv, own_sem, send, got, sib_send, sib_got, diag_got, part_send, part_got, part_own
    ) = refs[6 + KINDS :]
    dp_size, fsdp_size = lax.axis_size("dp"), lax.axis_size("fsdp")
    count = dp_size * fsdp_size
    me = lax.axis_index("dp") * fsdp_size + lax.axis_index("fsdp")
    z, x, y, core = place()
    sibling = device_at(z, x, y, 1 - core)
    x_next, y_next = device_at(z, 1 - x, y, core), device_at(z, x, 1 - y, core)
    greet_all(count, fsdp_size, me)
    pair = remote(mine[SQUARE].at[1 - core], theirs, pair_send, pair_recv, sibling)
    pair.start()

    def number(z_at, x_at, y_at):
        return (z_at * 2 + x_at) * 2 + y_at

    def to(way, a, z_at, x_at, y_at, target, part=None, src=None):
        k = number(z_at, x_at, y_at)
        if part is None:
            spot_at, recv = spot(outs, a, z_at, x_at, y_at, core), got.at[a, k]
        else:
            spot_at = spot_part(outs, a, z_at, x_at, y_at, core, part)
            recv = diag_got.at[a, z_at, part]
        return remote(spot_at if src is None else src, spot_at, send.at[way, a, k], recv, target)

    def to_sibling(a, z_at, x_at, y_at, src=None):
        spot_at = spot(outs, a, z_at, x_at, y_at, core)
        k = number(z_at, x_at, y_at)
        return remote(spot_at if src is None else src, spot_at, sib_send.at[a, k], sib_got.at[a, k], sibling)

    def from_sibling(a, z_at, x_at, y_at):
        spot_at = spot(outs, a, z_at, x_at, y_at, 1 - core)
        k = number(z_at, x_at, y_at)
        return remote(spot_at, spot_at, sib_send.at[a, k], sib_got.at[a, k], sibling)

    UP, DOWN, ACROSS_X, ACROSS_Y = range(4)
    sources = [own, mine[EXPAND], mine[REDUCE]]
    for a in (EXPAND, REDUCE, SQUARE):
        if a == SQUARE:
            row = lax.broadcasted_iota(jnp.int32, (192, 384), 0)
            col = lax.broadcasted_iota(jnp.int32, (192, 384), 1)
            here = (row + core * 192 == col).astype(jnp.float32).astype(jnp.bfloat16)
            there = (row + (1 - core) * 192 == col).astype(jnp.float32).astype(jnp.bfloat16)
            pair.wait_recv()
            for k in range(5):
                block = jnp.dot(mine[a][core, k], here, preferred_element_type=jnp.float32) + jnp.dot(
                    theirs[k], there, preferred_element_type=jnp.float32
                )
                own[k] = block.astype(jnp.bfloat16)
        pltpu.make_async_copy(sources[a], spot(outs, a, z, x, y, core), own_sem.at[a]).start()

        @pl.when(z < depth - 1)
        def _():
            to(UP, a, z, x, y, device_at(z + 1, x, y, core), src=sources[a]).start()

        @pl.when(z > 0)
        def _():
            to(DOWN, a, z, x, y, device_at(z - 1, x, y, core), src=sources[a]).start()

        to(ACROSS_X, a, z, x, y, x_next, src=sources[a]).start()
        to(ACROSS_Y, a, z, x, y, y_next, src=sources[a]).start()
        to_sibling(a, z, x, y, src=sources[a]).start()

    def sides(step, act):
        if step == 0:
            act(z)
            return
        for sign in (1, -1):
            z_at = z + sign * step

            @pl.when((z_at >= 0) & (z_at < depth))
            def _():
                act(z_at)

    def first(step):
        def act(z_at):
            for a in range(KINDS):
                to(UP, a, z_at, x, y, sibling).wait_recv()

                @pl.when((z_at < z) & (z < depth - 1))
                def _():
                    to(UP, a, z_at, x, y, device_at(z + 1, x, y, core)).start()

                @pl.when((z_at > z) & (z > 0))
                def _():
                    to(DOWN, a, z_at, x, y, device_at(z - 1, x, y, core)).start()

                to(ACROSS_X, a, z_at, x, y, x_next).start()
                to(ACROSS_Y, a, z_at, x, y, y_next).start()
                to_sibling(a, z_at, x, y).start()

        sides(step, act)

    def second(step):
        def act(z_at):
            for a in range(KINDS):
                to(UP, a, z_at, 1 - x, y, sibling).wait_recv()
                to(ACROSS_Y, a, z_at, 1 - x, y, y_next, 0).start()
                to_sibling(a, z_at, 1 - x, y).start()
                to(UP, a, z_at, x, 1 - y, sibling).wait_recv()
                to(ACROSS_X, a, z_at, x, 1 - y, x_next, 1).start()
                to_sibling(a, z_at, x, 1 - y).start()

        sides(step, act)

    def third(step):
        def act(z_at):
            for a in range(KINDS):
                for part in range(2):
                    to(UP, a, z_at, 1 - x, 1 - y, sibling, part).wait_recv()
                to_sibling(a, z_at, 1 - x, 1 - y).start()

        sides(step, act)

    turn_table(fold, table_ref, turned)

    def part_copy(k):
        target = lax.rem(me + k, count)
        return pltpu.make_async_remote_copy(
            src_ref=blocks.at[target],
            dst_ref=found.at[me],
            send_sem=part_send.at[k],
            recv_sem=part_got.at[k],
            device_id=(target // fsdp_size, lax.rem(target, fsdp_size)),
            device_id_type=MESH,
        )

    def serve(k, carry):
        target = lax.rem(me + k, count)
        blocks[target] = look_up(row_ref, group_ref, target, turned, rows, table_ref.shape[0])
        part_copy(k).start()
        return carry

    relays = []
    for step in range(1, depth + 2):
        if step < depth:
            relays.append((first, step))
        if 0 <= step - 1 < depth:
            relays.append((second, step - 1))
        if 0 <= step - 2 < depth:
            relays.append((third, step - 2))
    done = 1
    for n, (relay, step) in enumerate(relays):
        until = min(count, 1 + ((n + 1) * count) // len(relays)) if n < len(relays) - 1 else count
        lax.fori_loop(done, until, serve, 0)
        done = until
        relay(step)
    blocks[me] = look_up(row_ref, group_ref, me, turned, rows, table_ref.shape[0])
    own_part = pltpu.make_async_copy(blocks.at[me], found.at[me], part_own)
    own_part.start()

    pair.wait_send()
    for a in range(KINDS):
        pltpu.make_async_copy(sources[a], spot(outs, a, z, x, y, core), own_sem.at[a]).wait()

    def finish(z_at, carry):
        for a in range(KINDS):

            @pl.when((z_at <= z) & (z < depth - 1))
            def _():
                to(UP, a, z_at, x, y, x_next).wait_send()

            @pl.when((z_at >= z) & (z > 0))
            def _():
                to(DOWN, a, z_at, x, y, x_next).wait_send()

            to(ACROSS_X, a, z_at, x, y, x_next).wait_send()
            to(ACROSS_Y, a, z_at, x, y, y_next).wait_send()
            to(ACROSS_Y, a, z_at, 1 - x, y, y_next, 0).wait_send()
            to(ACROSS_X, a, z_at, x, 1 - y, x_next, 1).wait_send()
            for x_at in range(2):
                for y_at in range(2):
                    to_sibling(a, z_at, x_at, y_at).wait_send()
                    from_sibling(a, z_at, x_at, y_at).wait_recv()
        return carry

    lax.fori_loop(0, depth, finish, 0)
    own_part.wait()

    def end_part(k, carry):
        part_copy(k).wait()
        return carry

    lax.fori_loop(1, count, end_part, 0)


def run_front(row_all, group_all, table, square, expand, reduce_turned, call_id):
    depth = lax.axis_size("dp") // 2
    spots = 4 * depth
    count, tokens = row_all.shape
    feats, vocab = table.shape
    fold = fold_rows(vocab)
    blocks = (count, 2 * feats, tokens // 2)
    whole = pl.BlockSpec(memory_space=pltpu.VMEM)
    anywhere = pl.BlockSpec(memory_space=pl.ANY)
    return pl.pallas_call(
        functools.partial(front_kernel, fold, depth),
        out_shape=[
            jax.ShapeDtypeStruct(blocks, jnp.bfloat16),
            jax.ShapeDtypeStruct((5, 768, 768), jnp.bfloat16),
            jax.ShapeDtypeStruct((768, 3072), jnp.bfloat16),
            jax.ShapeDtypeStruct((768, 3072), jnp.bfloat16),
        ],
        in_specs=[pl.BlockSpec(memory_space=pltpu.SMEM)] + [whole] * 5,
        out_specs=[anywhere] * 4,
        scratch_shapes=[
            pltpu.VMEM((5, 48, 192), jnp.bfloat16),
            pltpu.VMEM((5, 48, 384), jnp.bfloat16),
            pltpu.VMEM((fold + 8, LANES), jnp.float32),
            pltpu.VMEM((tokens, LANES), jnp.float32),
            pltpu.VMEM(blocks, jnp.bfloat16),
            pltpu.SemaphoreType.DMA,
            pltpu.SemaphoreType.DMA,
            pltpu.SemaphoreType.DMA((KINDS,)),
            pltpu.SemaphoreType.DMA((4, KINDS, spots)),
            pltpu.SemaphoreType.DMA((KINDS, spots)),
            pltpu.SemaphoreType.DMA((KINDS, spots)),
            pltpu.SemaphoreType.DMA((KINDS, spots)),
            pltpu.SemaphoreType.DMA((KINDS, depth, 2)),
            pltpu.SemaphoreType.DMA((count,)),
            pltpu.SemaphoreType.DMA((count,)),
            pltpu.SemaphoreType.DMA,
        ],
        compiler_params=pltpu.CompilerParams(
            collective_id=call_id, has_side_effects=True, vmem_limit_bytes=VMEM_CAP
        ),
        name="front",
    )(row_all, group_all.reshape(count, 1, tokens), table, square, expand, reduce_turned)


class Reduction:
    def __init__(self, kinds, depth, grads, outs, work, buffers, sems):
        self.kinds, self.depth, self.grads, self.outs, self.own_work = kinds, depth, grads, outs, work
        count = len(kinds)
        self.paired, self.step_one, self.from_x, self.from_y, self.from_z = [
            dict(zip(kinds, buffers[k * count : (k + 1) * count])) for k in range(5)
        ]
        self.load_sem, self.pair_send, self.pair_got, self.send, self.one_got = sems[:5]
        self.x_got, self.y_got, self.z_got = sems[5:8]
        self.number = {a: n for n, a in enumerate(kinds)}
        z, x, y, core = place()
        self.z, self.x, self.y, self.core = z, x, y, core
        self.sibling = device_at(z, x, y, 1 - core)
        self.x_next, self.y_next = device_at(z, 1 - x, y, core), device_at(z, x, 1 - y, core)

    def work(self, a, z_at, x_at, y_at):
        if self.own_work is None:
            return spot(self.grads, a, z_at, x_at, y_at, self.core)
        return self.own_work[a].at[z_at * 2 + x_at, y_at]

    def load(self, a, z_at, x_at, y_at):
        return pltpu.make_async_copy(
            spot(self.grads, a, z_at, x_at, y_at, self.core),
            self.work(a, z_at, x_at, y_at),
            self.load_sem.at[self.number[a], z_at * 2 + x_at, y_at],
        )

    def pair(self, a, z_at, x_at, y_at):
        n, i = self.number[a], z_at * 2 + x_at
        return remote(
            spot(self.grads, a, z_at, x_at, y_at, 1 - self.core),
            self.paired[a].at[i, y_at],
            self.pair_send.at[n, i, y_at],
            self.pair_got.at[n, i, y_at],
            self.sibling,
        )

    def sides(self, step, act):
        if step == 0:
            act(self.z)
            return
        for sign in (1, -1):
            z_at = self.z + sign * step

            @pl.when((z_at >= 0) & (z_at < self.depth))
            def _():
                act(z_at)

    def begin(self):
        x, y = self.x, self.y
        for x_at, y_at in ((1 - x, 1 - y), (1 - x, y), (x, 1 - y), (x, y)):
            for step in range(self.depth - 1, -1, -1):

                def start(z_at):
                    for a in self.kinds:
                        if self.own_work is not None:
                            self.load(a, z_at, x_at, y_at).start()
                        self.pair(a, z_at, x_at, y_at).start()

                self.sides(step, start)

    def ready(self, a, z_at, x_at, y_at):
        if self.own_work is not None:
            self.load(a, z_at, x_at, y_at).wait()
        self.pair(a, z_at, x_at, y_at).wait_recv()

    def total(self, a, z_at, x_at, y_at, first, last, extra=()):
        here = self.work(a, z_at, x_at, y_at)
        paired = self.paired[a].at[z_at * 2 + x_at, y_at]

        def add(k, carry):
            step = block_step(here, a, k)
            value = step[...].astype(jnp.float32) + block_step(paired, a, k)[...].astype(jnp.float32)
            for buffer in extra:
                value = value + block_step(buffer, a, k)[...].astype(jnp.float32)
            step[...] = value.astype(jnp.bfloat16)
            return carry

        lax.fori_loop(first, last, add, 0)

    def diag_copy(self, a, z_at, part):
        n = self.number[a]
        return remote(
            block_part(self.work(a, z_at, 1 - self.x, 1 - self.y), a, part),
            block_part(self.step_one[a].at[z_at], a, part),
            self.send.at[part, n, z_at],
            self.one_got.at[n, part, z_at],
            self.y_next if part == 0 else self.x_next,
        )

    def diag(self, step):
        def act(z_at):
            for a in self.kinds:
                self.ready(a, z_at, 1 - self.x, 1 - self.y)
                self.total(a, z_at, 1 - self.x, 1 - self.y, 0, STEPS[a])
                for part in range(2):
                    self.diag_copy(a, z_at, part).start()

        self.sides(step, act)

    def x_copy(self, a, z_at):
        n = self.number[a]
        return remote(
            self.work(a, z_at, 1 - self.x, self.y),
            self.from_x[a].at[z_at],
            self.send.at[2, n, z_at],
            self.x_got.at[n, z_at],
            self.x_next,
        )

    def y_copy(self, a, z_at):
        n = self.number[a]
        return remote(
            self.work(a, z_at, self.x, 1 - self.y),
            self.from_y[a].at[z_at],
            self.send.at[3, n, z_at],
            self.y_got.at[n, z_at],
            self.y_next,
        )

    def columns(self, step):
        x, y = self.x, self.y

        def act(z_at):
            for a in self.kinds:
                middle, last = FIRST[a], STEPS[a]
                self.ready(a, z_at, 1 - x, y)
                self.diag_copy(a, z_at, 0).wait_recv()
                self.total(a, z_at, 1 - x, y, 0, middle, [self.step_one[a].at[z_at]])
                self.total(a, z_at, 1 - x, y, middle, last)
                self.x_copy(a, z_at).start()
                self.ready(a, z_at, x, 1 - y)
                self.diag_copy(a, z_at, 1).wait_recv()
                self.total(a, z_at, x, 1 - y, 0, middle)
                self.total(a, z_at, x, 1 - y, middle, last, [self.step_one[a].at[z_at]])
                self.y_copy(a, z_at).start()

        self.sides(step, act)

    def z_copy(self, a, z_at, side, target):
        n = self.number[a]
        return remote(
            self.work(a, z_at, self.x, self.y),
            self.from_z[a].at[side, z_at],
            self.send.at[4, n, z_at],
            self.z_got.at[n, side, z_at],
            target,
        )

    def line(self, step, keep=None):
        z, x, y, core, depth = self.z, self.x, self.y, self.core, self.depth

        def act(z_at):
            for a in self.kinds:
                self.ready(a, z_at, x, y)
                self.x_copy(a, z_at).wait_recv()
                self.y_copy(a, z_at).wait_recv()
                across = [self.from_x[a].at[z_at], self.from_y[a].at[z_at]]
                if step > 0:
                    upward = z_at > z
                    before = (upward & (z > 0)) | (jnp.logical_not(upward) & (z < depth - 1))
                    side = jnp.where(upward, 0, 1)

                    @pl.when(before)
                    def _():
                        self.z_copy(a, z_at, side, self.sibling).wait_recv()
                        self.total(a, z_at, x, y, 0, STEPS[a], across + [self.from_z[a].at[side, z_at]])

                    @pl.when(jnp.logical_not(before))
                    def _():
                        self.total(a, z_at, x, y, 0, STEPS[a], across)

                    @pl.when(upward)
                    def _():
                        self.z_copy(a, z_at, 0, device_at(z + 1, x, y, core)).start()

                    @pl.when(jnp.logical_not(upward))
                    def _():
                        self.z_copy(a, z_at, 1, device_at(z - 1, x, y, core)).start()
                else:
                    for side in range(2):
                        present = (z > 0) if side == 0 else (z < depth - 1)

                        @pl.when(present)
                        def _():
                            self.z_copy(a, z, side, self.sibling).wait_recv()

                        @pl.when(jnp.logical_not(present))
                        def _():
                            self.from_z[a][side, z] = jnp.zeros(BLOCKS[a], jnp.bfloat16)

                    here, paired = self.work(a, z, x, y), self.paired[a].at[z * 2 + x, y]

                    def finish(k, carry):
                        value = block_step(here, a, k)[...].astype(jnp.float32)
                        for buffer in [paired] + across + [self.from_z[a].at[0, z], self.from_z[a].at[1, z]]:
                            value = value + block_step(buffer, a, k)[...].astype(jnp.float32)
                        if a == SQUARE:
                            spare = self.outs[3]
                            low, high = value[:, :192], pltpu.roll(value, 192, 1)[:, :192]
                            self.outs[SQUARE][core, k] = jnp.where(core == 0, low, high)
                            spare[k] = jnp.where(core == 0, high, low)
                        else:
                            block_step(self.outs[a], a, k)[...] = value
                        return carry

                    lax.fori_loop(0, STEPS[a], finish, 0)

        self.sides(step, act)

    def groups(self):
        rounds = list(range(self.depth - 1, -1, -1))
        for k in range(self.depth + 2):
            group = []
            if k < self.depth:
                group.append((self.diag, rounds[k]))
            if 0 <= k - 1 < self.depth:
                group.append((self.columns, rounds[k - 1]))
            if 0 <= k - 2 < self.depth:
                group.append((self.line, rounds[k - 2]))
            yield group

    def finish(self):
        def wait(z_at, carry):
            for a in self.kinds:
                for x_at in range(2):
                    for y_at in range(2):
                        self.pair(a, z_at, x_at, y_at).wait_send()
                for part in range(2):
                    self.diag_copy(a, z_at, part).wait_send()
                self.x_copy(a, z_at).wait_send()
                self.y_copy(a, z_at).wait_send()

                @pl.when(z_at != self.z)
                def _():
                    self.z_copy(a, z_at, 0, self.sibling).wait_send()
            return carry

        lax.fori_loop(0, self.depth, wait, 0)


def reduction_scratch(kinds, depth):
    def buffers(*lead):
        return [pltpu.VMEM(lead + BLOCKS[a], jnp.bfloat16) for a in kinds]

    count = len(kinds)
    spots = pltpu.SemaphoreType.DMA((count, 2 * depth, 2))
    return (
        buffers(2 * depth, 2) + buffers(depth) + buffers(depth) + buffers(depth) + buffers(2, depth),
        [
            spots,
            spots,
            spots,
            pltpu.SemaphoreType.DMA((5, count, depth)),
            pltpu.SemaphoreType.DMA((count, 2, depth)),
            pltpu.SemaphoreType.DMA((count, depth)),
            pltpu.SemaphoreType.DMA((count, depth)),
            pltpu.SemaphoreType.DMA((count, 2, depth)),
        ],
    )


TILE = 128
PAIRS = HEADS // 2
GELU_IN = (2.0 / np.pi) ** 0.5


def dot_nn(left, right):
    return jnp.dot(left, right, preferred_element_type=jnp.float32)


def dot_nt(left, right):
    return lax.dot_general(left, right, (((1,), (1,)), ((), ())), preferred_element_type=jnp.float32)


def dot_tn(left, right):
    return lax.dot_general(left, right, (((0,), (0,)), ((), ())), preferred_element_type=jnp.float32)


def rows_at(index, size):
    return pl.ds(pl.multiple_of(index * size, size), size)


def split_heads(block):
    low = lax.broadcasted_iota(jnp.int32, block.shape, 1) < HEAD
    wide = block.astype(jnp.float32)
    first = jnp.where(low, wide, 0.0).astype(jnp.bfloat16)
    second = jnp.where(low, 0.0, wide).astype(jnp.bfloat16)
    return jnp.concatenate([first, second], axis=0)


def join_heads(stacked):
    return jnp.concatenate([stacked[:TILE], stacked[TILE:]], axis=1)


def pair_probs(query, keys_here, bias, mask):
    scores = dot_nt(split_heads(query), keys_here) * HEAD ** (-0.5) + bias
    scores = scores + mask
    raised = jnp.exp(scores - jnp.max(scores, axis=1, keepdims=True))
    return raised / jnp.sum(raised, axis=1, keepdims=True)


def pair_bias(bias_ref, pair):
    return jnp.concatenate([bias_ref[2 * pair], bias_ref[2 * pair + 1]], axis=0)


def tile_mask(mask_ref, tile):
    mask = mask_ref[tile]
    return jnp.concatenate([mask, mask], axis=0)


def hot_rows(rank_ref, rows, tokens):
    place = lax.broadcasted_iota(jnp.int32, (rows.size, tokens), 1)
    return (rank_ref[rows, :1] == place).astype(jnp.float32).astype(jnp.bfloat16)


def norm_rows(values, gain):
    scale = lax.rsqrt(jnp.mean(values * values, axis=1, keepdims=True) + NORM_EPS)
    return values * scale * gain


def gelu_parts(pre):
    inner = GELU_IN * (pre + 0.044715 * pre * pre * pre)
    return jnp.tanh(inner)


def forward_kernel(
    found_ref, rank_ref, square_ref, expand_ref, reduce_ref, gains_ref, bias_ref, mask_ref, pool_ref, length_ref,
    start_ref, query_ref, key_ref, value_ref, mixed_ref, middle_ref, ending_ref, low_ref, pooled_ref, embed_ref,
    inverse_ref, normed, pooled_sum,
):
    tokens = start_ref.shape[0]
    big = 512

    def begin(r, carry):
        rows = rows_at(r, 256)
        start = dot_nt(hot_rows(rank_ref, rows, tokens), found_ref[...])
        start_ref[rows, :] = start.astype(jnp.bfloat16)
        normed[rows, :] = norm_rows(start, gains_ref[0:1]).astype(jnp.bfloat16)
        return carry

    lax.fori_loop(0, tokens // 256, begin, 0)
    for k, target in enumerate((query_ref, key_ref, value_ref)):

        def project(r, carry):
            rows = rows_at(r, big)
            target[rows, :] = dot_nn(normed[rows, :], square_ref[k]).astype(jnp.bfloat16)
            return carry

        lax.fori_loop(0, tokens // big, project, 0)

    def attend(t, carry):
        rows = rows_at(t, TILE)
        mask = tile_mask(mask_ref, t)
        for pair in range(PAIRS):
            lanes = pl.ds(pair * TILE, TILE)
            probs = pair_probs(query_ref[rows, lanes], key_ref[rows, lanes], pair_bias(bias_ref, pair), mask)
            mixed = dot_nn(join_heads(probs).astype(jnp.bfloat16), split_heads(value_ref[rows, lanes]))
            mixed_ref[rows, lanes] = mixed.astype(jnp.bfloat16)
        return carry

    lax.fori_loop(0, tokens // TILE, attend, 0)

    def merge(r, carry):
        rows = rows_at(r, big)
        middle = start_ref[rows, :].astype(jnp.float32) + dot_nn(mixed_ref[rows, :], square_ref[3])
        middle_ref[rows, :] = middle
        ending_ref[rows, :] = middle
        normed[rows, :] = norm_rows(middle, gains_ref[1:2]).astype(jnp.bfloat16)
        return carry

    lax.fori_loop(0, tokens // big, merge, 0)
    wide = expand_ref.shape[1]

    def feed(c, carry):
        lanes = rows_at(c, D)

        def rows_of(r, inner):
            rows = rows_at(r, big)
            pre = dot_nn(normed[rows, :], expand_ref[:, lanes])
            act = (0.5 * pre * (1.0 + gelu_parts(pre))).astype(jnp.bfloat16)
            ending_ref[rows, :] += dot_nt(act, reduce_ref[:, lanes])
            return inner

        return lax.fori_loop(0, tokens // big, rows_of, carry)

    lax.fori_loop(0, wide // D, feed, 0)
    pooled_sum[...] = jnp.zeros_like(pooled_sum)

    def pool(r, carry):
        rows = rows_at(r, 256)
        output = norm_rows(ending_ref[rows, :], gains_ref[2:3])
        pooled_sum[...] += jnp.dot(
            pool_ref[:, rows], output, precision=HIGHEST, preferred_element_type=jnp.float32
        )
        return carry

    lax.fori_loop(0, tokens // 256, pool, 0)
    pooled = (pooled_sum[...] / length_ref[:, :1]).astype(jnp.bfloat16)
    pooled_ref[...] = pooled
    projected = dot_nn(pooled, square_ref[4])
    inverse = lax.rsqrt(jnp.sum(projected * projected, axis=1, keepdims=True) + NORM_EPS)
    embeds = projected * inverse
    embed_ref[...] = embeds
    low_ref[...] = embeds.astype(jnp.bfloat16)
    inverse_ref[...] = jnp.broadcast_to(inverse, inverse_ref.shape)


def run_forward(found, rank, square, expand, reduce_turned, gains, bias, mask, pool, lengths):
    tokens = found.shape[1]
    seqs = pool.shape[0]
    low = jnp.bfloat16
    flat = jax.ShapeDtypeStruct((tokens, D), low)
    full = jax.ShapeDtypeStruct((tokens, D), jnp.float32)
    return pl.pallas_call(
        forward_kernel,
        out_shape=[
            flat, flat, flat, flat, flat, full, full,
            jax.ShapeDtypeStruct((seqs, D), low),
            jax.ShapeDtypeStruct((seqs, D), low),
            jax.ShapeDtypeStruct((seqs, D), jnp.float32),
            jax.ShapeDtypeStruct((seqs, LANES), jnp.float32),
        ],
        scratch_shapes=[pltpu.VMEM((tokens, D), low), pltpu.VMEM((seqs, D), jnp.float32)],
        compiler_params=pltpu.CompilerParams(vmem_limit_bytes=VMEM_CAP),
        name="layer_forward",
    )(found, rank, square, expand, reduce_turned, gains, bias, mask, pool, lengths)


def norm_back_rows(values, gain, grad):
    scale = lax.rsqrt(jnp.mean(values * values, axis=1, keepdims=True) + NORM_EPS)
    weighted = grad * gain
    inner = jnp.mean(weighted * values, axis=1, keepdims=True)
    through = scale * weighted - values * (scale * scale * scale * inner)
    return through, jnp.sum(grad * values * scale, axis=0, keepdims=True)


def feed_back_kernel(
    grad_embed_ref, embed_ref, inverse_ref, pool_ref, length_ref, last_ref, middle_ref, ending_ref, expand_ref,
    reduce_ref, gains_ref,
    grad_expand_ref, grad_reduce_ref, grad_middle_ref, grad_low_ref, grad_proj_ref, grad_gains_ref,
    normed, normed_turned, end_low, end_turned, back,
):
    tokens = middle_ref.shape[0]
    embeds, grads = embed_ref[...], grad_embed_ref[...]
    grad_proj = inverse_ref[:, :1] * (grads - embeds * jnp.sum(grads * embeds, axis=1, keepdims=True))
    grad_proj = grad_proj.astype(jnp.bfloat16)
    grad_proj_ref[...] = grad_proj
    grad_pooled = dot_nt(grad_proj, last_ref[0]) / length_ref[:, :1]
    grad_gains_ref[...] = jnp.zeros_like(grad_gains_ref)

    def begin(r, carry):
        rows = rows_at(r, 256)
        grad_out = lax.dot_general(
            pool_ref[:, rows], grad_pooled, (((0,), (0,)), ((), ())), precision=HIGHEST,
            preferred_element_type=jnp.float32,
        )
        through, gain = norm_back_rows(ending_ref[rows, :], gains_ref[2:3], grad_out)
        grad_gains_ref[2:3] += gain
        grad_middle_ref[rows, :] = through
        end_low[rows, :] = through.astype(jnp.bfloat16)
        end_turned[:, rows] = through.T.astype(jnp.bfloat16)
        middle_normed = norm_rows(middle_ref[rows, :], gains_ref[1:2])
        normed[rows, :] = middle_normed.astype(jnp.bfloat16)
        normed_turned[:, rows] = middle_normed.T.astype(jnp.bfloat16)
        return carry

    lax.fori_loop(0, tokens // 256, begin, 0)
    back[...] = jnp.zeros_like(back)
    wide = expand_ref.shape[1]
    step = 384

    def feed(c, carry):
        lanes = rows_at(c, step)
        pre = dot_nn(normed[...], expand_ref[:, lanes])
        grad_act = dot_nn(end_low[...], reduce_ref[:, lanes])
        turn = gelu_parts(pre)
        act = (0.5 * pre * (1.0 + turn)).astype(jnp.bfloat16)
        slope = 0.5 * (1.0 + turn) + 0.5 * pre * (1.0 - turn * turn) * GELU_IN * (1.0 + 3.0 * 0.044715 * pre * pre)
        grad_pre = (grad_act * slope).astype(jnp.bfloat16)
        grad_reduce_ref[:, lanes] = dot_nn(end_turned[...], act).astype(jnp.bfloat16)
        grad_expand_ref[:, lanes] = dot_nn(normed_turned[...], grad_pre).astype(jnp.bfloat16)
        back[...] += dot_nt(grad_pre, expand_ref[:, lanes])
        return carry

    lax.fori_loop(0, wide // step, feed, 0)

    def end(r, carry):
        rows = rows_at(r, 256)
        through, gain = norm_back_rows(middle_ref[rows, :], gains_ref[1:2], back[rows, :])
        grad_gains_ref[1:2] += gain
        grad_middle = grad_middle_ref[rows, :] + through
        grad_middle_ref[rows, :] = grad_middle
        grad_low_ref[rows, :] = grad_middle.astype(jnp.bfloat16)
        return carry

    lax.fori_loop(0, tokens // 256, end, 0)


def run_feed_back(grad_embed, embeds, inverse, pool, lengths, square, middle, ending, expand, reduce_turned, gains):
    tokens = middle.shape[0]
    seqs = pool.shape[0]
    low = jnp.bfloat16
    whole = pl.BlockSpec(memory_space=pltpu.VMEM)
    return pl.pallas_call(
        feed_back_kernel,
        grid=(1,),
        out_shape=[
            jax.ShapeDtypeStruct(expand.shape, low),
            jax.ShapeDtypeStruct(reduce_turned.shape, low),
            jax.ShapeDtypeStruct((tokens, D), jnp.float32),
            jax.ShapeDtypeStruct((tokens, D), low),
            jax.ShapeDtypeStruct((seqs, D), low),
            jax.ShapeDtypeStruct((8, D), jnp.float32),
        ],
        in_specs=[whole] * 5
        + [pl.BlockSpec((1, D, D), lambda i: (4, 0, 0))]
        + [whole] * 5,
        out_specs=[whole] * 6,
        scratch_shapes=[
            pltpu.VMEM((tokens, D), low),
            pltpu.VMEM((D, tokens), low),
            pltpu.VMEM((tokens, D), low),
            pltpu.VMEM((D, tokens), low),
            pltpu.VMEM((tokens, D), jnp.float32),
        ],
        compiler_params=pltpu.CompilerParams(vmem_limit_bytes=VMEM_CAP),
        name="feed_backward",
    )(grad_embed, embeds, inverse, pool, lengths, square, middle, ending, expand, reduce_turned, gains)


def attend_back_steps(
    grad_middle_ref, grad_low_ref, grad_proj_ref, pooled_ref, start_ref, query_ref, key_ref, value_ref, mixed_ref,
    square_ref, gains_ref, bias_ref, mask_ref, rank_ref,
    grad_square_ref, grad_score_ref, grad_gain_ref, grad_mixed, turned, grad_query, grad_key, grad_value,
    between, squares_done, put,
):
    tokens = start_ref.shape[0]
    big = 512
    grad_square_ref[4] = dot_tn(pooled_ref[...], grad_proj_ref[...]).astype(jnp.bfloat16)

    def begin(r, carry):
        rows = rows_at(r, big)
        grad_mixed[rows, :] = dot_nt(grad_low_ref[rows, :], square_ref[3]).astype(jnp.bfloat16)
        turned[:, rows] = mixed_ref[rows, :].astype(jnp.float32).T.astype(jnp.bfloat16)
        return carry

    lax.fori_loop(0, tokens // big, begin, 0)

    def outer(target, right_ref):
        def part(r, carry):
            rows = rows_at(r, 384)
            grad_square_ref[target, rows, :] = dot_nn(turned[rows, :], right_ref[...]).astype(jnp.bfloat16)
            return carry

        lax.fori_loop(0, D // 384, part, 0)

    outer(3, grad_low_ref)
    grad_score_ref[...] = jnp.zeros_like(grad_score_ref)

    def attend(t, carry):
        rows = rows_at(t, TILE)
        mask = tile_mask(mask_ref, t)
        for pair in range(PAIRS):
            lanes = pl.ds(pair * TILE, TILE)
            query, keys_here = query_ref[rows, lanes], key_ref[rows, lanes]
            probs = pair_probs(query, keys_here, pair_bias(bias_ref, pair), mask)
            grads = split_heads(grad_mixed[rows, lanes])
            grad_probs = dot_nt(grads, value_ref[rows, lanes])
            grad_value[rows, lanes] = dot_tn(probs.astype(jnp.bfloat16), grads).astype(jnp.bfloat16)
            inner = jnp.sum(grad_probs * probs, axis=1, keepdims=True)
            grad_scores = (probs * (grad_probs - inner)).astype(jnp.bfloat16)
            kept = grad_scores.astype(jnp.float32)
            grad_score_ref[2 * pair] += kept[:TILE]
            grad_score_ref[2 * pair + 1] += kept[TILE:]
            grad_query[rows, lanes] = (
                dot_nn(join_heads(grad_scores), split_heads(keys_here)) * HEAD ** (-0.5)
            ).astype(jnp.bfloat16)
            grad_key[rows, lanes] = (dot_tn(grad_scores, split_heads(query)) * HEAD ** (-0.5)).astype(jnp.bfloat16)
        return carry

    tiles = tokens // TILE
    done = 0
    for n, act in enumerate(between):
        until = ((n + 1) * tiles) // (len(between) + 1)
        if until > done:
            lax.fori_loop(done, until, attend, 0)
        done = until
        act()
    lax.fori_loop(done, tiles, attend, 0)

    def renorm(r, carry):
        rows = rows_at(r, 256)
        normed = norm_rows(start_ref[rows, :].astype(jnp.float32), gains_ref[0:1])
        turned[:, rows] = normed.T.astype(jnp.bfloat16)
        return carry

    lax.fori_loop(0, tokens // 256, renorm, 0)
    outer(0, grad_query)
    outer(1, grad_key)
    outer(2, grad_value)
    squares_done()
    grad_gain_ref[...] = jnp.zeros_like(grad_gain_ref)

    def end(r, carry):
        rows = rows_at(r, 256)
        grad_normed = (
            dot_nt(grad_query[rows, :], square_ref[0])
            + dot_nt(grad_key[rows, :], square_ref[1])
            + dot_nt(grad_value[rows, :], square_ref[2])
        )
        through, gain = norm_back_rows(start_ref[rows, :].astype(jnp.float32), gains_ref[0:1], grad_normed)
        grad_gain_ref[0:1] += gain
        turned[:, rows] = (grad_middle_ref[rows, :] + through).T.astype(jnp.bfloat16)
        return carry

    lax.fori_loop(0, tokens // 256, end, 0)

    def merge(r, carry):
        rows = rows_at(r, 384)
        total = jnp.zeros((384, tokens), jnp.float32)
        for c in range(tokens // 256):
            at = pl.ds(c * 256, 256)
            total = total + dot_nn(turned[rows, at], hot_rows(rank_ref, at, tokens))
        put(r, total)
        return carry

    lax.fori_loop(0, D // 384, merge, 0)


def attend_back_kernel(*refs):
    ins, rest = refs[:14], refs[14:]
    grad_square_ref, grad_score_ref, grad_gain_ref, send_ref = rest[:4]

    def put(r, total):
        send_ref[rows_at(r, 384), :] = total.astype(jnp.bfloat16)

    attend_back_steps(*ins, grad_square_ref, grad_score_ref, grad_gain_ref, *rest[4:], [], lambda: None, put)


def attend_scratch(tokens):
    low = jnp.bfloat16
    return [
        pltpu.VMEM((tokens, D), low),
        pltpu.VMEM((D, tokens), low),
        pltpu.VMEM((tokens, D), low),
        pltpu.VMEM((tokens, D), low),
        pltpu.VMEM((tokens, D), low),
    ]


def run_attend_back(*ins):
    tokens = ins[0].shape[0]
    low = jnp.bfloat16
    return pl.pallas_call(
        attend_back_kernel,
        out_shape=[
            jax.ShapeDtypeStruct((5, D, D), low),
            jax.ShapeDtypeStruct((HEADS, TILE, TILE), jnp.float32),
            jax.ShapeDtypeStruct((8, D), jnp.float32),
            jax.ShapeDtypeStruct((D, tokens), low),
        ],
        scratch_shapes=attend_scratch(tokens),
        compiler_params=pltpu.CompilerParams(vmem_limit_bytes=VMEM_CAP),
        name="attend_backward",
    )(*ins)


FEED_KINDS = (EXPAND, REDUCE)
SQUARE_KINDS = (SQUARE,)
BACK_CAP = 62 * 1024 * 1024


def back_kernel(depth, *refs):
    ins, refs = refs[:14], refs[14:]
    grad_expand, grad_reduce = refs[:2]
    square_sum, expand_sum, reduce_sum, grad_score_ref, grad_gain_ref, returned = refs[2:8]
    grad_square, *steps = refs[8:14]
    blocks, spare, work_expand, work_reduce = refs[14:18]
    refs = refs[18:]
    feed_buffers, refs = refs[:10], refs[10:]
    feed_sems, refs = refs[:8], refs[8:]
    square_buffers, refs = refs[:5], refs[5:]
    square_sems, refs = refs[:8], refs[8:]
    part_send, part_got, part_own, end_send, end_got = refs
    dp_size, fsdp_size = lax.axis_size("dp"), lax.axis_size("fsdp")
    count = dp_size * fsdp_size
    me = lax.axis_index("dp") * fsdp_size + lax.axis_index("fsdp")
    greet_all(count, fsdp_size, me)
    grads = (grad_square, grad_expand, grad_reduce)
    outs = (square_sum, expand_sum, reduce_sum, spare)
    feed = Reduction(
        FEED_KINDS, depth, grads, outs, {EXPAND: work_expand, REDUCE: work_reduce}, feed_buffers, feed_sems
    )
    square = Reduction(SQUARE_KINDS, depth, grads, outs, None, square_buffers, square_sems)
    feed.begin()

    def relay(group):
        def act():
            for move, step in group:
                move(step)

        return act

    feats, half = blocks.shape[1] // 2, blocks.shape[2]

    def put(r, total):
        each = 384 // feats
        for p in range(each):
            part = total[p * feats : (p + 1) * feats]
            blocks[r * each + p] = jnp.concatenate([part[:, :half], part[:, half:]], axis=0).astype(jnp.bfloat16)

    attend_back_steps(
        *ins, grad_square, grad_score_ref, grad_gain_ref, *steps,
        [relay(group) for group in feed.groups()], square.begin, put,
    )

    def part_copy(k):
        target = lax.rem(me + k, count)
        return pltpu.make_async_remote_copy(
            src_ref=blocks.at[target],
            dst_ref=returned.at[me],
            send_sem=part_send.at[k],
            recv_sem=part_got.at[k],
            device_id=(target // fsdp_size, lax.rem(target, fsdp_size)),
            device_id_type=MESH,
        )

    def start_part(k, carry):
        part_copy(k).start()
        return carry

    lax.fori_loop(1, count, start_part, 0)
    own_part = pltpu.make_async_copy(blocks.at[me], returned.at[me], part_own)
    own_part.start()
    for group in square.groups():
        relay(group)()
    end_copy = remote(spare, square_sum.at[square.core], end_send, end_got, square.sibling)
    end_copy.start()
    feed.finish()
    square.finish()
    end_copy.wait_send()
    remote(spare, square_sum.at[1 - square.core], end_send, end_got, square.sibling).wait_recv()
    own_part.wait()

    def end_part(k, carry):
        part_copy(k).wait()
        return carry

    lax.fori_loop(1, count, end_part, 0)


def run_back(ins, grad_expand, grad_reduce, count, feats, call_id):
    depth = lax.axis_size("dp") // 2
    tokens = ins[0].shape[0]
    low = jnp.bfloat16
    blocks = (count, 2 * feats, tokens // 2)
    whole = pl.BlockSpec(memory_space=pltpu.VMEM)
    anywhere = pl.BlockSpec(memory_space=pl.ANY)
    feed_buffers, feed_sems = reduction_scratch(FEED_KINDS, depth)
    square_buffers, square_sems = reduction_scratch(SQUARE_KINDS, depth)
    return pl.pallas_call(
        functools.partial(back_kernel, depth),
        out_shape=[
            jax.ShapeDtypeStruct((2, 5, 48, 192), jnp.float32),
            jax.ShapeDtypeStruct((96, 768), jnp.float32),
            jax.ShapeDtypeStruct((192, 384), jnp.float32),
            jax.ShapeDtypeStruct((HEADS, TILE, TILE), jnp.float32),
            jax.ShapeDtypeStruct((8, D), jnp.float32),
            jax.ShapeDtypeStruct(blocks, low),
        ],
        in_specs=[whole] * 14 + [anywhere] * 2,
        out_specs=[whole] * 5 + [anywhere],
        scratch_shapes=[pltpu.VMEM((5, D, D), low)]
        + attend_scratch(tokens)
        + [
            pltpu.VMEM(blocks, low),
            pltpu.VMEM((5, 48, 192), jnp.float32),
            pltpu.VMEM((2 * depth, 2) + BLOCKS[EXPAND], low),
            pltpu.VMEM((2 * depth, 2) + BLOCKS[REDUCE], low),
        ]
        + feed_buffers
        + feed_sems
        + square_buffers
        + square_sems
        + [
            pltpu.SemaphoreType.DMA((count,)),
            pltpu.SemaphoreType.DMA((count,)),
            pltpu.SemaphoreType.DMA,
            pltpu.SemaphoreType.DMA,
            pltpu.SemaphoreType.DMA,
        ],
        compiler_params=pltpu.CompilerParams(
            collective_id=call_id, has_side_effects=True, vmem_limit_bytes=BACK_CAP
        ),
        name="back",
    )(*ins, grad_expand, grad_reduce)


def shards(
    embed_table,
    square_weights,
    expand_weight,
    reduce_weight,
    norm_gains,
    position_bias,
    log_scale,
    table_moment,
    table_second,
    square_moment,
    square_second,
    expand_moment,
    expand_second,
    reduce_moment,
    reduce_second,
    gains_moment,
    gains_second,
    position_moment,
    position_second,
    scale_moment,
    scale_second,
    query_tokens,
    answer_tokens,
    query_length,
    answer_length,
    premise_tokens,
    hypothesis_tokens,
    hard_negative,
):
    both = ("dp", "fsdp")
    dp_size, fsdp_size = lax.axis_size("dp"), lax.axis_size("fsdp")
    count = dp_size * fsdp_size
    direct = dp_size == 8 and fsdp_size == 4
    position = lax.axis_index(both)
    feats, vocab_size = embed_table.shape
    feats_pad = up8(feats)
    fold = fold_rows(vocab_size)
    query_rows = query_tokens.shape[0]
    nli_rows = premise_tokens.shape[0]
    short_length = query_tokens.shape[1]
    long_length = answer_tokens.shape[1]
    short_tokens = jnp.concatenate([query_tokens, premise_tokens, hypothesis_tokens], axis=0)
    lengths = jnp.concatenate(
        [query_length, jnp.full((2 * nli_rows,), short_length, jnp.int32), answer_length]
    )
    all_tokens = jnp.concatenate([short_tokens.reshape(-1), answer_tokens.reshape(-1)])
    token_count = all_tokens.shape[0]
    hypo_start = query_rows + nli_rows
    answer_start = query_rows + 2 * nli_rows
    seq_count = answer_start + query_rows
    seq_pad = -(-seq_count // 16) * 16
    split_at = short_tokens.shape[0] * short_length

    packed, rank = token_keys(all_tokens, fold)
    start_info = jnp.concatenate(
        [
            packed.reshape(-1, LANES).astype(jnp.float32),
            jnp.pad(hard_negative, (0, LANES - nli_rows)).reshape(1, LANES).astype(jnp.float32),
            jnp.pad(norm_gains, ((0, 7 - 3), (0, LANES - feats))),
        ],
        axis=0,
    )
    key_rows = token_count // LANES
    info_all = exchange(start_info[None], True, 0, "share_start")
    packed_all = info_all[:, :key_rows].astype(jnp.int32).reshape(count, 1, token_count)
    negative_all = info_all[:, key_rows, :nli_rows].astype(jnp.int32).reshape(-1)
    gains = info_all[:, key_rows + 1 : key_rows + 4, :feats].transpose(1, 0, 2).reshape(3, D)
    gains = jnp.pad(gains.astype(jnp.bfloat16).astype(jnp.float32), ((0, 5), (0, 0)))
    row_all, group_all = packed_all >> 2, packed_all & 3

    square_low = square_weights.astype(jnp.bfloat16)
    expand_low = expand_weight.astype(jnp.bfloat16)
    reduce_low = reduce_weight.astype(jnp.bfloat16).T
    table_low = embed_table.astype(jnp.bfloat16).astype(jnp.float32)
    if direct:
        square_pieces = square_low.reshape(5, 2, 48, 192).transpose(1, 0, 2, 3)
        found, square_all, expand_all, reduce_all = run_front(
            row_all[:, 0], group_all[:, 0], table_low, square_pieces, expand_low, reduce_low, 1
        )
    else:

        def whole(piece, row_name, column_name):
            axis = piece.ndim - 2
            wide = lax.all_gather(piece, column_name, axis=axis + 1, tiled=True)
            return lax.all_gather(wide, row_name, axis=axis, tiled=True)

        square_all = whole(square_low, "dp", "fsdp")
        expand_all = whole(expand_low, "dp", "fsdp")
        reduce_all = whole(reduce_low, "fsdp", "dp")
        if feats_pad > feats:
            table_low = jnp.pad(table_low, ((0, feats_pad - feats), (0, 0)))
        found = exchange(lookup(table_low, row_all, group_all), False, 2, "send_features")
    half = token_count // 2
    found = found.reshape(count, 2, feats_pad, half)[:, :, :feats]
    found = found.transpose(0, 2, 1, 3).reshape(D, token_count)

    sequence = np.concatenate(
        [
            np.repeat(np.arange(answer_start), short_length),
            answer_start + np.repeat(np.arange(query_rows), long_length),
        ]
    )
    inside = np.concatenate(
        [
            np.tile(np.arange(short_length), answer_start),
            np.tile(np.arange(long_length), query_rows),
        ]
    )
    lengths_pad = jnp.pad(lengths, (0, seq_pad - seq_count), constant_values=1)
    pool = (sequence[None, :] == np.arange(seq_pad)[:, None]) & (inside[None, :] < lengths_pad[:, None])
    token_ok = jnp.any(pool, axis=0).reshape(-1, 1, TILE)
    sequence_tiles = sequence.reshape(-1, TILE)
    together = sequence_tiles[:, :, None] == sequence_tiles[:, None, :]
    mask = jnp.where(together & token_ok, 0.0, -1e30).astype(jnp.float32)
    pool = pool.astype(jnp.float32)
    length_rows = jnp.broadcast_to(lengths_pad.astype(jnp.float32)[:, None], (seq_pad, LANES))
    rank_rows = jnp.broadcast_to(rank[:, None], (token_count, LANES))
    bias, onehot = attention_bias(position_bias, TILE)

    (start, queries, keys_here, values_here, mixed, middle, ending, embeds_low, pooled, embeds, inverse) = run_forward(
        found, rank_rows, square_all, expand_all, reduce_all, gains, bias, mask, pool, length_rows
    )
    gathered = exchange(embeds_low[None], True, 3, "share_embeds")
    queries_all = gathered[:, :query_rows].reshape(-1, D)
    premises_all = gathered[:, query_rows:hypo_start].reshape(-1, D)
    hypotheses_all = gathered[:, hypo_start:answer_start].reshape(-1, D)
    answers_all = gathered[:, answer_start:seq_count].reshape(-1, D)
    scale = jnp.exp(log_scale[0])

    def contrast(left, right, extra, own):
        sims = product_right(left, right)
        logits = scale * sims
        row_top = jnp.max(logits, axis=1, keepdims=True)
        raised = (1.0 + extra) * jnp.exp(logits - row_top)
        row_total = jnp.sum(raised, axis=1, keepdims=True)
        spread = row_top[:, 0] + jnp.log(row_total[:, 0])
        target_hit = jnp.eye(left.shape[0], dtype=jnp.float32)
        loss_sum = jnp.sum(spread - jnp.sum(target_hit * logits, axis=1))
        grad_logits = raised / row_total - target_hit
        grad_scale = jnp.sum(grad_logits * sims)
        grad_sims = (scale * grad_logits).astype(jnp.bfloat16)
        mine_left = lax.dynamic_slice_in_dim(grad_sims, position * own, own, 0)
        mine_right = lax.dynamic_slice_in_dim(grad_sims, position * own, own, 1)
        return (loss_sum, grad_scale, product(mine_left, right), product_left(mine_right, left))

    first_loss, first_dscale, grad_queries, grad_answers = contrast(
        queries_all, answers_all, 0.0, query_rows
    )
    negatives = (jnp.arange(hypotheses_all.shape[0])[None, :] == negative_all[:, None]).astype(
        jnp.float32
    )
    second_loss, second_dscale, grad_premises, grad_hypotheses = contrast(
        premises_all, hypotheses_all, negatives, nli_rows
    )
    grad_embeds = jnp.concatenate(
        [
            grad_queries,
            grad_premises,
            grad_hypotheses,
            grad_answers,
            jnp.zeros((seq_pad - seq_count, D), jnp.float32),
        ],
        axis=0,
    )
    (grad_expand, grad_reduce, grad_middle, grad_middle_low, grad_proj, late_gains) = run_feed_back(
        grad_embeds, embeds, inverse, pool, length_rows, square_all, middle, ending, expand_all, reduce_all, gains
    )
    back_ins = (
        grad_middle, grad_middle_low, grad_proj, pooled, start, queries, keys_here, values_here, mixed, square_all,
        gains, bias, mask, rank_rows,
    )
    if direct:
        (square_sum, expand_sum, reduce_sum, grad_scores, first_gain, returned) = run_back(
            back_ins, grad_expand, grad_reduce, count, feats, 5
        )
        square_sum = square_sum.transpose(1, 0, 2, 3).reshape(5, 96, 192)
    else:

        def shard(gradient, row_name, column_name):
            axis = gradient.ndim - 2
            part = lax.psum_scatter(
                gradient.astype(jnp.float32), row_name, scatter_dimension=axis, tiled=True
            )
            return lax.psum_scatter(part, column_name, scatter_dimension=axis + 1, tiled=True)

        (grad_square, grad_scores, first_gain, merged) = run_attend_back(*back_ins)
        square_sum = shard(grad_square, "dp", "fsdp")
        expand_sum = shard(grad_expand, "dp", "fsdp")
        reduce_sum = shard(grad_reduce, "fsdp", "dp")
        merged = merged.reshape(count, feats, 2, half).transpose(0, 2, 1, 3)
        if feats_pad > feats:
            merged = jnp.pad(merged, ((0, 0), (0, 0), (0, feats_pad - feats), (0, 0)))
        returned = exchange(merged.reshape(count, 2 * feats_pad, half), False, 4, "send_gradients")
    grad_table = scatter(returned, row_all, group_all, vocab_size)[:feats]
    grad_gains = jnp.concatenate([first_gain[:1], late_gains[1:3]], axis=0)
    grad_position = lax.dot_general(
        onehot, grad_scores.reshape(HEADS, TILE * TILE), (((0,), (1,)), ((), ())), precision=HIGHEST
    )
    grad_scale = ((first_dscale + second_dscale) * scale).reshape(1)
    reduced = (square_sum, expand_sum, reduce_sum.T)
    local_square = (
        jnp.sum(reduced[0] * reduced[0])
        + jnp.sum(reduced[1] * reduced[1])
        + jnp.sum(reduce_sum * reduce_sum)
        + jnp.sum(grad_table * grad_table)
    )
    small = jnp.concatenate([grad_gains.reshape(-1), grad_position.reshape(-1), local_square.reshape(1)])
    small_rows = -(-small.shape[0] // (8 * LANES)) * 8
    small = jnp.pad(small, (0, small_rows * LANES - small.shape[0])).reshape(1, small_rows, LANES)
    summed = jnp.sum(exchange(small, True, 6, "share_small"), axis=0).reshape(-1)
    gains_total = summed[: 3 * D].reshape(3, D)
    position_total = summed[3 * D : 3 * D + BUCKETS * HEADS].reshape(BUCKETS, HEADS)
    square_total = summed[3 * D + BUCKETS * HEADS]
    scale_total = grad_scale
    losses = jnp.stack([first_loss, second_loss])
    grad_gain_shard = lax.dynamic_slice_in_dim(gains_total, position * feats, feats, 1)
    gradient_norm = jnp.sqrt(
        square_total
        + jnp.sum(gains_total * gains_total)
        + jnp.sum(position_total * position_total)
        + jnp.sum(scale_total * scale_total)
    )
    factor = jnp.minimum(1.0, CLIP_NORM / gradient_norm)
    table_out = adam_update(embed_table, table_moment, table_second, grad_table, factor, TABLE_RATE)
    square_out = adam_update(
        square_weights, square_moment, square_second, reduced[0], factor, LEARN_RATE
    )
    expand_out = adam_update(
        expand_weight, expand_moment, expand_second, reduced[1], factor, LEARN_RATE
    )
    reduce_out = adam_update(
        reduce_weight, reduce_moment, reduce_second, reduced[2], factor, LEARN_RATE
    )
    gains_out = adam_update(
        norm_gains, gains_moment, gains_second, grad_gain_shard, factor, SMALL_RATE
    )
    position_out = adam_update(
        position_bias, position_moment, position_second, position_total, factor, SMALL_RATE
    )
    scale_out = adam_update(log_scale, scale_moment, scale_second, scale_total, factor, SMALL_RATE)
    return (
        *table_out,
        *square_out,
        *expand_out,
        *reduce_out,
        *gains_out,
        *position_out,
        *scale_out,
        losses,
        gradient_norm,
    )


def solution(mesh):
    return jax.shard_map(
        shards,
        mesh=mesh,
        in_specs=(
            P(("dp", "fsdp"), None),
            P(None, "dp", "fsdp"),
            P("dp", "fsdp"),
            P("dp", "fsdp"),
            P(None, ("dp", "fsdp")),
            P(),
            P(),
            P(("dp", "fsdp"), None),
            P(("dp", "fsdp"), None),
            P(None, "dp", "fsdp"),
            P(None, "dp", "fsdp"),
            P("dp", "fsdp"),
            P("dp", "fsdp"),
            P("dp", "fsdp"),
            P("dp", "fsdp"),
            P(None, ("dp", "fsdp")),
            P(None, ("dp", "fsdp")),
            P(),
            P(),
            P(),
            P(),
            P(("dp", "fsdp"), None),
            P(("dp", "fsdp"), None),
            P(("dp", "fsdp")),
            P(("dp", "fsdp")),
            P(("dp", "fsdp"), None),
            P(("dp", "fsdp"), None),
            P(("dp", "fsdp")),
        ),
        out_specs=(
            P(("dp", "fsdp"), None),
            P(("dp", "fsdp"), None),
            P(("dp", "fsdp"), None),
            P(None, "dp", "fsdp"),
            P(None, "dp", "fsdp"),
            P(None, "dp", "fsdp"),
            P("dp", "fsdp"),
            P("dp", "fsdp"),
            P("dp", "fsdp"),
            P("dp", "fsdp"),
            P("dp", "fsdp"),
            P("dp", "fsdp"),
            P(None, ("dp", "fsdp")),
            P(None, ("dp", "fsdp")),
            P(None, ("dp", "fsdp")),
            P(),
            P(),
            P(),
            P(),
            P(),
            P(),
            P(),
            P(),
        ),
        check_vma=False,
    )
```

```python
import functools

import jax
import jax.numpy as jnp
import numpy as np
from jax import lax
from jax.experimental import pallas as pl
from jax.experimental.pallas import tpu as pltpu
from jax.sharding import PartitionSpec as P

D = 768
HEADS = 12
HEAD = 64
BUCKETS = 32
MAXDIST = 128
STEP = 10


HIGHEST = lax.Precision.HIGHEST
NORM_EPS = 1e-06
LEARN_RATE = 0.03
TABLE_RATE = 0.4
SMALL_RATE = 0.5
BETA_ONE = 0.9
BETA_TWO = 0.999
ADAM_EPS = 1e-08
WEIGHT_DECAY = 0.01
CLIP_NORM = 0.5


def bucket_table(length):
    places = np.arange(length)
    offset = places[None, :] - places[:, None]
    half_count = BUCKETS // 2
    exact_count = half_count // 2
    upper = (offset > 0).astype(np.int64) * half_count
    distance = np.abs(offset)
    far_bucket = exact_count + (
        np.log(np.maximum(distance, 1) / exact_count)
        / np.log(MAXDIST / exact_count)
        * (half_count - exact_count)
    ).astype(np.int64)
    far_bucket = np.minimum(far_bucket, half_count - 1)
    return (upper + np.where(distance < exact_count, distance, far_bucket)).astype(np.int32)


def bucket_onehot(length):
    flat_table = bucket_table(length).reshape(-1)
    return jnp.asarray((flat_table[:, None] == np.arange(BUCKETS)[None, :]).astype(np.float32))


def product(left, right):
    return jnp.dot(left, right, preferred_element_type=jnp.float32)


def product_left(left, right):
    return lax.dot_general(
        left, right, (((0,), (0,)), ((), ())), preferred_element_type=jnp.float32
    )


def product_right(left, right):
    return lax.dot_general(
        left, right, (((1,), (1,)), ((), ())), preferred_element_type=jnp.float32
    )


def attention_bias(position_bias, length):
    onehot = bucket_onehot(length)
    flat_bias = jnp.dot(onehot, position_bias, precision=HIGHEST)
    return (jnp.transpose(flat_bias.reshape(length, length, HEADS), (2, 0, 1)), onehot)


def adam_update(weight, moment, second, grad, factor, rate):
    clipped = grad * factor
    moment_new = BETA_ONE * moment + (1 - BETA_ONE) * clipped
    second_new = BETA_TWO * second + (1 - BETA_TWO) * clipped * clipped
    moment_hat = moment_new / (1 - BETA_ONE**STEP)
    second_hat = second_new / (1 - BETA_TWO**STEP)
    updated = weight - rate * (
        moment_hat / (jnp.sqrt(second_hat) + ADAM_EPS) + WEIGHT_DECAY * weight
    )
    return (moment_new, second_new, updated)


LANES = 128
GROUPS = 4
SLOT = LANES // GROUPS
VMEM_CAP = 56 * 1024 * 1024

def fold_rows(vocab):
    per = -(-vocab // GROUPS)
    return -(-per // LANES) * LANES

def up8(n):
    return -(-n // 8) * 8

def eye():
    r = lax.broadcasted_iota(jnp.int32, (LANES, LANES), 0)
    c = lax.broadcasted_iota(jnp.int32, (LANES, LANES), 1)
    return (r == c).astype(jnp.float32).astype(jnp.bfloat16)

def turn_table(fold, table_ref, turned):
    feats, vocab = table_ref.shape
    pad = jnp.zeros((SLOT - feats, LANES), jnp.float32)

    def build(b, carry):
        parts = []
        for j in range(GROUPS):
            start = jnp.minimum(j * fold + b * LANES, vocab - LANES)
            start = pl.multiple_of(start, LANES)
            parts += [table_ref[:, pl.ds(start, LANES)], pad]
        tile = jnp.concatenate(parts, axis=0).astype(jnp.bfloat16).astype(jnp.float32)
        turned[pl.ds(pl.multiple_of(b * LANES, LANES), LANES), :] = tile.T
        return carry

    lax.fori_loop(0, fold // LANES, build, 0)
    turned[pl.ds(fold, 8), :] = jnp.zeros((8, LANES), jnp.float32)


def pick_group(rows, group, feats):
    tokens = rows.shape[0]
    wide = dot_nt(eye(), rows[...].astype(jnp.bfloat16))
    total = jnp.where(group == 0, wide[:SLOT], 0.0)
    for j in range(1, GROUPS):
        total = total + jnp.where(group == j, wide[j * SLOT : (j + 1) * SLOT], 0.0)
    half = tokens // 2
    return jnp.concatenate([total[:feats, :half], total[:feats, half:]], axis=0).astype(jnp.bfloat16)


def look_up(row_ref, group_ref, source, turned, rows, feats):
    tokens = rows.shape[0]
    batch = 32

    def fetch(b, carry):
        for k in range(batch):
            t = b * batch + k
            rows[pl.ds(t, 1), :] = turned[pl.ds(row_ref[source, t], 1), :]
        return carry

    lax.fori_loop(0, tokens // batch, fetch, 0)
    return pick_group(rows, group_ref[source], feats)


def lookup_kernel(fold, row_ref, group_ref, table_ref, out_ref, turned, rows):
    @pl.when(pl.program_id(0) == 0)
    def _():
        turn_table(fold, table_ref, turned)

    out_ref[0] = look_up(row_ref, group_ref, 0, turned, rows, table_ref.shape[0])


def lookup(table, rows_idx, groups_idx):
    feats, vocab = table.shape
    n, tokens = rows_idx.shape[0], rows_idx.shape[2]
    fold = fold_rows(vocab)
    return pl.pallas_call(
        functools.partial(lookup_kernel, fold),
        grid=(n,),
        out_shape=jax.ShapeDtypeStruct((n, 2 * feats, tokens // 2), jnp.bfloat16),
        in_specs=[
            pl.BlockSpec((None, 1, tokens), lambda s: (s, 0, 0), memory_space=pltpu.SMEM),
            pl.BlockSpec((1, 1, tokens), lambda s: (s, 0, 0)),
            pl.BlockSpec((feats, vocab), lambda s: (0, 0)),
        ],
        out_specs=pl.BlockSpec((1, 2 * feats, tokens // 2), lambda s: (s, 0, 0)),
        scratch_shapes=[pltpu.VMEM((fold + 8, LANES), jnp.float32), pltpu.VMEM((tokens, LANES), jnp.float32)],
        compiler_params=pltpu.CompilerParams(vmem_limit_bytes=VMEM_CAP),
        name="lookup",
    )(rows_idx, groups_idx, table)

def scatter_kernel(fold, row_ref, group_ref, grad_ref, out_ref, total, rows):
    feats, vocab = out_ref.shape
    tokens = rows.shape[0]
    step = pl.program_id(0)
    @pl.when(step == 0)
    def _():
        def clear(b, _):
            total[pl.ds(pl.multiple_of(b * LANES, LANES), LANES), :] = jnp.zeros((LANES, LANES), jnp.float32)
            return 0
        lax.fori_loop(0, fold // LANES, clear, 0)
        total[pl.ds(fold, 8), :] = jnp.zeros((8, LANES), jnp.float32)
    block = grad_ref[0].astype(jnp.float32)
    flat = jnp.concatenate([block[:feats], block[feats:]], axis=1)
    group = group_ref[0]
    pad = jnp.zeros((SLOT - feats, tokens), jnp.float32)
    parts = []
    for j in range(GROUPS):
        parts += [jnp.where(group == j, flat, 0.0), pad]
    spread = jnp.concatenate(parts, axis=0).astype(jnp.bfloat16)
    rows[...] = lax.dot_general(spread, eye(), (((0,), (0,)), ((), ())), preferred_element_type=jnp.float32)
    LN = 16
    stride = tokens // LN
    def add(i, _):
        at = [row_ref[0, 0, i + stride * k] for k in range(LN)]
        new = [total[pl.ds(at[k], 1), :] + rows[pl.ds(i + stride * k, 1), :] for k in range(LN)]
        for k in range(LN):
            total[pl.ds(at[k], 1), :] = new[k]
        return 0
    lax.fori_loop(0, stride, add, 0, unroll=2)
    @pl.when(step == pl.num_programs(0) - 1)
    def _():
        whole = (vocab - (GROUPS - 1) * fold) // LANES
        def turn(b, _):
            tile = total[pl.ds(pl.multiple_of(b * LANES, LANES), LANES), :].T
            for j in range(GROUPS):
                out_ref[:, pl.ds(pl.multiple_of(j * fold + b * LANES, LANES), LANES)] = tile[j * SLOT:j * SLOT + feats]
            return 0
        lax.fori_loop(0, whole, turn, 0)
        for b in range(whole, fold // LANES):
            tile = total[pl.ds(b * LANES, LANES), :].T
            for j in range(GROUPS - 1):
                out_ref[:, pl.ds(j * fold + b * LANES, LANES)] = tile[j * SLOT:j * SLOT + feats]

def scatter(grads, rows_idx, groups_idx, vocab):
    n, tokens = rows_idx.shape[0], rows_idx.shape[2]
    feats = grads.shape[1] // 2
    fold = fold_rows(vocab)
    return pl.pallas_call(
        functools.partial(scatter_kernel, fold),
        grid=(n,),
        out_shape=jax.ShapeDtypeStruct((feats, vocab), jnp.float32),
        in_specs=[
            pl.BlockSpec((1, 1, tokens), lambda s: (s, 0, 0), memory_space=pltpu.SMEM),
            pl.BlockSpec((1, 1, tokens), lambda s: (s, 0, 0)),
            pl.BlockSpec((1, 2 * feats, tokens // 2), lambda s: (s, 0, 0)),
        ],
        out_specs=pl.BlockSpec((feats, vocab), lambda s: (0, 0)),
        scratch_shapes=[pltpu.VMEM((fold + 8, LANES), jnp.float32), pltpu.VMEM((tokens, LANES), jnp.float32)],
        compiler_params=pltpu.CompilerParams(vmem_limit_bytes=VMEM_CAP),
        name="scatter",
    )(rows_idx, groups_idx, grads)

def token_keys(tokens, fold):
    count = tokens.shape[0]
    key = (tokens % fold) * GROUPS + tokens // fold
    places = jnp.arange(count, dtype=jnp.int32)
    same_before = (key[:, None] == key[None, :]) & (places[:, None] < places[None, :])
    first = ~jnp.any(same_before, axis=0)
    rank = jnp.sum(((key[None, :] < key[:, None]) & first[None, :]).astype(jnp.int32), axis=1)
    hit = (rank[:, None] == places[None, :]) & first[:, None]
    packed = GROUPS * fold + jnp.sum(jnp.where(hit, key[:, None] - GROUPS * fold, 0), axis=0)
    return packed, rank


MESH = pl.DeviceIdType.MESH


def greet_all(count, cols, me):
    barrier = pltpu.get_barrier_semaphore()

    def greet(k, carry):
        to = lax.rem(me + k, count)
        pl.semaphore_signal(barrier, inc=1, device_id=(to // cols, lax.rem(to, cols)), device_id_type=MESH)
        return carry

    lax.fori_loop(1, count, greet, 0)
    pl.semaphore_wait(barrier, count - 1)


def exchange_kernel(same, src, dst, send_sem, recv_sem, own_sem):
    rows, cols = lax.axis_size("dp"), lax.axis_size("fsdp")
    count = rows * cols
    me = lax.axis_index("dp") * cols + lax.axis_index("fsdp")
    barrier = pltpu.get_barrier_semaphore()

    def device(k):
        to = lax.rem(me + k, count)
        return (to // cols, lax.rem(to, cols))

    def greet(k, carry):
        pl.semaphore_signal(barrier, inc=1, device_id=device(k), device_id_type=MESH)
        return carry

    def copy(k):
        to = lax.rem(me + k, count)
        return pltpu.make_async_remote_copy(
            src_ref=src.at[0 if same else to],
            dst_ref=dst.at[me],
            send_sem=send_sem.at[k],
            recv_sem=recv_sem.at[k],
            device_id=device(k),
            device_id_type=MESH,
        )

    def start(k, carry):
        copy(k).start()
        return carry

    def end(k, carry):
        copy(k).wait()
        return carry

    lax.fori_loop(1, count, greet, 0)
    own = pltpu.make_async_copy(src.at[0 if same else me], dst.at[me], own_sem)
    own.start()
    pl.semaphore_wait(barrier, count - 1)
    lax.fori_loop(1, count, start, 0)
    own.wait()
    lax.fori_loop(1, count, end, 0)


def exchange(blocks, same, call_id, name):
    count = lax.axis_size("dp") * lax.axis_size("fsdp")
    return pl.pallas_call(
        functools.partial(exchange_kernel, same),
        out_shape=jax.ShapeDtypeStruct((count,) + blocks.shape[1:], blocks.dtype),
        in_specs=[pl.BlockSpec(memory_space=pl.ANY)],
        out_specs=pl.BlockSpec(memory_space=pl.ANY),
        scratch_shapes=[
            pltpu.SemaphoreType.DMA((count,)),
            pltpu.SemaphoreType.DMA((count,)),
            pltpu.SemaphoreType.DMA,
        ],
        compiler_params=pltpu.CompilerParams(collective_id=call_id, has_side_effects=True),
        name=name,
    )(blocks)


SQUARE, EXPAND, REDUCE = range(3)
KINDS = 3
STEPS = (5, 6, 4)
FIRST = (3, 3, 2)


def spot(refs, kind, z, x, y, core):
    dp = z * 2 + x
    column = y * 2 + core
    if kind == SQUARE:
        return refs[kind].at[
            :,
            pl.ds(pl.multiple_of(dp * 96 + core * 48, 16), 48),
            pl.ds(pl.multiple_of(y * 384, 128), 384),
        ]
    if kind == EXPAND:
        return refs[kind].at[
            pl.ds(pl.multiple_of(dp * 96, 16), 96), pl.ds(pl.multiple_of(column * 768, 128), 768)
        ]
    return refs[kind].at[
        pl.ds(pl.multiple_of(column * 192, 16), 192), pl.ds(pl.multiple_of(dp * 384, 128), 384)
    ]


def spot_part(refs, kind, z, x, y, core, part):
    dp = z * 2 + x
    column = y * 2 + core
    if kind == SQUARE:
        return refs[kind].at[
            pl.ds(0, 3) if part == 0 else pl.ds(3, 2),
            pl.ds(pl.multiple_of(dp * 96 + core * 48, 16), 48),
            pl.ds(pl.multiple_of(y * 384, 128), 384),
        ]
    if kind == EXPAND:
        return refs[kind].at[
            pl.ds(pl.multiple_of(dp * 96 + part * 48, 16), 48),
            pl.ds(pl.multiple_of(column * 768, 128), 768),
        ]
    return refs[kind].at[
        pl.ds(pl.multiple_of(column * 192 + part * 96, 16), 96),
        pl.ds(pl.multiple_of(dp * 384, 128), 384),
    ]


def block_part(ref, kind, part):
    if kind == SQUARE:
        return ref.at[pl.ds(0, 3) if part == 0 else pl.ds(3, 2)]
    half = 48 if kind == EXPAND else 96
    return ref.at[pl.ds(part * half, half)]


def block_step(ref, kind, k):
    if kind == SQUARE:
        return ref.at[k]
    rows = 16 if kind == EXPAND else 48
    return ref.at[pl.ds(pl.multiple_of(k * rows, 16), rows)]


BLOCKS = ((5, 48, 384), (96, 768), (192, 384))


def place():
    dp, fsdp = lax.axis_index("dp"), lax.axis_index("fsdp")
    return dp // 2, lax.rem(dp, 2), fsdp // 2, lax.rem(fsdp, 2)


def device_at(z, x, y, core):
    return (z * 2 + x, y * 2 + core)


def greet_neighbours(depth):
    z, x, y, core = place()
    barrier = pltpu.get_barrier_semaphore()

    def hello(target):
        pl.semaphore_signal(barrier, inc=1, device_id=target, device_id_type=MESH)

    hello(device_at(z, x, y, 1 - core))
    hello(device_at(z, 1 - x, y, core))
    hello(device_at(z, x, 1 - y, core))

    @pl.when(z > 0)
    def _():
        hello(device_at(z - 1, x, y, core))

    @pl.when(z < depth - 1)
    def _():
        hello(device_at(z + 1, x, y, core))

    above = jnp.where(z < depth - 1, 1, 0)
    below = jnp.where(z > 0, 1, 0)
    pl.semaphore_wait(barrier, 3 + above + below)


def remote(src, dst, send_sem, recv_sem, target):
    return pltpu.make_async_remote_copy(
        src_ref=src, dst_ref=dst, send_sem=send_sem, recv_sem=recv_sem,
        device_id=target, device_id_type=MESH)


class Gather:
    def __init__(self, kinds, depth, sources, outs, sems):
        self.kinds, self.depth, self.sources, self.outs = kinds, depth, sources, outs
        self.own_sem, self.send, self.got, self.sib_send, self.sib_got, self.diag_got = sems
        self.number = {a: n for n, a in enumerate(kinds)}
        z, x, y, core = place()
        self.z, self.x, self.y, self.core = z, x, y, core
        self.sibling = device_at(z, x, y, 1 - core)
        self.x_next, self.y_next = device_at(z, 1 - x, y, core), device_at(z, x, 1 - y, core)

    def to(self, way, a, z_at, x_at, y_at, target, part=None, src=None):
        n, k = self.number[a], (z_at * 2 + x_at) * 2 + y_at
        if part is None:
            spot_at, recv = spot(self.outs, a, z_at, x_at, y_at, self.core), self.got.at[n, k]
        else:
            spot_at = spot_part(self.outs, a, z_at, x_at, y_at, self.core, part)
            recv = self.diag_got.at[n, z_at, part]
        return remote(spot_at if src is None else src, spot_at, self.send.at[way, n, k], recv, target)

    def to_sibling(self, a, z_at, x_at, y_at, src=None, core=None):
        spot_at = spot(self.outs, a, z_at, x_at, y_at, self.core if core is None else core)
        n, k = self.number[a], (z_at * 2 + x_at) * 2 + y_at
        return remote(
            spot_at if src is None else src, spot_at, self.sib_send.at[n, k], self.sib_got.at[n, k], self.sibling
        )

    def own_copy(self, a):
        return pltpu.make_async_copy(
            self.sources[a], spot(self.outs, a, self.z, self.x, self.y, self.core), self.own_sem.at[self.number[a]]
        )

    def begin(self):
        z, x, y, core = self.z, self.x, self.y, self.core
        for a in self.kinds:
            source = self.sources[a]
            self.own_copy(a).start()

            @pl.when(z < self.depth - 1)
            def _():
                self.to(0, a, z, x, y, device_at(z + 1, x, y, core), src=source).start()

            @pl.when(z > 0)
            def _():
                self.to(1, a, z, x, y, device_at(z - 1, x, y, core), src=source).start()

            self.to(2, a, z, x, y, self.x_next, src=source).start()
            self.to(3, a, z, x, y, self.y_next, src=source).start()
            self.to_sibling(a, z, x, y, src=source).start()

    def sides(self, step, act):
        if step == 0:
            act(self.z)
            return
        for sign in (1, -1):
            z_at = self.z + sign * step

            @pl.when((z_at >= 0) & (z_at < self.depth))
            def _():
                act(z_at)

    def first(self, step):
        z, x, y, core = self.z, self.x, self.y, self.core

        def act(z_at):
            for a in self.kinds:
                self.to(0, a, z_at, x, y, self.sibling).wait_recv()

                @pl.when((z_at < z) & (z < self.depth - 1))
                def _():
                    self.to(0, a, z_at, x, y, device_at(z + 1, x, y, core)).start()

                @pl.when((z_at > z) & (z > 0))
                def _():
                    self.to(1, a, z_at, x, y, device_at(z - 1, x, y, core)).start()

                self.to(2, a, z_at, x, y, self.x_next).start()
                self.to(3, a, z_at, x, y, self.y_next).start()
                self.to_sibling(a, z_at, x, y).start()

        self.sides(step, act)

    def second(self, step):
        x, y = self.x, self.y

        def act(z_at):
            for a in self.kinds:
                self.to(0, a, z_at, 1 - x, y, self.sibling).wait_recv()
                self.to(3, a, z_at, 1 - x, y, self.y_next, 0).start()
                self.to_sibling(a, z_at, 1 - x, y).start()
                self.to(0, a, z_at, x, 1 - y, self.sibling).wait_recv()
                self.to(2, a, z_at, x, 1 - y, self.x_next, 1).start()
                self.to_sibling(a, z_at, x, 1 - y).start()

        self.sides(step, act)

    def third(self, step):
        x, y = self.x, self.y

        def act(z_at):
            for a in self.kinds:
                for part in range(2):
                    self.to(0, a, z_at, 1 - x, 1 - y, self.sibling, part).wait_recv()
                self.to_sibling(a, z_at, 1 - x, 1 - y).start()

        self.sides(step, act)

    def relays(self):
        for step in range(1, self.depth + 2):
            if step < self.depth:
                yield functools.partial(self.first, step)
            if 0 <= step - 1 < self.depth:
                yield functools.partial(self.second, step - 1)
            if 0 <= step - 2 < self.depth:
                yield functools.partial(self.third, step - 2)

    def arrive(self):
        for a in self.kinds:
            self.own_copy(a).wait()

        def wait(z_at, carry):
            for a in self.kinds:
                for x_at in range(2):
                    for y_at in range(2):
                        self.to_sibling(a, z_at, x_at, y_at, core=1 - self.core).wait_recv()
            return carry

        lax.fori_loop(0, self.depth, wait, 0)

    def finish(self):
        z, x, y = self.z, self.x, self.y

        def wait(z_at, carry):
            for a in self.kinds:

                @pl.when((z_at <= z) & (z < self.depth - 1))
                def _():
                    self.to(0, a, z_at, x, y, self.x_next).wait_send()

                @pl.when((z_at >= z) & (z > 0))
                def _():
                    self.to(1, a, z_at, x, y, self.x_next).wait_send()

                self.to(2, a, z_at, x, y, self.x_next).wait_send()
                self.to(3, a, z_at, x, y, self.y_next).wait_send()
                self.to(3, a, z_at, 1 - x, y, self.y_next, 0).wait_send()
                self.to(2, a, z_at, x, 1 - y, self.x_next, 1).wait_send()
                for x_at in range(2):
                    for y_at in range(2):
                        self.to_sibling(a, z_at, x_at, y_at).wait_send()
            return carry

        lax.fori_loop(0, self.depth, wait, 0)


def gather_sems(kinds, depth):
    count, spots = len(kinds), 4 * depth
    return [
        pltpu.SemaphoreType.DMA((count,)),
        pltpu.SemaphoreType.DMA((4, count, spots)),
        pltpu.SemaphoreType.DMA((count, spots)),
        pltpu.SemaphoreType.DMA((count, spots)),
        pltpu.SemaphoreType.DMA((count, spots)),
        pltpu.SemaphoreType.DMA((count, depth, 2)),
    ]


FEED_KINDS = (EXPAND, REDUCE)
SQUARE_KINDS = (SQUARE,)


def front_kernel(fold, depth, keys_ref, gains_ref, table_ref, square_in, *refs):
    found, square_out, keys_all, gains_all = refs[:4]
    theirs, own, turned, rows, blocks, row_low, row_all = refs[4:11]
    gather_sem, refs = refs[11:17], refs[17:]
    pair_send, pair_recv, part_send, part_got, part_own, keys_send, keys_got, gains_send, gains_got, near_sem = refs
    dp_size, fsdp_size = lax.axis_size("dp"), lax.axis_size("fsdp")
    count = dp_size * fsdp_size
    me = lax.axis_index("dp") * fsdp_size + lax.axis_index("fsdp")
    z, x, y, core = place()
    sibling = device_at(z, x, y, 1 - core)
    greet_all(count, fsdp_size, me)

    def info_copies(k):
        target = lax.rem(me + k, count)
        device = (target // fsdp_size, lax.rem(target, fsdp_size))
        return (
            remote(keys_ref, keys_all.at[me], keys_send.at[k], keys_got.at[k], device),
            remote(gains_ref, gains_all.at[me], gains_send.at[k], gains_got.at[k], device),
        )

    def start_info(k, carry):
        for copy in info_copies(k):
            copy.start()
        return carry

    lax.fori_loop(1, count, start_info, 0)
    keys_all[me] = keys_ref[...]
    gains_all[me] = gains_ref[...]
    pair = remote(square_in.at[1 - core], theirs, pair_send, pair_recv, sibling)
    pair.start()
    gather = Gather(SQUARE_KINDS, depth, {SQUARE: own}, {SQUARE: square_out}, gather_sem)
    row = lax.broadcasted_iota(jnp.int32, (192, 384), 0)
    col = lax.broadcasted_iota(jnp.int32, (192, 384), 1)
    here = (row + core * 192 == col).astype(jnp.float32).astype(jnp.bfloat16)
    there = (row + (1 - core) * 192 == col).astype(jnp.float32).astype(jnp.bfloat16)
    pair.wait_recv()
    for k in range(5):
        block = jnp.dot(square_in[core, k], here, preferred_element_type=jnp.float32) + jnp.dot(
            theirs[k], there, preferred_element_type=jnp.float32
        )
        own[k] = block.astype(jnp.bfloat16)
    gather.begin()
    turn_table(fold, table_ref, turned)

    def end_info(k, carry):
        for copy in info_copies(k):
            copy.wait()
        return carry

    lax.fori_loop(1, count, end_info, 0)
    key_rows = row_low.shape[0] // count

    def split_row(k, carry):
        row_low[pl.ds(pl.multiple_of(k * key_rows, 8), key_rows)] = keys_all[k, :key_rows] >> 2
        return carry

    lax.fori_loop(0, count, split_row, 0)
    near = pltpu.make_async_copy(row_low, row_all, near_sem)
    near.start()
    near.wait()

    def find(target):
        keys = keys_all[target]
        group = jnp.concatenate([keys[r : r + 1] for r in range(key_rows)], axis=1) & 3

        def fetch(r, carry):
            line = target * key_rows + r
            start = pl.multiple_of(r * LANES, LANES)
            for k in range(LANES):
                rows[pl.ds(start + k, 1), :] = turned[pl.ds(row_all[line, k], 1), :]
            return carry

        lax.fori_loop(0, key_rows, fetch, 0)
        return pick_group(rows, group, table_ref.shape[0])

    def part_copy(k):
        target = lax.rem(me + k, count)
        device = (target // fsdp_size, lax.rem(target, fsdp_size))
        return remote(blocks.at[target], found.at[me], part_send.at[k], part_got.at[k], device)

    def serve(k, carry):
        target = lax.rem(me + k, count)
        blocks[target] = find(target)
        part_copy(k).start()
        return carry

    relays = list(gather.relays())
    done = 1
    for n, relay in enumerate(relays):
        until = 1 + ((n + 1) * (count - 1)) // len(relays)
        lax.fori_loop(done, until, serve, 0)
        done = until
        relay()
    blocks[me] = find(me)
    own_part = pltpu.make_async_copy(blocks.at[me], found.at[me], part_own)
    own_part.start()
    pair.wait_send()
    gather.arrive()
    gather.finish()
    own_part.wait()

    def end_part(k, carry):
        part_copy(k).wait()
        return carry

    lax.fori_loop(1, count, end_part, 0)


def run_front(keys, gains, tokens, table, square, call_id):
    depth = lax.axis_size("dp") // 2
    count = lax.axis_size("dp") * lax.axis_size("fsdp")
    feats, vocab = table.shape
    fold = fold_rows(vocab)
    blocks = (count, 2 * feats, tokens // 2)
    whole = pl.BlockSpec(memory_space=pltpu.VMEM)
    anywhere = pl.BlockSpec(memory_space=pl.ANY)
    many = pltpu.SemaphoreType.DMA((count,))
    return pl.pallas_call(
        functools.partial(front_kernel, fold, depth),
        out_shape=[
            jax.ShapeDtypeStruct(blocks, jnp.bfloat16),
            jax.ShapeDtypeStruct((5, 768, 768), jnp.bfloat16),
            jax.ShapeDtypeStruct((count,) + keys.shape, keys.dtype),
            jax.ShapeDtypeStruct((count,) + gains.shape, gains.dtype),
        ],
        in_specs=[whole] * 4,
        out_specs=[anywhere] * 2 + [whole] * 2,
        scratch_shapes=[
            pltpu.VMEM((5, 48, 192), jnp.bfloat16),
            pltpu.VMEM((5, 48, 384), jnp.bfloat16),
            pltpu.VMEM((fold + 8, LANES), jnp.float32),
            pltpu.VMEM((tokens, LANES), jnp.float32),
            pltpu.VMEM(blocks, jnp.bfloat16),
            pltpu.VMEM((count * tokens // LANES, LANES), jnp.int32),
            pltpu.SMEM((count * tokens // LANES, LANES), jnp.int32),
        ]
        + gather_sems(SQUARE_KINDS, depth)
        + [pltpu.SemaphoreType.DMA, pltpu.SemaphoreType.DMA]
        + [many, many, pltpu.SemaphoreType.DMA]
        + [many] * 4
        + [pltpu.SemaphoreType.DMA],
        compiler_params=pltpu.CompilerParams(
            collective_id=call_id, has_side_effects=True, vmem_limit_bytes=VMEM_CAP
        ),
        name="front",
    )(keys, gains, table, square)


class Reduction:
    def __init__(self, kinds, depth, grads, outs, work, buffers, sems):
        self.kinds, self.depth, self.grads, self.outs, self.own_work = kinds, depth, grads, outs, work
        count = len(kinds)
        self.paired, self.step_one, self.from_x, self.from_y, self.from_z = [
            dict(zip(kinds, buffers[k * count : (k + 1) * count])) for k in range(5)
        ]
        self.load_sem, self.pair_send, self.pair_got, self.send, self.one_got = sems[:5]
        self.x_got, self.y_got, self.z_got = sems[5:8]
        self.number = {a: n for n, a in enumerate(kinds)}
        z, x, y, core = place()
        self.z, self.x, self.y, self.core = z, x, y, core
        self.sibling = device_at(z, x, y, 1 - core)
        self.x_next, self.y_next = device_at(z, 1 - x, y, core), device_at(z, x, 1 - y, core)

    def work(self, a, z_at, x_at, y_at):
        if self.own_work is None:
            return spot(self.grads, a, z_at, x_at, y_at, self.core)
        return self.own_work[a].at[z_at * 2 + x_at, y_at]

    def load(self, a, z_at, x_at, y_at):
        return pltpu.make_async_copy(
            spot(self.grads, a, z_at, x_at, y_at, self.core),
            self.work(a, z_at, x_at, y_at),
            self.load_sem.at[self.number[a], z_at * 2 + x_at, y_at],
        )

    def pair(self, a, z_at, x_at, y_at):
        n, i = self.number[a], z_at * 2 + x_at
        return remote(
            spot(self.grads, a, z_at, x_at, y_at, 1 - self.core),
            self.paired[a].at[i, y_at],
            self.pair_send.at[n, i, y_at],
            self.pair_got.at[n, i, y_at],
            self.sibling,
        )

    def sides(self, step, act):
        if step == 0:
            act(self.z)
            return
        for sign in (1, -1):
            z_at = self.z + sign * step

            @pl.when((z_at >= 0) & (z_at < self.depth))
            def _():
                act(z_at)

    def begin(self):
        x, y = self.x, self.y
        for x_at, y_at in ((1 - x, 1 - y), (1 - x, y), (x, 1 - y), (x, y)):
            for step in range(self.depth - 1, -1, -1):

                def start(z_at):
                    for a in self.kinds:
                        if self.own_work is not None:
                            self.load(a, z_at, x_at, y_at).start()
                        self.pair(a, z_at, x_at, y_at).start()

                self.sides(step, start)

    def ready(self, a, z_at, x_at, y_at):
        if self.own_work is not None:
            self.load(a, z_at, x_at, y_at).wait()
        self.pair(a, z_at, x_at, y_at).wait_recv()

    def total(self, a, z_at, x_at, y_at, first, last, extra=()):
        here = self.work(a, z_at, x_at, y_at)
        paired = self.paired[a].at[z_at * 2 + x_at, y_at]

        def add(k, carry):
            step = block_step(here, a, k)
            value = step[...].astype(jnp.float32) + block_step(paired, a, k)[...].astype(jnp.float32)
            for buffer in extra:
                value = value + block_step(buffer, a, k)[...].astype(jnp.float32)
            step[...] = value.astype(jnp.bfloat16)
            return carry

        lax.fori_loop(first, last, add, 0)

    def diag_copy(self, a, z_at, part):
        n = self.number[a]
        return remote(
            block_part(self.work(a, z_at, 1 - self.x, 1 - self.y), a, part),
            block_part(self.step_one[a].at[z_at], a, part),
            self.send.at[part, n, z_at],
            self.one_got.at[n, part, z_at],
            self.y_next if part == 0 else self.x_next,
        )

    def diag(self, step):
        def act(z_at):
            for a in self.kinds:
                self.ready(a, z_at, 1 - self.x, 1 - self.y)
                self.total(a, z_at, 1 - self.x, 1 - self.y, 0, STEPS[a])
                for part in range(2):
                    self.diag_copy(a, z_at, part).start()

        self.sides(step, act)

    def x_copy(self, a, z_at):
        n = self.number[a]
        return remote(
            self.work(a, z_at, 1 - self.x, self.y),
            self.from_x[a].at[z_at],
            self.send.at[2, n, z_at],
            self.x_got.at[n, z_at],
            self.x_next,
        )

    def y_copy(self, a, z_at):
        n = self.number[a]
        return remote(
            self.work(a, z_at, self.x, 1 - self.y),
            self.from_y[a].at[z_at],
            self.send.at[3, n, z_at],
            self.y_got.at[n, z_at],
            self.y_next,
        )

    def columns(self, step):
        x, y = self.x, self.y

        def act(z_at):
            for a in self.kinds:
                middle, last = FIRST[a], STEPS[a]
                self.ready(a, z_at, 1 - x, y)
                self.diag_copy(a, z_at, 0).wait_recv()
                self.total(a, z_at, 1 - x, y, 0, middle, [self.step_one[a].at[z_at]])
                self.total(a, z_at, 1 - x, y, middle, last)
                self.x_copy(a, z_at).start()
                self.ready(a, z_at, x, 1 - y)
                self.diag_copy(a, z_at, 1).wait_recv()
                self.total(a, z_at, x, 1 - y, 0, middle)
                self.total(a, z_at, x, 1 - y, middle, last, [self.step_one[a].at[z_at]])
                self.y_copy(a, z_at).start()

        self.sides(step, act)

    def z_copy(self, a, z_at, side, target):
        n = self.number[a]
        return remote(
            self.work(a, z_at, self.x, self.y),
            self.from_z[a].at[side, z_at],
            self.send.at[4, n, z_at],
            self.z_got.at[n, side, z_at],
            target,
        )

    def line(self, step, keep=None):
        z, x, y, core, depth = self.z, self.x, self.y, self.core, self.depth

        def act(z_at):
            for a in self.kinds:
                self.ready(a, z_at, x, y)
                self.x_copy(a, z_at).wait_recv()
                self.y_copy(a, z_at).wait_recv()
                across = [self.from_x[a].at[z_at], self.from_y[a].at[z_at]]
                if step > 0:
                    upward = z_at > z
                    before = (upward & (z > 0)) | (jnp.logical_not(upward) & (z < depth - 1))
                    side = jnp.where(upward, 0, 1)

                    @pl.when(before)
                    def _():
                        self.z_copy(a, z_at, side, self.sibling).wait_recv()
                        self.total(a, z_at, x, y, 0, STEPS[a], across + [self.from_z[a].at[side, z_at]])

                    @pl.when(jnp.logical_not(before))
                    def _():
                        self.total(a, z_at, x, y, 0, STEPS[a], across)

                    @pl.when(upward)
                    def _():
                        self.z_copy(a, z_at, 0, device_at(z + 1, x, y, core)).start()

                    @pl.when(jnp.logical_not(upward))
                    def _():
                        self.z_copy(a, z_at, 1, device_at(z - 1, x, y, core)).start()
                else:
                    for side in range(2):
                        present = (z > 0) if side == 0 else (z < depth - 1)

                        @pl.when(present)
                        def _():
                            self.z_copy(a, z, side, self.sibling).wait_recv()

                        @pl.when(jnp.logical_not(present))
                        def _():
                            self.from_z[a][side, z] = jnp.zeros(BLOCKS[a], jnp.bfloat16)

                    here, paired = self.work(a, z, x, y), self.paired[a].at[z * 2 + x, y]

                    def finish(k, carry):
                        value = block_step(here, a, k)[...].astype(jnp.float32)
                        for buffer in [paired] + across + [self.from_z[a].at[0, z], self.from_z[a].at[1, z]]:
                            value = value + block_step(buffer, a, k)[...].astype(jnp.float32)
                        if a == SQUARE:
                            spare = self.outs[3]
                            low, high = value[:, :192], pltpu.roll(value, 192, 1)[:, :192]
                            self.outs[SQUARE][core, k] = jnp.where(core == 0, low, high)
                            spare[k] = jnp.where(core == 0, high, low)
                        else:
                            block_step(self.outs[a], a, k)[...] = value
                        return carry

                    lax.fori_loop(0, STEPS[a], finish, 0)

        self.sides(step, act)

    def groups(self):
        rounds = list(range(self.depth - 1, -1, -1))
        for k in range(self.depth + 2):
            group = []
            if k < self.depth:
                group.append((self.diag, rounds[k]))
            if 0 <= k - 1 < self.depth:
                group.append((self.columns, rounds[k - 1]))
            if 0 <= k - 2 < self.depth:
                group.append((self.line, rounds[k - 2]))
            yield group

    def finish(self):
        def wait(z_at, carry):
            for a in self.kinds:
                for x_at in range(2):
                    for y_at in range(2):
                        self.pair(a, z_at, x_at, y_at).wait_send()
                for part in range(2):
                    self.diag_copy(a, z_at, part).wait_send()
                self.x_copy(a, z_at).wait_send()
                self.y_copy(a, z_at).wait_send()

                @pl.when(z_at != self.z)
                def _():
                    self.z_copy(a, z_at, 0, self.sibling).wait_send()
            return carry

        lax.fori_loop(0, self.depth, wait, 0)


def reduction_scratch(kinds, depth):
    def buffers(*lead):
        return [pltpu.VMEM(lead + BLOCKS[a], jnp.bfloat16) for a in kinds]

    count = len(kinds)
    spots = pltpu.SemaphoreType.DMA((count, 2 * depth, 2))
    return (
        buffers(2 * depth, 2) + buffers(depth) + buffers(depth) + buffers(depth) + buffers(2, depth),
        [
            spots,
            spots,
            spots,
            pltpu.SemaphoreType.DMA((5, count, depth)),
            pltpu.SemaphoreType.DMA((count, 2, depth)),
            pltpu.SemaphoreType.DMA((count, depth)),
            pltpu.SemaphoreType.DMA((count, depth)),
            pltpu.SemaphoreType.DMA((count, 2, depth)),
        ],
    )


TILE = 128
PAIRS = HEADS // 2
GELU_IN = (2.0 / np.pi) ** 0.5


def dot_nn(left, right):
    return jnp.dot(left, right, preferred_element_type=jnp.float32)


def dot_nt(left, right):
    return lax.dot_general(left, right, (((1,), (1,)), ((), ())), preferred_element_type=jnp.float32)


def dot_tn(left, right):
    return lax.dot_general(left, right, (((0,), (0,)), ((), ())), preferred_element_type=jnp.float32)


def rows_at(index, size):
    return pl.ds(pl.multiple_of(index * size, size), size)


def split_heads(block):
    low = lax.broadcasted_iota(jnp.int32, block.shape, 1) < HEAD
    wide = block.astype(jnp.float32)
    first = jnp.where(low, wide, 0.0).astype(jnp.bfloat16)
    second = jnp.where(low, 0.0, wide).astype(jnp.bfloat16)
    return jnp.concatenate([first, second], axis=0)


def join_heads(stacked):
    return jnp.concatenate([stacked[:TILE], stacked[TILE:]], axis=1)


def pair_probs(query, keys_here, bias, mask):
    scores = dot_nt(split_heads(query), keys_here) * HEAD ** (-0.5) + bias
    scores = scores + mask
    raised = jnp.exp(scores - jnp.max(scores, axis=1, keepdims=True))
    return raised / jnp.sum(raised, axis=1, keepdims=True)


def pair_bias(bias_ref, pair):
    return jnp.concatenate([bias_ref[2 * pair], bias_ref[2 * pair + 1]], axis=0)


def tile_mask(mask_ref, tile):
    mask = mask_ref[tile]
    return jnp.concatenate([mask, mask], axis=0)


def hot_rows(rank_ref, rows, tokens):
    place = lax.broadcasted_iota(jnp.int32, (rows.size, tokens), 1)
    return (rank_ref[rows, :1] == place).astype(jnp.float32).astype(jnp.bfloat16)


def norm_rows(values, gain):
    scale = lax.rsqrt(jnp.mean(values * values, axis=1, keepdims=True) + NORM_EPS)
    return values * scale * gain


def gelu_parts(pre):
    inner = GELU_IN * (pre + 0.044715 * pre * pre * pre)
    return jnp.tanh(inner)


def forward_steps(
    found_ref, rank_ref, square_ref, gains_ref, bias_ref, mask_ref, pool_ref, length_ref,
    start_ref, query_ref, key_ref, value_ref, mixed_ref, middle_ref, ending_ref, low_ref, pooled_ref, embed_ref,
    inverse_ref, normed, pooled_sum, wide_found, low_found, expand_ref, reduce_ref, between, before_feed,
):
    between = list(between)

    def relay(count):
        for _ in range(min(count, len(between))):
            between.pop(0)()

    tokens = start_ref.shape[0]
    big = 512
    feats, half = found_ref.shape[1] // 2, found_ref.shape[2]

    def assemble(p, carry):
        block = found_ref[p].astype(jnp.float32)
        at = pl.ds(pl.multiple_of(p * feats, 8), feats)
        wide_found[at, :half] = block[:feats]
        wide_found[at, half:] = block[feats:]
        return carry

    lax.fori_loop(0, found_ref.shape[0], assemble, 0)
    low_found[...] = wide_found[...].astype(jnp.bfloat16)

    def begin(r, carry):
        rows = rows_at(r, 256)
        start = dot_nt(hot_rows(rank_ref, rows, tokens), low_found[...])
        start_ref[rows, :] = start.astype(jnp.bfloat16)
        normed[rows, :] = norm_rows(start, gains_ref[0:1]).astype(jnp.bfloat16)
        return carry

    lax.fori_loop(0, tokens // 256, begin, 0)
    relay(1)
    for k, target in enumerate((query_ref, key_ref, value_ref)):

        def project(r, carry):
            rows = rows_at(r, big)
            target[rows, :] = dot_nn(normed[rows, :], square_ref[k]).astype(jnp.bfloat16)
            return carry

        lax.fori_loop(0, tokens // big, project, 0)
        relay(1)

    def attend(t, carry):
        rows = rows_at(t, TILE)
        mask = tile_mask(mask_ref, t)
        for pair in range(PAIRS):
            lanes = pl.ds(pair * TILE, TILE)
            probs = pair_probs(query_ref[rows, lanes], key_ref[rows, lanes], pair_bias(bias_ref, pair), mask)
            mixed = dot_nn(join_heads(probs).astype(jnp.bfloat16), split_heads(value_ref[rows, lanes]))
            mixed_ref[rows, lanes] = mixed.astype(jnp.bfloat16)
        return carry

    tiles = tokens // TILE
    if between:
        for t in range(tiles):
            lax.fori_loop(t, t + 1, attend, 0)
            relay(1)
    else:
        lax.fori_loop(0, tiles, attend, 0)

    def merge(r, carry):
        rows = rows_at(r, big)
        middle = start_ref[rows, :].astype(jnp.float32) + dot_nn(mixed_ref[rows, :], square_ref[3])
        middle_ref[rows, :] = middle
        ending_ref[rows, :] = middle
        normed[rows, :] = norm_rows(middle, gains_ref[1:2]).astype(jnp.bfloat16)
        return carry

    lax.fori_loop(0, tokens // big, merge, 0)
    relay(len(between))
    before_feed()
    wide = expand_ref.shape[1]

    def feed(c, carry):
        lanes = rows_at(c, D)

        def rows_of(r, inner):
            rows = rows_at(r, big)
            pre = dot_nn(normed[rows, :], expand_ref[:, lanes])
            act = (0.5 * pre * (1.0 + gelu_parts(pre))).astype(jnp.bfloat16)
            ending_ref[rows, :] += dot_nt(act, reduce_ref[:, lanes])
            return inner

        return lax.fori_loop(0, tokens // big, rows_of, carry)

    lax.fori_loop(0, wide // D, feed, 0)
    pooled_sum[...] = jnp.zeros_like(pooled_sum)

    def pool(r, carry):
        rows = rows_at(r, 256)
        output = norm_rows(ending_ref[rows, :], gains_ref[2:3])
        pooled_sum[...] += jnp.dot(
            pool_ref[:, rows], output, precision=HIGHEST, preferred_element_type=jnp.float32
        )
        return carry

    lax.fori_loop(0, tokens // 256, pool, 0)
    pooled = (pooled_sum[...] / length_ref[:, :1]).astype(jnp.bfloat16)
    pooled_ref[...] = pooled
    projected = dot_nn(pooled, square_ref[4])
    inverse = lax.rsqrt(jnp.sum(projected * projected, axis=1, keepdims=True) + NORM_EPS)
    embeds = projected * inverse
    embed_ref[...] = embeds
    low_ref[...] = embeds.astype(jnp.bfloat16)
    inverse_ref[...] = jnp.broadcast_to(inverse, inverse_ref.shape)


def forward_kernel(*refs):
    ins, expand_ref, reduce_ref, rest = refs[:8], refs[8], refs[9], refs[10:]
    forward_steps(*ins, *rest, expand_ref, reduce_ref, [], lambda: None)


def relayed_forward_kernel(depth, *refs):
    ins, expand_in, reduce_in = refs[:8], refs[8], refs[9]
    outs, expand_out, reduce_out = refs[10:21], refs[21], refs[22]
    steps, expand_all, reduce_all = refs[23:27], refs[27], refs[28]
    sems, save = refs[29:35], refs[35]
    greet_neighbours(depth)
    gather = Gather(
        FEED_KINDS, depth, {EXPAND: expand_in, REDUCE: reduce_in}, {EXPAND: expand_all, REDUCE: reduce_all}, sems
    )
    gather.begin()

    def saves():
        return (
            pltpu.make_async_copy(expand_all, expand_out, save.at[0]),
            pltpu.make_async_copy(reduce_all, reduce_out, save.at[1]),
        )

    def before_feed():
        gather.arrive()
        for copy in saves():
            copy.start()

    forward_steps(*ins, *outs, *steps, expand_all, reduce_all, gather.relays(), before_feed)
    gather.finish()
    for copy in saves():
        copy.wait()


def forward_outs(tokens, seqs):
    flat = jax.ShapeDtypeStruct((tokens, D), jnp.bfloat16)
    full = jax.ShapeDtypeStruct((tokens, D), jnp.float32)
    few = jax.ShapeDtypeStruct((seqs, D), jnp.bfloat16)
    return [
        flat, flat, flat, flat, flat, full, full, few, few,
        jax.ShapeDtypeStruct((seqs, D), jnp.float32),
        jax.ShapeDtypeStruct((seqs, LANES), jnp.float32),
    ]


def forward_scratch(tokens, seqs):
    return [
        pltpu.VMEM((tokens, D), jnp.bfloat16),
        pltpu.VMEM((seqs, D), jnp.float32),
        pltpu.VMEM((D, tokens), jnp.float32),
        pltpu.VMEM((D, tokens), jnp.bfloat16),
    ]


def run_forward(ins, expand, reduce_turned):
    tokens, seqs = ins[1].shape[0], ins[6].shape[0]
    return pl.pallas_call(
        forward_kernel,
        out_shape=forward_outs(tokens, seqs),
        scratch_shapes=forward_scratch(tokens, seqs),
        compiler_params=pltpu.CompilerParams(vmem_limit_bytes=VMEM_CAP),
        name="layer_forward",
    )(*ins, expand, reduce_turned)


def run_relayed_forward(ins, expand_piece, reduce_piece, call_id):
    depth = lax.axis_size("dp") // 2
    tokens, seqs = ins[1].shape[0], ins[6].shape[0]
    weight = (768, 3072)
    outs = forward_outs(tokens, seqs)
    whole = pl.BlockSpec(memory_space=pltpu.VMEM)
    anywhere = pl.BlockSpec(memory_space=pl.ANY)
    return pl.pallas_call(
        functools.partial(relayed_forward_kernel, depth),
        out_shape=outs + [jax.ShapeDtypeStruct(weight, jnp.bfloat16)] * 2,
        in_specs=[whole] * (len(ins) + 2),
        out_specs=[whole] * len(outs) + [anywhere] * 2,
        scratch_shapes=forward_scratch(tokens, seqs)
        + [pltpu.VMEM(weight, jnp.bfloat16)] * 2
        + gather_sems(FEED_KINDS, depth)
        + [pltpu.SemaphoreType.DMA((2,))],
        compiler_params=pltpu.CompilerParams(
            collective_id=call_id, has_side_effects=True, vmem_limit_bytes=VMEM_CAP
        ),
        name="layer_forward",
    )(*ins, expand_piece, reduce_piece)


def norm_back_rows(values, gain, grad):
    scale = lax.rsqrt(jnp.mean(values * values, axis=1, keepdims=True) + NORM_EPS)
    weighted = grad * gain
    inner = jnp.mean(weighted * values, axis=1, keepdims=True)
    through = scale * weighted - values * (scale * scale * scale * inner)
    return through, jnp.sum(grad * values * scale, axis=0, keepdims=True)


def feed_back_kernel(
    grad_embed_ref, embed_ref, inverse_ref, pool_ref, length_ref, last_ref, middle_ref, ending_ref, expand_ref,
    reduce_ref, gains_ref,
    grad_expand_ref, grad_reduce_ref, grad_middle_ref, grad_low_ref, grad_proj_ref, grad_gains_ref,
    normed, normed_turned, end_low, end_turned, back,
):
    tokens = middle_ref.shape[0]
    embeds, grads = embed_ref[...], grad_embed_ref[...]
    grad_proj = inverse_ref[:, :1] * (grads - embeds * jnp.sum(grads * embeds, axis=1, keepdims=True))
    grad_proj = grad_proj.astype(jnp.bfloat16)
    grad_proj_ref[...] = grad_proj
    grad_pooled = dot_nt(grad_proj, last_ref[0]) / length_ref[:, :1]
    grad_gains_ref[...] = jnp.zeros_like(grad_gains_ref)

    def begin(r, carry):
        rows = rows_at(r, 256)
        grad_out = lax.dot_general(
            pool_ref[:, rows], grad_pooled, (((0,), (0,)), ((), ())), precision=HIGHEST,
            preferred_element_type=jnp.float32,
        )
        through, gain = norm_back_rows(ending_ref[rows, :], gains_ref[2:3], grad_out)
        grad_gains_ref[2:3] += gain
        grad_middle_ref[rows, :] = through
        end_low[rows, :] = through.astype(jnp.bfloat16)
        end_turned[:, rows] = through.T.astype(jnp.bfloat16)
        middle_normed = norm_rows(middle_ref[rows, :], gains_ref[1:2])
        normed[rows, :] = middle_normed.astype(jnp.bfloat16)
        normed_turned[:, rows] = middle_normed.T.astype(jnp.bfloat16)
        return carry

    lax.fori_loop(0, tokens // 256, begin, 0)
    back[...] = jnp.zeros_like(back)
    wide = expand_ref.shape[1]
    step = 384

    def feed(c, carry):
        lanes = rows_at(c, step)
        pre = dot_nn(normed[...], expand_ref[:, lanes])
        grad_act = dot_nn(end_low[...], reduce_ref[:, lanes])
        turn = gelu_parts(pre)
        act = (0.5 * pre * (1.0 + turn)).astype(jnp.bfloat16)
        slope = 0.5 * (1.0 + turn) + 0.5 * pre * (1.0 - turn * turn) * GELU_IN * (1.0 + 3.0 * 0.044715 * pre * pre)
        grad_pre = (grad_act * slope).astype(jnp.bfloat16)
        grad_reduce_ref[:, lanes] = dot_nn(end_turned[...], act).astype(jnp.bfloat16)
        grad_expand_ref[:, lanes] = dot_nn(normed_turned[...], grad_pre).astype(jnp.bfloat16)
        back[...] += dot_nt(grad_pre, expand_ref[:, lanes])
        return carry

    lax.fori_loop(0, wide // step, feed, 0)

    def end(r, carry):
        rows = rows_at(r, 256)
        through, gain = norm_back_rows(middle_ref[rows, :], gains_ref[1:2], back[rows, :])
        grad_gains_ref[1:2] += gain
        grad_middle = grad_middle_ref[rows, :] + through
        grad_middle_ref[rows, :] = grad_middle
        grad_low_ref[rows, :] = grad_middle.astype(jnp.bfloat16)
        return carry

    lax.fori_loop(0, tokens // 256, end, 0)


def run_feed_back(grad_embed, embeds, inverse, pool, lengths, square, middle, ending, expand, reduce_turned, gains):
    tokens = middle.shape[0]
    seqs = pool.shape[0]
    low = jnp.bfloat16
    whole = pl.BlockSpec(memory_space=pltpu.VMEM)
    return pl.pallas_call(
        feed_back_kernel,
        grid=(1,),
        out_shape=[
            jax.ShapeDtypeStruct(expand.shape, low),
            jax.ShapeDtypeStruct(reduce_turned.shape, low),
            jax.ShapeDtypeStruct((tokens, D), jnp.float32),
            jax.ShapeDtypeStruct((tokens, D), low),
            jax.ShapeDtypeStruct((seqs, D), low),
            jax.ShapeDtypeStruct((8, D), jnp.float32),
        ],
        in_specs=[whole] * 5
        + [pl.BlockSpec((1, D, D), lambda i: (4, 0, 0))]
        + [whole] * 5,
        out_specs=[whole] * 6,
        scratch_shapes=[
            pltpu.VMEM((tokens, D), low),
            pltpu.VMEM((D, tokens), low),
            pltpu.VMEM((tokens, D), low),
            pltpu.VMEM((D, tokens), low),
            pltpu.VMEM((tokens, D), jnp.float32),
        ],
        compiler_params=pltpu.CompilerParams(vmem_limit_bytes=VMEM_CAP),
        name="feed_backward",
    )(grad_embed, embeds, inverse, pool, lengths, square, middle, ending, expand, reduce_turned, gains)


def attend_back_steps(
    grad_middle_ref, grad_low_ref, grad_proj_ref, pooled_ref, start_ref, query_ref, key_ref, value_ref, mixed_ref,
    square_ref, gains_ref, bias_ref, mask_ref, rank_ref,
    grad_square_ref, grad_score_ref, grad_gain_ref, grad_mixed, turned, grad_query, grad_key, grad_value,
    between, squares_done, put,
):
    tokens = start_ref.shape[0]
    big = 512
    grad_square_ref[4] = dot_tn(pooled_ref[...], grad_proj_ref[...]).astype(jnp.bfloat16)

    def begin(r, carry):
        rows = rows_at(r, big)
        grad_mixed[rows, :] = dot_nt(grad_low_ref[rows, :], square_ref[3]).astype(jnp.bfloat16)
        turned[:, rows] = mixed_ref[rows, :].astype(jnp.float32).T.astype(jnp.bfloat16)
        return carry

    lax.fori_loop(0, tokens // big, begin, 0)

    def outer(target, right_ref):
        def part(r, carry):
            rows = rows_at(r, 384)
            grad_square_ref[target, rows, :] = dot_nn(turned[rows, :], right_ref[...]).astype(jnp.bfloat16)
            return carry

        lax.fori_loop(0, D // 384, part, 0)

    outer(3, grad_low_ref)
    grad_score_ref[...] = jnp.zeros_like(grad_score_ref)

    def attend(t, carry):
        rows = rows_at(t, TILE)
        mask = tile_mask(mask_ref, t)
        for pair in range(PAIRS):
            lanes = pl.ds(pair * TILE, TILE)
            query, keys_here = query_ref[rows, lanes], key_ref[rows, lanes]
            probs = pair_probs(query, keys_here, pair_bias(bias_ref, pair), mask)
            grads = split_heads(grad_mixed[rows, lanes])
            grad_probs = dot_nt(grads, value_ref[rows, lanes])
            grad_value[rows, lanes] = dot_tn(probs.astype(jnp.bfloat16), grads).astype(jnp.bfloat16)
            inner = jnp.sum(grad_probs * probs, axis=1, keepdims=True)
            grad_scores = (probs * (grad_probs - inner)).astype(jnp.bfloat16)
            kept = grad_scores.astype(jnp.float32)
            grad_score_ref[2 * pair] += kept[:TILE]
            grad_score_ref[2 * pair + 1] += kept[TILE:]
            grad_query[rows, lanes] = (
                dot_nn(join_heads(grad_scores), split_heads(keys_here)) * HEAD ** (-0.5)
            ).astype(jnp.bfloat16)
            grad_key[rows, lanes] = (dot_tn(grad_scores, split_heads(query)) * HEAD ** (-0.5)).astype(jnp.bfloat16)
        return carry

    tiles = tokens // TILE
    done = 0
    for n, act in enumerate(between):
        until = ((n + 1) * tiles) // (len(between) + 1)
        if until > done:
            lax.fori_loop(done, until, attend, 0)
        done = until
        act()
    lax.fori_loop(done, tiles, attend, 0)

    def renorm(r, carry):
        rows = rows_at(r, 256)
        normed = norm_rows(start_ref[rows, :].astype(jnp.float32), gains_ref[0:1])
        turned[:, rows] = normed.T.astype(jnp.bfloat16)
        return carry

    lax.fori_loop(0, tokens // 256, renorm, 0)
    outer(0, grad_query)
    outer(1, grad_key)
    outer(2, grad_value)
    squares_done()
    grad_gain_ref[...] = jnp.zeros_like(grad_gain_ref)

    def end(r, carry):
        rows = rows_at(r, 256)
        grad_normed = (
            dot_nt(grad_query[rows, :], square_ref[0])
            + dot_nt(grad_key[rows, :], square_ref[1])
            + dot_nt(grad_value[rows, :], square_ref[2])
        )
        through, gain = norm_back_rows(start_ref[rows, :].astype(jnp.float32), gains_ref[0:1], grad_normed)
        grad_gain_ref[0:1] += gain
        turned[:, rows] = (grad_middle_ref[rows, :] + through).T.astype(jnp.bfloat16)
        return carry

    lax.fori_loop(0, tokens // 256, end, 0)

    def merge(r, carry):
        rows = rows_at(r, 384)
        total = jnp.zeros((384, tokens), jnp.float32)
        for c in range(tokens // 256):
            at = pl.ds(c * 256, 256)
            total = total + dot_nn(turned[rows, at], hot_rows(rank_ref, at, tokens))
        put(r, total)
        return carry

    lax.fori_loop(0, D // 384, merge, 0)


def attend_back_kernel(*refs):
    ins, rest = refs[:14], refs[14:]
    grad_square_ref, grad_score_ref, grad_gain_ref, send_ref = rest[:4]

    def put(r, total):
        send_ref[rows_at(r, 384), :] = total.astype(jnp.bfloat16)

    attend_back_steps(*ins, grad_square_ref, grad_score_ref, grad_gain_ref, *rest[4:], [], lambda: None, put)


def attend_scratch(tokens):
    low = jnp.bfloat16
    return [
        pltpu.VMEM((tokens, D), low),
        pltpu.VMEM((D, tokens), low),
        pltpu.VMEM((tokens, D), low),
        pltpu.VMEM((tokens, D), low),
        pltpu.VMEM((tokens, D), low),
    ]


def run_attend_back(*ins):
    tokens = ins[0].shape[0]
    low = jnp.bfloat16
    return pl.pallas_call(
        attend_back_kernel,
        out_shape=[
            jax.ShapeDtypeStruct((5, D, D), low),
            jax.ShapeDtypeStruct((HEADS, TILE, TILE), jnp.float32),
            jax.ShapeDtypeStruct((8, D), jnp.float32),
            jax.ShapeDtypeStruct((D, tokens), low),
        ],
        scratch_shapes=attend_scratch(tokens),
        compiler_params=pltpu.CompilerParams(vmem_limit_bytes=VMEM_CAP),
        name="attend_backward",
    )(*ins)


BACK_CAP = 62 * 1024 * 1024


def back_kernel(depth, *refs):
    ins, refs = refs[:14], refs[14:]
    grad_expand, grad_reduce = refs[:2]
    square_sum, expand_sum, reduce_sum, grad_score_ref, grad_gain_ref, returned = refs[2:8]
    grad_square, *steps = refs[8:14]
    blocks, spare, work_expand, work_reduce = refs[14:18]
    refs = refs[18:]
    feed_buffers, refs = refs[:10], refs[10:]
    feed_sems, refs = refs[:8], refs[8:]
    square_buffers, refs = refs[:5], refs[5:]
    square_sems, refs = refs[:8], refs[8:]
    part_send, part_got, part_own, end_send, end_got = refs
    dp_size, fsdp_size = lax.axis_size("dp"), lax.axis_size("fsdp")
    count = dp_size * fsdp_size
    me = lax.axis_index("dp") * fsdp_size + lax.axis_index("fsdp")
    greet_all(count, fsdp_size, me)
    grads = (grad_square, grad_expand, grad_reduce)
    outs = (square_sum, expand_sum, reduce_sum, spare)
    feed = Reduction(
        FEED_KINDS, depth, grads, outs, {EXPAND: work_expand, REDUCE: work_reduce}, feed_buffers, feed_sems
    )
    square = Reduction(SQUARE_KINDS, depth, grads, outs, None, square_buffers, square_sems)
    feed.begin()

    def relay(group):
        def act():
            for move, step in group:
                move(step)

        return act

    feats, half = blocks.shape[1] // 2, blocks.shape[2]

    def put(r, total):
        each = 384 // feats
        for p in range(each):
            part = total[p * feats : (p + 1) * feats]
            blocks[r * each + p] = jnp.concatenate([part[:, :half], part[:, half:]], axis=0).astype(jnp.bfloat16)

    attend_back_steps(
        *ins, grad_square, grad_score_ref, grad_gain_ref, *steps,
        [relay(group) for group in feed.groups()], square.begin, put,
    )

    def part_copy(k):
        target = lax.rem(me + k, count)
        return pltpu.make_async_remote_copy(
            src_ref=blocks.at[target],
            dst_ref=returned.at[me],
            send_sem=part_send.at[k],
            recv_sem=part_got.at[k],
            device_id=(target // fsdp_size, lax.rem(target, fsdp_size)),
            device_id_type=MESH,
        )

    def start_part(k, carry):
        part_copy(k).start()
        return carry

    lax.fori_loop(1, count, start_part, 0)
    own_part = pltpu.make_async_copy(blocks.at[me], returned.at[me], part_own)
    own_part.start()
    for group in square.groups():
        relay(group)()
    end_copy = remote(spare, square_sum.at[square.core], end_send, end_got, square.sibling)
    end_copy.start()
    feed.finish()
    square.finish()
    end_copy.wait_send()
    remote(spare, square_sum.at[1 - square.core], end_send, end_got, square.sibling).wait_recv()
    own_part.wait()

    def end_part(k, carry):
        part_copy(k).wait()
        return carry

    lax.fori_loop(1, count, end_part, 0)


def run_back(ins, grad_expand, grad_reduce, count, feats, call_id):
    depth = lax.axis_size("dp") // 2
    tokens = ins[0].shape[0]
    low = jnp.bfloat16
    blocks = (count, 2 * feats, tokens // 2)
    whole = pl.BlockSpec(memory_space=pltpu.VMEM)
    anywhere = pl.BlockSpec(memory_space=pl.ANY)
    feed_buffers, feed_sems = reduction_scratch(FEED_KINDS, depth)
    square_buffers, square_sems = reduction_scratch(SQUARE_KINDS, depth)
    return pl.pallas_call(
        functools.partial(back_kernel, depth),
        out_shape=[
            jax.ShapeDtypeStruct((2, 5, 48, 192), jnp.float32),
            jax.ShapeDtypeStruct((96, 768), jnp.float32),
            jax.ShapeDtypeStruct((192, 384), jnp.float32),
            jax.ShapeDtypeStruct((HEADS, TILE, TILE), jnp.float32),
            jax.ShapeDtypeStruct((8, D), jnp.float32),
            jax.ShapeDtypeStruct(blocks, low),
        ],
        in_specs=[whole] * 14 + [anywhere] * 2,
        out_specs=[whole] * 5 + [anywhere],
        scratch_shapes=[pltpu.VMEM((5, D, D), low)]
        + attend_scratch(tokens)
        + [
            pltpu.VMEM(blocks, low),
            pltpu.VMEM((5, 48, 192), jnp.float32),
            pltpu.VMEM((2 * depth, 2) + BLOCKS[EXPAND], low),
            pltpu.VMEM((2 * depth, 2) + BLOCKS[REDUCE], low),
        ]
        + feed_buffers
        + feed_sems
        + square_buffers
        + square_sems
        + [
            pltpu.SemaphoreType.DMA((count,)),
            pltpu.SemaphoreType.DMA((count,)),
            pltpu.SemaphoreType.DMA,
            pltpu.SemaphoreType.DMA,
            pltpu.SemaphoreType.DMA,
        ],
        compiler_params=pltpu.CompilerParams(
            collective_id=call_id, has_side_effects=True, vmem_limit_bytes=BACK_CAP
        ),
        name="back",
    )(*ins, grad_expand, grad_reduce)


def loss_kernel(
    query_rows, nli_rows, embeds_ref, negative_ref, scale_ref, grad_ref, stats_ref, everyone, grad_sims, turned_sims,
    send, got, hand_send, hand_got,
):
    dp_size, fsdp_size = lax.axis_size("dp"), lax.axis_size("fsdp")
    count = dp_size * fsdp_size
    chips = count // 2
    slots = embeds_ref.shape[0]
    dp, fsdp = lax.axis_index("dp"), lax.axis_index("fsdp")
    me = dp * fsdp_size + fsdp
    core = lax.rem(fsdp, 2)
    chip = me // 2
    sibling = (dp, fsdp + 1 - 2 * core)
    greet_all(count, fsdp_size, me)

    def device(number):
        return (number // fsdp_size, lax.rem(number, fsdp_size))

    def across(k):
        target = lax.rem(chip + k, chips) * 2 + core
        return remote(embeds_ref, everyone.at[me], send.at[k], got.at[k], device(target))

    def hand(k, of):
        source = lax.rem(chip + chips - k, chips) * 2 + of
        return remote(everyone.at[source], everyone.at[source], hand_send.at[k], hand_got.at[k], sibling)

    def start(k, carry):
        across(k).start()
        return carry

    def relay(k, carry):
        across(k).wait_recv()
        hand(k, core).start()
        return carry

    def end(k, carry):
        across(k).wait_send()
        hand(k, core).wait_send()
        hand(k, 1 - core).wait_recv()
        return carry

    first = remote(embeds_ref, everyone.at[me], hand_send.at[0], hand_got.at[0], sibling)
    first.start()
    everyone[me] = embeds_ref[...]
    lax.fori_loop(1, chips, start, 0)
    lax.fori_loop(1, chips, relay, 0)
    lax.fori_loop(1, chips, end, 0)
    first.wait_send()
    hand(0, 1 - core).wait_recv()

    total_rows = count * slots
    embeds = everyone[...].reshape(total_rows, D)
    scale = jnp.exp(scale_ref[...])
    sims = dot_nt(embeds, embeds)
    row = lax.broadcasted_iota(jnp.int32, sims.shape, 0)
    col = lax.broadcasted_iota(jnp.int32, sims.shape, 1)
    row_slot, col_slot = row & (slots - 1), col & (slots - 1)
    hypo, answer = query_rows + nli_rows, query_rows + 2 * nli_rows
    is_query = row_slot < query_rows
    is_premise = (row_slot >= query_rows) & (row_slot < hypo)
    is_hypo = (col_slot >= hypo) & (col_slot < answer)
    is_answer = (col_slot >= answer) & (col_slot < answer + query_rows)
    allowed = (is_query & is_answer) | (is_premise & is_hypo)
    target = (is_query & (col == row + answer)) | (is_premise & (col == row + nli_rows))
    target = jnp.where(target, 1.0, 0.0)
    logits = scale * sims
    shown = jnp.where(allowed, logits, -1e30)
    row_top = jnp.max(shown, axis=1, keepdims=True)
    weight = jnp.where(negative_ref[:, :1] == col, 2.0, 1.0)
    raised = jnp.where(allowed, weight * jnp.exp(shown - row_top), 0.0)
    left = is_query | is_premise
    row_total = jnp.where(left[:, :1], jnp.sum(raised, axis=1, keepdims=True), 1.0)
    hits = jnp.sum(jnp.where(target > 0.0, logits, 0.0), axis=1, keepdims=True)
    losses = jnp.where(left[:, :1], row_top + jnp.log(row_total), 0.0) - hits
    first_loss = jnp.sum(jnp.where(is_query[:, :1], losses, 0.0), keepdims=True)
    second_loss = jnp.sum(jnp.where(is_premise[:, :1], losses, 0.0), keepdims=True)
    grad_logits = raised / row_total - target
    grad_scale = scale * jnp.sum(grad_logits * sims, keepdims=True)
    lane = lax.broadcasted_iota(jnp.int32, stats_ref.shape, 1)
    stats_ref[...] = jnp.where(lane == 0, first_loss, jnp.where(lane == 1, second_loss, grad_scale))
    grads = scale * grad_logits
    grad_sims[...] = grads
    turned_sims[...] = grads.T
    own = pl.ds(pl.multiple_of(me * slots, 8), slots)
    grad_ref[...] = dot_nn(grad_sims[own, :].astype(jnp.bfloat16), embeds) + dot_nn(
        turned_sims[own, :].astype(jnp.bfloat16), embeds
    )


def run_loss(embeds, negative, log_scale, query_rows, nli_rows, call_id):
    count = lax.axis_size("dp") * lax.axis_size("fsdp")
    slots = embeds.shape[0]
    square = (count * slots, count * slots)
    chips = count // 2
    return pl.pallas_call(
        functools.partial(loss_kernel, query_rows, nli_rows),
        out_shape=[jax.ShapeDtypeStruct((slots, D), jnp.float32), jax.ShapeDtypeStruct((8, LANES), jnp.float32)],
        scratch_shapes=[
            pltpu.VMEM((count, slots, D), jnp.bfloat16),
            pltpu.VMEM(square, jnp.float32),
            pltpu.VMEM(square, jnp.float32),
            pltpu.SemaphoreType.DMA((chips,)),
            pltpu.SemaphoreType.DMA((chips,)),
            pltpu.SemaphoreType.DMA((chips,)),
            pltpu.SemaphoreType.DMA((chips,)),
        ],
        compiler_params=pltpu.CompilerParams(
            collective_id=call_id, has_side_effects=True, vmem_limit_bytes=VMEM_CAP
        ),
        name="loss",
    )(embeds, negative, log_scale)


def shards(
    embed_table,
    square_weights,
    expand_weight,
    reduce_weight,
    norm_gains,
    position_bias,
    log_scale,
    table_moment,
    table_second,
    square_moment,
    square_second,
    expand_moment,
    expand_second,
    reduce_moment,
    reduce_second,
    gains_moment,
    gains_second,
    position_moment,
    position_second,
    scale_moment,
    scale_second,
    query_tokens,
    answer_tokens,
    query_length,
    answer_length,
    premise_tokens,
    hypothesis_tokens,
    hard_negative,
):
    both = ("dp", "fsdp")
    dp_size, fsdp_size = lax.axis_size("dp"), lax.axis_size("fsdp")
    count = dp_size * fsdp_size
    direct = dp_size == 8 and fsdp_size == 4
    position = lax.axis_index(both)
    feats, vocab_size = embed_table.shape
    feats_pad = up8(feats)
    fold = fold_rows(vocab_size)
    query_rows = query_tokens.shape[0]
    nli_rows = premise_tokens.shape[0]
    short_length = query_tokens.shape[1]
    long_length = answer_tokens.shape[1]
    short_tokens = jnp.concatenate([query_tokens, premise_tokens, hypothesis_tokens], axis=0)
    lengths = jnp.concatenate(
        [query_length, jnp.full((2 * nli_rows,), short_length, jnp.int32), answer_length]
    )
    all_tokens = jnp.concatenate([short_tokens.reshape(-1), answer_tokens.reshape(-1)])
    token_count = all_tokens.shape[0]
    hypo_start = query_rows + nli_rows
    answer_start = query_rows + 2 * nli_rows
    seq_count = answer_start + query_rows
    seq_pad = -(-seq_count // 16) * 16
    split_at = short_tokens.shape[0] * short_length

    packed, rank = token_keys(all_tokens, fold)
    key_rows = token_count // LANES
    info = jnp.concatenate(
        [
            packed.reshape(key_rows, LANES),
            jnp.pad(hard_negative, (0, LANES - nli_rows)).reshape(1, LANES),
            jnp.zeros((7, LANES), jnp.int32),
        ],
        axis=0,
    )
    own_gains = jnp.pad(norm_gains, ((0, 5), (0, LANES - feats)))
    square_low = square_weights.astype(jnp.bfloat16)
    expand_low = expand_weight.astype(jnp.bfloat16)
    reduce_low = reduce_weight.astype(jnp.bfloat16).T
    half = token_count // 2
    if direct:
        square_pieces = square_low.reshape(5, 2, 48, 192).transpose(1, 0, 2, 3)
        found, square_all, info_all, gains_all = run_front(
            info, own_gains, token_count, embed_table, square_pieces, 1
        )
    else:
        info_all = exchange(info[None], True, 0, "share_keys")
        gains_all = exchange(own_gains[None], True, 6, "share_gains")

        def whole(piece, row_name, column_name):
            axis = piece.ndim - 2
            wide = lax.all_gather(piece, column_name, axis=axis + 1, tiled=True)
            return lax.all_gather(wide, row_name, axis=axis, tiled=True)

        square_all = whole(square_low, "dp", "fsdp")
        expand_all = whole(expand_low, "dp", "fsdp")
        reduce_all = whole(reduce_low, "fsdp", "dp")
        padded = jnp.pad(embed_table, ((0, feats_pad - feats), (0, 0)))
        key_all = info_all[:, :key_rows].reshape(count, 1, token_count)
        found = exchange(lookup(padded, key_all >> 2, key_all & 3), False, 8, "send_features")
        found = found.reshape(count, 2, feats_pad, half)[:, :, :feats]
        found = found.transpose(1, 0, 2, 3).reshape(1, 2 * D, half)
    packed_all = info_all[:, :key_rows].reshape(count, 1, token_count)
    row_all, group_all = packed_all >> 2, packed_all & 3
    negative_all = info_all[:, key_rows, :nli_rows]
    gains = gains_all[:, :3, :feats].transpose(1, 0, 2).reshape(3, D)
    gains = jnp.pad(gains.astype(jnp.bfloat16).astype(jnp.float32), ((0, 5), (0, 0)))

    sequence = np.concatenate(
        [
            np.repeat(np.arange(answer_start), short_length),
            answer_start + np.repeat(np.arange(query_rows), long_length),
        ]
    )
    inside = np.concatenate(
        [
            np.tile(np.arange(short_length), answer_start),
            np.tile(np.arange(long_length), query_rows),
        ]
    )
    lengths_pad = jnp.pad(lengths, (0, seq_pad - seq_count), constant_values=1)
    pool = (sequence[None, :] == np.arange(seq_pad)[:, None]) & (inside[None, :] < lengths_pad[:, None])
    token_ok = jnp.any(pool, axis=0).reshape(-1, 1, TILE)
    sequence_tiles = sequence.reshape(-1, TILE)
    together = sequence_tiles[:, :, None] == sequence_tiles[:, None, :]
    mask = jnp.where(together & token_ok, 0.0, -1e30).astype(jnp.float32)
    pool = pool.astype(jnp.float32)
    length_rows = jnp.broadcast_to(lengths_pad.astype(jnp.float32)[:, None], (seq_pad, LANES))
    rank_rows = jnp.broadcast_to(rank[:, None], (token_count, LANES))
    bias, onehot = attention_bias(position_bias, TILE)

    forward_ins = (found, rank_rows, square_all, gains, bias, mask, pool, length_rows)
    if direct:
        *forward_all, expand_all, reduce_all = run_relayed_forward(forward_ins, expand_low, reduce_low, 2)
    else:
        forward_all = run_forward(forward_ins, expand_all, reduce_all)
    (start, queries, keys_here, values_here, mixed, middle, ending, embeds_low, pooled, embeds, inverse) = forward_all
    if direct:
        negative_place = (negative_all // nli_rows) * seq_pad + hypo_start + negative_all % nli_rows
        negative_place = jnp.pad(
            negative_place, ((0, 0), (query_rows, seq_pad - hypo_start)), constant_values=-1
        )
        negative_place = jnp.broadcast_to(negative_place.reshape(-1, 1), (count * seq_pad, LANES))
        grad_embeds, stats = run_loss(
            embeds_low, negative_place, log_scale.reshape(1, 1), query_rows, nli_rows, 3
        )
        losses, grad_scale = stats[0, :2], stats[0, 2:3]
    else:
        gathered = exchange(embeds_low[None], True, 3, "share_embeds")
        queries_all = gathered[:, :query_rows].reshape(-1, D)
        premises_all = gathered[:, query_rows:hypo_start].reshape(-1, D)
        hypotheses_all = gathered[:, hypo_start:answer_start].reshape(-1, D)
        answers_all = gathered[:, answer_start:seq_count].reshape(-1, D)
        scale = jnp.exp(log_scale[0])

        def contrast(left, right, extra, own):
            sims = product_right(left, right)
            logits = scale * sims
            row_top = jnp.max(logits, axis=1, keepdims=True)
            raised = (1.0 + extra) * jnp.exp(logits - row_top)
            row_total = jnp.sum(raised, axis=1, keepdims=True)
            spread = row_top[:, 0] + jnp.log(row_total[:, 0])
            target_hit = jnp.eye(left.shape[0], dtype=jnp.float32)
            loss_sum = jnp.sum(spread - jnp.sum(target_hit * logits, axis=1))
            grad_logits = raised / row_total - target_hit
            grad_scale = jnp.sum(grad_logits * sims)
            grad_sims = (scale * grad_logits).astype(jnp.bfloat16)
            mine_left = lax.dynamic_slice_in_dim(grad_sims, position * own, own, 0)
            mine_right = lax.dynamic_slice_in_dim(grad_sims, position * own, own, 1)
            return (loss_sum, grad_scale, product(mine_left, right), product_left(mine_right, left))

        first_loss, first_dscale, grad_queries, grad_answers = contrast(
            queries_all, answers_all, 0.0, query_rows
        )
        negatives = (jnp.arange(hypotheses_all.shape[0])[None, :] == negative_all.reshape(-1)[:, None]).astype(
            jnp.float32
        )
        second_loss, second_dscale, grad_premises, grad_hypotheses = contrast(
            premises_all, hypotheses_all, negatives, nli_rows
        )
        grad_embeds = jnp.concatenate(
            [
                grad_queries,
                grad_premises,
                grad_hypotheses,
                grad_answers,
                jnp.zeros((seq_pad - seq_count, D), jnp.float32),
            ],
            axis=0,
        )
        losses = jnp.stack([first_loss, second_loss])
        grad_scale = ((first_dscale + second_dscale) * scale).reshape(1)
    (grad_expand, grad_reduce, grad_middle, grad_middle_low, grad_proj, late_gains) = run_feed_back(
        grad_embeds, embeds, inverse, pool, length_rows, square_all, middle, ending, expand_all, reduce_all, gains
    )
    back_ins = (
        grad_middle, grad_middle_low, grad_proj, pooled, start, queries, keys_here, values_here, mixed, square_all,
        gains, bias, mask, rank_rows,
    )
    if direct:
        (square_sum, expand_sum, reduce_sum, grad_scores, first_gain, returned) = run_back(
            back_ins, grad_expand, grad_reduce, count, feats, 5
        )
        square_sum = square_sum.transpose(1, 0, 2, 3).reshape(5, 96, 192)
    else:

        def shard(gradient, row_name, column_name):
            axis = gradient.ndim - 2
            part = lax.psum_scatter(
                gradient.astype(jnp.float32), row_name, scatter_dimension=axis, tiled=True
            )
            return lax.psum_scatter(part, column_name, scatter_dimension=axis + 1, tiled=True)

        (grad_square, grad_scores, first_gain, merged) = run_attend_back(*back_ins)
        square_sum = shard(grad_square, "dp", "fsdp")
        expand_sum = shard(grad_expand, "dp", "fsdp")
        reduce_sum = shard(grad_reduce, "fsdp", "dp")
        merged = merged.reshape(count, feats, 2, half).transpose(0, 2, 1, 3)
        if feats_pad > feats:
            merged = jnp.pad(merged, ((0, 0), (0, 0), (0, feats_pad - feats), (0, 0)))
        returned = exchange(merged.reshape(count, 2 * feats_pad, half), False, 4, "send_gradients")
    grad_table = scatter(returned, row_all, group_all, vocab_size)[:feats]
    grad_gains = jnp.concatenate([first_gain[:1], late_gains[1:3]], axis=0)
    grad_position = lax.dot_general(
        onehot, grad_scores.reshape(HEADS, TILE * TILE), (((0,), (1,)), ((), ())), precision=HIGHEST
    )
    reduced = (square_sum, expand_sum, reduce_sum.T)
    local_square = (
        jnp.sum(reduced[0] * reduced[0])
        + jnp.sum(reduced[1] * reduced[1])
        + jnp.sum(reduce_sum * reduce_sum)
        + jnp.sum(grad_table * grad_table)
    )
    small = jnp.concatenate([grad_gains.reshape(-1), grad_position.reshape(-1), local_square.reshape(1)])
    small_rows = -(-small.shape[0] // (8 * LANES)) * 8
    small = jnp.pad(small, (0, small_rows * LANES - small.shape[0])).reshape(1, small_rows, LANES)
    summed = jnp.sum(exchange(small, True, 7, "share_small"), axis=0).reshape(-1)
    gains_total = summed[: 3 * D].reshape(3, D)
    position_total = summed[3 * D : 3 * D + BUCKETS * HEADS].reshape(BUCKETS, HEADS)
    square_total = summed[3 * D + BUCKETS * HEADS]
    scale_total = grad_scale
    grad_gain_shard = lax.dynamic_slice_in_dim(gains_total, position * feats, feats, 1)
    gradient_norm = jnp.sqrt(
        square_total
        + jnp.sum(gains_total * gains_total)
        + jnp.sum(position_total * position_total)
        + jnp.sum(scale_total * scale_total)
    )
    factor = jnp.minimum(1.0, CLIP_NORM / gradient_norm)
    table_out = adam_update(embed_table, table_moment, table_second, grad_table, factor, TABLE_RATE)
    square_out = adam_update(
        square_weights, square_moment, square_second, reduced[0], factor, LEARN_RATE
    )
    expand_out = adam_update(
        expand_weight, expand_moment, expand_second, reduced[1], factor, LEARN_RATE
    )
    reduce_out = adam_update(
        reduce_weight, reduce_moment, reduce_second, reduced[2], factor, LEARN_RATE
    )
    gains_out = adam_update(
        norm_gains, gains_moment, gains_second, grad_gain_shard, factor, SMALL_RATE
    )
    position_out = adam_update(
        position_bias, position_moment, position_second, position_total, factor, SMALL_RATE
    )
    scale_out = adam_update(log_scale, scale_moment, scale_second, scale_total, factor, SMALL_RATE)
    return (
        *table_out,
        *square_out,
        *expand_out,
        *reduce_out,
        *gains_out,
        *position_out,
        *scale_out,
        losses,
        gradient_norm,
    )


def solution(mesh):
    return jax.shard_map(
        shards,
        mesh=mesh,
        in_specs=(
            P(("dp", "fsdp"), None),
            P(None, "dp", "fsdp"),
            P("dp", "fsdp"),
            P("dp", "fsdp"),
            P(None, ("dp", "fsdp")),
            P(),
            P(),
            P(("dp", "fsdp"), None),
            P(("dp", "fsdp"), None),
            P(None, "dp", "fsdp"),
            P(None, "dp", "fsdp"),
            P("dp", "fsdp"),
            P("dp", "fsdp"),
            P("dp", "fsdp"),
            P("dp", "fsdp"),
            P(None, ("dp", "fsdp")),
            P(None, ("dp", "fsdp")),
            P(),
            P(),
            P(),
            P(),
            P(("dp", "fsdp"), None),
            P(("dp", "fsdp"), None),
            P(("dp", "fsdp")),
            P(("dp", "fsdp")),
            P(("dp", "fsdp"), None),
            P(("dp", "fsdp"), None),
            P(("dp", "fsdp")),
        ),
        out_specs=(
            P(("dp", "fsdp"), None),
            P(("dp", "fsdp"), None),
            P(("dp", "fsdp"), None),
            P(None, "dp", "fsdp"),
            P(None, "dp", "fsdp"),
            P(None, "dp", "fsdp"),
            P("dp", "fsdp"),
            P("dp", "fsdp"),
            P("dp", "fsdp"),
            P("dp", "fsdp"),
            P("dp", "fsdp"),
            P("dp", "fsdp"),
            P(None, ("dp", "fsdp")),
            P(None, ("dp", "fsdp")),
            P(None, ("dp", "fsdp")),
            P(),
            P(),
            P(),
            P(),
            P(),
            P(),
            P(),
            P(),
        ),
        check_vma=False,
    )
```

```python
import functools

import jax
import jax.numpy as jnp
import numpy as np
from jax import lax
from jax.experimental import pallas as pl
from jax.experimental.pallas import tpu as pltpu
from jax.sharding import PartitionSpec as P

D = 768
HEADS = 12
HEAD = 64
BUCKETS = 32
MAXDIST = 128
STEP = 10


HIGHEST = lax.Precision.HIGHEST
NORM_EPS = 1e-06
LEARN_RATE = 0.03
TABLE_RATE = 0.4
SMALL_RATE = 0.5
BETA_ONE = 0.9
BETA_TWO = 0.999
ADAM_EPS = 1e-08
WEIGHT_DECAY = 0.01
CLIP_NORM = 0.5


def bucket_table(length):
    places = np.arange(length)
    offset = places[None, :] - places[:, None]
    half_count = BUCKETS // 2
    exact_count = half_count // 2
    upper = (offset > 0).astype(np.int64) * half_count
    distance = np.abs(offset)
    far_bucket = exact_count + (
        np.log(np.maximum(distance, 1) / exact_count)
        / np.log(MAXDIST / exact_count)
        * (half_count - exact_count)
    ).astype(np.int64)
    far_bucket = np.minimum(far_bucket, half_count - 1)
    return (upper + np.where(distance < exact_count, distance, far_bucket)).astype(np.int32)


def bucket_onehot(length):
    flat_table = bucket_table(length).reshape(-1)
    return jnp.asarray((flat_table[:, None] == np.arange(BUCKETS)[None, :]).astype(np.float32))


def product(left, right):
    return jnp.dot(left, right, preferred_element_type=jnp.float32)


def product_left(left, right):
    return lax.dot_general(
        left, right, (((0,), (0,)), ((), ())), preferred_element_type=jnp.float32
    )


def product_right(left, right):
    return lax.dot_general(
        left, right, (((1,), (1,)), ((), ())), preferred_element_type=jnp.float32
    )


def attention_bias(position_bias, length):
    onehot = bucket_onehot(length)
    flat_bias = jnp.dot(onehot, position_bias, precision=HIGHEST)
    return (jnp.transpose(flat_bias.reshape(length, length, HEADS), (2, 0, 1)), onehot)


def adam_update(weight, moment, second, grad, factor, rate):
    clipped = grad * factor
    moment_new = BETA_ONE * moment + (1 - BETA_ONE) * clipped
    second_new = BETA_TWO * second + (1 - BETA_TWO) * clipped * clipped
    moment_hat = moment_new / (1 - BETA_ONE**STEP)
    second_hat = second_new / (1 - BETA_TWO**STEP)
    updated = weight - rate * (
        moment_hat / (jnp.sqrt(second_hat) + ADAM_EPS) + WEIGHT_DECAY * weight
    )
    return (moment_new, second_new, updated)


LANES = 128
GROUPS = 4
SLOT = LANES // GROUPS
VMEM_CAP = 56 * 1024 * 1024

def fold_rows(vocab):
    per = -(-vocab // GROUPS)
    return -(-per // LANES) * LANES

def up8(n):
    return -(-n // 8) * 8

def eye():
    r = lax.broadcasted_iota(jnp.int32, (LANES, LANES), 0)
    c = lax.broadcasted_iota(jnp.int32, (LANES, LANES), 1)
    return (r == c).astype(jnp.float32).astype(jnp.bfloat16)

def turn_table(fold, table_ref, turned):
    feats, vocab = table_ref.shape
    pad = jnp.zeros((SLOT - feats, LANES), jnp.float32)

    def build(b, carry):
        parts = []
        for j in range(GROUPS):
            start = jnp.minimum(j * fold + b * LANES, vocab - LANES)
            start = pl.multiple_of(start, LANES)
            parts += [table_ref[:, pl.ds(start, LANES)], pad]
        tile = jnp.concatenate(parts, axis=0).astype(jnp.bfloat16).astype(jnp.float32)
        turned[pl.ds(pl.multiple_of(b * LANES, LANES), LANES), :] = tile.T
        return carry

    lax.fori_loop(0, fold // LANES, build, 0)
    turned[pl.ds(fold, 8), :] = jnp.zeros((8, LANES), jnp.float32)


def pick_group(rows, group, feats):
    tokens = rows.shape[0]
    wide = dot_nt(eye(), rows[...].astype(jnp.bfloat16))
    total = jnp.where(group == 0, wide[:SLOT], 0.0)
    for j in range(1, GROUPS):
        total = total + jnp.where(group == j, wide[j * SLOT : (j + 1) * SLOT], 0.0)
    half = tokens // 2
    return jnp.concatenate([total[:feats, :half], total[:feats, half:]], axis=0).astype(jnp.bfloat16)


def look_up(row_ref, group_ref, source, turned, rows, feats):
    tokens = rows.shape[0]
    batch = 32

    def fetch(b, carry):
        for k in range(batch):
            t = b * batch + k
            rows[pl.ds(t, 1), :] = turned[pl.ds(row_ref[source, t], 1), :]
        return carry

    lax.fori_loop(0, tokens // batch, fetch, 0)
    return pick_group(rows, group_ref[source], feats)


def lookup_kernel(fold, row_ref, group_ref, table_ref, out_ref, turned, rows):
    @pl.when(pl.program_id(0) == 0)
    def _():
        turn_table(fold, table_ref, turned)

    out_ref[0] = look_up(row_ref, group_ref, 0, turned, rows, table_ref.shape[0])


def lookup(table, rows_idx, groups_idx):
    feats, vocab = table.shape
    n, tokens = rows_idx.shape[0], rows_idx.shape[2]
    fold = fold_rows(vocab)
    return pl.pallas_call(
        functools.partial(lookup_kernel, fold),
        grid=(n,),
        out_shape=jax.ShapeDtypeStruct((n, 2 * feats, tokens // 2), jnp.bfloat16),
        in_specs=[
            pl.BlockSpec((None, 1, tokens), lambda s: (s, 0, 0), memory_space=pltpu.SMEM),
            pl.BlockSpec((1, 1, tokens), lambda s: (s, 0, 0)),
            pl.BlockSpec((feats, vocab), lambda s: (0, 0)),
        ],
        out_specs=pl.BlockSpec((1, 2 * feats, tokens // 2), lambda s: (s, 0, 0)),
        scratch_shapes=[pltpu.VMEM((fold + 8, LANES), jnp.float32), pltpu.VMEM((tokens, LANES), jnp.float32)],
        compiler_params=pltpu.CompilerParams(vmem_limit_bytes=VMEM_CAP),
        name="lookup",
    )(rows_idx, groups_idx, table)

def scatter_kernel(fold, row_ref, group_ref, grad_ref, out_ref, squares_ref, total, rows):
    feats, vocab = out_ref.shape
    tokens = rows.shape[0]
    step = pl.program_id(0)
    @pl.when(step == 0)
    def _():
        def clear(b, _):
            total[pl.ds(pl.multiple_of(b * LANES, LANES), LANES), :] = jnp.zeros((LANES, LANES), jnp.float32)
            return 0
        lax.fori_loop(0, fold // LANES, clear, 0)
        total[pl.ds(fold, 8), :] = jnp.zeros((8, LANES), jnp.float32)
    flat = []
    for half in range(2):
        block = grad_ref[half, 0].astype(jnp.float32)
        flat += [block[:feats], block[feats:]]
    flat = jnp.concatenate(flat, axis=1)
    group = group_ref[0]
    pad = jnp.zeros((SLOT - feats, tokens), jnp.float32)
    parts = []
    for j in range(GROUPS):
        parts += [jnp.where(group == j, flat, 0.0), pad]
    rows[...] = jnp.concatenate(parts, axis=0).T
    lines = tokens // LANES
    ways = 32 // lines
    per = LANES // ways
    for half in range(2):
        for l in range(per):
            spots = [(r, l + per * w) for r in range(half * lines // 2, (half + 1) * lines // 2) for w in range(ways)]
            at = [row_ref[r, c] for r, c in spots]
            new = [
                total[pl.ds(at[n], 1), :] + rows[pl.ds(r * LANES + c, 1), :] for n, (r, c) in enumerate(spots)
            ]
            for n in range(len(spots)):
                total[pl.ds(at[n], 1), :] = new[n]

    @pl.when(step == pl.num_programs(0) - 1)
    def _():
        whole = (vocab - (GROUPS - 1) * fold) // LANES
        def turn(b, squares):
            tile = total[pl.ds(pl.multiple_of(b * LANES, LANES), LANES), :].T
            for j in range(GROUPS):
                out_ref[:, pl.ds(pl.multiple_of(j * fold + b * LANES, LANES), LANES)] = tile[j * SLOT : j * SLOT + feats]
            return squares + tile * tile

        squares = lax.fori_loop(0, whole, turn, jnp.zeros((LANES, LANES), jnp.float32))
        for b in range(whole, fold // LANES):
            tile = total[pl.ds(b * LANES, LANES), :].T
            for j in range(GROUPS - 1):
                out_ref[:, pl.ds(j * fold + b * LANES, LANES)] = tile[j * SLOT : j * SLOT + feats]
            squares = squares + tile * tile
        squares_ref[...] = jnp.sum(squares.reshape(LANES // 8, 8, LANES), axis=0)


def scatter(grads, rows_idx, groups_idx, vocab):
    n, tokens = rows_idx.shape[0], rows_idx.shape[2]
    feats = grads.shape[2] // 2
    fold = fold_rows(vocab)
    return pl.pallas_call(
        functools.partial(scatter_kernel, fold),
        grid=(n,),
        out_shape=[jax.ShapeDtypeStruct((feats, vocab), jnp.float32), jax.ShapeDtypeStruct((8, LANES), jnp.float32)],
        in_specs=[
            pl.BlockSpec((tokens // LANES, LANES), lambda s: (s, 0), memory_space=pltpu.SMEM),
            pl.BlockSpec((1, 1, tokens), lambda s: (s, 0, 0)),
            pl.BlockSpec((2, 1, 2 * feats, tokens // 4), lambda s: (0, s, 0, 0)),
        ],
        out_specs=[pl.BlockSpec((feats, vocab), lambda s: (0, 0)), pl.BlockSpec((8, LANES), lambda s: (0, 0))],
        scratch_shapes=[pltpu.VMEM((fold + 8, LANES), jnp.float32), pltpu.VMEM((tokens, LANES), jnp.float32)],
        compiler_params=pltpu.CompilerParams(vmem_limit_bytes=VMEM_CAP),
        name="scatter",
    )(rows_idx.reshape(-1, LANES), groups_idx, grads)

def token_keys(tokens, fold):
    count = tokens.shape[0]
    key = (tokens % fold) * GROUPS + tokens // fold
    places = jnp.arange(count, dtype=jnp.int32)
    half = count // 2
    together = (places[:, None] < half) == (places[None, :] < half)
    same_before = together & (key[:, None] == key[None, :]) & (places[:, None] < places[None, :])
    first = ~jnp.any(same_before, axis=0)
    rank = jnp.sum((together & (key[None, :] < key[:, None]) & first[None, :]).astype(jnp.int32), axis=1)
    rank = rank + jnp.where(places < half, 0, half)
    hit = (rank[:, None] == places[None, :]) & first[:, None]
    packed = GROUPS * fold + jnp.sum(jnp.where(hit, key[:, None] - GROUPS * fold, 0), axis=0)
    return packed, rank


MESH = pl.DeviceIdType.MESH


def greet_all(count, cols, me):
    barrier = pltpu.get_barrier_semaphore()

    def greet(k, carry):
        to = lax.rem(me + k, count)
        pl.semaphore_signal(barrier, inc=1, device_id=(to // cols, lax.rem(to, cols)), device_id_type=MESH)
        return carry

    lax.fori_loop(1, count, greet, 0)
    pl.semaphore_wait(barrier, count - 1)


def exchange_kernel(same, src, dst, send_sem, recv_sem, own_sem):
    rows, cols = lax.axis_size("dp"), lax.axis_size("fsdp")
    count = rows * cols
    me = lax.axis_index("dp") * cols + lax.axis_index("fsdp")
    barrier = pltpu.get_barrier_semaphore()

    def device(k):
        to = lax.rem(me + k, count)
        return (to // cols, lax.rem(to, cols))

    def greet(k, carry):
        pl.semaphore_signal(barrier, inc=1, device_id=device(k), device_id_type=MESH)
        return carry

    def copy(k):
        to = lax.rem(me + k, count)
        return pltpu.make_async_remote_copy(
            src_ref=src.at[0 if same else to],
            dst_ref=dst.at[me],
            send_sem=send_sem.at[k],
            recv_sem=recv_sem.at[k],
            device_id=device(k),
            device_id_type=MESH,
        )

    def start(k, carry):
        copy(k).start()
        return carry

    def end(k, carry):
        copy(k).wait()
        return carry

    lax.fori_loop(1, count, greet, 0)
    own = pltpu.make_async_copy(src.at[0 if same else me], dst.at[me], own_sem)
    own.start()
    pl.semaphore_wait(barrier, count - 1)
    lax.fori_loop(1, count, start, 0)
    own.wait()
    lax.fori_loop(1, count, end, 0)


def exchange(blocks, same, call_id, name):
    count = lax.axis_size("dp") * lax.axis_size("fsdp")
    return pl.pallas_call(
        functools.partial(exchange_kernel, same),
        out_shape=jax.ShapeDtypeStruct((count,) + blocks.shape[1:], blocks.dtype),
        in_specs=[pl.BlockSpec(memory_space=pl.ANY)],
        out_specs=pl.BlockSpec(memory_space=pl.ANY),
        scratch_shapes=[
            pltpu.SemaphoreType.DMA((count,)),
            pltpu.SemaphoreType.DMA((count,)),
            pltpu.SemaphoreType.DMA,
        ],
        compiler_params=pltpu.CompilerParams(collective_id=call_id, has_side_effects=True),
        name=name,
    )(blocks)


SQUARE, EXPAND, REDUCE, EARLY, LATE = range(5)
STEPS = (5, 6, 4, 2, 3)
FIRST = (3, 3, 2, 1, 2)
SPANS = {SQUARE: (0, 5), EARLY: (3, 2), LATE: (0, 3)}


def spot(refs, kind, z, x, y, core):
    dp = z * 2 + x
    column = y * 2 + core
    if kind in SPANS:
        return refs[SQUARE].at[
            pl.ds(*SPANS[kind]),
            pl.ds(pl.multiple_of(dp * 96 + core * 48, 16), 48),
            pl.ds(pl.multiple_of(y * 384, 128), 384),
        ]
    if kind == EXPAND:
        return refs[kind].at[
            pl.ds(pl.multiple_of(dp * 96, 16), 96), pl.ds(pl.multiple_of(column * 768, 128), 768)
        ]
    return refs[kind].at[
        pl.ds(pl.multiple_of(column * 192, 16), 192), pl.ds(pl.multiple_of(dp * 384, 128), 384)
    ]


def spot_part(refs, kind, z, x, y, core, part):
    dp = z * 2 + x
    column = y * 2 + core
    if kind == SQUARE:
        return refs[kind].at[
            pl.ds(0, 3) if part == 0 else pl.ds(3, 2),
            pl.ds(pl.multiple_of(dp * 96 + core * 48, 16), 48),
            pl.ds(pl.multiple_of(y * 384, 128), 384),
        ]
    if kind == EXPAND:
        return refs[kind].at[
            pl.ds(pl.multiple_of(dp * 96 + part * 48, 16), 48),
            pl.ds(pl.multiple_of(column * 768, 128), 768),
        ]
    return refs[kind].at[
        pl.ds(pl.multiple_of(column * 192 + part * 96, 16), 96),
        pl.ds(pl.multiple_of(dp * 384, 128), 384),
    ]


def block_step(ref, kind, k):
    if kind in SPANS:
        return ref.at[k]
    rows = 16 if kind == EXPAND else 48
    return ref.at[pl.ds(pl.multiple_of(k * rows, 16), rows)]


BLOCKS = ((5, 48, 384), (96, 768), (192, 384), (2, 48, 384), (3, 48, 384))


def place():
    dp, fsdp = lax.axis_index("dp"), lax.axis_index("fsdp")
    return dp // 2, lax.rem(dp, 2), fsdp // 2, lax.rem(fsdp, 2)


def device_at(z, x, y, core):
    return (z * 2 + x, y * 2 + core)


def greet_neighbours(depth):
    z, x, y, core = place()
    barrier = pltpu.get_barrier_semaphore()

    def hello(target):
        pl.semaphore_signal(barrier, inc=1, device_id=target, device_id_type=MESH)

    hello(device_at(z, x, y, 1 - core))
    hello(device_at(z, 1 - x, y, core))
    hello(device_at(z, x, 1 - y, core))

    @pl.when(z > 0)
    def _():
        hello(device_at(z - 1, x, y, core))

    @pl.when(z < depth - 1)
    def _():
        hello(device_at(z + 1, x, y, core))

    above = jnp.where(z < depth - 1, 1, 0)
    below = jnp.where(z > 0, 1, 0)
    pl.semaphore_wait(barrier, 3 + above + below)


def remote(src, dst, send_sem, recv_sem, target):
    return pltpu.make_async_remote_copy(
        src_ref=src, dst_ref=dst, send_sem=send_sem, recv_sem=recv_sem,
        device_id=target, device_id_type=MESH)


class Gather:
    def __init__(self, kinds, depth, sources, outs, sems):
        self.kinds, self.depth, self.sources, self.outs = kinds, depth, sources, outs
        self.own_sem, self.send, self.got, self.sib_send, self.sib_got, self.diag_got = sems
        self.number = {a: n for n, a in enumerate(kinds)}
        z, x, y, core = place()
        self.z, self.x, self.y, self.core = z, x, y, core
        self.sibling = device_at(z, x, y, 1 - core)
        self.x_next, self.y_next = device_at(z, 1 - x, y, core), device_at(z, x, 1 - y, core)

    def to(self, way, a, z_at, x_at, y_at, target, part=None, src=None):
        n, k = self.number[a], (z_at * 2 + x_at) * 2 + y_at
        if part is None:
            spot_at, recv = spot(self.outs, a, z_at, x_at, y_at, self.core), self.got.at[n, k]
        else:
            spot_at = spot_part(self.outs, a, z_at, x_at, y_at, self.core, part)
            recv = self.diag_got.at[n, z_at, part]
        return remote(spot_at if src is None else src, spot_at, self.send.at[way, n, k], recv, target)

    def to_sibling(self, a, z_at, x_at, y_at, src=None, core=None):
        spot_at = spot(self.outs, a, z_at, x_at, y_at, self.core if core is None else core)
        n, k = self.number[a], (z_at * 2 + x_at) * 2 + y_at
        return remote(
            spot_at if src is None else src, spot_at, self.sib_send.at[n, k], self.sib_got.at[n, k], self.sibling
        )

    def own_copy(self, a):
        return pltpu.make_async_copy(
            self.sources[a], spot(self.outs, a, self.z, self.x, self.y, self.core), self.own_sem.at[self.number[a]]
        )

    def begin(self, kinds):
        z, x, y, core = self.z, self.x, self.y, self.core
        for a in kinds:
            source = self.sources[a]
            self.own_copy(a).start()

            @pl.when(z < self.depth - 1)
            def _():
                self.to(0, a, z, x, y, device_at(z + 1, x, y, core), src=source).start()

            @pl.when(z > 0)
            def _():
                self.to(1, a, z, x, y, device_at(z - 1, x, y, core), src=source).start()

            self.to(2, a, z, x, y, self.x_next, src=source).start()
            self.to(3, a, z, x, y, self.y_next, src=source).start()
            self.to_sibling(a, z, x, y, src=source).start()

    def sides(self, step, act):
        if step == 0:
            act(self.z)
            return
        for sign in (1, -1):
            z_at = self.z + sign * step

            @pl.when((z_at >= 0) & (z_at < self.depth))
            def _():
                act(z_at)

    def first(self, step):
        z, x, y, core = self.z, self.x, self.y, self.core

        def act(z_at):
            for a in self.kinds:
                self.to(0, a, z_at, x, y, self.sibling).wait_recv()

                @pl.when((z_at < z) & (z < self.depth - 1))
                def _():
                    self.to(0, a, z_at, x, y, device_at(z + 1, x, y, core)).start()

                @pl.when((z_at > z) & (z > 0))
                def _():
                    self.to(1, a, z_at, x, y, device_at(z - 1, x, y, core)).start()

                self.to(2, a, z_at, x, y, self.x_next).start()
                self.to(3, a, z_at, x, y, self.y_next).start()
                self.to_sibling(a, z_at, x, y).start()

        self.sides(step, act)

    def second(self, step):
        x, y = self.x, self.y

        def act(z_at):
            for a in self.kinds:
                self.to(0, a, z_at, 1 - x, y, self.sibling).wait_recv()
                self.to(3, a, z_at, 1 - x, y, self.y_next, 0).start()
                self.to_sibling(a, z_at, 1 - x, y).start()
                self.to(0, a, z_at, x, 1 - y, self.sibling).wait_recv()
                self.to(2, a, z_at, x, 1 - y, self.x_next, 1).start()
                self.to_sibling(a, z_at, x, 1 - y).start()

        self.sides(step, act)

    def third(self, step):
        x, y = self.x, self.y

        def act(z_at):
            for a in self.kinds:
                for part in range(2):
                    self.to(0, a, z_at, 1 - x, 1 - y, self.sibling, part).wait_recv()
                self.to_sibling(a, z_at, 1 - x, 1 - y).start()

        self.sides(step, act)

    def relays(self):
        for step in range(1, self.depth + 2):
            if step < self.depth:
                yield functools.partial(self.first, step)
            if 0 <= step - 1 < self.depth:
                yield functools.partial(self.second, step - 1)
            if 0 <= step - 2 < self.depth:
                yield functools.partial(self.third, step - 2)

    def arrive(self):
        for a in self.kinds:
            self.own_copy(a).wait()

        def wait(z_at, carry):
            for a in self.kinds:
                for x_at in range(2):
                    for y_at in range(2):
                        self.to_sibling(a, z_at, x_at, y_at, core=1 - self.core).wait_recv()
            return carry

        lax.fori_loop(0, self.depth, wait, 0)

    def finish(self):
        z, x, y = self.z, self.x, self.y

        def wait(z_at, carry):
            for a in self.kinds:

                @pl.when((z_at <= z) & (z < self.depth - 1))
                def _():
                    self.to(0, a, z_at, x, y, self.x_next).wait_send()

                @pl.when((z_at >= z) & (z > 0))
                def _():
                    self.to(1, a, z_at, x, y, self.x_next).wait_send()

                self.to(2, a, z_at, x, y, self.x_next).wait_send()
                self.to(3, a, z_at, x, y, self.y_next).wait_send()
                self.to(3, a, z_at, 1 - x, y, self.y_next, 0).wait_send()
                self.to(2, a, z_at, x, 1 - y, self.x_next, 1).wait_send()
                for x_at in range(2):
                    for y_at in range(2):
                        self.to_sibling(a, z_at, x_at, y_at).wait_send()
            return carry

        lax.fori_loop(0, self.depth, wait, 0)


def gather_sems(kinds, depth):
    count, spots = len(kinds), 4 * depth
    return [
        pltpu.SemaphoreType.DMA((count,)),
        pltpu.SemaphoreType.DMA((4, count, spots)),
        pltpu.SemaphoreType.DMA((count, spots)),
        pltpu.SemaphoreType.DMA((count, spots)),
        pltpu.SemaphoreType.DMA((count, spots)),
        pltpu.SemaphoreType.DMA((count, depth, 2)),
    ]


BY_Y = (EXPAND, EARLY)
FIRST_KINDS = (EXPAND, REDUCE, EARLY)
LAST_KINDS = (LATE,)
FRONT_KINDS = (SQUARE, EXPAND)
LATER_KINDS = (REDUCE,)


def front_kernel(fold, depth, keys_ref, gains_ref, table_ref, square_in, expand_in, *refs):
    found, square_out, expand_out, keys_all, gains_all = refs[:5]
    refs = refs[1:]
    theirs, own, turned, rows, blocks, row_low, row_all = refs[4:11]
    gather_sem, refs = refs[11:17], refs[17:]
    pair_send, pair_recv, part_send, part_got, part_own, keys_send, keys_got, gains_send, gains_got, near_sem = refs
    dp_size, fsdp_size = lax.axis_size("dp"), lax.axis_size("fsdp")
    count = dp_size * fsdp_size
    me = lax.axis_index("dp") * fsdp_size + lax.axis_index("fsdp")
    z, x, y, core = place()
    sibling = device_at(z, x, y, 1 - core)
    greet_all(count, fsdp_size, me)

    def info_copies(k):
        target = lax.rem(me + k, count)
        device = (target // fsdp_size, lax.rem(target, fsdp_size))
        return (
            remote(keys_ref, keys_all.at[me], keys_send.at[k], keys_got.at[k], device),
            remote(gains_ref, gains_all.at[me], gains_send.at[k], gains_got.at[k], device),
        )

    def start_info(k, carry):
        for copy in info_copies(k):
            copy.start()
        return carry

    lax.fori_loop(1, count, start_info, 0)
    keys_all[me] = keys_ref[...]
    gains_all[me] = gains_ref[...]
    pair = remote(square_in.at[1 - core], theirs, pair_send, pair_recv, sibling)
    pair.start()
    gather = Gather(
        FRONT_KINDS, depth, {SQUARE: own, EXPAND: expand_in}, {SQUARE: square_out, EXPAND: expand_out}, gather_sem
    )
    gather.begin((EXPAND,))
    row = lax.broadcasted_iota(jnp.int32, (192, 384), 0)
    col = lax.broadcasted_iota(jnp.int32, (192, 384), 1)
    here = (row + core * 192 == col).astype(jnp.float32).astype(jnp.bfloat16)
    there = (row + (1 - core) * 192 == col).astype(jnp.float32).astype(jnp.bfloat16)
    pair.wait_recv()
    for k in range(5):
        block = jnp.dot(square_in[core, k], here, preferred_element_type=jnp.float32) + jnp.dot(
            theirs[k], there, preferred_element_type=jnp.float32
        )
        own[k] = block.astype(jnp.bfloat16)
    gather.begin((SQUARE,))
    turn_table(fold, table_ref, turned)

    def end_info(k, carry):
        for copy in info_copies(k):
            copy.wait()
        return carry

    lax.fori_loop(1, count, end_info, 0)
    key_rows = row_low.shape[0] // count

    def split_row(k, carry):
        row_low[pl.ds(pl.multiple_of(k * key_rows, 8), key_rows)] = keys_all[k, :key_rows] >> 2
        return carry

    lax.fori_loop(0, count, split_row, 0)
    near = pltpu.make_async_copy(row_low, row_all, near_sem)
    near.start()
    near.wait()

    def find(target):
        keys = keys_all[target]
        group = jnp.concatenate([keys[r : r + 1] for r in range(key_rows)], axis=1) & 3

        def fetch(r, carry):
            line = target * key_rows + r
            start = pl.multiple_of(r * LANES, LANES)
            for k in range(LANES):
                rows[pl.ds(start + k, 1), :] = turned[pl.ds(row_all[line, k], 1), :]
            return carry

        lax.fori_loop(0, key_rows, fetch, 0)
        return pick_group(rows, group, table_ref.shape[0])

    def part_copy(k):
        target = lax.rem(me + k, count)
        device = (target // fsdp_size, lax.rem(target, fsdp_size))
        return remote(blocks.at[target], found.at[me], part_send.at[k], part_got.at[k], device)

    def serve(k, carry):
        target = lax.rem(me + k, count)
        blocks[target] = find(target)
        part_copy(k).start()
        return carry

    relays = list(gather.relays())
    done = 1
    for n, relay in enumerate(relays):
        until = 1 + ((n + 1) * (count - 1)) // len(relays)
        lax.fori_loop(done, until, serve, 0)
        done = until
        relay()
    blocks[me] = find(me)
    own_part = pltpu.make_async_copy(blocks.at[me], found.at[me], part_own)
    own_part.start()
    pair.wait_send()
    gather.arrive()
    gather.finish()
    own_part.wait()

    def end_part(k, carry):
        part_copy(k).wait()
        return carry

    lax.fori_loop(1, count, end_part, 0)


def run_front(keys, gains, tokens, table, square, expand, call_id):
    depth = lax.axis_size("dp") // 2
    count = lax.axis_size("dp") * lax.axis_size("fsdp")
    feats, vocab = table.shape
    fold = fold_rows(vocab)
    blocks = (count, 2 * feats, tokens // 2)
    whole = pl.BlockSpec(memory_space=pltpu.VMEM)
    anywhere = pl.BlockSpec(memory_space=pl.ANY)
    many = pltpu.SemaphoreType.DMA((count,))
    return pl.pallas_call(
        functools.partial(front_kernel, fold, depth),
        out_shape=[
            jax.ShapeDtypeStruct(blocks, jnp.bfloat16),
            jax.ShapeDtypeStruct((5, 768, 768), jnp.bfloat16),
            jax.ShapeDtypeStruct((768, 3072), jnp.bfloat16),
            jax.ShapeDtypeStruct((count,) + keys.shape, keys.dtype),
            jax.ShapeDtypeStruct((count,) + gains.shape, gains.dtype),
        ],
        in_specs=[whole] * 5,
        out_specs=[anywhere] * 3 + [whole] * 2,
        scratch_shapes=[
            pltpu.VMEM((5, 48, 192), jnp.bfloat16),
            pltpu.VMEM((5, 48, 384), jnp.bfloat16),
            pltpu.VMEM((fold + 8, LANES), jnp.float32),
            pltpu.VMEM((tokens, LANES), jnp.float32),
            pltpu.VMEM(blocks, jnp.bfloat16),
            pltpu.VMEM((count * tokens // LANES, LANES), jnp.int32),
            pltpu.SMEM((count * tokens // LANES, LANES), jnp.int32),
        ]
        + gather_sems(FRONT_KINDS, depth)
        + [pltpu.SemaphoreType.DMA, pltpu.SemaphoreType.DMA]
        + [many, many, pltpu.SemaphoreType.DMA]
        + [many] * 4
        + [pltpu.SemaphoreType.DMA],
        compiler_params=pltpu.CompilerParams(
            collective_id=call_id, has_side_effects=True, vmem_limit_bytes=VMEM_CAP
        ),
        name="front",
    )(keys, gains, table, square, expand)


class Reduction:
    def __init__(self, kinds, depth, grads, outs, work, buffers, sems):
        self.kinds, self.depth, self.grads, self.outs, self.own_work = kinds, depth, grads, outs, work
        count = len(kinds)
        self.paired, self.step_one, self.from_x, self.from_y, self.from_z = [
            dict(zip(kinds, buffers[k * count : (k + 1) * count])) for k in range(5)
        ]
        self.load_sem, self.pair_send, self.pair_got, self.send, self.one_got = sems[:5]
        self.x_got, self.y_got, self.z_got = sems[5:8]
        self.number = {a: n for n, a in enumerate(kinds)}
        z, x, y, core = place()
        self.z, self.x, self.y, self.core = z, x, y, core
        self.sibling = device_at(z, x, y, 1 - core)
        self.x_next, self.y_next = device_at(z, 1 - x, y, core), device_at(z, x, 1 - y, core)

    def piece(self, ref, a, z_at, x_at, y_at):
        i = z_at * 2 + x_at
        if a == EXPAND:
            return ref.at[y_at, pl.ds(pl.multiple_of(i * 96, 16), 96)]
        if a == REDUCE:
            return ref.at[y_at, :, pl.ds(pl.multiple_of(i * 384, 128), 384)]
        return ref.at[i, :, :, pl.ds(pl.multiple_of(y_at * 384, 128), 384)]

    def work(self, a, z_at, x_at, y_at):
        if a in SPANS:
            return spot(self.grads, a, z_at, x_at, y_at, self.core)
        return self.piece(self.own_work[a], a, z_at, x_at, y_at)

    def half(self, a, y_at, core):
        column = y_at * 2 + core
        if a == EXPAND:
            return self.grads[a].at[:, pl.ds(pl.multiple_of(column * 768, 128), 768)]
        return self.grads[a].at[pl.ds(pl.multiple_of(column * 192, 16), 192)]

    def load(self, a, y_at):
        return pltpu.make_async_copy(
            self.half(a, y_at, self.core), self.own_work[a].at[y_at], self.load_sem.at[self.number[a], y_at]
        )

    def pair(self, a, at):
        n = self.number[a]
        if a in SPANS:
            source = self.grads[SQUARE].at[
                pl.ds(*SPANS[a]), pl.ds(pl.multiple_of(at * 96 + (1 - self.core) * 48, 16), 48)
            ]
        else:
            source = self.half(a, at, 1 - self.core)
        return remote(source, self.paired[a].at[at], self.pair_send.at[n, at], self.pair_got.at[n, at], self.sibling)

    def each_pair(self, a, act):
        if a not in SPANS:
            act(1 - self.y)
            act(self.y)
            return

        def one(i, carry):
            act(i)
            return carry

        lax.fori_loop(0, 2 * self.depth, one, 0)

    def sides(self, step, act):
        if step == 0:
            act(self.z)
            return
        for sign in (1, -1):
            z_at = self.z + sign * step

            @pl.when((z_at >= 0) & (z_at < self.depth))
            def _():
                act(z_at)

    def begin(self, kinds):
        for a in kinds:

            def start(at):
                if a not in SPANS:
                    self.load(a, at).start()
                self.pair(a, at).start()

            self.each_pair(a, start)

    def ready(self, last):
        for a in self.kinds:
            if a in SPANS:
                if not last:
                    self.each_pair(a, lambda at: self.pair(a, at).wait_recv())
            else:
                y_at = self.y if last else 1 - self.y
                self.load(a, y_at).wait()
                self.pair(a, y_at).wait_recv()

    def total(self, a, z_at, x_at, y_at, extra=()):
        here = self.work(a, z_at, x_at, y_at)
        paired = self.piece(self.paired[a], a, z_at, x_at, y_at)

        value = here[...] + paired[...]
        for buffer in extra:
            value = value + buffer[...]
        here[...] = value

    def diag_copy(self, a, z_at):
        n = self.number[a]
        return remote(
            self.work(a, z_at, 1 - self.x, 1 - self.y),
            self.step_one[a].at[z_at],
            self.send.at[0, n, z_at],
            self.one_got.at[n, z_at],
            self.y_next if a in BY_Y else self.x_next,
        )

    def diag(self, step):
        def act(z_at):
            for a in self.kinds:
                self.total(a, z_at, 1 - self.x, 1 - self.y)
                self.diag_copy(a, z_at).start()

        if step == self.depth - 1:
            self.ready(False)
        self.sides(step, act)

    def x_copy(self, a, z_at):
        n = self.number[a]
        return remote(
            self.work(a, z_at, 1 - self.x, self.y),
            self.from_x[a].at[z_at],
            self.send.at[2, n, z_at],
            self.x_got.at[n, z_at],
            self.x_next,
        )

    def y_copy(self, a, z_at):
        n = self.number[a]
        return remote(
            self.work(a, z_at, self.x, 1 - self.y),
            self.from_y[a].at[z_at],
            self.send.at[3, n, z_at],
            self.y_got.at[n, z_at],
            self.y_next,
        )

    def columns(self, step):
        x, y = self.x, self.y

        def act(z_at):
            for a in self.kinds:
                received = [self.step_one[a].at[z_at]]
                self.diag_copy(a, z_at).wait_recv()
                self.total(a, z_at, 1 - x, y, received if a in BY_Y else ())
                self.x_copy(a, z_at).start()
                self.total(a, z_at, x, 1 - y, () if a in BY_Y else received)
                self.y_copy(a, z_at).start()

        if step == self.depth - 1:
            self.ready(True)
        self.sides(step, act)

    def z_copy(self, a, z_at, side, target):
        n = self.number[a]
        return remote(
            self.work(a, z_at, self.x, self.y),
            self.from_z[a].at[side, z_at],
            self.send.at[4, n, z_at],
            self.z_got.at[n, side, z_at],
            target,
        )

    def line(self, step, keep=None):
        z, x, y, core, depth = self.z, self.x, self.y, self.core, self.depth

        def act(z_at):
            for a in self.kinds:
                self.x_copy(a, z_at).wait_recv()
                self.y_copy(a, z_at).wait_recv()
                across = [self.from_x[a].at[z_at], self.from_y[a].at[z_at]]
                if step > 0:
                    upward = z_at > z
                    before = (upward & (z > 0)) | (jnp.logical_not(upward) & (z < depth - 1))
                    side = jnp.where(upward, 0, 1)

                    @pl.when(before)
                    def _():
                        self.z_copy(a, z_at, side, self.sibling).wait_recv()
                        self.total(a, z_at, x, y, across + [self.from_z[a].at[side, z_at]])

                    @pl.when(jnp.logical_not(before))
                    def _():
                        self.total(a, z_at, x, y, across)

                    @pl.when(upward)
                    def _():
                        self.z_copy(a, z_at, 0, device_at(z + 1, x, y, core)).start()

                    @pl.when(jnp.logical_not(upward))
                    def _():
                        self.z_copy(a, z_at, 1, device_at(z - 1, x, y, core)).start()
                else:
                    for side in range(2):
                        present = (z > 0) if side == 0 else (z < depth - 1)

                        @pl.when(present)
                        def _():
                            self.z_copy(a, z, side, self.sibling).wait_recv()

                        @pl.when(jnp.logical_not(present))
                        def _():
                            self.from_z[a][side, z] = jnp.zeros(BLOCKS[a], jnp.bfloat16)

                    here, paired = self.work(a, z, x, y), self.piece(self.paired[a], a, z, x, y)

                    def finish(k, carry):
                        value = block_step(here, a, k)[...].astype(jnp.float32)
                        for buffer in [paired] + across + [self.from_z[a].at[0, z], self.from_z[a].at[1, z]]:
                            value = value + block_step(buffer, a, k)[...].astype(jnp.float32)
                        if a in SPANS:
                            spare, at = self.outs[3], k + SPANS[a][0]
                            low, high = value[:, :192], pltpu.roll(value, 192, 1)[:, :192]
                            self.outs[SQUARE][core, at] = jnp.where(core == 0, low, high)
                            spare[at] = jnp.where(core == 0, high, low)
                        else:
                            block_step(self.outs[a], a, k)[...] = value
                        return carry

                    lax.fori_loop(0, STEPS[a], finish, 0)

        self.sides(step, act)

    def groups(self):
        rounds = list(range(self.depth - 1, -1, -1))
        for k in range(self.depth + 2):
            group = []
            if k < self.depth:
                group.append((self.diag, rounds[k]))
            if 0 <= k - 1 < self.depth:
                group.append((self.columns, rounds[k - 1]))
            if 0 <= k - 2 < self.depth:
                group.append((self.line, rounds[k - 2]))
            yield group

    def finish(self):
        def wait(z_at, carry):
            for a in self.kinds:
                self.diag_copy(a, z_at).wait_send()
                self.x_copy(a, z_at).wait_send()
                self.y_copy(a, z_at).wait_send()

                @pl.when(z_at != self.z)
                def _():
                    self.z_copy(a, z_at, 0, self.sibling).wait_send()
            return carry

        lax.fori_loop(0, self.depth, wait, 0)
        for a in self.kinds:
            self.each_pair(a, lambda at: self.pair(a, at).wait_send())


def pair_shape(a, depth):
    if a == EXPAND:
        return (2, depth * 192, 768)
    if a == REDUCE:
        return (2, 192, depth * 768)
    return (2 * depth, SPANS[a][1], 48, 768)


def reduction_scratch(kinds, depth):
    def buffers(*lead):
        return [pltpu.VMEM(lead + BLOCKS[a], jnp.bfloat16) for a in kinds]

    count = len(kinds)
    spots = pltpu.SemaphoreType.DMA((count, 2 * depth))
    return (
        [pltpu.VMEM(pair_shape(a, depth), jnp.bfloat16) for a in kinds]
        + buffers(depth) + buffers(depth) + buffers(depth) + buffers(2, depth),
        [
            spots,
            spots,
            spots,
            pltpu.SemaphoreType.DMA((5, count, depth)),
            pltpu.SemaphoreType.DMA((count, depth)),
            pltpu.SemaphoreType.DMA((count, depth)),
            pltpu.SemaphoreType.DMA((count, depth)),
            pltpu.SemaphoreType.DMA((count, 2, depth)),
        ],
    )


TILE = 128
PAIRS = HEADS // 2
GELU_IN = (2.0 / np.pi) ** 0.5


def dot_nn(left, right):
    return jnp.dot(left, right, preferred_element_type=jnp.float32)


def dot_nt(left, right):
    return lax.dot_general(left, right, (((1,), (1,)), ((), ())), preferred_element_type=jnp.float32)


def dot_tn(left, right):
    return lax.dot_general(left, right, (((0,), (0,)), ((), ())), preferred_element_type=jnp.float32)


def rows_at(index, size):
    return pl.ds(pl.multiple_of(index * size, size), size)


def split_heads(block):
    low = lax.broadcasted_iota(jnp.int32, block.shape, 1) < HEAD
    wide = block.astype(jnp.float32)
    first = jnp.where(low, wide, 0.0).astype(jnp.bfloat16)
    second = jnp.where(low, 0.0, wide).astype(jnp.bfloat16)
    return jnp.concatenate([first, second], axis=0)


def join_heads(stacked):
    return jnp.concatenate([stacked[:TILE], stacked[TILE:]], axis=1)


def pair_probs(query, keys_here, bias, mask):
    scores = dot_nt(split_heads(query), keys_here) * HEAD ** (-0.5) + bias
    scores = scores + mask
    raised = jnp.exp(scores - jnp.max(scores, axis=1, keepdims=True))
    return raised / jnp.sum(raised, axis=1, keepdims=True)


def pair_bias(bias_ref, pair):
    return jnp.concatenate([bias_ref[2 * pair], bias_ref[2 * pair + 1]], axis=0)


def tile_mask(mask_ref, tile):
    mask = mask_ref[tile]
    return jnp.concatenate([mask, mask], axis=0)


def hot_rows(rank_ref, rows, slots, first=0):
    place = lax.broadcasted_iota(jnp.int32, (rows.size, slots), 1) + first
    return (rank_ref[rows, :1] == place).astype(jnp.float32).astype(jnp.bfloat16)


def norm_rows(values, gain):
    scale = lax.rsqrt(jnp.mean(values * values, axis=1, keepdims=True) + NORM_EPS)
    return values * scale * gain


def gelu_parts(pre):
    inner = GELU_IN * (pre + 0.044715 * pre * pre * pre)
    return jnp.tanh(inner)


def forward_steps(
    found_ref, rank_ref, square_ref, gains_ref, bias_ref, mask_ref, pool_ref, length_ref,
    start_ref, query_ref, key_ref, value_ref, mixed_ref, middle_ref, ending_ref, low_ref, pooled_ref, embed_ref,
    inverse_ref, normed, pooled_sum, wide_found, low_found, expand_ref, reduce_ref, between, before_feed,
):
    between = list(between)

    def relay(count):
        for _ in range(min(count, len(between))):
            between.pop(0)()

    tokens = start_ref.shape[0]
    big = 512
    feats, half = found_ref.shape[1] // 2, found_ref.shape[2]

    def assemble(p, carry):
        block = found_ref[p].astype(jnp.float32)
        at = pl.ds(pl.multiple_of(p * feats, 8), feats)
        wide_found[at, :half] = block[:feats]
        wide_found[at, half:] = block[feats:]
        return carry

    lax.fori_loop(0, found_ref.shape[0], assemble, 0)
    low_found[...] = wide_found[...].astype(jnp.bfloat16)

    def begin(r, carry):
        rows = rows_at(r, 256)
        start = dot_nt(hot_rows(rank_ref, rows, tokens), low_found[...])
        start_ref[rows, :] = start.astype(jnp.bfloat16)
        normed[rows, :] = norm_rows(start, gains_ref[0:1]).astype(jnp.bfloat16)
        return carry

    lax.fori_loop(0, tokens // 256, begin, 0)
    relay(1)
    for k, target in enumerate((query_ref, key_ref, value_ref)):

        def project(r, carry):
            rows = rows_at(r, big)
            target[rows, :] = dot_nn(normed[rows, :], square_ref[k]).astype(jnp.bfloat16)
            return carry

        lax.fori_loop(0, tokens // big, project, 0)
        relay(1)

    def attend(t, carry):
        rows = rows_at(t, TILE)
        mask = tile_mask(mask_ref, t)
        for pair in range(PAIRS):
            lanes = pl.ds(pair * TILE, TILE)
            probs = pair_probs(query_ref[rows, lanes], key_ref[rows, lanes], pair_bias(bias_ref, pair), mask)
            mixed = dot_nn(join_heads(probs).astype(jnp.bfloat16), split_heads(value_ref[rows, lanes]))
            mixed_ref[rows, lanes] = mixed.astype(jnp.bfloat16)
        return carry

    tiles = tokens // TILE
    if between:
        for t in range(tiles):
            lax.fori_loop(t, t + 1, attend, 0)
            relay(1)
    else:
        lax.fori_loop(0, tiles, attend, 0)

    def merge(r, carry):
        rows = rows_at(r, big)
        middle = start_ref[rows, :].astype(jnp.float32) + dot_nn(mixed_ref[rows, :], square_ref[3])
        middle_ref[rows, :] = middle
        ending_ref[rows, :] = middle
        normed[rows, :] = norm_rows(middle, gains_ref[1:2]).astype(jnp.bfloat16)
        return carry

    lax.fori_loop(0, tokens // big, merge, 0)
    relay(len(between))
    before_feed()
    wide = expand_ref.shape[1]

    def feed(c, carry):
        lanes = rows_at(c, D)

        def rows_of(r, inner):
            rows = rows_at(r, big)
            pre = dot_nn(normed[rows, :], expand_ref[:, lanes])
            act = (0.5 * pre * (1.0 + gelu_parts(pre))).astype(jnp.bfloat16)
            ending_ref[rows, :] += dot_nt(act, reduce_ref[:, lanes])
            return inner

        return lax.fori_loop(0, tokens // big, rows_of, carry)

    lax.fori_loop(0, wide // D, feed, 0)
    pooled_sum[...] = jnp.zeros_like(pooled_sum)

    def pool(r, carry):
        rows = rows_at(r, 256)
        output = norm_rows(ending_ref[rows, :], gains_ref[2:3])
        pooled_sum[...] += jnp.dot(
            pool_ref[:, rows], output, precision=HIGHEST, preferred_element_type=jnp.float32
        )
        return carry

    lax.fori_loop(0, tokens // 256, pool, 0)
    pooled = (pooled_sum[...] / length_ref[:, :1]).astype(jnp.bfloat16)
    pooled_ref[...] = pooled
    projected = dot_nn(pooled, square_ref[4])
    inverse = lax.rsqrt(jnp.sum(projected * projected, axis=1, keepdims=True) + NORM_EPS)
    embeds = projected * inverse
    embed_ref[...] = embeds
    low_ref[...] = embeds.astype(jnp.bfloat16)
    inverse_ref[...] = jnp.broadcast_to(inverse, inverse_ref.shape)


def forward_kernel(*refs):
    ins, expand_ref, reduce_ref, rest = refs[:8], refs[8], refs[9], refs[10:]
    forward_steps(*ins, *rest, expand_ref, reduce_ref, [], lambda: None)


def relayed_forward_kernel(depth, *refs):
    ins, expand_ref, reduce_in = refs[:8], refs[8], refs[9]
    outs, reduce_out = refs[10:21], refs[21]
    steps, reduce_all = refs[22:26], refs[26]
    sems, save_sem = refs[27:33], refs[33]
    greet_neighbours(depth)
    gather = Gather(LATER_KINDS, depth, {REDUCE: reduce_in}, {REDUCE: reduce_all}, sems)
    gather.begin(LATER_KINDS)
    save = pltpu.make_async_copy(reduce_all, reduce_out, save_sem)

    def before_feed():
        gather.arrive()
        save.start()

    forward_steps(*ins, *outs, *steps, expand_ref, reduce_all, gather.relays(), before_feed)
    gather.finish()
    save.wait()


def forward_outs(tokens, seqs):
    flat = jax.ShapeDtypeStruct((tokens, D), jnp.bfloat16)
    full = jax.ShapeDtypeStruct((tokens, D), jnp.float32)
    few = jax.ShapeDtypeStruct((seqs, D), jnp.bfloat16)
    return [
        flat, flat, flat, flat, flat, full, full, few, few,
        jax.ShapeDtypeStruct((seqs, D), jnp.float32),
        jax.ShapeDtypeStruct((seqs, LANES), jnp.float32),
    ]


def forward_scratch(tokens, seqs):
    return [
        pltpu.VMEM((tokens, D), jnp.bfloat16),
        pltpu.VMEM((seqs, D), jnp.float32),
        pltpu.VMEM((D, tokens), jnp.float32),
        pltpu.VMEM((D, tokens), jnp.bfloat16),
    ]


def run_forward(ins, expand, reduce_turned):
    tokens, seqs = ins[1].shape[0], ins[6].shape[0]
    return pl.pallas_call(
        forward_kernel,
        out_shape=forward_outs(tokens, seqs),
        scratch_shapes=forward_scratch(tokens, seqs),
        compiler_params=pltpu.CompilerParams(vmem_limit_bytes=VMEM_CAP),
        name="layer_forward",
    )(*ins, expand, reduce_turned)


def run_relayed_forward(ins, expand, reduce_piece, call_id):
    depth = lax.axis_size("dp") // 2
    tokens, seqs = ins[1].shape[0], ins[6].shape[0]
    weight = (768, 3072)
    outs = forward_outs(tokens, seqs)
    whole = pl.BlockSpec(memory_space=pltpu.VMEM)
    anywhere = pl.BlockSpec(memory_space=pl.ANY)
    return pl.pallas_call(
        functools.partial(relayed_forward_kernel, depth),
        out_shape=outs + [jax.ShapeDtypeStruct(weight, jnp.bfloat16)],
        in_specs=[whole] * (len(ins) + 2),
        out_specs=[whole] * len(outs) + [anywhere],
        scratch_shapes=forward_scratch(tokens, seqs)
        + [pltpu.VMEM(weight, jnp.bfloat16)]
        + gather_sems(LATER_KINDS, depth)
        + [pltpu.SemaphoreType.DMA],
        compiler_params=pltpu.CompilerParams(
            collective_id=call_id, has_side_effects=True, vmem_limit_bytes=VMEM_CAP
        ),
        name="layer_forward",
    )(*ins, expand, reduce_piece)


def norm_back_rows(values, gain, grad):
    scale = lax.rsqrt(jnp.mean(values * values, axis=1, keepdims=True) + NORM_EPS)
    weighted = grad * gain
    inner = jnp.mean(weighted * values, axis=1, keepdims=True)
    through = scale * weighted - values * (scale * scale * scale * inner)
    return through, jnp.sum(grad * values * scale, axis=0, keepdims=True)


def feed_back_kernel(
    grad_embed_ref, embed_ref, inverse_ref, pool_ref, length_ref, last_ref, middle_ref, ending_ref, expand_ref,
    reduce_ref, gains_ref,
    grad_expand_ref, grad_reduce_ref, grad_middle_ref, grad_proj_ref, grad_gains_ref,
    normed, normed_turned, end_low, end_turned, back,
):
    tokens = middle_ref.shape[0]
    embeds, grads = embed_ref[...], grad_embed_ref[...]
    grad_proj = inverse_ref[:, :1] * (grads - embeds * jnp.sum(grads * embeds, axis=1, keepdims=True))
    grad_proj = grad_proj.astype(jnp.bfloat16)
    grad_proj_ref[...] = grad_proj
    grad_pooled = dot_nt(grad_proj, last_ref[0]) / length_ref[:, :1]
    grad_gains_ref[...] = jnp.zeros_like(grad_gains_ref)

    def begin(r, carry):
        rows = rows_at(r, 256)
        grad_out = lax.dot_general(
            pool_ref[:, rows], grad_pooled, (((0,), (0,)), ((), ())), precision=HIGHEST,
            preferred_element_type=jnp.float32,
        )
        through, gain = norm_back_rows(ending_ref[rows, :], gains_ref[2:3], grad_out)
        grad_gains_ref[2:3] += gain
        grad_middle_ref[rows, :] = through
        end_low[rows, :] = through.astype(jnp.bfloat16)
        end_turned[:, rows] = through.T.astype(jnp.bfloat16)
        middle_normed = norm_rows(middle_ref[rows, :], gains_ref[1:2])
        normed[rows, :] = middle_normed.astype(jnp.bfloat16)
        normed_turned[:, rows] = middle_normed.T.astype(jnp.bfloat16)
        return carry

    lax.fori_loop(0, tokens // 256, begin, 0)
    back[...] = jnp.zeros_like(back)
    wide = expand_ref.shape[1]
    step = 384

    def feed(c, carry):
        lanes = rows_at(c, step)
        pre = dot_nn(normed[...], expand_ref[:, lanes])
        grad_act = dot_nn(end_low[...], reduce_ref[:, lanes])
        turn = gelu_parts(pre)
        act = (0.5 * pre * (1.0 + turn)).astype(jnp.bfloat16)
        slope = 0.5 * (1.0 + turn) + 0.5 * pre * (1.0 - turn * turn) * GELU_IN * (1.0 + 3.0 * 0.044715 * pre * pre)
        grad_pre = (grad_act * slope).astype(jnp.bfloat16)
        grad_reduce_ref[:, lanes] = dot_nn(end_turned[...], act).astype(jnp.bfloat16)
        grad_expand_ref[:, lanes] = dot_nn(normed_turned[...], grad_pre).astype(jnp.bfloat16)
        back[...] += dot_nt(grad_pre, expand_ref[:, lanes])
        return carry

    lax.fori_loop(0, wide // step, feed, 0)

    def end(r, carry):
        rows = rows_at(r, 256)
        through, gain = norm_back_rows(middle_ref[rows, :], gains_ref[1:2], back[rows, :])
        grad_gains_ref[1:2] += gain
        grad_middle_ref[rows, :] += through
        return carry

    lax.fori_loop(0, tokens // 256, end, 0)


def run_feed_back(grad_embed, embeds, inverse, pool, lengths, square, middle, ending, expand, reduce_turned, gains):
    tokens = middle.shape[0]
    seqs = pool.shape[0]
    low = jnp.bfloat16
    whole = pl.BlockSpec(memory_space=pltpu.VMEM)
    return pl.pallas_call(
        feed_back_kernel,
        grid=(1,),
        out_shape=[
            jax.ShapeDtypeStruct(expand.shape, low),
            jax.ShapeDtypeStruct(reduce_turned.shape, low),
            jax.ShapeDtypeStruct((tokens, D), jnp.float32),
            jax.ShapeDtypeStruct((seqs, D), low),
            jax.ShapeDtypeStruct((8, D), jnp.float32),
        ],
        in_specs=[whole] * 5
        + [pl.BlockSpec((1, D, D), lambda i: (4, 0, 0))]
        + [whole] * 5,
        out_specs=[whole] * 5,
        scratch_shapes=[
            pltpu.VMEM((tokens, D), low),
            pltpu.VMEM((D, tokens), low),
            pltpu.VMEM((tokens, D), low),
            pltpu.VMEM((D, tokens), low),
            pltpu.VMEM((tokens, D), jnp.float32),
        ],
        compiler_params=pltpu.CompilerParams(vmem_limit_bytes=VMEM_CAP),
        name="feed_backward",
    )(grad_embed, embeds, inverse, pool, lengths, square, middle, ending, expand, reduce_turned, gains)


def attend_back_steps(
    grad_middle_ref, grad_proj_ref, pooled_ref, start_ref, query_ref, key_ref, value_ref, mixed_ref,
    square_ref, gains_ref, bias_ref, mask_ref, rank_ref,
    grad_square_ref, grad_score_ref, grad_gain_ref, grad_mixed, turned, grad_query, grad_key, grad_value,
    turned_half, between, early_done, squares_done, put,
):
    tokens = start_ref.shape[0]
    big = 512
    grad_square_ref[4] = dot_tn(pooled_ref[...], grad_proj_ref[...]).astype(jnp.bfloat16)

    def begin(r, carry):
        rows = rows_at(r, big)
        grad_mixed[rows, :] = dot_nt(grad_middle_ref[rows, :].astype(jnp.bfloat16), square_ref[3]).astype(
            jnp.bfloat16
        )
        turned[:, rows] = mixed_ref[rows, :].astype(jnp.float32).T.astype(jnp.bfloat16)
        return carry

    lax.fori_loop(0, tokens // big, begin, 0)

    def outer(target, right_ref):
        def part(r, carry):
            rows = rows_at(r, 384)
            grad_square_ref[target, rows, :] = dot_nn(turned[rows, :], right_ref[...].astype(jnp.bfloat16)).astype(
                jnp.bfloat16
            )
            return carry

        lax.fori_loop(0, D // 384, part, 0)

    outer(3, grad_middle_ref)
    early_done()
    grad_score_ref[...] = jnp.zeros_like(grad_score_ref)

    def attend(t, carry):
        rows = rows_at(t, TILE)
        mask = tile_mask(mask_ref, t)
        for pair in range(PAIRS):
            lanes = pl.ds(pair * TILE, TILE)
            query, keys_here = query_ref[rows, lanes], key_ref[rows, lanes]
            probs = pair_probs(query, keys_here, pair_bias(bias_ref, pair), mask)
            grads = split_heads(grad_mixed[rows, lanes])
            grad_probs = dot_nt(grads, value_ref[rows, lanes])
            grad_value[rows, lanes] = dot_tn(probs.astype(jnp.bfloat16), grads).astype(jnp.bfloat16)
            inner = jnp.sum(grad_probs * probs, axis=1, keepdims=True)
            grad_scores = (probs * (grad_probs - inner)).astype(jnp.bfloat16)
            kept = grad_scores.astype(jnp.float32)
            grad_score_ref[2 * pair] += kept[:TILE]
            grad_score_ref[2 * pair + 1] += kept[TILE:]
            grad_query[rows, lanes] = (
                dot_nn(join_heads(grad_scores), split_heads(keys_here)) * HEAD ** (-0.5)
            ).astype(jnp.bfloat16)
            grad_key[rows, lanes] = (dot_tn(grad_scores, split_heads(query)) * HEAD ** (-0.5)).astype(jnp.bfloat16)
        return carry

    tiles = tokens // TILE
    between = list(between)
    part = tokens // 2

    def relay(place, number):
        for spot_name, spot_number, act in between:
            if (spot_name, spot_number) == (place, number):
                act()

    grad_gain_ref[...] = jnp.zeros_like(grad_gain_ref)

    def attend_half(half):
        for t in range(half * tiles // 2, (half + 1) * tiles // 2):
            lax.fori_loop(t, t + 1, attend, 0)
            relay("tile", t)

    def end_half(half):
        def end(r, carry):
            rows = pl.ds(pl.multiple_of(half * part + r * 256, 256), 256)
            grad_normed = (
                dot_nt(grad_query[rows, :], square_ref[0])
                + dot_nt(grad_key[rows, :], square_ref[1])
                + dot_nt(grad_value[rows, :], square_ref[2])
            )
            through, gain = norm_back_rows(start_ref[rows, :].astype(jnp.float32), gains_ref[0:1], grad_normed)
            grad_gain_ref[0:1] += gain
            turned_half[:, rows_at(r, 256)] = (grad_middle_ref[rows, :] + through).T.astype(jnp.bfloat16)
            return carry

        lax.fori_loop(0, part // 256, end, 0)

        def merge(r, carry):
            rows = rows_at(r, 384)
            total = jnp.zeros((384, part), jnp.float32)
            for c in range(part // 256):
                hot = hot_rows(rank_ref, pl.ds(half * part + c * 256, 256), part, half * part)
                total = total + dot_nn(turned_half[rows, c * 256 : (c + 1) * 256], hot)
            put(half, r, total)
            return carry

        lax.fori_loop(0, D // 384, merge, 0)
        put(half, None, None)

    attend_half(0)
    end_half(0)
    relay("end", 0)
    attend_half(1)

    def renorm(r, carry):
        rows = rows_at(r, 256)
        normed = norm_rows(start_ref[rows, :].astype(jnp.float32), gains_ref[0:1])
        turned[:, rows] = normed.T.astype(jnp.bfloat16)
        return carry

    lax.fori_loop(0, tokens // 256, renorm, 0)
    relay("norm", 0)
    outer(0, grad_query)
    relay("outer", 0)
    outer(1, grad_key)
    relay("outer", 1)
    outer(2, grad_value)
    squares_done()
    relay("outer", 2)
    end_half(1)
    relay("end", 1)


def attend_back_kernel(*refs):
    ins, rest = refs[:13], refs[13:]
    grad_square_ref, grad_score_ref, grad_gain_ref, send_ref = rest[:4]

    def put(half, r, total):
        if r is not None:
            part = total.shape[1]
            send_ref[rows_at(r, 384), half * part : (half + 1) * part] = total.astype(jnp.bfloat16)

    nothing = lambda: None
    attend_back_steps(
        *ins, grad_square_ref, grad_score_ref, grad_gain_ref, *rest[4:], [], nothing, nothing, put
    )


def attend_scratch(tokens):
    low = jnp.bfloat16
    return [
        pltpu.VMEM((tokens, D), low),
        pltpu.VMEM((D, tokens), low),
        pltpu.VMEM((tokens, D), low),
        pltpu.VMEM((tokens, D), low),
        pltpu.VMEM((tokens, D), low),
        pltpu.VMEM((D, tokens // 2), low),
    ]


def run_attend_back(*ins):
    tokens = ins[0].shape[0]
    low = jnp.bfloat16
    return pl.pallas_call(
        attend_back_kernel,
        out_shape=[
            jax.ShapeDtypeStruct((5, D, D), low),
            jax.ShapeDtypeStruct((HEADS, TILE, TILE), jnp.float32),
            jax.ShapeDtypeStruct((8, D), jnp.float32),
            jax.ShapeDtypeStruct((D, tokens), low),
        ],
        scratch_shapes=attend_scratch(tokens),
        compiler_params=pltpu.CompilerParams(vmem_limit_bytes=VMEM_CAP),
        name="attend_backward",
    )(*ins)


BACK_CAP = 64 * 1024 * 1024 - 128 * 1024


HIGH = 32
SEGMENTS = 8
EARLY_PLAN = (("tile", 3), ("outer", 0), ("end", 1), ("dense", 1), ("dense", 3), ("dense", 5))
LATE_PLAN = (("dense", 6), ("dense", 7), ("dense", 9), ("dense", 11), ("dense", 13), ("dense", 15))


def back_kernel(depth, *refs):
    ins, refs = refs[:13], refs[13:]
    keys_ref, grad_expand, grad_reduce = refs[:3]
    square_sum, expand_sum, reduce_sum, grad_score_ref, grad_gain_ref, squares_ref, table_ref = refs[3:10]
    grad_square, *steps = refs[10:17]
    blocks, spare, work_expand, work_reduce, returned, places = refs[17:23]
    refs = refs[23:]
    turned = steps[1]
    count_first, count_last = 5 * len(FIRST_KINDS), 5 * len(LAST_KINDS)
    first_buffers, refs = refs[:count_first], refs[count_first:]
    first_sems, refs = refs[:8], refs[8:]
    last_buffers, refs = refs[:count_last], refs[count_last:]
    last_sems, refs = refs[:8], refs[8:]
    part_send, part_got, part_own, end_send, end_got = refs
    dp_size, fsdp_size = lax.axis_size("dp"), lax.axis_size("fsdp")
    count = dp_size * fsdp_size
    me = lax.axis_index("dp") * fsdp_size + lax.axis_index("fsdp")
    greet_all(count, fsdp_size, me)
    grads = (grad_square, grad_expand, grad_reduce)
    outs = (square_sum, expand_sum, reduce_sum, spare)
    work = {EXPAND: work_expand, REDUCE: work_reduce}
    early = Reduction(FIRST_KINDS, depth, grads, outs, work, first_buffers, first_sems)
    late = Reduction(LAST_KINDS, depth, grads, outs, work, last_buffers, last_sems)
    early.begin((EXPAND, REDUCE))
    early_groups, late_groups = list(early.groups()), list(late.groups())

    def relay(group):
        def act():
            for move, step in group:
                move(step)

        return act

    feats, quarter = blocks.shape[2] // 2, blocks.shape[3]

    def part_copy(half, k):
        target = lax.rem(me + k, count)
        device = (target // fsdp_size, lax.rem(target, fsdp_size))
        return remote(
            blocks.at[half, target], returned.at[half, me], part_send.at[half, k], part_got.at[half, k], device
        )

    def own_part(half):
        return pltpu.make_async_copy(blocks.at[half, me], returned.at[half, me], part_own.at[half])

    def put(half, r, total):
        if r is None:

            def start_part(k, carry):
                part_copy(half, k).start()
                return carry

            lax.fori_loop(1, count, start_part, 0)
            own_part(half).start()
            return
        each = 384 // feats
        for p in range(each):
            part = total[p * feats : (p + 1) * feats]
            blocks[half, r * each + p] = jnp.concatenate(
                [part[:, :quarter], part[:, quarter:]], axis=0
            ).astype(jnp.bfloat16)

    attend_back_steps(
        *ins, grad_square, grad_score_ref, grad_gain_ref, *steps,
        [(*place_at, relay(group)) for place_at, group in zip(EARLY_PLAN, early_groups)],
        lambda: early.begin((EARLY,)),
        lambda: late.begin((LATE,)),
        put,
    )

    def end_copy(number, kind, of):
        span = pl.ds(*SPANS[kind])
        return remote(
            spare.at[span], square_sum.at[of, span], end_send.at[number], end_got.at[number], early.sibling
        )

    core = early.core
    table_ref[...] = jnp.zeros_like(table_ref)
    vocab = table_ref.shape[1]
    batch = 2
    segments = 4
    slots = 2 * quarter
    lines = slots // LANES

    def add_rows(half, n, carry):
        for b in range(batch):
            k = n * batch + b

            @pl.when(k > 0)
            def _():
                part_copy(half, k).wait_recv()

            source = lax.rem(me + count - k, count)
            block = returned[half, source].astype(jnp.float32)
            keys = keys_ref[source]
            for c in range(lines):
                key = keys[half * lines + c : half * lines + c + 1]
                number = (key >> 2) + (key & 3) * fold_rows(vocab)
                at = pl.ds(b * slots + c * LANES, LANES)
                places[0:1, at] = number & 1023
                first = 0 if c < lines // 2 else feats
                low = (c % (lines // 2)) * LANES
                piece = block[first : first + feats, low : low + LANES]
                high = number >> 10
                spread = [jnp.where(high == g, piece, 0.0) for g in range(HIGH)]
                turned[:, at] = jnp.concatenate(spread, axis=0).astype(jnp.bfloat16)
        for w in range(4):
            window = 256
            row = lax.broadcasted_iota(jnp.int32, (window, batch * slots), 0) + w * window
            hot = (row == places[0:1]).astype(jnp.float32).astype(jnp.bfloat16)
            total = dot_nt(turned[...], hot)
            for g in range(HIGH):
                start = g * 1024 + w * window
                width = min(window, vocab - start)
                if width > 0:
                    table_ref[:, start : start + width] += total[g * feats : (g + 1) * feats, :width]
        return carry

    plan = list(zip(EARLY_PLAN, early_groups)) + list(zip(LATE_PLAN, late_groups))
    for half in range(2):
        own_part(half).wait()
        each = count // batch // SEGMENTS
        for segment in range(SEGMENTS):
            lax.fori_loop(segment * each, (segment + 1) * each, functools.partial(add_rows, half), 0)
            for place_at, group in plan:
                if place_at == ("dense", half * SEGMENTS + segment):
                    relay(group)()
                    if group is early_groups[-1]:
                        end_copy(0, EARLY, core).start()
    end_copy(1, LATE, core).start()
    early.finish()
    late.finish()
    for number, kind in enumerate((EARLY, LATE)):
        end_copy(number, kind, core).wait_send()
        end_copy(number, kind, 1 - core).wait_recv()
    squares = jnp.zeros((1, 1), jnp.float32)
    for sums in (square_sum, expand_sum, reduce_sum):
        value = sums[...].reshape(-1, sums.shape[-1])
        squares = squares + jnp.sum(value * value, keepdims=True)
    for g in range(HIGH):
        value = table_ref[:, g * 1024 : min(vocab, (g + 1) * 1024)]
        squares = squares + jnp.sum(value * value, keepdims=True)
    squares_ref[...] = jnp.broadcast_to(squares, squares_ref.shape)
    for half in range(2):

        def end_part(k, carry):
            part_copy(half, k).wait_send()
            return carry

        lax.fori_loop(1, count, end_part, 0)


def run_back(ins, keys, grad_expand, grad_reduce, feats, vocab, call_id):
    depth = lax.axis_size("dp") // 2
    tokens = ins[0].shape[0]
    low = jnp.bfloat16
    count = keys.shape[0]
    blocks = (2, count, 2 * feats, tokens // 4)
    whole = pl.BlockSpec(memory_space=pltpu.VMEM)
    anywhere = pl.BlockSpec(memory_space=pl.ANY)
    first_buffers, first_sems = reduction_scratch(FIRST_KINDS, depth)
    last_buffers, last_sems = reduction_scratch(LAST_KINDS, depth)
    return pl.pallas_call(
        functools.partial(back_kernel, depth),
        out_shape=[
            jax.ShapeDtypeStruct((2, 5, 48, 192), jnp.float32),
            jax.ShapeDtypeStruct((96, 768), jnp.float32),
            jax.ShapeDtypeStruct((192, 384), jnp.float32),
            jax.ShapeDtypeStruct((HEADS, TILE, TILE), jnp.float32),
            jax.ShapeDtypeStruct((8, D), jnp.float32),
            jax.ShapeDtypeStruct((8, LANES), jnp.float32),
            jax.ShapeDtypeStruct((feats, vocab), jnp.float32),
        ],
        in_specs=[whole] * 14 + [anywhere] * 2,
        out_specs=[whole] * 7,
        scratch_shapes=[pltpu.VMEM((5, D, D), low)]
        + attend_scratch(tokens)
        + [
            pltpu.VMEM(blocks, low),
            pltpu.VMEM((5, 48, 192), jnp.float32),
            pltpu.VMEM(pair_shape(EXPAND, depth), low),
            pltpu.VMEM(pair_shape(REDUCE, depth), low),
            pltpu.VMEM(blocks, low),
            pltpu.VMEM((8, tokens), jnp.int32),
        ]
        + first_buffers
        + first_sems
        + last_buffers
        + last_sems
        + [
            pltpu.SemaphoreType.DMA((2, count)),
            pltpu.SemaphoreType.DMA((2, count)),
            pltpu.SemaphoreType.DMA((2,)),
            pltpu.SemaphoreType.DMA((2,)),
            pltpu.SemaphoreType.DMA((2,)),
        ],
        compiler_params=pltpu.CompilerParams(
            collective_id=call_id, has_side_effects=True, vmem_limit_bytes=BACK_CAP
        ),
        name="back",
    )(*ins, keys, grad_expand, grad_reduce)


def share_chips(own_ref, everyone, send, got, hand_send, hand_got):
    dp_size, fsdp_size = lax.axis_size("dp"), lax.axis_size("fsdp")
    count = dp_size * fsdp_size
    chips = count // 2
    dp, fsdp = lax.axis_index("dp"), lax.axis_index("fsdp")
    me = dp * fsdp_size + fsdp
    core = lax.rem(fsdp, 2)
    chip = me // 2
    sibling = (dp, fsdp + 1 - 2 * core)
    greet_all(count, fsdp_size, me)

    def device(number):
        return (number // fsdp_size, lax.rem(number, fsdp_size))

    def across(k):
        target = lax.rem(chip + k, chips) * 2 + core
        return remote(own_ref, everyone.at[me], send.at[k], got.at[k], device(target))

    def hand(k, of):
        source = lax.rem(chip + chips - k, chips) * 2 + of
        return remote(everyone.at[source], everyone.at[source], hand_send.at[k], hand_got.at[k], sibling)

    def start(k, carry):
        across(k).start()
        return carry

    def relay(k, carry):
        across(k).wait_recv()
        hand(k, core).start()
        return carry

    def end(k, carry):
        across(k).wait_send()
        hand(k, core).wait_send()
        hand(k, 1 - core).wait_recv()
        return carry

    first = remote(own_ref, everyone.at[me], hand_send.at[0], hand_got.at[0], sibling)
    first.start()
    everyone[me] = own_ref[...]
    lax.fori_loop(1, chips, start, 0)
    lax.fori_loop(1, chips, relay, 0)
    lax.fori_loop(1, chips, end, 0)
    first.wait_send()
    hand(0, 1 - core).wait_recv()
    return me


def total_kernel(
    first_gain, late_gains, position_ref, table_squares, layer_squares, scale_ref, total_ref, norm_ref, tile,
    everyone, send, got, hand_send, hand_got,
):
    gains = first_gain[...] + late_gains[...]
    rows = [jnp.sum(table_squares[...], axis=0, keepdims=True), layer_squares[0:1]]
    rows += [position_ref[k : k + 1] for k in range(3)]
    for k in range(3):
        rows += [gains[k : k + 1, c * LANES : (c + 1) * LANES] for c in range(D // LANES)]
    rows.append(jnp.zeros((tile.shape[0] - len(rows), LANES), jnp.float32))
    tile[...] = jnp.concatenate(rows, axis=0)
    share_chips(tile, everyone, send, got, hand_send, hand_got)

    def add(k, total):
        return total + everyone[k]

    total = lax.fori_loop(1, everyone.shape[0], add, everyone[0])
    total_ref[...] = total
    row = lax.broadcasted_iota(jnp.int32, total.shape, 0)
    lane = lax.broadcasted_iota(jnp.int32, total.shape, 1)
    squares = jnp.where(row == 0, total, jnp.where(row == 1, jnp.where(lane == 0, total, 0.0), total * total))
    norm = jnp.sqrt(jnp.sum(squares, keepdims=True) + scale_ref[...] * scale_ref[...])
    norm_ref[...] = jnp.broadcast_to(norm, norm_ref.shape)


def run_total(first_gain, late_gains, position, table_squares, layer_squares, grad_scale, call_id):
    count = lax.axis_size("dp") * lax.axis_size("fsdp")
    few = pltpu.SemaphoreType.DMA((count // 2,))
    return pl.pallas_call(
        total_kernel,
        out_shape=[jax.ShapeDtypeStruct((24, LANES), jnp.float32), jax.ShapeDtypeStruct((8, LANES), jnp.float32)],
        scratch_shapes=[
            pltpu.VMEM((24, LANES), jnp.float32),
            pltpu.VMEM((count, 24, LANES), jnp.float32),
            few, few, few, few,
        ],
        compiler_params=pltpu.CompilerParams(
            collective_id=call_id, has_side_effects=True, vmem_limit_bytes=VMEM_CAP
        ),
        name="total",
    )(first_gain, late_gains, position, table_squares, layer_squares, grad_scale)


def loss_kernel(
    query_rows, nli_rows, embeds_ref, negative_ref, scale_ref, grad_ref, stats_ref, everyone, grad_sims, turned_sims,
    send, got, hand_send, hand_got,
):
    count = everyone.shape[0]
    slots = embeds_ref.shape[0]
    me = share_chips(embeds_ref, everyone, send, got, hand_send, hand_got)
    total_rows = count * slots
    embeds = everyone[...].reshape(total_rows, D)
    scale = jnp.exp(scale_ref[...])
    sims = dot_nt(embeds, embeds)
    row = lax.broadcasted_iota(jnp.int32, sims.shape, 0)
    col = lax.broadcasted_iota(jnp.int32, sims.shape, 1)
    row_slot, col_slot = row & (slots - 1), col & (slots - 1)
    hypo, answer = query_rows + nli_rows, query_rows + 2 * nli_rows
    is_query = row_slot < query_rows
    is_premise = (row_slot >= query_rows) & (row_slot < hypo)
    is_hypo = (col_slot >= hypo) & (col_slot < answer)
    is_answer = (col_slot >= answer) & (col_slot < answer + query_rows)
    allowed = (is_query & is_answer) | (is_premise & is_hypo)
    target = (is_query & (col == row + answer)) | (is_premise & (col == row + nli_rows))
    target = jnp.where(target, 1.0, 0.0)
    logits = scale * sims
    shown = jnp.where(allowed, logits, -1e30)
    row_top = jnp.max(shown, axis=1, keepdims=True)
    weight = jnp.where(negative_ref[:, :1] == col, 2.0, 1.0)
    raised = jnp.where(allowed, weight * jnp.exp(shown - row_top), 0.0)
    left = is_query | is_premise
    row_total = jnp.where(left[:, :1], jnp.sum(raised, axis=1, keepdims=True), 1.0)
    hits = jnp.sum(jnp.where(target > 0.0, logits, 0.0), axis=1, keepdims=True)
    losses = jnp.where(left[:, :1], row_top + jnp.log(row_total), 0.0) - hits
    first_loss = jnp.sum(jnp.where(is_query[:, :1], losses, 0.0), keepdims=True)
    second_loss = jnp.sum(jnp.where(is_premise[:, :1], losses, 0.0), keepdims=True)
    grad_logits = raised / row_total - target
    grad_scale = scale * jnp.sum(grad_logits * sims, keepdims=True)
    lane = lax.broadcasted_iota(jnp.int32, stats_ref.shape, 1)
    stats_ref[...] = jnp.where(lane == 0, first_loss, jnp.where(lane == 1, second_loss, grad_scale))
    grads = scale * grad_logits
    grad_sims[...] = grads
    turned_sims[...] = grads.T
    own = pl.ds(pl.multiple_of(me * slots, 8), slots)
    grad_ref[...] = dot_nn(grad_sims[own, :].astype(jnp.bfloat16), embeds) + dot_nn(
        turned_sims[own, :].astype(jnp.bfloat16), embeds
    )


def run_loss(embeds, negative, log_scale, query_rows, nli_rows, call_id):
    count = lax.axis_size("dp") * lax.axis_size("fsdp")
    slots = embeds.shape[0]
    square = (count * slots, count * slots)
    chips = count // 2
    return pl.pallas_call(
        functools.partial(loss_kernel, query_rows, nli_rows),
        out_shape=[jax.ShapeDtypeStruct((slots, D), jnp.float32), jax.ShapeDtypeStruct((8, LANES), jnp.float32)],
        scratch_shapes=[
            pltpu.VMEM((count, slots, D), jnp.bfloat16),
            pltpu.VMEM(square, jnp.float32),
            pltpu.VMEM(square, jnp.float32),
            pltpu.SemaphoreType.DMA((chips,)),
            pltpu.SemaphoreType.DMA((chips,)),
            pltpu.SemaphoreType.DMA((chips,)),
            pltpu.SemaphoreType.DMA((chips,)),
        ],
        compiler_params=pltpu.CompilerParams(
            collective_id=call_id, has_side_effects=True, vmem_limit_bytes=VMEM_CAP
        ),
        name="loss",
    )(embeds, negative, log_scale)


def shards(
    embed_table,
    square_weights,
    expand_weight,
    reduce_weight,
    norm_gains,
    position_bias,
    log_scale,
    table_moment,
    table_second,
    square_moment,
    square_second,
    expand_moment,
    expand_second,
    reduce_moment,
    reduce_second,
    gains_moment,
    gains_second,
    position_moment,
    position_second,
    scale_moment,
    scale_second,
    query_tokens,
    answer_tokens,
    query_length,
    answer_length,
    premise_tokens,
    hypothesis_tokens,
    hard_negative,
):
    both = ("dp", "fsdp")
    dp_size, fsdp_size = lax.axis_size("dp"), lax.axis_size("fsdp")
    count = dp_size * fsdp_size
    direct = dp_size == 8 and fsdp_size == 4
    position = lax.axis_index(both)
    feats, vocab_size = embed_table.shape
    feats_pad = up8(feats)
    fold = fold_rows(vocab_size)
    query_rows = query_tokens.shape[0]
    nli_rows = premise_tokens.shape[0]
    short_length = query_tokens.shape[1]
    long_length = answer_tokens.shape[1]
    short_tokens = jnp.concatenate([query_tokens, premise_tokens, hypothesis_tokens], axis=0)
    lengths = jnp.concatenate(
        [query_length, jnp.full((2 * nli_rows,), short_length, jnp.int32), answer_length]
    )
    all_tokens = jnp.concatenate([short_tokens.reshape(-1), answer_tokens.reshape(-1)])
    token_count = all_tokens.shape[0]
    hypo_start = query_rows + nli_rows
    answer_start = query_rows + 2 * nli_rows
    seq_count = answer_start + query_rows
    seq_pad = -(-seq_count // 16) * 16
    split_at = short_tokens.shape[0] * short_length

    packed, rank = token_keys(all_tokens, fold)
    key_rows = token_count // LANES
    info = jnp.concatenate(
        [
            packed.reshape(key_rows, LANES),
            jnp.pad(hard_negative, (0, LANES - nli_rows)).reshape(1, LANES),
            jnp.zeros((7, LANES), jnp.int32),
        ],
        axis=0,
    )
    own_gains = jnp.pad(norm_gains, ((0, 5), (0, LANES - feats)))
    square_low = square_weights.astype(jnp.bfloat16)
    expand_low = expand_weight.astype(jnp.bfloat16)
    reduce_low = reduce_weight.astype(jnp.bfloat16).T
    half = token_count // 2
    if direct:
        square_pieces = square_low.reshape(5, 2, 48, 192).transpose(1, 0, 2, 3)
        found, square_all, expand_all, info_all, gains_all = run_front(
            info, own_gains, token_count, embed_table, square_pieces, expand_low, 1
        )
    else:
        info_all = exchange(info[None], True, 0, "share_keys")
        gains_all = exchange(own_gains[None], True, 6, "share_gains")

        def whole(piece, row_name, column_name):
            axis = piece.ndim - 2
            wide = lax.all_gather(piece, column_name, axis=axis + 1, tiled=True)
            return lax.all_gather(wide, row_name, axis=axis, tiled=True)

        square_all = whole(square_low, "dp", "fsdp")
        expand_all = whole(expand_low, "dp", "fsdp")
        reduce_all = whole(reduce_low, "fsdp", "dp")
        padded = jnp.pad(embed_table, ((0, feats_pad - feats), (0, 0)))
        key_all = info_all[:, :key_rows].reshape(count, 1, token_count)
        found = exchange(lookup(padded, key_all >> 2, key_all & 3), False, 8, "send_features")
        found = found.reshape(count, 2, feats_pad, half)[:, :, :feats]
        found = found.transpose(1, 0, 2, 3).reshape(1, 2 * D, half)
    packed_all = info_all[:, :key_rows].reshape(count, 1, token_count)
    row_all, group_all = packed_all >> 2, packed_all & 3
    negative_all = info_all[:, key_rows, :nli_rows]
    gains = gains_all[:, :3, :feats].transpose(1, 0, 2).reshape(3, D)
    gains = jnp.pad(gains.astype(jnp.bfloat16).astype(jnp.float32), ((0, 5), (0, 0)))

    sequence = np.concatenate(
        [
            np.repeat(np.arange(answer_start), short_length),
            answer_start + np.repeat(np.arange(query_rows), long_length),
        ]
    )
    inside = np.concatenate(
        [
            np.tile(np.arange(short_length), answer_start),
            np.tile(np.arange(long_length), query_rows),
        ]
    )
    lengths_pad = jnp.pad(lengths, (0, seq_pad - seq_count), constant_values=1)
    pool = (sequence[None, :] == np.arange(seq_pad)[:, None]) & (inside[None, :] < lengths_pad[:, None])
    token_ok = jnp.any(pool, axis=0).reshape(-1, 1, TILE)
    sequence_tiles = sequence.reshape(-1, TILE)
    together = sequence_tiles[:, :, None] == sequence_tiles[:, None, :]
    mask = jnp.where(together & token_ok, 0.0, -1e30).astype(jnp.float32)
    pool = pool.astype(jnp.float32)
    length_rows = jnp.broadcast_to(lengths_pad.astype(jnp.float32)[:, None], (seq_pad, LANES))
    rank_rows = jnp.broadcast_to(rank[:, None], (token_count, LANES))
    bias, onehot = attention_bias(position_bias, TILE)

    forward_ins = (found, rank_rows, square_all, gains, bias, mask, pool, length_rows)
    if direct:
        *forward_all, reduce_all = run_relayed_forward(forward_ins, expand_all, reduce_low, 2)
    else:
        forward_all = run_forward(forward_ins, expand_all, reduce_all)
    (start, queries, keys_here, values_here, mixed, middle, ending, embeds_low, pooled, embeds, inverse) = forward_all
    if direct:
        negative_place = (negative_all // nli_rows) * seq_pad + hypo_start + negative_all % nli_rows
        negative_place = jnp.pad(
            negative_place, ((0, 0), (query_rows, seq_pad - hypo_start)), constant_values=-1
        )
        negative_place = jnp.broadcast_to(negative_place.reshape(-1, 1), (count * seq_pad, LANES))
        grad_embeds, stats = run_loss(
            embeds_low, negative_place, log_scale.reshape(1, 1), query_rows, nli_rows, 3
        )
        losses, grad_scale = stats[0, :2], stats[0, 2:3]
    else:
        gathered = exchange(embeds_low[None], True, 3, "share_embeds")
        queries_all = gathered[:, :query_rows].reshape(-1, D)
        premises_all = gathered[:, query_rows:hypo_start].reshape(-1, D)
        hypotheses_all = gathered[:, hypo_start:answer_start].reshape(-1, D)
        answers_all = gathered[:, answer_start:seq_count].reshape(-1, D)
        scale = jnp.exp(log_scale[0])

        def contrast(left, right, extra, own):
            sims = product_right(left, right)
            logits = scale * sims
            row_top = jnp.max(logits, axis=1, keepdims=True)
            raised = (1.0 + extra) * jnp.exp(logits - row_top)
            row_total = jnp.sum(raised, axis=1, keepdims=True)
            spread = row_top[:, 0] + jnp.log(row_total[:, 0])
            target_hit = jnp.eye(left.shape[0], dtype=jnp.float32)
            loss_sum = jnp.sum(spread - jnp.sum(target_hit * logits, axis=1))
            grad_logits = raised / row_total - target_hit
            grad_scale = jnp.sum(grad_logits * sims)
            grad_sims = (scale * grad_logits).astype(jnp.bfloat16)
            mine_left = lax.dynamic_slice_in_dim(grad_sims, position * own, own, 0)
            mine_right = lax.dynamic_slice_in_dim(grad_sims, position * own, own, 1)
            return (loss_sum, grad_scale, product(mine_left, right), product_left(mine_right, left))

        first_loss, first_dscale, grad_queries, grad_answers = contrast(
            queries_all, answers_all, 0.0, query_rows
        )
        negatives = (jnp.arange(hypotheses_all.shape[0])[None, :] == negative_all.reshape(-1)[:, None]).astype(
            jnp.float32
        )
        second_loss, second_dscale, grad_premises, grad_hypotheses = contrast(
            premises_all, hypotheses_all, negatives, nli_rows
        )
        grad_embeds = jnp.concatenate(
            [
                grad_queries,
                grad_premises,
                grad_hypotheses,
                grad_answers,
                jnp.zeros((seq_pad - seq_count, D), jnp.float32),
            ],
            axis=0,
        )
        losses = jnp.stack([first_loss, second_loss])
        grad_scale = ((first_dscale + second_dscale) * scale).reshape(1)
    (grad_expand, grad_reduce, grad_middle, grad_proj, late_gains) = run_feed_back(
        grad_embeds, embeds, inverse, pool, length_rows, square_all, middle, ending, expand_all, reduce_all, gains
    )
    back_ins = (
        grad_middle, grad_proj, pooled, start, queries, keys_here, values_here, mixed, square_all,
        gains, bias, mask, rank_rows,
    )
    if direct:
        (square_sum, expand_sum, reduce_sum, grad_scores, first_gain, layer_squares, grad_table) = run_back(
            back_ins, info_all, grad_expand, grad_reduce, feats, vocab_size, 5
        )
        table_squares = jnp.zeros((8, LANES), jnp.float32)
        square_sum = square_sum.transpose(1, 0, 2, 3).reshape(5, 96, 192)
    else:

        def shard(gradient, row_name, column_name):
            axis = gradient.ndim - 2
            part = lax.psum_scatter(
                gradient.astype(jnp.float32), row_name, scatter_dimension=axis, tiled=True
            )
            return lax.psum_scatter(part, column_name, scatter_dimension=axis + 1, tiled=True)

        (grad_square, grad_scores, first_gain, merged) = run_attend_back(*back_ins)
        square_sum = shard(grad_square, "dp", "fsdp")
        expand_sum = shard(grad_expand, "dp", "fsdp")
        reduce_sum = shard(grad_reduce, "fsdp", "dp")
        layer_squares = jnp.full(
            (8, LANES), sum(jnp.sum(part * part) for part in (square_sum, expand_sum, reduce_sum)), jnp.float32
        )
        merged = merged.reshape(count, feats, 2, 2, half // 2).transpose(2, 0, 3, 1, 4)
        if feats_pad > feats:
            merged = jnp.pad(merged, ((0, 0), (0, 0), (0, 0), (0, feats_pad - feats), (0, 0)))
        merged = merged.reshape(2, count, 2 * feats_pad, half // 2)
        returned = jnp.stack(
            [exchange(merged[n], False, 9 + n, ("send_early", "send_late")[n]) for n in range(2)]
        )
        grad_table, table_squares = scatter(returned, row_all, group_all, vocab_size)
        grad_table = grad_table[:feats]
    grad_position = lax.dot_general(
        onehot, grad_scores.reshape(HEADS, TILE * TILE), (((0,), (1,)), ((), ())), precision=HIGHEST
    )
    reduced = (square_sum, expand_sum, reduce_sum.T)
    total, norm = run_total(
        first_gain,
        late_gains,
        grad_position.reshape(-1, LANES),
        table_squares,
        layer_squares,
        grad_scale.reshape(1, 1),
        7,
    )
    position_total = total[2:5].reshape(BUCKETS, HEADS)
    gains_total = total[5:23].reshape(3, D)
    scale_total = grad_scale
    gradient_norm = norm[0, 0]
    grad_gain_shard = lax.dynamic_slice_in_dim(gains_total, position * feats, feats, 1)
    factor = jnp.minimum(1.0, CLIP_NORM / gradient_norm)
    table_out = adam_update(embed_table, table_moment, table_second, grad_table, factor, TABLE_RATE)
    square_out = adam_update(
        square_weights, square_moment, square_second, reduced[0], factor, LEARN_RATE
    )
    expand_out = adam_update(
        expand_weight, expand_moment, expand_second, reduced[1], factor, LEARN_RATE
    )
    reduce_out = adam_update(
        reduce_weight, reduce_moment, reduce_second, reduced[2], factor, LEARN_RATE
    )
    gains_out = adam_update(
        norm_gains, gains_moment, gains_second, grad_gain_shard, factor, SMALL_RATE
    )
    position_out = adam_update(
        position_bias, position_moment, position_second, position_total, factor, SMALL_RATE
    )
    scale_out = adam_update(log_scale, scale_moment, scale_second, scale_total, factor, SMALL_RATE)
    return (
        *table_out,
        *square_out,
        *expand_out,
        *reduce_out,
        *gains_out,
        *position_out,
        *scale_out,
        losses,
        gradient_norm,
    )


def solution(mesh):
    return jax.shard_map(
        shards,
        mesh=mesh,
        in_specs=(
            P(("dp", "fsdp"), None),
            P(None, "dp", "fsdp"),
            P("dp", "fsdp"),
            P("dp", "fsdp"),
            P(None, ("dp", "fsdp")),
            P(),
            P(),
            P(("dp", "fsdp"), None),
            P(("dp", "fsdp"), None),
            P(None, "dp", "fsdp"),
            P(None, "dp", "fsdp"),
            P("dp", "fsdp"),
            P("dp", "fsdp"),
            P("dp", "fsdp"),
            P("dp", "fsdp"),
            P(None, ("dp", "fsdp")),
            P(None, ("dp", "fsdp")),
            P(),
            P(),
            P(),
            P(),
            P(("dp", "fsdp"), None),
            P(("dp", "fsdp"), None),
            P(("dp", "fsdp")),
            P(("dp", "fsdp")),
            P(("dp", "fsdp"), None),
            P(("dp", "fsdp"), None),
            P(("dp", "fsdp")),
        ),
        out_specs=(
            P(("dp", "fsdp"), None),
            P(("dp", "fsdp"), None),
            P(("dp", "fsdp"), None),
            P(None, "dp", "fsdp"),
            P(None, "dp", "fsdp"),
            P(None, "dp", "fsdp"),
            P("dp", "fsdp"),
            P("dp", "fsdp"),
            P("dp", "fsdp"),
            P("dp", "fsdp"),
            P("dp", "fsdp"),
            P("dp", "fsdp"),
            P(None, ("dp", "fsdp")),
            P(None, ("dp", "fsdp")),
            P(None, ("dp", "fsdp")),
            P(),
            P(),
            P(),
            P(),
            P(),
            P(),
            P(),
            P(),
        ),
        check_vma=False,
    )
```

```python
import functools

import jax
import jax.numpy as jnp
import numpy as np
from jax import lax
from jax.experimental import pallas as pl
from jax.experimental.pallas import tpu as pltpu
from jax.sharding import PartitionSpec as P

D = 768
HEADS = 12
HEAD = 64
BUCKETS = 32
MAXDIST = 128
STEP = 10


HIGHEST = lax.Precision.HIGHEST
NORM_EPS = 1e-06
LEARN_RATE = 0.03
TABLE_RATE = 0.4
SMALL_RATE = 0.5
BETA_ONE = 0.9
BETA_TWO = 0.999
ADAM_EPS = 1e-08
WEIGHT_DECAY = 0.01
CLIP_NORM = 0.5


def bucket_table(length):
    places = np.arange(length)
    offset = places[None, :] - places[:, None]
    half_count = BUCKETS // 2
    exact_count = half_count // 2
    upper = (offset > 0).astype(np.int64) * half_count
    distance = np.abs(offset)
    far_bucket = exact_count + (
        np.log(np.maximum(distance, 1) / exact_count)
        / np.log(MAXDIST / exact_count)
        * (half_count - exact_count)
    ).astype(np.int64)
    far_bucket = np.minimum(far_bucket, half_count - 1)
    return (upper + np.where(distance < exact_count, distance, far_bucket)).astype(np.int32)


def bucket_onehot(length):
    flat_table = bucket_table(length).reshape(-1)
    return jnp.asarray((flat_table[:, None] == np.arange(BUCKETS)[None, :]).astype(np.float32))


def product(left, right):
    return jnp.dot(left, right, preferred_element_type=jnp.float32)


def product_left(left, right):
    return lax.dot_general(
        left, right, (((0,), (0,)), ((), ())), preferred_element_type=jnp.float32
    )


def product_right(left, right):
    return lax.dot_general(
        left, right, (((1,), (1,)), ((), ())), preferred_element_type=jnp.float32
    )


def attention_bias(position_bias, length):
    onehot = bucket_onehot(length)
    flat_bias = jnp.dot(onehot, position_bias, precision=HIGHEST)
    return (jnp.transpose(flat_bias.reshape(length, length, HEADS), (2, 0, 1)), onehot)


def adam_update(weight, moment, second, grad, factor, rate):
    clipped = grad * factor
    moment_new = BETA_ONE * moment + (1 - BETA_ONE) * clipped
    second_new = BETA_TWO * second + (1 - BETA_TWO) * clipped * clipped
    moment_hat = moment_new / (1 - BETA_ONE**STEP)
    second_hat = second_new / (1 - BETA_TWO**STEP)
    updated = weight - rate * (
        moment_hat / (jnp.sqrt(second_hat) + ADAM_EPS) + WEIGHT_DECAY * weight
    )
    return (moment_new, second_new, updated)


LANES = 128
GROUPS = 4
SLOT = LANES // GROUPS
VMEM_CAP = 56 * 1024 * 1024

def fold_rows(vocab):
    per = -(-vocab // GROUPS)
    return -(-per // LANES) * LANES

def up8(n):
    return -(-n // 8) * 8

def eye():
    r = lax.broadcasted_iota(jnp.int32, (LANES, LANES), 0)
    c = lax.broadcasted_iota(jnp.int32, (LANES, LANES), 1)
    return (r == c).astype(jnp.float32).astype(jnp.bfloat16)

def turn_table(fold, table_ref, turned):
    feats, vocab = table_ref.shape
    pad = jnp.zeros((SLOT - feats, LANES), jnp.float32)

    def build(b, carry):
        parts = []
        for j in range(GROUPS):
            start = jnp.minimum(j * fold + b * LANES, vocab - LANES)
            start = pl.multiple_of(start, LANES)
            parts += [table_ref[:, pl.ds(start, LANES)], pad]
        tile = jnp.concatenate(parts, axis=0).astype(jnp.bfloat16).astype(jnp.float32)
        turned[pl.ds(pl.multiple_of(b * LANES, LANES), LANES), :] = tile.T
        return carry

    lax.fori_loop(0, fold // LANES, build, 0)
    turned[pl.ds(fold, 8), :] = jnp.zeros((8, LANES), jnp.float32)


def pick_group(rows, group, feats):
    tokens = rows.shape[0]
    wide = dot_nt(eye(), rows[...].astype(jnp.bfloat16))
    total = jnp.where(group == 0, wide[:SLOT], 0.0)
    for j in range(1, GROUPS):
        total = total + jnp.where(group == j, wide[j * SLOT : (j + 1) * SLOT], 0.0)
    half = tokens // 2
    return jnp.concatenate([total[:feats, :half], total[:feats, half:]], axis=0).astype(jnp.bfloat16)


def look_up(row_ref, group_ref, source, turned, rows, feats):
    tokens = rows.shape[0]
    batch = 32

    def fetch(b, carry):
        for k in range(batch):
            t = b * batch + k
            rows[pl.ds(t, 1), :] = turned[pl.ds(row_ref[source, t], 1), :]
        return carry

    lax.fori_loop(0, tokens // batch, fetch, 0)
    return pick_group(rows, group_ref[source], feats)


def lookup_kernel(fold, row_ref, group_ref, table_ref, out_ref, turned, rows):
    @pl.when(pl.program_id(0) == 0)
    def _():
        turn_table(fold, table_ref, turned)

    out_ref[0] = look_up(row_ref, group_ref, 0, turned, rows, table_ref.shape[0])


def lookup(table, rows_idx, groups_idx):
    feats, vocab = table.shape
    n, tokens = rows_idx.shape[0], rows_idx.shape[2]
    fold = fold_rows(vocab)
    return pl.pallas_call(
        functools.partial(lookup_kernel, fold),
        grid=(n,),
        out_shape=jax.ShapeDtypeStruct((n, 2 * feats, tokens // 2), jnp.bfloat16),
        in_specs=[
            pl.BlockSpec((None, 1, tokens), lambda s: (s, 0, 0), memory_space=pltpu.SMEM),
            pl.BlockSpec((1, 1, tokens), lambda s: (s, 0, 0)),
            pl.BlockSpec((feats, vocab), lambda s: (0, 0)),
        ],
        out_specs=pl.BlockSpec((1, 2 * feats, tokens // 2), lambda s: (s, 0, 0)),
        scratch_shapes=[pltpu.VMEM((fold + 8, LANES), jnp.float32), pltpu.VMEM((tokens, LANES), jnp.float32)],
        compiler_params=pltpu.CompilerParams(vmem_limit_bytes=VMEM_CAP),
        name="lookup",
    )(rows_idx, groups_idx, table)

def scatter_kernel(fold, row_ref, group_ref, grad_ref, out_ref, squares_ref, total, rows):
    feats, vocab = out_ref.shape
    tokens = rows.shape[0]
    step = pl.program_id(0)
    @pl.when(step == 0)
    def _():
        def clear(b, _):
            total[pl.ds(pl.multiple_of(b * LANES, LANES), LANES), :] = jnp.zeros((LANES, LANES), jnp.float32)
            return 0
        lax.fori_loop(0, fold // LANES, clear, 0)
        total[pl.ds(fold, 8), :] = jnp.zeros((8, LANES), jnp.float32)
    flat = []
    for half in range(2):
        block = grad_ref[half, 0].astype(jnp.float32)
        flat += [block[:feats], block[feats:]]
    flat = jnp.concatenate(flat, axis=1)
    group = group_ref[0]
    pad = jnp.zeros((SLOT - feats, tokens), jnp.float32)
    parts = []
    for j in range(GROUPS):
        parts += [jnp.where(group == j, flat, 0.0), pad]
    rows[...] = jnp.concatenate(parts, axis=0).T
    lines = tokens // LANES
    ways = 32 // lines
    per = LANES // ways
    for half in range(2):
        for l in range(per):
            spots = [(r, l + per * w) for r in range(half * lines // 2, (half + 1) * lines // 2) for w in range(ways)]
            at = [row_ref[r, c] for r, c in spots]
            new = [
                total[pl.ds(at[n], 1), :] + rows[pl.ds(r * LANES + c, 1), :] for n, (r, c) in enumerate(spots)
            ]
            for n in range(len(spots)):
                total[pl.ds(at[n], 1), :] = new[n]

    @pl.when(step == pl.num_programs(0) - 1)
    def _():
        whole = (vocab - (GROUPS - 1) * fold) // LANES
        def turn(b, squares):
            tile = total[pl.ds(pl.multiple_of(b * LANES, LANES), LANES), :].T
            for j in range(GROUPS):
                out_ref[:, pl.ds(pl.multiple_of(j * fold + b * LANES, LANES), LANES)] = tile[j * SLOT : j * SLOT + feats]
            return squares + tile * tile

        squares = lax.fori_loop(0, whole, turn, jnp.zeros((LANES, LANES), jnp.float32))
        for b in range(whole, fold // LANES):
            tile = total[pl.ds(b * LANES, LANES), :].T
            for j in range(GROUPS - 1):
                out_ref[:, pl.ds(j * fold + b * LANES, LANES)] = tile[j * SLOT : j * SLOT + feats]
            squares = squares + tile * tile
        squares_ref[...] = jnp.sum(squares.reshape(LANES // 8, 8, LANES), axis=0)


def scatter(grads, rows_idx, groups_idx, vocab):
    n, tokens = rows_idx.shape[0], rows_idx.shape[2]
    feats = grads.shape[2] // 2
    fold = fold_rows(vocab)
    return pl.pallas_call(
        functools.partial(scatter_kernel, fold),
        grid=(n,),
        out_shape=[jax.ShapeDtypeStruct((feats, vocab), jnp.float32), jax.ShapeDtypeStruct((8, LANES), jnp.float32)],
        in_specs=[
            pl.BlockSpec((tokens // LANES, LANES), lambda s: (s, 0), memory_space=pltpu.SMEM),
            pl.BlockSpec((1, 1, tokens), lambda s: (s, 0, 0)),
            pl.BlockSpec((2, 1, 2 * feats, tokens // 4), lambda s: (0, s, 0, 0)),
        ],
        out_specs=[pl.BlockSpec((feats, vocab), lambda s: (0, 0)), pl.BlockSpec((8, LANES), lambda s: (0, 0))],
        scratch_shapes=[pltpu.VMEM((fold + 8, LANES), jnp.float32), pltpu.VMEM((tokens, LANES), jnp.float32)],
        compiler_params=pltpu.CompilerParams(vmem_limit_bytes=VMEM_CAP),
        name="scatter",
    )(rows_idx.reshape(-1, LANES), groups_idx, grads)

def token_keys(tokens, fold):
    count = tokens.shape[0]
    key = (tokens % fold) * GROUPS + tokens // fold
    places = jnp.arange(count, dtype=jnp.int32)
    half = count // 2
    together = (places[:, None] < half) == (places[None, :] < half)
    same_before = together & (key[:, None] == key[None, :]) & (places[:, None] < places[None, :])
    first = ~jnp.any(same_before, axis=0)
    rank = jnp.sum((together & (key[None, :] < key[:, None]) & first[None, :]).astype(jnp.int32), axis=1)
    rank = rank + jnp.where(places < half, 0, half)
    hit = (rank[:, None] == places[None, :]) & first[:, None]
    packed = GROUPS * fold + jnp.sum(jnp.where(hit, key[:, None] - GROUPS * fold, 0), axis=0)
    return packed, rank


MESH = pl.DeviceIdType.MESH


def greet_all(count, cols, me):
    barrier = pltpu.get_barrier_semaphore()

    def greet(k, carry):
        to = lax.rem(me + k, count)
        pl.semaphore_signal(barrier, inc=1, device_id=(to // cols, lax.rem(to, cols)), device_id_type=MESH)
        return carry

    lax.fori_loop(1, count, greet, 0)
    pl.semaphore_wait(barrier, count - 1)


def exchange_kernel(same, src, dst, send_sem, recv_sem, own_sem):
    rows, cols = lax.axis_size("dp"), lax.axis_size("fsdp")
    count = rows * cols
    me = lax.axis_index("dp") * cols + lax.axis_index("fsdp")
    barrier = pltpu.get_barrier_semaphore()

    def device(k):
        to = lax.rem(me + k, count)
        return (to // cols, lax.rem(to, cols))

    def greet(k, carry):
        pl.semaphore_signal(barrier, inc=1, device_id=device(k), device_id_type=MESH)
        return carry

    def copy(k):
        to = lax.rem(me + k, count)
        return pltpu.make_async_remote_copy(
            src_ref=src.at[0 if same else to],
            dst_ref=dst.at[me],
            send_sem=send_sem.at[k],
            recv_sem=recv_sem.at[k],
            device_id=device(k),
            device_id_type=MESH,
        )

    def start(k, carry):
        copy(k).start()
        return carry

    def end(k, carry):
        copy(k).wait()
        return carry

    lax.fori_loop(1, count, greet, 0)
    own = pltpu.make_async_copy(src.at[0 if same else me], dst.at[me], own_sem)
    own.start()
    pl.semaphore_wait(barrier, count - 1)
    lax.fori_loop(1, count, start, 0)
    own.wait()
    lax.fori_loop(1, count, end, 0)


def exchange(blocks, same, call_id, name):
    count = lax.axis_size("dp") * lax.axis_size("fsdp")
    return pl.pallas_call(
        functools.partial(exchange_kernel, same),
        out_shape=jax.ShapeDtypeStruct((count,) + blocks.shape[1:], blocks.dtype),
        in_specs=[pl.BlockSpec(memory_space=pl.ANY)],
        out_specs=pl.BlockSpec(memory_space=pl.ANY),
        scratch_shapes=[
            pltpu.SemaphoreType.DMA((count,)),
            pltpu.SemaphoreType.DMA((count,)),
            pltpu.SemaphoreType.DMA,
        ],
        compiler_params=pltpu.CompilerParams(collective_id=call_id, has_side_effects=True),
        name=name,
    )(blocks)


SQUARE, EXPAND, REDUCE, EARLY, LATE = range(5)
STEPS = (5, 6, 4, 2, 3)
FIRST = (3, 3, 2, 1, 2)
SPANS = {SQUARE: (0, 5), EARLY: (3, 2), LATE: (0, 3)}


def spot(refs, kind, z, x, y, core):
    dp = z * 2 + x
    column = y * 2 + core
    if kind in SPANS:
        return refs[SQUARE].at[
            pl.ds(*SPANS[kind]),
            pl.ds(pl.multiple_of(dp * 96 + core * 48, 16), 48),
            pl.ds(pl.multiple_of(y * 384, 128), 384),
        ]
    if kind == EXPAND:
        return refs[kind].at[
            pl.ds(pl.multiple_of(dp * 96, 16), 96), pl.ds(pl.multiple_of(column * 768, 128), 768)
        ]
    return refs[kind].at[
        pl.ds(pl.multiple_of(column * 192, 16), 192), pl.ds(pl.multiple_of(dp * 384, 128), 384)
    ]


def spot_part(refs, kind, z, x, y, core, part):
    dp = z * 2 + x
    column = y * 2 + core
    if kind == SQUARE:
        return refs[kind].at[
            pl.ds(0, 3) if part == 0 else pl.ds(3, 2),
            pl.ds(pl.multiple_of(dp * 96 + core * 48, 16), 48),
            pl.ds(pl.multiple_of(y * 384, 128), 384),
        ]
    if kind == EXPAND:
        return refs[kind].at[
            pl.ds(pl.multiple_of(dp * 96 + part * 48, 16), 48),
            pl.ds(pl.multiple_of(column * 768, 128), 768),
        ]
    return refs[kind].at[
        pl.ds(pl.multiple_of(column * 192 + part * 96, 16), 96),
        pl.ds(pl.multiple_of(dp * 384, 128), 384),
    ]


def block_step(ref, kind, k):
    if kind in SPANS:
        return ref.at[k]
    rows = 16 if kind == EXPAND else 48
    return ref.at[pl.ds(pl.multiple_of(k * rows, 16), rows)]


BLOCKS = ((5, 48, 384), (96, 768), (192, 384), (2, 48, 384), (3, 48, 384))


def place():
    dp, fsdp = lax.axis_index("dp"), lax.axis_index("fsdp")
    return dp // 2, lax.rem(dp, 2), fsdp // 2, lax.rem(fsdp, 2)


def device_at(z, x, y, core):
    return (z * 2 + x, y * 2 + core)


def greet_neighbours(depth):
    z, x, y, core = place()
    barrier = pltpu.get_barrier_semaphore()

    def hello(target):
        pl.semaphore_signal(barrier, inc=1, device_id=target, device_id_type=MESH)

    hello(device_at(z, x, y, 1 - core))
    hello(device_at(z, 1 - x, y, core))
    hello(device_at(z, x, 1 - y, core))

    @pl.when(z > 0)
    def _():
        hello(device_at(z - 1, x, y, core))

    @pl.when(z < depth - 1)
    def _():
        hello(device_at(z + 1, x, y, core))

    above = jnp.where(z < depth - 1, 1, 0)
    below = jnp.where(z > 0, 1, 0)
    pl.semaphore_wait(barrier, 3 + above + below)


def remote(src, dst, send_sem, recv_sem, target):
    return pltpu.make_async_remote_copy(
        src_ref=src, dst_ref=dst, send_sem=send_sem, recv_sem=recv_sem,
        device_id=target, device_id_type=MESH)


class Gather:
    def __init__(self, kinds, depth, sources, outs, sems):
        self.kinds, self.depth, self.sources, self.outs = kinds, depth, sources, outs
        self.own_sem, self.send, self.got, self.sib_send, self.sib_got, self.diag_got = sems
        self.number = {a: n for n, a in enumerate(kinds)}
        z, x, y, core = place()
        self.z, self.x, self.y, self.core = z, x, y, core
        self.sibling = device_at(z, x, y, 1 - core)
        self.x_next, self.y_next = device_at(z, 1 - x, y, core), device_at(z, x, 1 - y, core)

    def to(self, way, a, z_at, x_at, y_at, target, part=None, src=None):
        n, k = self.number[a], (z_at * 2 + x_at) * 2 + y_at
        if part is None:
            spot_at, recv = spot(self.outs, a, z_at, x_at, y_at, self.core), self.got.at[n, k]
        else:
            spot_at = spot_part(self.outs, a, z_at, x_at, y_at, self.core, part)
            recv = self.diag_got.at[n, z_at, part]
        return remote(spot_at if src is None else src, spot_at, self.send.at[way, n, k], recv, target)

    def to_sibling(self, a, z_at, x_at, y_at, src=None, core=None):
        spot_at = spot(self.outs, a, z_at, x_at, y_at, self.core if core is None else core)
        n, k = self.number[a], (z_at * 2 + x_at) * 2 + y_at
        return remote(
            spot_at if src is None else src, spot_at, self.sib_send.at[n, k], self.sib_got.at[n, k], self.sibling
        )

    def own_copy(self, a):
        return pltpu.make_async_copy(
            self.sources[a], spot(self.outs, a, self.z, self.x, self.y, self.core), self.own_sem.at[self.number[a]]
        )

    def begin(self, kinds):
        z, x, y, core = self.z, self.x, self.y, self.core
        for a in kinds:
            source = self.sources[a]
            self.own_copy(a).start()

            @pl.when(z < self.depth - 1)
            def _():
                self.to(0, a, z, x, y, device_at(z + 1, x, y, core), src=source).start()

            @pl.when(z > 0)
            def _():
                self.to(1, a, z, x, y, device_at(z - 1, x, y, core), src=source).start()

            self.to(2, a, z, x, y, self.x_next, src=source).start()
            self.to(3, a, z, x, y, self.y_next, src=source).start()
            self.to_sibling(a, z, x, y, src=source).start()

    def sides(self, step, act):
        if step == 0:
            act(self.z)
            return
        for sign in (1, -1):
            z_at = self.z + sign * step

            @pl.when((z_at >= 0) & (z_at < self.depth))
            def _():
                act(z_at)

    def first(self, step):
        z, x, y, core = self.z, self.x, self.y, self.core

        def act(z_at):
            for a in self.kinds:
                self.to(0, a, z_at, x, y, self.sibling).wait_recv()

                @pl.when((z_at < z) & (z < self.depth - 1))
                def _():
                    self.to(0, a, z_at, x, y, device_at(z + 1, x, y, core)).start()

                @pl.when((z_at > z) & (z > 0))
                def _():
                    self.to(1, a, z_at, x, y, device_at(z - 1, x, y, core)).start()

                self.to(2, a, z_at, x, y, self.x_next).start()
                self.to(3, a, z_at, x, y, self.y_next).start()
                self.to_sibling(a, z_at, x, y).start()

        self.sides(step, act)

    def second(self, step):
        x, y = self.x, self.y

        def act(z_at):
            for a in self.kinds:
                self.to(0, a, z_at, 1 - x, y, self.sibling).wait_recv()
                self.to(3, a, z_at, 1 - x, y, self.y_next, 0).start()
                self.to_sibling(a, z_at, 1 - x, y).start()
                self.to(0, a, z_at, x, 1 - y, self.sibling).wait_recv()
                self.to(2, a, z_at, x, 1 - y, self.x_next, 1).start()
                self.to_sibling(a, z_at, x, 1 - y).start()

        self.sides(step, act)

    def third(self, step):
        x, y = self.x, self.y

        def act(z_at):
            for a in self.kinds:
                for part in range(2):
                    self.to(0, a, z_at, 1 - x, 1 - y, self.sibling, part).wait_recv()
                self.to_sibling(a, z_at, 1 - x, 1 - y).start()

        self.sides(step, act)

    def relays(self):
        for step in range(1, self.depth + 2):
            if step < self.depth:
                yield functools.partial(self.first, step)
            if 0 <= step - 1 < self.depth:
                yield functools.partial(self.second, step - 1)
            if 0 <= step - 2 < self.depth:
                yield functools.partial(self.third, step - 2)

    def arrive(self):
        for a in self.kinds:
            self.own_copy(a).wait()

        def wait(z_at, carry):
            for a in self.kinds:
                for x_at in range(2):
                    for y_at in range(2):
                        self.to_sibling(a, z_at, x_at, y_at, core=1 - self.core).wait_recv()
            return carry

        lax.fori_loop(0, self.depth, wait, 0)

    def finish(self):
        z, x, y = self.z, self.x, self.y

        def wait(z_at, carry):
            for a in self.kinds:

                @pl.when((z_at <= z) & (z < self.depth - 1))
                def _():
                    self.to(0, a, z_at, x, y, self.x_next).wait_send()

                @pl.when((z_at >= z) & (z > 0))
                def _():
                    self.to(1, a, z_at, x, y, self.x_next).wait_send()

                self.to(2, a, z_at, x, y, self.x_next).wait_send()
                self.to(3, a, z_at, x, y, self.y_next).wait_send()
                self.to(3, a, z_at, 1 - x, y, self.y_next, 0).wait_send()
                self.to(2, a, z_at, x, 1 - y, self.x_next, 1).wait_send()
                for x_at in range(2):
                    for y_at in range(2):
                        self.to_sibling(a, z_at, x_at, y_at).wait_send()
            return carry

        lax.fori_loop(0, self.depth, wait, 0)


def gather_sems(kinds, depth):
    count, spots = len(kinds), 4 * depth
    return [
        pltpu.SemaphoreType.DMA((count,)),
        pltpu.SemaphoreType.DMA((4, count, spots)),
        pltpu.SemaphoreType.DMA((count, spots)),
        pltpu.SemaphoreType.DMA((count, spots)),
        pltpu.SemaphoreType.DMA((count, spots)),
        pltpu.SemaphoreType.DMA((count, depth, 2)),
    ]


BY_Y = (EXPAND, EARLY)
FIRST_KINDS = (EXPAND, REDUCE, EARLY)
LAST_KINDS = (LATE,)
FRONT_KINDS = (SQUARE, EXPAND)
LATER_KINDS = (REDUCE,)


def front_kernel(fold, depth, keys_ref, gains_in, table_ref, square_f32, expand_f32, *refs):
    found, square_out, expand_out, keys_all, gains_all = refs[:5]
    refs = refs[1:]
    theirs, own, turned, rows, blocks, row_low, row_all = refs[4:11]
    square_in, expand_in, gains_ref = refs[11:14]
    gather_sem, refs = refs[14:20], refs[20:]
    pair_send, pair_recv, part_send, part_got, part_own, keys_send, keys_got, gains_send, gains_got, near_sem = refs
    dp_size, fsdp_size = lax.axis_size("dp"), lax.axis_size("fsdp")
    count = dp_size * fsdp_size
    me = lax.axis_index("dp") * fsdp_size + lax.axis_index("fsdp")
    z, x, y, core = place()
    sibling = device_at(z, x, y, 1 - core)
    gains_ref[...] = jnp.zeros_like(gains_ref)
    gains_ref[: gains_in.shape[0], : gains_in.shape[1]] = gains_in[...]
    expand_in[...] = expand_f32[...].astype(jnp.bfloat16)
    for c in range(2):
        for k in range(5):
            square_in[c, k] = square_f32[k, c * 48 : (c + 1) * 48].astype(jnp.bfloat16)
    greet_all(count, fsdp_size, me)

    def info_copies(k):
        target = lax.rem(me + k, count)
        device = (target // fsdp_size, lax.rem(target, fsdp_size))
        return (
            remote(keys_ref, keys_all.at[me], keys_send.at[k], keys_got.at[k], device),
            remote(gains_ref, gains_all.at[me], gains_send.at[k], gains_got.at[k], device),
        )

    def start_info(k, carry):
        for copy in info_copies(k):
            copy.start()
        return carry

    lax.fori_loop(1, count, start_info, 0)
    keys_all[me] = keys_ref[...]
    gains_all[me] = gains_ref[...]
    pair = remote(square_in.at[1 - core], theirs, pair_send, pair_recv, sibling)
    pair.start()
    gather = Gather(
        FRONT_KINDS, depth, {SQUARE: own, EXPAND: expand_in}, {SQUARE: square_out, EXPAND: expand_out}, gather_sem
    )
    gather.begin((EXPAND,))
    row = lax.broadcasted_iota(jnp.int32, (192, 384), 0)
    col = lax.broadcasted_iota(jnp.int32, (192, 384), 1)
    here = (row + core * 192 == col).astype(jnp.float32).astype(jnp.bfloat16)
    there = (row + (1 - core) * 192 == col).astype(jnp.float32).astype(jnp.bfloat16)
    pair.wait_recv()
    for k in range(5):
        block = jnp.dot(square_in[core, k], here, preferred_element_type=jnp.float32) + jnp.dot(
            theirs[k], there, preferred_element_type=jnp.float32
        )
        own[k] = block.astype(jnp.bfloat16)
    gather.begin((SQUARE,))
    turn_table(fold, table_ref, turned)

    def end_info(k, carry):
        for copy in info_copies(k):
            copy.wait()
        return carry

    lax.fori_loop(1, count, end_info, 0)
    key_rows = row_low.shape[0] // count

    def split_row(k, carry):
        row_low[pl.ds(pl.multiple_of(k * key_rows, 8), key_rows)] = keys_all[k, :key_rows] >> 2
        return carry

    lax.fori_loop(0, count, split_row, 0)
    near = pltpu.make_async_copy(row_low, row_all, near_sem)
    near.start()
    near.wait()

    def find(target):
        keys = keys_all[target]
        group = jnp.concatenate([keys[r : r + 1] for r in range(key_rows)], axis=1) & 3

        def fetch(r, carry):
            line = target * key_rows + r
            start = pl.multiple_of(r * LANES, LANES)
            for k in range(LANES):
                rows[pl.ds(start + k, 1), :] = turned[pl.ds(row_all[line, k], 1), :]
            return carry

        lax.fori_loop(0, key_rows, fetch, 0)
        return pick_group(rows, group, table_ref.shape[0])

    def part_copy(k):
        target = lax.rem(me + k, count)
        device = (target // fsdp_size, lax.rem(target, fsdp_size))
        return remote(blocks.at[target], found.at[me], part_send.at[k], part_got.at[k], device)

    def serve(k, carry):
        target = lax.rem(me + k, count)
        blocks[target] = find(target)
        part_copy(k).start()
        return carry

    relays = list(gather.relays())
    done = 1
    for n, relay in enumerate(relays):
        until = 1 + ((n + 1) * (count - 1)) // len(relays)
        lax.fori_loop(done, until, serve, 0)
        done = until
        relay()
    blocks[me] = find(me)
    own_part = pltpu.make_async_copy(blocks.at[me], found.at[me], part_own)
    own_part.start()
    pair.wait_send()
    gather.arrive()
    gather.finish()
    own_part.wait()

    def end_part(k, carry):
        part_copy(k).wait()
        return carry

    lax.fori_loop(1, count, end_part, 0)


def run_front(keys, gains, tokens, table, square, expand, call_id):
    depth = lax.axis_size("dp") // 2
    count = lax.axis_size("dp") * lax.axis_size("fsdp")
    feats, vocab = table.shape
    fold = fold_rows(vocab)
    blocks = (count, 2 * feats, tokens // 2)
    whole = pl.BlockSpec(memory_space=pltpu.VMEM)
    anywhere = pl.BlockSpec(memory_space=pl.ANY)
    many = pltpu.SemaphoreType.DMA((count,))
    return pl.pallas_call(
        functools.partial(front_kernel, fold, depth),
        out_shape=[
            jax.ShapeDtypeStruct(blocks, jnp.bfloat16),
            jax.ShapeDtypeStruct((5, 768, 768), jnp.bfloat16),
            jax.ShapeDtypeStruct((768, 3072), jnp.bfloat16),
            jax.ShapeDtypeStruct((count,) + keys.shape, keys.dtype),
            jax.ShapeDtypeStruct((count, 8, LANES), gains.dtype),
        ],
        in_specs=[whole] * 5,
        out_specs=[anywhere] * 3 + [whole] * 2,
        scratch_shapes=[
            pltpu.VMEM((5, 48, 192), jnp.bfloat16),
            pltpu.VMEM((5, 48, 384), jnp.bfloat16),
            pltpu.VMEM((fold + 8, LANES), jnp.float32),
            pltpu.VMEM((tokens, LANES), jnp.float32),
            pltpu.VMEM(blocks, jnp.bfloat16),
            pltpu.VMEM((count * tokens // LANES, LANES), jnp.int32),
            pltpu.SMEM((count * tokens // LANES, LANES), jnp.int32),
            pltpu.VMEM((2, 5, 48, 192), jnp.bfloat16),
            pltpu.VMEM((96, 768), jnp.bfloat16),
            pltpu.VMEM((8, LANES), jnp.float32),
        ]
        + gather_sems(FRONT_KINDS, depth)
        + [pltpu.SemaphoreType.DMA, pltpu.SemaphoreType.DMA]
        + [many, many, pltpu.SemaphoreType.DMA]
        + [many] * 4
        + [pltpu.SemaphoreType.DMA],
        compiler_params=pltpu.CompilerParams(
            collective_id=call_id, has_side_effects=True, vmem_limit_bytes=VMEM_CAP
        ),
        name="front",
    )(keys, gains, table, square, expand)


class Reduction:
    def __init__(self, kinds, depth, grads, outs, work, buffers, sems):
        self.kinds, self.depth, self.grads, self.outs, self.own_work = kinds, depth, grads, outs, work
        count = len(kinds)
        self.paired, self.step_one, self.from_x, self.from_y, self.from_z = [
            dict(zip(kinds, buffers[k * count : (k + 1) * count])) for k in range(5)
        ]
        self.load_sem, self.pair_send, self.pair_got, self.send, self.one_got = sems[:5]
        self.x_got, self.y_got, self.z_got = sems[5:8]
        self.number = {a: n for n, a in enumerate(kinds)}
        z, x, y, core = place()
        self.z, self.x, self.y, self.core = z, x, y, core
        self.sibling = device_at(z, x, y, 1 - core)
        self.x_next, self.y_next = device_at(z, 1 - x, y, core), device_at(z, x, 1 - y, core)

    def piece(self, ref, a, z_at, x_at, y_at):
        i = z_at * 2 + x_at
        if a == EXPAND:
            return ref.at[y_at, pl.ds(pl.multiple_of(i * 96, 16), 96)]
        if a == REDUCE:
            return ref.at[y_at, :, pl.ds(pl.multiple_of(i * 384, 128), 384)]
        return ref.at[i, :, :, pl.ds(pl.multiple_of(y_at * 384, 128), 384)]

    def work(self, a, z_at, x_at, y_at):
        if a in SPANS:
            return spot(self.grads, a, z_at, x_at, y_at, self.core)
        return self.piece(self.own_work[a], a, z_at, x_at, y_at)

    def half(self, a, y_at, core):
        column = y_at * 2 + core
        if a == EXPAND:
            return self.grads[a].at[:, pl.ds(pl.multiple_of(column * 768, 128), 768)]
        return self.grads[a].at[pl.ds(pl.multiple_of(column * 192, 16), 192)]

    def load(self, a, y_at):
        return pltpu.make_async_copy(
            self.half(a, y_at, self.core), self.own_work[a].at[y_at], self.load_sem.at[self.number[a], y_at]
        )

    def pair(self, a, at):
        n = self.number[a]
        if a in SPANS:
            source = self.grads[SQUARE].at[
                pl.ds(*SPANS[a]), pl.ds(pl.multiple_of(at * 96 + (1 - self.core) * 48, 16), 48)
            ]
        else:
            source = self.half(a, at, 1 - self.core)
        return remote(source, self.paired[a].at[at], self.pair_send.at[n, at], self.pair_got.at[n, at], self.sibling)

    def each_pair(self, a, act):
        if a not in SPANS:
            act(1 - self.y)
            act(self.y)
            return

        def one(i, carry):
            act(i)
            return carry

        lax.fori_loop(0, 2 * self.depth, one, 0)

    def sides(self, step, act):
        if step == 0:
            act(self.z)
            return
        for sign in (1, -1):
            z_at = self.z + sign * step

            @pl.when((z_at >= 0) & (z_at < self.depth))
            def _():
                act(z_at)

    def begin(self, kinds):
        for a in kinds:

            def start(at):
                if a not in SPANS:
                    self.load(a, at).start()
                self.pair(a, at).start()

            self.each_pair(a, start)

    def ready(self, last):
        for a in self.kinds:
            if a in SPANS:
                if not last:
                    self.each_pair(a, lambda at: self.pair(a, at).wait_recv())
            else:
                y_at = self.y if last else 1 - self.y
                self.load(a, y_at).wait()
                self.pair(a, y_at).wait_recv()

    def total(self, a, z_at, x_at, y_at, extra=()):
        here = self.work(a, z_at, x_at, y_at)
        paired = self.piece(self.paired[a], a, z_at, x_at, y_at)

        value = here[...] + paired[...]
        for buffer in extra:
            value = value + buffer[...]
        here[...] = value

    def diag_copy(self, a, z_at):
        n = self.number[a]
        return remote(
            self.work(a, z_at, 1 - self.x, 1 - self.y),
            self.step_one[a].at[z_at],
            self.send.at[0, n, z_at],
            self.one_got.at[n, z_at],
            self.y_next if a in BY_Y else self.x_next,
        )

    def diag(self, step):
        def act(z_at):
            for a in self.kinds:
                self.total(a, z_at, 1 - self.x, 1 - self.y)
                self.diag_copy(a, z_at).start()

        if step == self.depth - 1:
            self.ready(False)
        self.sides(step, act)

    def x_copy(self, a, z_at):
        n = self.number[a]
        return remote(
            self.work(a, z_at, 1 - self.x, self.y),
            self.from_x[a].at[z_at],
            self.send.at[2, n, z_at],
            self.x_got.at[n, z_at],
            self.x_next,
        )

    def y_copy(self, a, z_at):
        n = self.number[a]
        return remote(
            self.work(a, z_at, self.x, 1 - self.y),
            self.from_y[a].at[z_at],
            self.send.at[3, n, z_at],
            self.y_got.at[n, z_at],
            self.y_next,
        )

    def columns(self, step):
        x, y = self.x, self.y

        def act(z_at):
            for a in self.kinds:
                received = [self.step_one[a].at[z_at]]
                self.diag_copy(a, z_at).wait_recv()
                self.total(a, z_at, 1 - x, y, received if a in BY_Y else ())
                self.x_copy(a, z_at).start()
                self.total(a, z_at, x, 1 - y, () if a in BY_Y else received)
                self.y_copy(a, z_at).start()

        if step == self.depth - 1:
            self.ready(True)
        self.sides(step, act)

    def z_copy(self, a, z_at, side, target):
        n = self.number[a]
        return remote(
            self.work(a, z_at, self.x, self.y),
            self.from_z[a].at[side, z_at],
            self.send.at[4, n, z_at],
            self.z_got.at[n, side, z_at],
            target,
        )

    def line(self, step, keep=None):
        z, x, y, core, depth = self.z, self.x, self.y, self.core, self.depth

        def act(z_at):
            for a in self.kinds:
                self.x_copy(a, z_at).wait_recv()
                self.y_copy(a, z_at).wait_recv()
                across = [self.from_x[a].at[z_at], self.from_y[a].at[z_at]]
                if step > 0:
                    upward = z_at > z
                    before = (upward & (z > 0)) | (jnp.logical_not(upward) & (z < depth - 1))
                    side = jnp.where(upward, 0, 1)

                    @pl.when(before)
                    def _():
                        self.z_copy(a, z_at, side, self.sibling).wait_recv()
                        self.total(a, z_at, x, y, across + [self.from_z[a].at[side, z_at]])

                    @pl.when(jnp.logical_not(before))
                    def _():
                        self.total(a, z_at, x, y, across)

                    @pl.when(upward)
                    def _():
                        self.z_copy(a, z_at, 0, device_at(z + 1, x, y, core)).start()

                    @pl.when(jnp.logical_not(upward))
                    def _():
                        self.z_copy(a, z_at, 1, device_at(z - 1, x, y, core)).start()
                else:
                    for side in range(2):
                        present = (z > 0) if side == 0 else (z < depth - 1)

                        @pl.when(present)
                        def _():
                            self.z_copy(a, z, side, self.sibling).wait_recv()

                        @pl.when(jnp.logical_not(present))
                        def _():
                            self.from_z[a][side, z] = jnp.zeros(BLOCKS[a], jnp.bfloat16)

                    here, paired = self.work(a, z, x, y), self.piece(self.paired[a], a, z, x, y)

                    def finish(k, carry):
                        value = block_step(here, a, k)[...].astype(jnp.float32)
                        for buffer in [paired] + across + [self.from_z[a].at[0, z], self.from_z[a].at[1, z]]:
                            value = value + block_step(buffer, a, k)[...].astype(jnp.float32)
                        if a in SPANS:
                            spare, at = self.outs[3], k + SPANS[a][0]
                            low, high = value[:, :192], pltpu.roll(value, 192, 1)[:, :192]
                            self.outs[SQUARE][core, at] = jnp.where(core == 0, low, high)
                            spare[at] = jnp.where(core == 0, high, low)
                        else:
                            block_step(self.outs[a], a, k)[...] = value
                        return carry

                    lax.fori_loop(0, STEPS[a], finish, 0)

        self.sides(step, act)

    def groups(self):
        rounds = list(range(self.depth - 1, -1, -1))
        for k in range(self.depth + 2):
            group = []
            if k < self.depth:
                group.append((self.diag, rounds[k]))
            if 0 <= k - 1 < self.depth:
                group.append((self.columns, rounds[k - 1]))
            if 0 <= k - 2 < self.depth:
                group.append((self.line, rounds[k - 2]))
            yield group

    def finish(self):
        def wait(z_at, carry):
            for a in self.kinds:
                self.diag_copy(a, z_at).wait_send()
                self.x_copy(a, z_at).wait_send()
                self.y_copy(a, z_at).wait_send()

                @pl.when(z_at != self.z)
                def _():
                    self.z_copy(a, z_at, 0, self.sibling).wait_send()
            return carry

        lax.fori_loop(0, self.depth, wait, 0)
        for a in self.kinds:
            self.each_pair(a, lambda at: self.pair(a, at).wait_send())


def pair_shape(a, depth):
    if a == EXPAND:
        return (2, depth * 192, 768)
    if a == REDUCE:
        return (2, 192, depth * 768)
    return (2 * depth, SPANS[a][1], 48, 768)


def reduction_scratch(kinds, depth):
    def buffers(*lead):
        return [pltpu.VMEM(lead + BLOCKS[a], jnp.bfloat16) for a in kinds]

    count = len(kinds)
    spots = pltpu.SemaphoreType.DMA((count, 2 * depth))
    return (
        [pltpu.VMEM(pair_shape(a, depth), jnp.bfloat16) for a in kinds]
        + buffers(depth) + buffers(depth) + buffers(depth) + buffers(2, depth),
        [
            spots,
            spots,
            spots,
            pltpu.SemaphoreType.DMA((5, count, depth)),
            pltpu.SemaphoreType.DMA((count, depth)),
            pltpu.SemaphoreType.DMA((count, depth)),
            pltpu.SemaphoreType.DMA((count, depth)),
            pltpu.SemaphoreType.DMA((count, 2, depth)),
        ],
    )


TILE = 128
PAIRS = HEADS // 2
GELU_IN = (2.0 / np.pi) ** 0.5


def dot_nn(left, right):
    return jnp.dot(left, right, preferred_element_type=jnp.float32)


def dot_nt(left, right):
    return lax.dot_general(left, right, (((1,), (1,)), ((), ())), preferred_element_type=jnp.float32)


def dot_tn(left, right):
    return lax.dot_general(left, right, (((0,), (0,)), ((), ())), preferred_element_type=jnp.float32)


def rows_at(index, size):
    return pl.ds(pl.multiple_of(index * size, size), size)


def split_heads(block):
    low = lax.broadcasted_iota(jnp.int32, block.shape, 1) < HEAD
    wide = block.astype(jnp.float32)
    first = jnp.where(low, wide, 0.0).astype(jnp.bfloat16)
    second = jnp.where(low, 0.0, wide).astype(jnp.bfloat16)
    return jnp.concatenate([first, second], axis=0)


def join_heads(stacked):
    return jnp.concatenate([stacked[:TILE], stacked[TILE:]], axis=1)


def pair_probs(query, keys_here, bias, mask):
    scores = dot_nt(split_heads(query), keys_here) * HEAD ** (-0.5) + bias
    scores = scores + mask
    raised = jnp.exp(scores - jnp.max(scores, axis=1, keepdims=True))
    return raised / jnp.sum(raised, axis=1, keepdims=True)


def pair_bias(bias_ref, pair):
    return jnp.concatenate([bias_ref[2 * pair], bias_ref[2 * pair + 1]], axis=0)


def tile_mask(mask_ref, tile):
    mask = mask_ref[tile]
    return jnp.concatenate([mask, mask], axis=0)


def hot_rows(rank_ref, rows, slots, first=0):
    place = lax.broadcasted_iota(jnp.int32, (rows.size, slots), 1) + first
    return (rank_ref[rows, :1] == place).astype(jnp.float32).astype(jnp.bfloat16)


def norm_rows(values, gain):
    scale = lax.rsqrt(jnp.mean(values * values, axis=1, keepdims=True) + NORM_EPS)
    return values * scale * gain


def gelu_parts(pre):
    inner = GELU_IN * (pre + 0.044715 * pre * pre * pre)
    return jnp.tanh(inner)


def forward_steps(
    found_ref, rank_ref, square_ref, gains_ref, bias_ref, mask_ref, pool_ref, length_ref,
    start_ref, query_ref, key_ref, value_ref, mixed_ref, middle_ref, ending_ref, low_ref, pooled_ref, embed_ref,
    inverse_ref, normed, pooled_sum, wide_found, low_found, expand_ref, reduce_ref, between, before_feed, need,
):
    between = list(between)

    def relay(count):
        for _ in range(min(count, len(between))):
            between.pop(0)()

    tokens = start_ref.shape[0]
    big = 512
    feats, half = found_ref.shape[1] // 2, found_ref.shape[2]
    need(0)

    def assemble(p, carry):
        block = found_ref[p].astype(jnp.float32)
        at = pl.ds(pl.multiple_of(p * feats, 8), feats)
        wide_found[at, :half] = block[:feats]
        wide_found[at, half:] = block[feats:]
        return carry

    lax.fori_loop(0, found_ref.shape[0], assemble, 0)
    low_found[...] = wide_found[...].astype(jnp.bfloat16)

    def begin(r, carry):
        rows = rows_at(r, 256)
        start = dot_nt(hot_rows(rank_ref, rows, tokens), low_found[...])
        start_ref[rows, :] = start.astype(jnp.bfloat16)
        normed[rows, :] = norm_rows(start, gains_ref[0:1]).astype(jnp.bfloat16)
        return carry

    lax.fori_loop(0, tokens // 256, begin, 0)
    relay(1)
    need(1)
    for k, target in enumerate((query_ref, key_ref, value_ref)):

        def project(r, carry):
            rows = rows_at(r, big)
            target[rows, :] = dot_nn(normed[rows, :], square_ref[k]).astype(jnp.bfloat16)
            return carry

        lax.fori_loop(0, tokens // big, project, 0)
        relay(1)

    def attend(t, carry):
        rows = rows_at(t, TILE)
        mask = tile_mask(mask_ref, t)
        for pair in range(PAIRS):
            lanes = pl.ds(pair * TILE, TILE)
            probs = pair_probs(query_ref[rows, lanes], key_ref[rows, lanes], pair_bias(bias_ref, pair), mask)
            mixed = dot_nn(join_heads(probs).astype(jnp.bfloat16), split_heads(value_ref[rows, lanes]))
            mixed_ref[rows, lanes] = mixed.astype(jnp.bfloat16)
        return carry

    tiles = tokens // TILE
    need(2)
    if between:
        for t in range(tiles):
            lax.fori_loop(t, t + 1, attend, 0)
            relay(1)
    else:
        lax.fori_loop(0, tiles, attend, 0)

    def merge(r, carry):
        rows = rows_at(r, big)
        middle = start_ref[rows, :].astype(jnp.float32) + dot_nn(mixed_ref[rows, :], square_ref[3])
        middle_ref[rows, :] = middle
        ending_ref[rows, :] = middle
        normed[rows, :] = norm_rows(middle, gains_ref[1:2]).astype(jnp.bfloat16)
        return carry

    lax.fori_loop(0, tokens // big, merge, 0)
    relay(len(between))
    before_feed()
    wide = expand_ref.shape[1]

    def feed(c, carry):
        lanes = rows_at(c, D)

        def rows_of(r, inner):
            rows = rows_at(r, big)
            pre = dot_nn(normed[rows, :], expand_ref[:, lanes])
            act = (0.5 * pre * (1.0 + gelu_parts(pre))).astype(jnp.bfloat16)
            ending_ref[rows, :] += dot_nt(act, reduce_ref[:, lanes])
            return inner

        return lax.fori_loop(0, tokens // big, rows_of, carry)

    lax.fori_loop(0, wide // D, feed, 0)
    pooled_sum[...] = jnp.zeros_like(pooled_sum)

    def pool(r, carry):
        rows = rows_at(r, 256)
        output = norm_rows(ending_ref[rows, :], gains_ref[2:3])
        pooled_sum[...] += jnp.dot(
            pool_ref[:, rows], output, precision=HIGHEST, preferred_element_type=jnp.float32
        )
        return carry

    lax.fori_loop(0, tokens // 256, pool, 0)
    pooled = (pooled_sum[...] / length_ref[:, :1]).astype(jnp.bfloat16)
    pooled_ref[...] = pooled
    projected = dot_nn(pooled, square_ref[4])
    inverse = lax.rsqrt(jnp.sum(projected * projected, axis=1, keepdims=True) + NORM_EPS)
    embeds = projected * inverse
    embed_ref[...] = embeds
    low_ref[...] = embeds.astype(jnp.bfloat16)
    inverse_ref[...] = jnp.broadcast_to(inverse, inverse_ref.shape)


def forward_kernel(*refs):
    ins, expand_ref, reduce_ref, rest = refs[:8], refs[8], refs[9], refs[10:]
    forward_steps(*ins, *rest, expand_ref, reduce_ref, [], lambda: None, lambda stage: None)


FORWARD_STAGES = ((0, 1), (2,), (4, 5), (8,))


def relayed_forward_kernel(depth, *refs):
    given, reduce_in = list(refs[:9]), refs[9]
    outs, reduce_out = refs[10:21], refs[21]
    steps, reduce_all = refs[22:26], refs[26]
    sems, save_sem = refs[27:33], refs[33]
    need = stage_loads(given, FORWARD_STAGES, refs[34:40], refs[40])
    greet_neighbours(depth)
    gather = Gather(LATER_KINDS, depth, {REDUCE: reduce_in}, {REDUCE: reduce_all}, sems)
    gather.begin(LATER_KINDS)
    save = pltpu.make_async_copy(reduce_all, reduce_out, save_sem)

    def before_feed():
        need(3)
        gather.arrive()
        save.start()

    forward_steps(*given[:8], *outs, *steps, given[8], reduce_all, gather.relays(), before_feed, need)
    gather.finish()
    save.wait()


def stage_loads(given, stages, homes, sem):
    loads, n = [], 0
    for stage in stages:
        group = []
        for at in stage:
            group.append(pltpu.make_async_copy(given[at], homes[n], sem.at[n]))
            given[at] = homes[n]
            n += 1
        loads.append(group)
    for group in loads:
        for load in group:
            load.start()

    def need(stage):
        for load in loads[stage]:
            load.wait()

    return need


def stage_specs(arrays, stages):
    whole = pl.BlockSpec(memory_space=pltpu.VMEM)
    anywhere = pl.BlockSpec(memory_space=pl.ANY)
    order = [at for stage in stages for at in stage]
    specs = [anywhere if at in order else whole for at in range(len(arrays))]
    homes = [pltpu.VMEM(arrays[at].shape, arrays[at].dtype) for at in order]
    return specs, homes, pltpu.SemaphoreType.DMA((len(order),))


def forward_outs(tokens, seqs):
    flat = jax.ShapeDtypeStruct((tokens, D), jnp.bfloat16)
    full = jax.ShapeDtypeStruct((tokens, D), jnp.float32)
    few = jax.ShapeDtypeStruct((seqs, D), jnp.bfloat16)
    return [
        flat, flat, flat, flat, flat, full, full, few, few,
        jax.ShapeDtypeStruct((seqs, D), jnp.float32),
        jax.ShapeDtypeStruct((seqs, LANES), jnp.float32),
    ]


def forward_scratch(tokens, seqs):
    return [
        pltpu.VMEM((tokens, D), jnp.bfloat16),
        pltpu.VMEM((seqs, D), jnp.float32),
        pltpu.VMEM((D, tokens), jnp.float32),
        pltpu.VMEM((D, tokens), jnp.bfloat16),
    ]


def run_forward(ins, expand, reduce_turned):
    tokens, seqs = ins[1].shape[0], ins[6].shape[0]
    return pl.pallas_call(
        forward_kernel,
        out_shape=forward_outs(tokens, seqs),
        scratch_shapes=forward_scratch(tokens, seqs),
        compiler_params=pltpu.CompilerParams(vmem_limit_bytes=VMEM_CAP),
        name="layer_forward",
    )(*ins, expand, reduce_turned)


def run_relayed_forward(ins, expand, reduce_piece, call_id):
    depth = lax.axis_size("dp") // 2
    tokens, seqs = ins[1].shape[0], ins[6].shape[0]
    weight = (768, 3072)
    outs = forward_outs(tokens, seqs)
    whole = pl.BlockSpec(memory_space=pltpu.VMEM)
    anywhere = pl.BlockSpec(memory_space=pl.ANY)
    specs, homes, load_sem = stage_specs((*ins, expand), FORWARD_STAGES)
    return pl.pallas_call(
        functools.partial(relayed_forward_kernel, depth),
        out_shape=outs + [jax.ShapeDtypeStruct(weight, jnp.bfloat16)],
        in_specs=specs + [whole],
        out_specs=[whole] * len(outs) + [anywhere],
        scratch_shapes=forward_scratch(tokens, seqs)
        + [pltpu.VMEM(weight, jnp.bfloat16)]
        + gather_sems(LATER_KINDS, depth)
        + [pltpu.SemaphoreType.DMA]
        + homes
        + [load_sem],
        compiler_params=pltpu.CompilerParams(
            collective_id=call_id, has_side_effects=True, vmem_limit_bytes=VMEM_CAP
        ),
        name="layer_forward",
    )(*ins, expand, reduce_piece)


def norm_back_rows(values, gain, grad):
    scale = lax.rsqrt(jnp.mean(values * values, axis=1, keepdims=True) + NORM_EPS)
    weighted = grad * gain
    inner = jnp.mean(weighted * values, axis=1, keepdims=True)
    through = scale * weighted - values * (scale * scale * scale * inner)
    return through, jnp.sum(grad * values * scale, axis=0, keepdims=True)


def feed_norms(middle_ref, gains_ref, normed, normed_turned):
    def step(r, carry):
        rows = rows_at(r, 256)
        middle_normed = norm_rows(middle_ref[rows, :], gains_ref[1:2])
        normed[rows, :] = middle_normed.astype(jnp.bfloat16)
        normed_turned[:, rows] = middle_normed.T.astype(jnp.bfloat16)
        return carry

    lax.fori_loop(0, middle_ref.shape[0] // 256, step, 0)


def feed_back_steps(
    grads, embed_ref, inverse_ref, pool_ref, length_ref, last_ref, middle_ref, ending_ref, expand_ref,
    reduce_ref, gains_ref,
    grad_expand_ref, grad_reduce_ref, grad_middle_ref, grad_proj_ref, grad_gains_ref,
    normed, normed_turned, end_low, end_turned, back, before_feed, saved,
):
    tokens = middle_ref.shape[0]
    embeds = embed_ref[...]
    grad_proj = inverse_ref[:, :1] * (grads - embeds * jnp.sum(grads * embeds, axis=1, keepdims=True))
    grad_proj = grad_proj.astype(jnp.bfloat16)
    grad_proj_ref[...] = grad_proj
    grad_pooled = dot_nt(grad_proj, last_ref[...]) / length_ref[:, :1]
    grad_gains_ref[...] = jnp.zeros_like(grad_gains_ref)

    def begin(r, carry):
        rows = rows_at(r, 256)
        grad_out = lax.dot_general(
            pool_ref[:, rows], grad_pooled, (((0,), (0,)), ((), ())), precision=HIGHEST,
            preferred_element_type=jnp.float32,
        )
        through, gain = norm_back_rows(ending_ref[rows, :], gains_ref[2:3], grad_out)
        grad_gains_ref[2:3] += gain
        grad_middle_ref[rows, :] = through
        end_low[rows, :] = through.astype(jnp.bfloat16)
        end_turned[:, rows] = through.T.astype(jnp.bfloat16)
        return carry

    lax.fori_loop(0, tokens // 256, begin, 0)
    before_feed()
    back[...] = jnp.zeros_like(back)
    wide = expand_ref.shape[1]
    step = FEED_STEP

    def feed(c, carry):
        lanes = rows_at(c, step)
        pre = dot_nn(normed[...], expand_ref[:, lanes])
        grad_act = dot_nn(end_low[...], reduce_ref[:, lanes])
        turn = gelu_parts(pre)
        act = (0.5 * pre * (1.0 + turn)).astype(jnp.bfloat16)
        slope = 0.5 * (1.0 + turn) + 0.5 * pre * (1.0 - turn * turn) * GELU_IN * (1.0 + 3.0 * 0.044715 * pre * pre)
        grad_pre = (grad_act * slope).astype(jnp.bfloat16)
        grad_reduce_ref[:, lanes] = dot_nn(end_turned[...], act).astype(jnp.bfloat16)
        grad_expand_ref[:, lanes] = dot_nn(normed_turned[...], grad_pre).astype(jnp.bfloat16)
        back[...] += dot_nt(grad_pre, expand_ref[:, lanes])
        saved(c)
        return carry

    lax.fori_loop(0, wide // step, feed, 0)

    def end(r, carry):
        rows = rows_at(r, 256)
        through, gain = norm_back_rows(middle_ref[rows, :], gains_ref[1:2], back[rows, :])
        grad_gains_ref[1:2] += gain
        grad_middle_ref[rows, :] += through
        return carry

    lax.fori_loop(0, tokens // 256, end, 0)


def feed_back_kernel(*refs):
    grads, (embed, inverse, pool, length, last, middle, ending, expand, reduce_turned, gains), rest = (
        refs[0], refs[1:11], refs[11:]
    )
    feed_norms(middle, gains, rest[5], rest[6])
    feed_back_steps(
        grads[...], embed, inverse, pool, length, last.at[0], middle, ending, expand, reduce_turned, gains, *rest,
        lambda: None, lambda c: None,
    )


FEED_STEP = 384


def loss_feed_kernel(query_rows, nli_rows, *refs):
    low_ref, negative_ref, scale_ref, embed_ref, inverse_ref, pool_ref, length_ref, gains_ref = refs[:8]
    square_hbm, middle_hbm, ending_hbm, expand_hbm, reduce_hbm = refs[8:13]
    grad_expand_out, grad_reduce_out, grad_middle_ref, grad_proj_ref, grad_gains_ref, stats_ref = refs[13:19]
    normed, normed_turned, end_low, end_turned, back = refs[19:24]
    last, middle, ending, expand, reduce_turned, grad_expand, grad_reduce = refs[24:31]
    everyone, grad_sims, turned_sims = refs[31:34]
    exchange_sems, load_sem, save_sem = refs[34:38], refs[38], refs[39]
    pairs = (
        (middle_hbm, middle), (ending_hbm, ending), (square_hbm.at[4], last), (expand_hbm, expand),
        (reduce_hbm, reduce_turned),
    )
    loads = [pltpu.make_async_copy(src, dst, load_sem.at[n]) for n, (src, dst) in enumerate(pairs)]
    for load in loads:
        load.start()

    def meanwhile():
        loads[0].wait()
        feed_norms(middle, gains_ref, normed, normed_turned)

    me = share_chips(low_ref, everyone, *exchange_sems, meanwhile)
    grads = loss_steps(
        query_rows, nli_rows, me, low_ref.shape[0], negative_ref, scale_ref, stats_ref, everyone, grad_sims,
        turned_sims,
    )
    loads[1].wait()
    loads[2].wait()

    def before_feed():
        loads[3].wait()
        loads[4].wait()

    def saves(c):
        lanes = rows_at(c, FEED_STEP)
        return (
            pltpu.make_async_copy(grad_expand.at[:, lanes], grad_expand_out.at[:, lanes], save_sem.at[0, c]),
            pltpu.make_async_copy(grad_reduce.at[:, lanes], grad_reduce_out.at[:, lanes], save_sem.at[1, c]),
        )

    def saved(c):
        for save in saves(c):
            save.start()

    feed_back_steps(
        grads, embed_ref, inverse_ref, pool_ref, length_ref, last, middle, ending, expand, reduce_turned, gains_ref,
        grad_expand, grad_reduce, grad_middle_ref, grad_proj_ref, grad_gains_ref,
        normed, normed_turned, end_low, end_turned, back, before_feed, saved,
    )

    def end(c, carry):
        for save in saves(c):
            save.wait()
        return carry

    lax.fori_loop(0, expand.shape[1] // FEED_STEP, end, 0)


def feed_scratch(tokens):
    low = jnp.bfloat16
    return [
        pltpu.VMEM((tokens, D), low),
        pltpu.VMEM((D, tokens), low),
        pltpu.VMEM((tokens, D), low),
        pltpu.VMEM((D, tokens), low),
        pltpu.VMEM((tokens, D), jnp.float32),
    ]


def run_loss_feed(
    embeds_low, negative, log_scale, embeds, inverse, pool, lengths, gains, square, middle, ending, expand,
    reduce_turned, query_rows, nli_rows, call_id,
):
    count = lax.axis_size("dp") * lax.axis_size("fsdp")
    tokens, seqs = middle.shape[0], pool.shape[0]
    low = jnp.bfloat16
    whole = pl.BlockSpec(memory_space=pltpu.VMEM)
    anywhere = pl.BlockSpec(memory_space=pl.ANY)
    few = pltpu.SemaphoreType.DMA((count // 2,))
    weight = pltpu.VMEM(expand.shape, low)
    pairs = pltpu.VMEM((count * seqs, count * seqs), jnp.float32)
    return pl.pallas_call(
        functools.partial(loss_feed_kernel, query_rows, nli_rows),
        out_shape=[
            jax.ShapeDtypeStruct(expand.shape, low),
            jax.ShapeDtypeStruct(reduce_turned.shape, low),
            jax.ShapeDtypeStruct((tokens, D), jnp.float32),
            jax.ShapeDtypeStruct((seqs, D), low),
            jax.ShapeDtypeStruct((8, D), jnp.float32),
            jax.ShapeDtypeStruct((8, LANES), jnp.float32),
        ],
        in_specs=[whole] * 8 + [anywhere] * 5,
        out_specs=[anywhere] * 2 + [whole] * 4,
        scratch_shapes=feed_scratch(tokens)
        + [
            pltpu.VMEM((D, D), low),
            pltpu.VMEM((tokens, D), jnp.float32),
            pltpu.VMEM((tokens, D), jnp.float32),
            weight, weight, weight, weight,
            pltpu.VMEM((count, seqs, D), low),
            pairs, pairs,
            few, few, few, few,
            pltpu.SemaphoreType.DMA((5,)),
            pltpu.SemaphoreType.DMA((2, expand.shape[1] // FEED_STEP)),
        ],
        compiler_params=pltpu.CompilerParams(
            collective_id=call_id, has_side_effects=True, vmem_limit_bytes=VMEM_CAP
        ),
        name="loss_feed",
    )(
        embeds_low, negative, log_scale, embeds, inverse, pool, lengths, gains, square, middle, ending, expand,
        reduce_turned,
    )


def run_feed_back(grad_embed, embeds, inverse, pool, lengths, square, middle, ending, expand, reduce_turned, gains):
    tokens = middle.shape[0]
    seqs = pool.shape[0]
    low = jnp.bfloat16
    whole = pl.BlockSpec(memory_space=pltpu.VMEM)
    return pl.pallas_call(
        feed_back_kernel,
        grid=(1,),
        out_shape=[
            jax.ShapeDtypeStruct(expand.shape, low),
            jax.ShapeDtypeStruct(reduce_turned.shape, low),
            jax.ShapeDtypeStruct((tokens, D), jnp.float32),
            jax.ShapeDtypeStruct((seqs, D), low),
            jax.ShapeDtypeStruct((8, D), jnp.float32),
        ],
        in_specs=[whole] * 5
        + [pl.BlockSpec((1, D, D), lambda i: (4, 0, 0))]
        + [whole] * 5,
        out_specs=[whole] * 5,
        scratch_shapes=[
            pltpu.VMEM((tokens, D), low),
            pltpu.VMEM((D, tokens), low),
            pltpu.VMEM((tokens, D), low),
            pltpu.VMEM((D, tokens), low),
            pltpu.VMEM((tokens, D), jnp.float32),
        ],
        compiler_params=pltpu.CompilerParams(vmem_limit_bytes=VMEM_CAP),
        name="feed_backward",
    )(grad_embed, embeds, inverse, pool, lengths, square, middle, ending, expand, reduce_turned, gains)


def attend_back_steps(
    grad_middle_ref, grad_proj_ref, pooled_ref, start_ref, query_ref, key_ref, value_ref, mixed_ref,
    square_ref, gains_ref, bias_ref, mask_ref, rank_ref,
    grad_square_ref, grad_score_ref, grad_gain_ref, grad_mixed, turned, grad_query, grad_key, grad_value,
    turned_half, between, early_done, squares_done, put, need,
):
    tokens = start_ref.shape[0]
    big = 512
    need(0)
    grad_square_ref[4] = dot_tn(pooled_ref[...], grad_proj_ref[...]).astype(jnp.bfloat16)

    def begin(r, carry):
        rows = rows_at(r, big)
        grad_mixed[rows, :] = dot_nt(grad_middle_ref[rows, :].astype(jnp.bfloat16), square_ref[3]).astype(
            jnp.bfloat16
        )
        turned[:, rows] = mixed_ref[rows, :].astype(jnp.float32).T.astype(jnp.bfloat16)
        return carry

    lax.fori_loop(0, tokens // big, begin, 0)

    def outer(target, right_ref):
        def part(r, carry):
            rows = rows_at(r, 384)
            grad_square_ref[target, rows, :] = dot_nn(turned[rows, :], right_ref[...].astype(jnp.bfloat16)).astype(
                jnp.bfloat16
            )
            return carry

        lax.fori_loop(0, D // 384, part, 0)

    outer(3, grad_middle_ref)
    early_done()
    grad_score_ref[...] = jnp.zeros_like(grad_score_ref)

    def attend(t, carry):
        rows = rows_at(t, TILE)
        mask = tile_mask(mask_ref, t)
        for pair in range(PAIRS):
            lanes = pl.ds(pair * TILE, TILE)
            query, keys_here = query_ref[rows, lanes], key_ref[rows, lanes]
            probs = pair_probs(query, keys_here, pair_bias(bias_ref, pair), mask)
            grads = split_heads(grad_mixed[rows, lanes])
            grad_probs = dot_nt(grads, value_ref[rows, lanes])
            grad_value[rows, lanes] = dot_tn(probs.astype(jnp.bfloat16), grads).astype(jnp.bfloat16)
            inner = jnp.sum(grad_probs * probs, axis=1, keepdims=True)
            grad_scores = (probs * (grad_probs - inner)).astype(jnp.bfloat16)
            kept = grad_scores.astype(jnp.float32)
            grad_score_ref[2 * pair] += kept[:TILE]
            grad_score_ref[2 * pair + 1] += kept[TILE:]
            grad_query[rows, lanes] = (
                dot_nn(join_heads(grad_scores), split_heads(keys_here)) * HEAD ** (-0.5)
            ).astype(jnp.bfloat16)
            grad_key[rows, lanes] = (dot_tn(grad_scores, split_heads(query)) * HEAD ** (-0.5)).astype(jnp.bfloat16)
        return carry

    tiles = tokens // TILE
    between = list(between)
    part = tokens // 2

    def relay(place, number):
        for spot_name, spot_number, act in between:
            if (spot_name, spot_number) == (place, number):
                act()

    grad_gain_ref[...] = jnp.zeros_like(grad_gain_ref)

    def attend_half(half):
        for t in range(half * tiles // 2, (half + 1) * tiles // 2):
            lax.fori_loop(t, t + 1, attend, 0)
            relay("tile", t)

    def end_half(half):
        def end(r, carry):
            rows = pl.ds(pl.multiple_of(half * part + r * 256, 256), 256)
            grad_normed = (
                dot_nt(grad_query[rows, :], square_ref[0])
                + dot_nt(grad_key[rows, :], square_ref[1])
                + dot_nt(grad_value[rows, :], square_ref[2])
            )
            through, gain = norm_back_rows(start_ref[rows, :].astype(jnp.float32), gains_ref[0:1], grad_normed)
            grad_gain_ref[0:1] += gain
            turned_half[:, rows_at(r, 256)] = (grad_middle_ref[rows, :] + through).T.astype(jnp.bfloat16)
            return carry

        lax.fori_loop(0, part // 256, end, 0)

        def merge(r, carry):
            rows = rows_at(r, 384)
            total = jnp.zeros((384, part), jnp.float32)
            for c in range(part // 256):
                hot = hot_rows(rank_ref, pl.ds(half * part + c * 256, 256), part, half * part)
                total = total + dot_nn(turned_half[rows, c * 256 : (c + 1) * 256], hot)
            put(half, r, total)
            return carry

        lax.fori_loop(0, D // 384, merge, 0)
        put(half, None, None)

    need(1)
    attend_half(0)
    need(2)
    end_half(0)
    relay("end", 0)
    attend_half(1)

    def renorm(r, carry):
        rows = rows_at(r, 256)
        normed = norm_rows(start_ref[rows, :].astype(jnp.float32), gains_ref[0:1])
        turned[:, rows] = normed.T.astype(jnp.bfloat16)
        return carry

    lax.fori_loop(0, tokens // 256, renorm, 0)
    relay("norm", 0)
    outer(0, grad_query)
    relay("outer", 0)
    outer(1, grad_key)
    relay("outer", 1)
    outer(2, grad_value)
    squares_done()
    relay("outer", 2)
    end_half(1)
    relay("end", 1)


def attend_back_kernel(*refs):
    ins, rest = refs[:13], refs[13:]
    grad_square_ref, grad_score_ref, grad_gain_ref, send_ref = rest[:4]

    def put(half, r, total):
        if r is not None:
            part = total.shape[1]
            send_ref[rows_at(r, 384), half * part : (half + 1) * part] = total.astype(jnp.bfloat16)

    nothing = lambda: None
    attend_back_steps(
        *ins, grad_square_ref, grad_score_ref, grad_gain_ref, *rest[4:], [], nothing, nothing, put, lambda stage: None
    )


def attend_scratch(tokens):
    low = jnp.bfloat16
    return [
        pltpu.VMEM((tokens, D), low),
        pltpu.VMEM((D, tokens), low),
        pltpu.VMEM((tokens, D), low),
        pltpu.VMEM((tokens, D), low),
        pltpu.VMEM((tokens, D), low),
        pltpu.VMEM((D, tokens // 2), low),
    ]


def run_attend_back(*ins):
    tokens = ins[0].shape[0]
    low = jnp.bfloat16
    return pl.pallas_call(
        attend_back_kernel,
        out_shape=[
            jax.ShapeDtypeStruct((5, D, D), low),
            jax.ShapeDtypeStruct((HEADS, TILE, TILE), jnp.float32),
            jax.ShapeDtypeStruct((8, D), jnp.float32),
            jax.ShapeDtypeStruct((D, tokens), low),
        ],
        scratch_shapes=attend_scratch(tokens),
        compiler_params=pltpu.CompilerParams(vmem_limit_bytes=VMEM_CAP),
        name="attend_backward",
    )(*ins)


BACK_CAP = 64 * 1024 * 1024 - 128 * 1024


BACK_STAGES = ((0, 8, 7), (4, 5, 6, 10, 11), (3, 12))
HIGH = 32
SEGMENTS = 8
EARLY_PLAN = (("tile", 3), ("outer", 0), ("end", 1), ("dense", 1), ("dense", 3), ("dense", 5))
LATE_PLAN = (("dense", 6), ("dense", 7), ("dense", 9), ("dense", 11), ("dense", 13), ("dense", 15))


def back_kernel(depth, *refs):
    ins, refs = list(refs[:13]), refs[13:]
    keys_ref, grad_expand, grad_reduce = refs[:3]
    square_sum, expand_sum, reduce_sum, grad_score_ref, grad_gain_ref, squares_ref, table_ref = refs[3:10]
    grad_square, *steps = refs[10:17]
    blocks, spare, work_expand, work_reduce, returned, places = refs[17:23]
    refs = refs[23:]
    turned = steps[1]
    count_first, count_last = 5 * len(FIRST_KINDS), 5 * len(LAST_KINDS)
    first_buffers, refs = refs[:count_first], refs[count_first:]
    first_sems, refs = refs[:8], refs[8:]
    last_buffers, refs = refs[:count_last], refs[count_last:]
    last_sems, refs = refs[:8], refs[8:]
    part_send, part_got, part_own, end_send, end_got = refs[:5]
    need = stage_loads(ins, BACK_STAGES, refs[5:15], refs[15])
    dp_size, fsdp_size = lax.axis_size("dp"), lax.axis_size("fsdp")
    count = dp_size * fsdp_size
    me = lax.axis_index("dp") * fsdp_size + lax.axis_index("fsdp")
    greet_all(count, fsdp_size, me)
    grads = (grad_square, grad_expand, grad_reduce)
    outs = (square_sum, expand_sum, reduce_sum, spare)
    work = {EXPAND: work_expand, REDUCE: work_reduce}
    early = Reduction(FIRST_KINDS, depth, grads, outs, work, first_buffers, first_sems)
    late = Reduction(LAST_KINDS, depth, grads, outs, work, last_buffers, last_sems)
    early.begin((EXPAND, REDUCE))
    early_groups, late_groups = list(early.groups()), list(late.groups())

    def relay(group):
        def act():
            for move, step in group:
                move(step)

        return act

    feats, quarter = blocks.shape[2] // 2, blocks.shape[3]

    def part_copy(half, k):
        target = lax.rem(me + k, count)
        device = (target // fsdp_size, lax.rem(target, fsdp_size))
        return remote(
            blocks.at[half, target], returned.at[half, me], part_send.at[half, k], part_got.at[half, k], device
        )

    def own_part(half):
        return pltpu.make_async_copy(blocks.at[half, me], returned.at[half, me], part_own.at[half])

    def put(half, r, total):
        if r is None:

            def start_part(k, carry):
                part_copy(half, k).start()
                return carry

            lax.fori_loop(1, count, start_part, 0)
            own_part(half).start()
            return
        each = 384 // feats
        for p in range(each):
            part = total[p * feats : (p + 1) * feats]
            blocks[half, r * each + p] = jnp.concatenate(
                [part[:, :quarter], part[:, quarter:]], axis=0
            ).astype(jnp.bfloat16)

    attend_back_steps(
        *ins, grad_square, grad_score_ref, grad_gain_ref, *steps,
        [(*place_at, relay(group)) for place_at, group in zip(EARLY_PLAN, early_groups)],
        lambda: early.begin((EARLY,)),
        lambda: late.begin((LATE,)),
        put,
        need,
    )

    def end_copy(number, kind, of):
        span = pl.ds(*SPANS[kind])
        return remote(
            spare.at[span], square_sum.at[of, span], end_send.at[number], end_got.at[number], early.sibling
        )

    core = early.core
    table_ref[...] = jnp.zeros_like(table_ref)
    vocab = table_ref.shape[1]
    batch = 2
    segments = 4
    slots = 2 * quarter
    lines = slots // LANES

    def add_rows(half, n, carry):
        for b in range(batch):
            k = n * batch + b

            @pl.when(k > 0)
            def _():
                part_copy(half, k).wait_recv()

            source = lax.rem(me + count - k, count)
            block = returned[half, source].astype(jnp.float32)
            keys = keys_ref[source]
            for c in range(lines):
                key = keys[half * lines + c : half * lines + c + 1]
                number = (key >> 2) + (key & 3) * fold_rows(vocab)
                at = pl.ds(b * slots + c * LANES, LANES)
                places[0:1, at] = number & 1023
                first = 0 if c < lines // 2 else feats
                low = (c % (lines // 2)) * LANES
                piece = block[first : first + feats, low : low + LANES]
                high = number >> 10
                spread = [jnp.where(high == g, piece, 0.0) for g in range(HIGH)]
                turned[:, at] = jnp.concatenate(spread, axis=0).astype(jnp.bfloat16)
        for w in range(4):
            window = 256
            row = lax.broadcasted_iota(jnp.int32, (window, batch * slots), 0) + w * window
            hot = (row == places[0:1]).astype(jnp.float32).astype(jnp.bfloat16)
            total = dot_nt(turned[...], hot)
            for g in range(HIGH):
                start = g * 1024 + w * window
                width = min(window, vocab - start)
                if width > 0:
                    table_ref[:, start : start + width] += total[g * feats : (g + 1) * feats, :width]
        return carry

    plan = list(zip(EARLY_PLAN, early_groups)) + list(zip(LATE_PLAN, late_groups))
    for half in range(2):
        own_part(half).wait()
        each = count // batch // SEGMENTS
        for segment in range(SEGMENTS):
            lax.fori_loop(segment * each, (segment + 1) * each, functools.partial(add_rows, half), 0)
            for place_at, group in plan:
                if place_at == ("dense", half * SEGMENTS + segment):
                    relay(group)()
                    if group is early_groups[-1]:
                        end_copy(0, EARLY, core).start()
    end_copy(1, LATE, core).start()
    early.finish()
    late.finish()
    for number, kind in enumerate((EARLY, LATE)):
        end_copy(number, kind, core).wait_send()
        end_copy(number, kind, 1 - core).wait_recv()
    squares = jnp.zeros((1, 1), jnp.float32)
    for sums in (square_sum, expand_sum, reduce_sum):
        value = sums[...].reshape(-1, sums.shape[-1])
        squares = squares + jnp.sum(value * value, keepdims=True)
    for g in range(HIGH):
        value = table_ref[:, g * 1024 : min(vocab, (g + 1) * 1024)]
        squares = squares + jnp.sum(value * value, keepdims=True)
    squares_ref[...] = jnp.broadcast_to(squares, squares_ref.shape)
    for half in range(2):

        def end_part(k, carry):
            part_copy(half, k).wait_send()
            return carry

        lax.fori_loop(1, count, end_part, 0)


def run_back(ins, keys, grad_expand, grad_reduce, feats, vocab, call_id):
    depth = lax.axis_size("dp") // 2
    tokens = ins[0].shape[0]
    low = jnp.bfloat16
    count = keys.shape[0]
    blocks = (2, count, 2 * feats, tokens // 4)
    whole = pl.BlockSpec(memory_space=pltpu.VMEM)
    anywhere = pl.BlockSpec(memory_space=pl.ANY)
    specs, homes, load_sem = stage_specs(ins, BACK_STAGES)
    first_buffers, first_sems = reduction_scratch(FIRST_KINDS, depth)
    last_buffers, last_sems = reduction_scratch(LAST_KINDS, depth)
    return pl.pallas_call(
        functools.partial(back_kernel, depth),
        out_shape=[
            jax.ShapeDtypeStruct((2, 5, 48, 192), jnp.float32),
            jax.ShapeDtypeStruct((96, 768), jnp.float32),
            jax.ShapeDtypeStruct((192, 384), jnp.float32),
            jax.ShapeDtypeStruct((HEADS, TILE, TILE), jnp.float32),
            jax.ShapeDtypeStruct((8, D), jnp.float32),
            jax.ShapeDtypeStruct((8, LANES), jnp.float32),
            jax.ShapeDtypeStruct((feats, vocab), jnp.float32),
        ],
        in_specs=specs + [whole] + [anywhere] * 2,
        out_specs=[whole] * 7,
        scratch_shapes=[pltpu.VMEM((5, D, D), low)]
        + attend_scratch(tokens)
        + [
            pltpu.VMEM(blocks, low),
            pltpu.VMEM((5, 48, 192), jnp.float32),
            pltpu.VMEM(pair_shape(EXPAND, depth), low),
            pltpu.VMEM(pair_shape(REDUCE, depth), low),
            pltpu.VMEM(blocks, low),
            pltpu.VMEM((8, tokens), jnp.int32),
        ]
        + first_buffers
        + first_sems
        + last_buffers
        + last_sems
        + [
            pltpu.SemaphoreType.DMA((2, count)),
            pltpu.SemaphoreType.DMA((2, count)),
            pltpu.SemaphoreType.DMA((2,)),
            pltpu.SemaphoreType.DMA((2,)),
            pltpu.SemaphoreType.DMA((2,)),
        ]
        + homes
        + [load_sem],
        compiler_params=pltpu.CompilerParams(
            collective_id=call_id, has_side_effects=True, vmem_limit_bytes=BACK_CAP
        ),
        name="back",
    )(*ins, keys, grad_expand, grad_reduce)


def share_chips(own_ref, everyone, send, got, hand_send, hand_got, meanwhile=None):
    dp_size, fsdp_size = lax.axis_size("dp"), lax.axis_size("fsdp")
    count = dp_size * fsdp_size
    chips = count // 2
    dp, fsdp = lax.axis_index("dp"), lax.axis_index("fsdp")
    me = dp * fsdp_size + fsdp
    core = lax.rem(fsdp, 2)
    chip = me // 2
    sibling = (dp, fsdp + 1 - 2 * core)
    greet_all(count, fsdp_size, me)

    def device(number):
        return (number // fsdp_size, lax.rem(number, fsdp_size))

    def across(k):
        target = lax.rem(chip + k, chips) * 2 + core
        return remote(own_ref, everyone.at[me], send.at[k], got.at[k], device(target))

    def hand(k, of):
        source = lax.rem(chip + chips - k, chips) * 2 + of
        return remote(everyone.at[source], everyone.at[source], hand_send.at[k], hand_got.at[k], sibling)

    def start(k, carry):
        across(k).start()
        return carry

    def relay(k, carry):
        across(k).wait_recv()
        hand(k, core).start()
        return carry

    def end(k, carry):
        across(k).wait_send()
        hand(k, core).wait_send()
        hand(k, 1 - core).wait_recv()
        return carry

    first = remote(own_ref, everyone.at[me], hand_send.at[0], hand_got.at[0], sibling)
    first.start()
    everyone[me] = own_ref[...]
    lax.fori_loop(1, chips, start, 0)
    if meanwhile is not None:
        meanwhile()
    lax.fori_loop(1, chips, relay, 0)
    lax.fori_loop(1, chips, end, 0)
    first.wait_send()
    hand(0, 1 - core).wait_recv()
    return me


def total_kernel(
    first_gain, late_gains, position_ref, squares_ref, stats_ref, total_ref, norm_ref, tile,
    everyone, send, got, hand_send, hand_got,
):
    gains = first_gain[...] + late_gains[...]
    rows = [squares_ref[0:1]]
    rows += [position_ref[k : k + 1] for k in range(3)]
    for k in range(3):
        rows += [gains[k : k + 1, c * LANES : (c + 1) * LANES] for c in range(D // LANES)]
    rows.append(jnp.zeros((tile.shape[0] - len(rows), LANES), jnp.float32))
    tile[...] = jnp.concatenate(rows, axis=0)
    share_chips(tile, everyone, send, got, hand_send, hand_got)

    def add(k, total):
        return total + everyone[k]

    total = lax.fori_loop(1, everyone.shape[0], add, everyone[0])
    total_ref[...] = total
    row = lax.broadcasted_iota(jnp.int32, total.shape, 0)
    lane = lax.broadcasted_iota(jnp.int32, total.shape, 1)
    squares = jnp.where(row == 0, jnp.where(lane == 0, total, 0.0), total * total)
    grad_scale = stats_ref[0:1, 2:3]
    norm = jnp.sqrt(jnp.sum(squares, keepdims=True) + grad_scale * grad_scale)
    norm_ref[...] = jnp.broadcast_to(norm, norm_ref.shape)


def run_total(first_gain, late_gains, position, squares, stats, call_id):
    count = lax.axis_size("dp") * lax.axis_size("fsdp")
    few = pltpu.SemaphoreType.DMA((count // 2,))
    return pl.pallas_call(
        total_kernel,
        out_shape=[jax.ShapeDtypeStruct((24, LANES), jnp.float32), jax.ShapeDtypeStruct((8, LANES), jnp.float32)],
        scratch_shapes=[
            pltpu.VMEM((24, LANES), jnp.float32),
            pltpu.VMEM((count, 24, LANES), jnp.float32),
            few, few, few, few,
        ],
        compiler_params=pltpu.CompilerParams(
            collective_id=call_id, has_side_effects=True, vmem_limit_bytes=VMEM_CAP
        ),
        name="total",
    )(first_gain, late_gains, position, squares, stats)


def loss_steps(query_rows, nli_rows, me, slots, negative_ref, scale_ref, stats_ref, everyone, grad_sims, turned_sims):
    count = everyone.shape[0]
    total_rows = count * slots
    embeds = everyone[...].reshape(total_rows, D)
    scale = jnp.exp(scale_ref[...])
    sims = dot_nt(embeds, embeds)
    row = lax.broadcasted_iota(jnp.int32, sims.shape, 0)
    col = lax.broadcasted_iota(jnp.int32, sims.shape, 1)
    row_slot, col_slot = row & (slots - 1), col & (slots - 1)
    hypo, answer = query_rows + nli_rows, query_rows + 2 * nli_rows
    is_query = row_slot < query_rows
    is_premise = (row_slot >= query_rows) & (row_slot < hypo)
    is_hypo = (col_slot >= hypo) & (col_slot < answer)
    is_answer = (col_slot >= answer) & (col_slot < answer + query_rows)
    allowed = (is_query & is_answer) | (is_premise & is_hypo)
    target = (is_query & (col == row + answer)) | (is_premise & (col == row + nli_rows))
    target = jnp.where(target, 1.0, 0.0)
    logits = scale * sims
    shown = jnp.where(allowed, logits, -1e30)
    row_top = jnp.max(shown, axis=1, keepdims=True)
    weight = jnp.where(negative_ref[:, :1] == col, 2.0, 1.0)
    raised = jnp.where(allowed, weight * jnp.exp(shown - row_top), 0.0)
    left = is_query | is_premise
    row_total = jnp.where(left[:, :1], jnp.sum(raised, axis=1, keepdims=True), 1.0)
    hits = jnp.sum(jnp.where(target > 0.0, logits, 0.0), axis=1, keepdims=True)
    losses = jnp.where(left[:, :1], row_top + jnp.log(row_total), 0.0) - hits
    first_loss = jnp.sum(jnp.where(is_query[:, :1], losses, 0.0), keepdims=True)
    second_loss = jnp.sum(jnp.where(is_premise[:, :1], losses, 0.0), keepdims=True)
    grad_logits = raised / row_total - target
    grad_scale = scale * jnp.sum(grad_logits * sims, keepdims=True)
    lane = lax.broadcasted_iota(jnp.int32, stats_ref.shape, 1)
    stats_ref[...] = jnp.where(lane == 0, first_loss, jnp.where(lane == 1, second_loss, grad_scale))
    grads = scale * grad_logits
    grad_sims[...] = grads
    turned_sims[...] = grads.T
    own = pl.ds(pl.multiple_of(me * slots, 8), slots)
    return dot_nn(grad_sims[own, :].astype(jnp.bfloat16), embeds) + dot_nn(
        turned_sims[own, :].astype(jnp.bfloat16), embeds
    )


def shards(
    embed_table,
    square_weights,
    expand_weight,
    reduce_weight,
    norm_gains,
    position_bias,
    log_scale,
    table_moment,
    table_second,
    square_moment,
    square_second,
    expand_moment,
    expand_second,
    reduce_moment,
    reduce_second,
    gains_moment,
    gains_second,
    position_moment,
    position_second,
    scale_moment,
    scale_second,
    query_tokens,
    answer_tokens,
    query_length,
    answer_length,
    premise_tokens,
    hypothesis_tokens,
    hard_negative,
):
    both = ("dp", "fsdp")
    dp_size, fsdp_size = lax.axis_size("dp"), lax.axis_size("fsdp")
    count = dp_size * fsdp_size
    direct = dp_size == 8 and fsdp_size == 4
    position = lax.axis_index(both)
    feats, vocab_size = embed_table.shape
    feats_pad = up8(feats)
    fold = fold_rows(vocab_size)
    query_rows = query_tokens.shape[0]
    nli_rows = premise_tokens.shape[0]
    short_length = query_tokens.shape[1]
    long_length = answer_tokens.shape[1]
    short_tokens = jnp.concatenate([query_tokens, premise_tokens, hypothesis_tokens], axis=0)
    lengths = jnp.concatenate(
        [query_length, jnp.full((2 * nli_rows,), short_length, jnp.int32), answer_length]
    )
    all_tokens = jnp.concatenate([short_tokens.reshape(-1), answer_tokens.reshape(-1)])
    token_count = all_tokens.shape[0]
    hypo_start = query_rows + nli_rows
    answer_start = query_rows + 2 * nli_rows
    seq_count = answer_start + query_rows
    seq_pad = -(-seq_count // 16) * 16
    split_at = short_tokens.shape[0] * short_length

    packed, rank = token_keys(all_tokens, fold)
    key_rows = token_count // LANES
    info = jnp.concatenate(
        [
            packed.reshape(key_rows, LANES),
            jnp.pad(hard_negative, (0, LANES - nli_rows)).reshape(1, LANES),
            jnp.zeros((7, LANES), jnp.int32),
        ],
        axis=0,
    )
    square_low = square_weights.astype(jnp.bfloat16)
    expand_low = expand_weight.astype(jnp.bfloat16)
    reduce_low = reduce_weight.astype(jnp.bfloat16).T
    half = token_count // 2
    if direct:
        found, square_all, expand_all, info_all, gains_all = run_front(
            info, norm_gains, token_count, embed_table, square_weights, expand_weight, 1
        )
    else:
        info_all = exchange(info[None], True, 0, "share_keys")
        own_gains = jnp.pad(norm_gains, ((0, 5), (0, LANES - feats)))
        gains_all = exchange(own_gains[None], True, 6, "share_gains")

        def whole(piece, row_name, column_name):
            axis = piece.ndim - 2
            wide = lax.all_gather(piece, column_name, axis=axis + 1, tiled=True)
            return lax.all_gather(wide, row_name, axis=axis, tiled=True)

        square_all = whole(square_low, "dp", "fsdp")
        expand_all = whole(expand_low, "dp", "fsdp")
        reduce_all = whole(reduce_low, "fsdp", "dp")
        padded = jnp.pad(embed_table, ((0, feats_pad - feats), (0, 0)))
        key_all = info_all[:, :key_rows].reshape(count, 1, token_count)
        found = exchange(lookup(padded, key_all >> 2, key_all & 3), False, 8, "send_features")
        found = found.reshape(count, 2, feats_pad, half)[:, :, :feats]
        found = found.transpose(1, 0, 2, 3).reshape(1, 2 * D, half)
    packed_all = info_all[:, :key_rows].reshape(count, 1, token_count)
    row_all, group_all = packed_all >> 2, packed_all & 3
    negative_all = info_all[:, key_rows, :nli_rows]
    gains = gains_all[:, :3, :feats].transpose(1, 0, 2).reshape(3, D)
    gains = jnp.pad(gains.astype(jnp.bfloat16).astype(jnp.float32), ((0, 5), (0, 0)))

    sequence = np.concatenate(
        [
            np.repeat(np.arange(answer_start), short_length),
            answer_start + np.repeat(np.arange(query_rows), long_length),
        ]
    )
    inside = np.concatenate(
        [
            np.tile(np.arange(short_length), answer_start),
            np.tile(np.arange(long_length), query_rows),
        ]
    )
    lengths_pad = jnp.pad(lengths, (0, seq_pad - seq_count), constant_values=1)
    pool = (sequence[None, :] == np.arange(seq_pad)[:, None]) & (inside[None, :] < lengths_pad[:, None])
    token_ok = jnp.any(pool, axis=0).reshape(-1, 1, TILE)
    sequence_tiles = sequence.reshape(-1, TILE)
    together = sequence_tiles[:, :, None] == sequence_tiles[:, None, :]
    mask = jnp.where(together & token_ok, 0.0, -1e30).astype(jnp.float32)
    pool = pool.astype(jnp.float32)
    length_rows = jnp.broadcast_to(lengths_pad.astype(jnp.float32)[:, None], (seq_pad, LANES))
    rank_rows = jnp.broadcast_to(rank[:, None], (token_count, LANES))
    bias, onehot = attention_bias(position_bias, TILE)

    forward_ins = (found, rank_rows, square_all, gains, bias, mask, pool, length_rows)
    if direct:
        *forward_all, reduce_all = run_relayed_forward(forward_ins, expand_all, reduce_low, 2)
    else:
        forward_all = run_forward(forward_ins, expand_all, reduce_all)
    (start, queries, keys_here, values_here, mixed, middle, ending, embeds_low, pooled, embeds, inverse) = forward_all
    if direct:
        negative_place = (negative_all // nli_rows) * seq_pad + hypo_start + negative_all % nli_rows
        negative_place = jnp.pad(
            negative_place, ((0, 0), (query_rows, seq_pad - hypo_start)), constant_values=-1
        )
        negative_place = jnp.broadcast_to(negative_place.reshape(-1, 1), (count * seq_pad, LANES))
        (grad_expand, grad_reduce, grad_middle, grad_proj, late_gains, stats) = run_loss_feed(
            embeds_low, negative_place, log_scale.reshape(1, 1), embeds, inverse, pool, length_rows, gains,
            square_all, middle, ending, expand_all, reduce_all, query_rows, nli_rows, 3,
        )
        losses, grad_scale = stats[0, :2], stats[0, 2:3]
    else:
        gathered = exchange(embeds_low[None], True, 3, "share_embeds")
        queries_all = gathered[:, :query_rows].reshape(-1, D)
        premises_all = gathered[:, query_rows:hypo_start].reshape(-1, D)
        hypotheses_all = gathered[:, hypo_start:answer_start].reshape(-1, D)
        answers_all = gathered[:, answer_start:seq_count].reshape(-1, D)
        scale = jnp.exp(log_scale[0])

        def contrast(left, right, extra, own):
            sims = product_right(left, right)
            logits = scale * sims
            row_top = jnp.max(logits, axis=1, keepdims=True)
            raised = (1.0 + extra) * jnp.exp(logits - row_top)
            row_total = jnp.sum(raised, axis=1, keepdims=True)
            spread = row_top[:, 0] + jnp.log(row_total[:, 0])
            target_hit = jnp.eye(left.shape[0], dtype=jnp.float32)
            loss_sum = jnp.sum(spread - jnp.sum(target_hit * logits, axis=1))
            grad_logits = raised / row_total - target_hit
            grad_scale = jnp.sum(grad_logits * sims)
            grad_sims = (scale * grad_logits).astype(jnp.bfloat16)
            mine_left = lax.dynamic_slice_in_dim(grad_sims, position * own, own, 0)
            mine_right = lax.dynamic_slice_in_dim(grad_sims, position * own, own, 1)
            return (loss_sum, grad_scale, product(mine_left, right), product_left(mine_right, left))

        first_loss, first_dscale, grad_queries, grad_answers = contrast(
            queries_all, answers_all, 0.0, query_rows
        )
        negatives = (jnp.arange(hypotheses_all.shape[0])[None, :] == negative_all.reshape(-1)[:, None]).astype(
            jnp.float32
        )
        second_loss, second_dscale, grad_premises, grad_hypotheses = contrast(
            premises_all, hypotheses_all, negatives, nli_rows
        )
        grad_embeds = jnp.concatenate(
            [
                grad_queries,
                grad_premises,
                grad_hypotheses,
                grad_answers,
                jnp.zeros((seq_pad - seq_count, D), jnp.float32),
            ],
            axis=0,
        )
        losses = jnp.stack([first_loss, second_loss])
        grad_scale = ((first_dscale + second_dscale) * scale).reshape(1)
        stats = jnp.broadcast_to(grad_scale, (8, LANES))
        (grad_expand, grad_reduce, grad_middle, grad_proj, late_gains) = run_feed_back(
            grad_embeds, embeds, inverse, pool, length_rows, square_all, middle, ending, expand_all, reduce_all, gains
        )
    back_ins = (
        grad_middle, grad_proj, pooled, start, queries, keys_here, values_here, mixed, square_all,
        gains, bias, mask, rank_rows,
    )
    if direct:
        (square_sum, expand_sum, reduce_sum, grad_scores, first_gain, layer_squares, grad_table) = run_back(
            back_ins, info_all, grad_expand, grad_reduce, feats, vocab_size, 5
        )

        square_sum = square_sum.transpose(1, 0, 2, 3).reshape(5, 96, 192)
    else:

        def shard(gradient, row_name, column_name):
            axis = gradient.ndim - 2
            part = lax.psum_scatter(
                gradient.astype(jnp.float32), row_name, scatter_dimension=axis, tiled=True
            )
            return lax.psum_scatter(part, column_name, scatter_dimension=axis + 1, tiled=True)

        (grad_square, grad_scores, first_gain, merged) = run_attend_back(*back_ins)
        square_sum = shard(grad_square, "dp", "fsdp")
        expand_sum = shard(grad_expand, "dp", "fsdp")
        reduce_sum = shard(grad_reduce, "fsdp", "dp")
        layer_squares = jnp.full(
            (8, LANES), sum(jnp.sum(part * part) for part in (square_sum, expand_sum, reduce_sum)), jnp.float32
        )
        merged = merged.reshape(count, feats, 2, 2, half // 2).transpose(2, 0, 3, 1, 4)
        if feats_pad > feats:
            merged = jnp.pad(merged, ((0, 0), (0, 0), (0, 0), (0, feats_pad - feats), (0, 0)))
        merged = merged.reshape(2, count, 2 * feats_pad, half // 2)
        returned = jnp.stack(
            [exchange(merged[n], False, 9 + n, ("send_early", "send_late")[n]) for n in range(2)]
        )
        grad_table, table_squares = scatter(returned, row_all, group_all, vocab_size)
        grad_table = grad_table[:feats]
        layer_squares = layer_squares + jnp.sum(table_squares)
    grad_position = lax.dot_general(
        onehot, grad_scores.reshape(HEADS, TILE * TILE), (((0,), (1,)), ((), ())), precision=HIGHEST
    )
    reduced = (square_sum, expand_sum, reduce_sum.T)
    total, norm = run_total(
        first_gain,
        late_gains,
        grad_position.reshape(-1, LANES),
        layer_squares,
        stats,
        7,
    )
    position_total = total[1:4].reshape(BUCKETS, HEADS)
    gains_total = total[4:22].reshape(3, D)
    scale_total = grad_scale
    gradient_norm = norm[0, 0]
    grad_gain_shard = lax.dynamic_slice_in_dim(gains_total, position * feats, feats, 1)
    factor = jnp.minimum(1.0, CLIP_NORM / gradient_norm)
    table_out = adam_update(embed_table, table_moment, table_second, grad_table, factor, TABLE_RATE)
    square_out = adam_update(
        square_weights, square_moment, square_second, reduced[0], factor, LEARN_RATE
    )
    expand_out = adam_update(
        expand_weight, expand_moment, expand_second, reduced[1], factor, LEARN_RATE
    )
    reduce_out = adam_update(
        reduce_weight, reduce_moment, reduce_second, reduced[2], factor, LEARN_RATE
    )
    gains_out = adam_update(
        norm_gains, gains_moment, gains_second, grad_gain_shard, factor, SMALL_RATE
    )
    position_out = adam_update(
        position_bias, position_moment, position_second, position_total, factor, SMALL_RATE
    )
    scale_out = adam_update(log_scale, scale_moment, scale_second, scale_total, factor, SMALL_RATE)
    return (
        *table_out,
        *square_out,
        *expand_out,
        *reduce_out,
        *gains_out,
        *position_out,
        *scale_out,
        losses,
        gradient_norm,
    )


def solution(mesh):
    return jax.shard_map(
        shards,
        mesh=mesh,
        in_specs=(
            P(("dp", "fsdp"), None),
            P(None, "dp", "fsdp"),
            P("dp", "fsdp"),
            P("dp", "fsdp"),
            P(None, ("dp", "fsdp")),
            P(),
            P(),
            P(("dp", "fsdp"), None),
            P(("dp", "fsdp"), None),
            P(None, "dp", "fsdp"),
            P(None, "dp", "fsdp"),
            P("dp", "fsdp"),
            P("dp", "fsdp"),
            P("dp", "fsdp"),
            P("dp", "fsdp"),
            P(None, ("dp", "fsdp")),
            P(None, ("dp", "fsdp")),
            P(),
            P(),
            P(),
            P(),
            P(("dp", "fsdp"), None),
            P(("dp", "fsdp"), None),
            P(("dp", "fsdp")),
            P(("dp", "fsdp")),
            P(("dp", "fsdp"), None),
            P(("dp", "fsdp"), None),
            P(("dp", "fsdp")),
        ),
        out_specs=(
            P(("dp", "fsdp"), None),
            P(("dp", "fsdp"), None),
            P(("dp", "fsdp"), None),
            P(None, "dp", "fsdp"),
            P(None, "dp", "fsdp"),
            P(None, "dp", "fsdp"),
            P("dp", "fsdp"),
            P("dp", "fsdp"),
            P("dp", "fsdp"),
            P("dp", "fsdp"),
            P("dp", "fsdp"),
            P("dp", "fsdp"),
            P(None, ("dp", "fsdp")),
            P(None, ("dp", "fsdp")),
            P(None, ("dp", "fsdp")),
            P(),
            P(),
            P(),
            P(),
            P(),
            P(),
            P(),
            P(),
        ),
        check_vma=False,
    )
```

```python
import functools

import jax
import jax.numpy as jnp
import numpy as np
from jax import lax
from jax.experimental import pallas as pl
from jax.experimental.pallas import tpu as pltpu
from jax.sharding import PartitionSpec as P

D = 768
HEADS = 12
HEAD = 64
BUCKETS = 32
MAXDIST = 128
STEP = 10


HIGHEST = lax.Precision.HIGHEST
NORM_EPS = 1e-06
LEARN_RATE = 0.03
TABLE_RATE = 0.4
SMALL_RATE = 0.5
BETA_ONE = 0.9
BETA_TWO = 0.999
ADAM_EPS = 1e-08
WEIGHT_DECAY = 0.01
CLIP_NORM = 0.5


def bucket_table(length):
    places = np.arange(length)
    offset = places[None, :] - places[:, None]
    half_count = BUCKETS // 2
    exact_count = half_count // 2
    upper = (offset > 0).astype(np.int64) * half_count
    distance = np.abs(offset)
    far_bucket = exact_count + (
        np.log(np.maximum(distance, 1) / exact_count)
        / np.log(MAXDIST / exact_count)
        * (half_count - exact_count)
    ).astype(np.int64)
    far_bucket = np.minimum(far_bucket, half_count - 1)
    return (upper + np.where(distance < exact_count, distance, far_bucket)).astype(np.int32)


def bucket_onehot(length):
    flat_table = bucket_table(length).reshape(-1)
    return jnp.asarray((flat_table[:, None] == np.arange(BUCKETS)[None, :]).astype(np.float32))


def product(left, right):
    return jnp.dot(left, right, preferred_element_type=jnp.float32)


def product_left(left, right):
    return lax.dot_general(
        left, right, (((0,), (0,)), ((), ())), preferred_element_type=jnp.float32
    )


def product_right(left, right):
    return lax.dot_general(
        left, right, (((1,), (1,)), ((), ())), preferred_element_type=jnp.float32
    )


def attention_bias(position_bias, length):
    onehot = bucket_onehot(length)
    flat_bias = jnp.dot(onehot, position_bias, precision=HIGHEST)
    return (jnp.transpose(flat_bias.reshape(length, length, HEADS), (2, 0, 1)), onehot)


def adam_update(weight, moment, second, grad, factor, rate):
    clipped = grad * factor
    moment_new = BETA_ONE * moment + (1 - BETA_ONE) * clipped
    second_new = BETA_TWO * second + (1 - BETA_TWO) * clipped * clipped
    moment_hat = moment_new / (1 - BETA_ONE**STEP)
    second_hat = second_new / (1 - BETA_TWO**STEP)
    updated = weight - rate * (
        moment_hat / (jnp.sqrt(second_hat) + ADAM_EPS) + WEIGHT_DECAY * weight
    )
    return (moment_new, second_new, updated)


LANES = 128
GROUPS = 4
SLOT = LANES // GROUPS
VMEM_CAP = 56 * 1024 * 1024

def fold_rows(vocab):
    per = -(-vocab // GROUPS)
    return -(-per // LANES) * LANES

def up8(n):
    return -(-n // 8) * 8

def eye():
    r = lax.broadcasted_iota(jnp.int32, (LANES, LANES), 0)
    c = lax.broadcasted_iota(jnp.int32, (LANES, LANES), 1)
    return (r == c).astype(jnp.float32).astype(jnp.bfloat16)

def turn_table(fold, table_ref, turned):
    feats, vocab = table_ref.shape
    pad = jnp.zeros((SLOT - feats, LANES), jnp.float32)

    def build(b, carry):
        parts = []
        for j in range(GROUPS):
            start = jnp.minimum(j * fold + b * LANES, vocab - LANES)
            start = pl.multiple_of(start, LANES)
            parts += [table_ref[:, pl.ds(start, LANES)], pad]
        tile = jnp.concatenate(parts, axis=0).astype(jnp.bfloat16).astype(jnp.float32)
        turned[pl.ds(pl.multiple_of(b * LANES, LANES), LANES), :] = tile.T
        return carry

    lax.fori_loop(0, fold // LANES, build, 0)
    turned[pl.ds(fold, 8), :] = jnp.zeros((8, LANES), jnp.float32)


def pick_group(rows, group, feats):
    tokens = rows.shape[0]
    wide = dot_nt(eye(), rows[...].astype(jnp.bfloat16))
    total = jnp.where(group == 0, wide[:SLOT], 0.0)
    for j in range(1, GROUPS):
        total = total + jnp.where(group == j, wide[j * SLOT : (j + 1) * SLOT], 0.0)
    half = tokens // 2
    return jnp.concatenate([total[:feats, :half], total[:feats, half:]], axis=0).astype(jnp.bfloat16)


def look_up(row_ref, group_ref, source, turned, rows, feats):
    tokens = rows.shape[0]
    batch = 32

    def fetch(b, carry):
        for k in range(batch):
            t = b * batch + k
            rows[pl.ds(t, 1), :] = turned[pl.ds(row_ref[source, t], 1), :]
        return carry

    lax.fori_loop(0, tokens // batch, fetch, 0)
    return pick_group(rows, group_ref[source], feats)


def lookup_kernel(fold, row_ref, group_ref, table_ref, out_ref, turned, rows):
    @pl.when(pl.program_id(0) == 0)
    def _():
        turn_table(fold, table_ref, turned)

    out_ref[0] = look_up(row_ref, group_ref, 0, turned, rows, table_ref.shape[0])


def lookup(table, rows_idx, groups_idx):
    feats, vocab = table.shape
    n, tokens = rows_idx.shape[0], rows_idx.shape[2]
    fold = fold_rows(vocab)
    return pl.pallas_call(
        functools.partial(lookup_kernel, fold),
        grid=(n,),
        out_shape=jax.ShapeDtypeStruct((n, 2 * feats, tokens // 2), jnp.bfloat16),
        in_specs=[
            pl.BlockSpec((None, 1, tokens), lambda s: (s, 0, 0), memory_space=pltpu.SMEM),
            pl.BlockSpec((1, 1, tokens), lambda s: (s, 0, 0)),
            pl.BlockSpec((feats, vocab), lambda s: (0, 0)),
        ],
        out_specs=pl.BlockSpec((1, 2 * feats, tokens // 2), lambda s: (s, 0, 0)),
        scratch_shapes=[pltpu.VMEM((fold + 8, LANES), jnp.float32), pltpu.VMEM((tokens, LANES), jnp.float32)],
        compiler_params=pltpu.CompilerParams(vmem_limit_bytes=VMEM_CAP),
        name="lookup",
    )(rows_idx, groups_idx, table)

def scatter_kernel(fold, row_ref, group_ref, grad_ref, out_ref, squares_ref, total, rows):
    feats, vocab = out_ref.shape
    tokens = rows.shape[0]
    step = pl.program_id(0)
    @pl.when(step == 0)
    def _():
        def clear(b, _):
            total[pl.ds(pl.multiple_of(b * LANES, LANES), LANES), :] = jnp.zeros((LANES, LANES), jnp.float32)
            return 0
        lax.fori_loop(0, fold // LANES, clear, 0)
        total[pl.ds(fold, 8), :] = jnp.zeros((8, LANES), jnp.float32)
    flat = []
    for half in range(2):
        block = grad_ref[half, 0].astype(jnp.float32)
        flat += [block[:feats], block[feats:]]
    flat = jnp.concatenate(flat, axis=1)
    group = group_ref[0]
    pad = jnp.zeros((SLOT - feats, tokens), jnp.float32)
    parts = []
    for j in range(GROUPS):
        parts += [jnp.where(group == j, flat, 0.0), pad]
    rows[...] = jnp.concatenate(parts, axis=0).T
    lines = tokens // LANES
    ways = 32 // lines
    per = LANES // ways
    for half in range(2):
        for l in range(per):
            spots = [(r, l + per * w) for r in range(half * lines // 2, (half + 1) * lines // 2) for w in range(ways)]
            at = [row_ref[r, c] for r, c in spots]
            new = [
                total[pl.ds(at[n], 1), :] + rows[pl.ds(r * LANES + c, 1), :] for n, (r, c) in enumerate(spots)
            ]
            for n in range(len(spots)):
                total[pl.ds(at[n], 1), :] = new[n]

    @pl.when(step == pl.num_programs(0) - 1)
    def _():
        whole = (vocab - (GROUPS - 1) * fold) // LANES
        def turn(b, squares):
            tile = total[pl.ds(pl.multiple_of(b * LANES, LANES), LANES), :].T
            for j in range(GROUPS):
                out_ref[:, pl.ds(pl.multiple_of(j * fold + b * LANES, LANES), LANES)] = tile[j * SLOT : j * SLOT + feats]
            return squares + tile * tile

        squares = lax.fori_loop(0, whole, turn, jnp.zeros((LANES, LANES), jnp.float32))
        for b in range(whole, fold // LANES):
            tile = total[pl.ds(b * LANES, LANES), :].T
            for j in range(GROUPS - 1):
                out_ref[:, pl.ds(j * fold + b * LANES, LANES)] = tile[j * SLOT : j * SLOT + feats]
            squares = squares + tile * tile
        squares_ref[...] = jnp.sum(squares.reshape(LANES // 8, 8, LANES), axis=0)


def scatter(grads, rows_idx, groups_idx, vocab):
    n, tokens = rows_idx.shape[0], rows_idx.shape[2]
    feats = grads.shape[2] // 2
    fold = fold_rows(vocab)
    return pl.pallas_call(
        functools.partial(scatter_kernel, fold),
        grid=(n,),
        out_shape=[jax.ShapeDtypeStruct((feats, vocab), jnp.float32), jax.ShapeDtypeStruct((8, LANES), jnp.float32)],
        in_specs=[
            pl.BlockSpec((tokens // LANES, LANES), lambda s: (s, 0), memory_space=pltpu.SMEM),
            pl.BlockSpec((1, 1, tokens), lambda s: (s, 0, 0)),
            pl.BlockSpec((2, 1, 2 * feats, tokens // 4), lambda s: (0, s, 0, 0)),
        ],
        out_specs=[pl.BlockSpec((feats, vocab), lambda s: (0, 0)), pl.BlockSpec((8, LANES), lambda s: (0, 0))],
        scratch_shapes=[pltpu.VMEM((fold + 8, LANES), jnp.float32), pltpu.VMEM((tokens, LANES), jnp.float32)],
        compiler_params=pltpu.CompilerParams(vmem_limit_bytes=VMEM_CAP),
        name="scatter",
    )(rows_idx.reshape(-1, LANES), groups_idx, grads)

def token_keys(tokens, fold):
    count = tokens.shape[0]
    key = (tokens % fold) * GROUPS + tokens // fold
    places = jnp.arange(count, dtype=jnp.int32)
    half = count // 2
    together = (places[:, None] < half) == (places[None, :] < half)
    same_before = together & (key[:, None] == key[None, :]) & (places[:, None] < places[None, :])
    first = ~jnp.any(same_before, axis=0)
    rank = jnp.sum((together & (key[None, :] < key[:, None]) & first[None, :]).astype(jnp.int32), axis=1)
    rank = rank + jnp.where(places < half, 0, half)
    hit = (rank[:, None] == places[None, :]) & first[:, None]
    packed = GROUPS * fold + jnp.sum(jnp.where(hit, key[:, None] - GROUPS * fold, 0), axis=0)
    return packed, rank


MESH = pl.DeviceIdType.MESH


def greet_all(count, cols, me):
    barrier = pltpu.get_barrier_semaphore()

    def greet(k, carry):
        to = lax.rem(me + k, count)
        pl.semaphore_signal(barrier, inc=1, device_id=(to // cols, lax.rem(to, cols)), device_id_type=MESH)
        return carry

    lax.fori_loop(1, count, greet, 0)
    pl.semaphore_wait(barrier, count - 1)


def exchange_kernel(same, src, dst, send_sem, recv_sem, own_sem):
    rows, cols = lax.axis_size("dp"), lax.axis_size("fsdp")
    count = rows * cols
    me = lax.axis_index("dp") * cols + lax.axis_index("fsdp")
    barrier = pltpu.get_barrier_semaphore()

    def device(k):
        to = lax.rem(me + k, count)
        return (to // cols, lax.rem(to, cols))

    def greet(k, carry):
        pl.semaphore_signal(barrier, inc=1, device_id=device(k), device_id_type=MESH)
        return carry

    def copy(k):
        to = lax.rem(me + k, count)
        return pltpu.make_async_remote_copy(
            src_ref=src.at[0 if same else to],
            dst_ref=dst.at[me],
            send_sem=send_sem.at[k],
            recv_sem=recv_sem.at[k],
            device_id=device(k),
            device_id_type=MESH,
        )

    def start(k, carry):
        copy(k).start()
        return carry

    def end(k, carry):
        copy(k).wait()
        return carry

    lax.fori_loop(1, count, greet, 0)
    own = pltpu.make_async_copy(src.at[0 if same else me], dst.at[me], own_sem)
    own.start()
    pl.semaphore_wait(barrier, count - 1)
    lax.fori_loop(1, count, start, 0)
    own.wait()
    lax.fori_loop(1, count, end, 0)


def exchange(blocks, same, call_id, name):
    count = lax.axis_size("dp") * lax.axis_size("fsdp")
    return pl.pallas_call(
        functools.partial(exchange_kernel, same),
        out_shape=jax.ShapeDtypeStruct((count,) + blocks.shape[1:], blocks.dtype),
        in_specs=[pl.BlockSpec(memory_space=pl.ANY)],
        out_specs=pl.BlockSpec(memory_space=pl.ANY),
        scratch_shapes=[
            pltpu.SemaphoreType.DMA((count,)),
            pltpu.SemaphoreType.DMA((count,)),
            pltpu.SemaphoreType.DMA,
        ],
        compiler_params=pltpu.CompilerParams(collective_id=call_id, has_side_effects=True),
        name=name,
    )(blocks)


SQUARE, EXPAND, REDUCE, EARLY, LATE = range(5)
STEPS = (5, 6, 4, 2, 3)
FIRST = (3, 3, 2, 1, 2)
SPANS = {SQUARE: (0, 5), EARLY: (3, 2), LATE: (0, 3)}


def spot(refs, kind, z, x, y, core):
    dp = z * 2 + x
    column = y * 2 + core
    if kind in SPANS:
        return refs[SQUARE].at[
            pl.ds(*SPANS[kind]),
            pl.ds(pl.multiple_of(dp * 96 + core * 48, 16), 48),
            pl.ds(pl.multiple_of(y * 384, 128), 384),
        ]
    if kind == EXPAND:
        return refs[kind].at[
            pl.ds(pl.multiple_of(dp * 96, 16), 96), pl.ds(pl.multiple_of(column * 768, 128), 768)
        ]
    return refs[kind].at[
        pl.ds(pl.multiple_of(column * 192, 16), 192), pl.ds(pl.multiple_of(dp * 384, 128), 384)
    ]


def spot_part(refs, kind, z, x, y, core, part):
    dp = z * 2 + x
    column = y * 2 + core
    if kind == SQUARE:
        return refs[kind].at[
            pl.ds(0, 3) if part == 0 else pl.ds(3, 2),
            pl.ds(pl.multiple_of(dp * 96 + core * 48, 16), 48),
            pl.ds(pl.multiple_of(y * 384, 128), 384),
        ]
    if kind == EXPAND:
        return refs[kind].at[
            pl.ds(pl.multiple_of(dp * 96 + part * 48, 16), 48),
            pl.ds(pl.multiple_of(column * 768, 128), 768),
        ]
    return refs[kind].at[
        pl.ds(pl.multiple_of(column * 192 + part * 96, 16), 96),
        pl.ds(pl.multiple_of(dp * 384, 128), 384),
    ]


def block_step(ref, kind, k):
    if kind in SPANS:
        return ref.at[k]
    rows = 16 if kind == EXPAND else 48
    return ref.at[pl.ds(pl.multiple_of(k * rows, 16), rows)]


BLOCKS = ((5, 48, 384), (96, 768), (192, 384), (2, 48, 384), (3, 48, 384))


def place():
    dp, fsdp = lax.axis_index("dp"), lax.axis_index("fsdp")
    return dp // 2, lax.rem(dp, 2), fsdp // 2, lax.rem(fsdp, 2)


def device_at(z, x, y, core):
    return (z * 2 + x, y * 2 + core)


def greet_neighbours(depth):
    z, x, y, core = place()
    barrier = pltpu.get_barrier_semaphore()

    def hello(target):
        pl.semaphore_signal(barrier, inc=1, device_id=target, device_id_type=MESH)

    hello(device_at(z, x, y, 1 - core))
    hello(device_at(z, 1 - x, y, core))
    hello(device_at(z, x, 1 - y, core))

    @pl.when(z > 0)
    def _():
        hello(device_at(z - 1, x, y, core))

    @pl.when(z < depth - 1)
    def _():
        hello(device_at(z + 1, x, y, core))

    above = jnp.where(z < depth - 1, 1, 0)
    below = jnp.where(z > 0, 1, 0)
    pl.semaphore_wait(barrier, 3 + above + below)


def remote(src, dst, send_sem, recv_sem, target):
    return pltpu.make_async_remote_copy(
        src_ref=src, dst_ref=dst, send_sem=send_sem, recv_sem=recv_sem,
        device_id=target, device_id_type=MESH)


class Gather:
    def __init__(self, kinds, depth, sources, outs, sems):
        self.kinds, self.depth, self.sources, self.outs = kinds, depth, sources, outs
        self.own_sem, self.send, self.got, self.sib_send, self.sib_got, self.diag_got = sems
        self.number = {a: n for n, a in enumerate(kinds)}
        z, x, y, core = place()
        self.z, self.x, self.y, self.core = z, x, y, core
        self.sibling = device_at(z, x, y, 1 - core)
        self.x_next, self.y_next = device_at(z, 1 - x, y, core), device_at(z, x, 1 - y, core)

    def to(self, way, a, z_at, x_at, y_at, target, part=None, src=None):
        n, k = self.number[a], (z_at * 2 + x_at) * 2 + y_at
        if part is None:
            spot_at, recv = spot(self.outs, a, z_at, x_at, y_at, self.core), self.got.at[n, k]
        else:
            spot_at = spot_part(self.outs, a, z_at, x_at, y_at, self.core, part)
            recv = self.diag_got.at[n, z_at, part]
        return remote(spot_at if src is None else src, spot_at, self.send.at[way, n, k], recv, target)

    def to_sibling(self, a, z_at, x_at, y_at, src=None, core=None):
        spot_at = spot(self.outs, a, z_at, x_at, y_at, self.core if core is None else core)
        n, k = self.number[a], (z_at * 2 + x_at) * 2 + y_at
        return remote(
            spot_at if src is None else src, spot_at, self.sib_send.at[n, k], self.sib_got.at[n, k], self.sibling
        )

    def own_copy(self, a):
        return pltpu.make_async_copy(
            self.sources[a], spot(self.outs, a, self.z, self.x, self.y, self.core), self.own_sem.at[self.number[a]]
        )

    def begin(self, kinds):
        z, x, y, core = self.z, self.x, self.y, self.core
        for a in kinds:
            source = self.sources[a]
            self.own_copy(a).start()

            @pl.when(z < self.depth - 1)
            def _():
                self.to(0, a, z, x, y, device_at(z + 1, x, y, core), src=source).start()

            @pl.when(z > 0)
            def _():
                self.to(1, a, z, x, y, device_at(z - 1, x, y, core), src=source).start()

            self.to(2, a, z, x, y, self.x_next, src=source).start()
            self.to(3, a, z, x, y, self.y_next, src=source).start()
            self.to_sibling(a, z, x, y, src=source).start()

    def sides(self, step, act):
        if step == 0:
            act(self.z)
            return
        for sign in (1, -1):
            z_at = self.z + sign * step

            @pl.when((z_at >= 0) & (z_at < self.depth))
            def _():
                act(z_at)

    def first(self, step):
        z, x, y, core = self.z, self.x, self.y, self.core

        def act(z_at):
            for a in self.kinds:
                self.to(0, a, z_at, x, y, self.sibling).wait_recv()

                @pl.when((z_at < z) & (z < self.depth - 1))
                def _():
                    self.to(0, a, z_at, x, y, device_at(z + 1, x, y, core)).start()

                @pl.when((z_at > z) & (z > 0))
                def _():
                    self.to(1, a, z_at, x, y, device_at(z - 1, x, y, core)).start()

                self.to(2, a, z_at, x, y, self.x_next).start()
                self.to(3, a, z_at, x, y, self.y_next).start()
                self.to_sibling(a, z_at, x, y).start()

        self.sides(step, act)

    def second(self, step):
        x, y = self.x, self.y

        def act(z_at):
            for a in self.kinds:
                self.to(0, a, z_at, 1 - x, y, self.sibling).wait_recv()
                self.to(3, a, z_at, 1 - x, y, self.y_next, 0).start()
                self.to_sibling(a, z_at, 1 - x, y).start()
                self.to(0, a, z_at, x, 1 - y, self.sibling).wait_recv()
                self.to(2, a, z_at, x, 1 - y, self.x_next, 1).start()
                self.to_sibling(a, z_at, x, 1 - y).start()

        self.sides(step, act)

    def third(self, step):
        x, y = self.x, self.y

        def act(z_at):
            for a in self.kinds:
                for part in range(2):
                    self.to(0, a, z_at, 1 - x, 1 - y, self.sibling, part).wait_recv()
                self.to_sibling(a, z_at, 1 - x, 1 - y).start()

        self.sides(step, act)

    def relays(self):
        for step in range(1, self.depth + 2):
            if step < self.depth:
                yield functools.partial(self.first, step)
            if 0 <= step - 1 < self.depth:
                yield functools.partial(self.second, step - 1)
            if 0 <= step - 2 < self.depth:
                yield functools.partial(self.third, step - 2)

    def arrive(self):
        for a in self.kinds:
            self.own_copy(a).wait()

        def wait(z_at, carry):
            for a in self.kinds:
                for x_at in range(2):
                    for y_at in range(2):
                        self.to_sibling(a, z_at, x_at, y_at, core=1 - self.core).wait_recv()
            return carry

        lax.fori_loop(0, self.depth, wait, 0)

    def finish(self):
        z, x, y = self.z, self.x, self.y

        def wait(z_at, carry):
            for a in self.kinds:

                @pl.when((z_at <= z) & (z < self.depth - 1))
                def _():
                    self.to(0, a, z_at, x, y, self.x_next).wait_send()

                @pl.when((z_at >= z) & (z > 0))
                def _():
                    self.to(1, a, z_at, x, y, self.x_next).wait_send()

                self.to(2, a, z_at, x, y, self.x_next).wait_send()
                self.to(3, a, z_at, x, y, self.y_next).wait_send()
                self.to(3, a, z_at, 1 - x, y, self.y_next, 0).wait_send()
                self.to(2, a, z_at, x, 1 - y, self.x_next, 1).wait_send()
                for x_at in range(2):
                    for y_at in range(2):
                        self.to_sibling(a, z_at, x_at, y_at).wait_send()
            return carry

        lax.fori_loop(0, self.depth, wait, 0)


def gather_sems(kinds, depth):
    count, spots = len(kinds), 4 * depth
    return [
        pltpu.SemaphoreType.DMA((count,)),
        pltpu.SemaphoreType.DMA((4, count, spots)),
        pltpu.SemaphoreType.DMA((count, spots)),
        pltpu.SemaphoreType.DMA((count, spots)),
        pltpu.SemaphoreType.DMA((count, spots)),
        pltpu.SemaphoreType.DMA((count, depth, 2)),
    ]


BY_Y = (EXPAND, EARLY)
FIRST_KINDS = (EXPAND, REDUCE, EARLY)
LAST_KINDS = (LATE,)
FRONT_KINDS = (SQUARE, EXPAND)
LATER_KINDS = (REDUCE,)


def front_kernel(fold, depth, keys_ref, gains_in, table_ref, square_f32, expand_f32, *refs):
    found, square_out, expand_out, keys_all, gains_all = refs[:5]
    refs = refs[1:]
    theirs, own, turned, rows, blocks, row_low, row_all = refs[4:11]
    square_in, expand_in, gains_ref = refs[11:14]
    gather_sem, refs = refs[14:20], refs[20:]
    pair_send, pair_recv, part_send, part_got, part_own, keys_send, keys_got, gains_send, gains_got, near_sem = refs
    dp_size, fsdp_size = lax.axis_size("dp"), lax.axis_size("fsdp")
    count = dp_size * fsdp_size
    me = lax.axis_index("dp") * fsdp_size + lax.axis_index("fsdp")
    z, x, y, core = place()
    sibling = device_at(z, x, y, 1 - core)
    gains_ref[...] = jnp.zeros_like(gains_ref)
    gains_ref[: gains_in.shape[0], : gains_in.shape[1]] = gains_in[...]
    expand_in[...] = expand_f32[...].astype(jnp.bfloat16)
    for c in range(2):
        for k in range(5):
            square_in[c, k] = square_f32[k, c * 48 : (c + 1) * 48].astype(jnp.bfloat16)
    greet_all(count, fsdp_size, me)

    def info_copies(k):
        target = lax.rem(me + k, count)
        device = (target // fsdp_size, lax.rem(target, fsdp_size))
        return (
            remote(keys_ref, keys_all.at[me], keys_send.at[k], keys_got.at[k], device),
            remote(gains_ref, gains_all.at[me], gains_send.at[k], gains_got.at[k], device),
        )

    def start_info(k, carry):
        for copy in info_copies(k):
            copy.start()
        return carry

    lax.fori_loop(1, count, start_info, 0)
    keys_all[me] = keys_ref[...]
    gains_all[me] = gains_ref[...]
    pair = remote(square_in.at[1 - core], theirs, pair_send, pair_recv, sibling)
    pair.start()
    gather = Gather(
        FRONT_KINDS, depth, {SQUARE: own, EXPAND: expand_in}, {SQUARE: square_out, EXPAND: expand_out}, gather_sem
    )
    gather.begin((EXPAND,))
    row = lax.broadcasted_iota(jnp.int32, (192, 384), 0)
    col = lax.broadcasted_iota(jnp.int32, (192, 384), 1)
    here = (row + core * 192 == col).astype(jnp.float32).astype(jnp.bfloat16)
    there = (row + (1 - core) * 192 == col).astype(jnp.float32).astype(jnp.bfloat16)
    pair.wait_recv()
    for k in range(5):
        block = jnp.dot(square_in[core, k], here, preferred_element_type=jnp.float32) + jnp.dot(
            theirs[k], there, preferred_element_type=jnp.float32
        )
        own[k] = block.astype(jnp.bfloat16)
    gather.begin((SQUARE,))
    turn_table(fold, table_ref, turned)

    def end_info(k, carry):
        for copy in info_copies(k):
            copy.wait()
        return carry

    lax.fori_loop(1, count, end_info, 0)
    key_rows = row_low.shape[0] // count

    def split_row(k, carry):
        row_low[pl.ds(pl.multiple_of(k * key_rows, 8), key_rows)] = keys_all[k, :key_rows] >> 2
        return carry

    lax.fori_loop(0, count, split_row, 0)
    near = pltpu.make_async_copy(row_low, row_all, near_sem)
    near.start()
    near.wait()

    def find(target):
        keys = keys_all[target]
        group = jnp.concatenate([keys[r : r + 1] for r in range(key_rows)], axis=1) & 3

        def fetch(r, carry):
            line = target * key_rows + r
            start = pl.multiple_of(r * LANES, LANES)
            for k in range(LANES):
                rows[pl.ds(start + k, 1), :] = turned[pl.ds(row_all[line, k], 1), :]
            return carry

        lax.fori_loop(0, key_rows, fetch, 0)
        return pick_group(rows, group, table_ref.shape[0])

    def part_copy(k):
        target = lax.rem(me + k, count)
        device = (target // fsdp_size, lax.rem(target, fsdp_size))
        return remote(blocks.at[target], found.at[me], part_send.at[k], part_got.at[k], device)

    def serve(k, carry):
        target = lax.rem(me + k, count)
        blocks[target] = find(target)
        part_copy(k).start()
        return carry

    relays = list(gather.relays())
    done = 1
    for n, relay in enumerate(relays):
        until = 1 + ((n + 1) * (count - 1)) // len(relays)
        lax.fori_loop(done, until, serve, 0)
        done = until
        relay()
    blocks[me] = find(me)
    own_part = pltpu.make_async_copy(blocks.at[me], found.at[me], part_own)
    own_part.start()
    pair.wait_send()
    gather.arrive()
    gather.finish()
    own_part.wait()

    def end_part(k, carry):
        part_copy(k).wait()
        return carry

    lax.fori_loop(1, count, end_part, 0)


def run_front(keys, gains, tokens, table, square, expand, call_id):
    depth = lax.axis_size("dp") // 2
    count = lax.axis_size("dp") * lax.axis_size("fsdp")
    feats, vocab = table.shape
    fold = fold_rows(vocab)
    blocks = (count, 2 * feats, tokens // 2)
    whole = pl.BlockSpec(memory_space=pltpu.VMEM)
    anywhere = pl.BlockSpec(memory_space=pl.ANY)
    many = pltpu.SemaphoreType.DMA((count,))
    return pl.pallas_call(
        functools.partial(front_kernel, fold, depth),
        out_shape=[
            jax.ShapeDtypeStruct(blocks, jnp.bfloat16),
            jax.ShapeDtypeStruct((5, 768, 768), jnp.bfloat16),
            jax.ShapeDtypeStruct((768, 3072), jnp.bfloat16),
            jax.ShapeDtypeStruct((count,) + keys.shape, keys.dtype),
            jax.ShapeDtypeStruct((count, 8, LANES), gains.dtype),
        ],
        in_specs=[whole] * 5,
        out_specs=[anywhere] * 3 + [whole] * 2,
        scratch_shapes=[
            pltpu.VMEM((5, 48, 192), jnp.bfloat16),
            pltpu.VMEM((5, 48, 384), jnp.bfloat16),
            pltpu.VMEM((fold + 8, LANES), jnp.float32),
            pltpu.VMEM((tokens, LANES), jnp.float32),
            pltpu.VMEM(blocks, jnp.bfloat16),
            pltpu.VMEM((count * tokens // LANES, LANES), jnp.int32),
            pltpu.SMEM((count * tokens // LANES, LANES), jnp.int32),
            pltpu.VMEM((2, 5, 48, 192), jnp.bfloat16),
            pltpu.VMEM((96, 768), jnp.bfloat16),
            pltpu.VMEM((8, LANES), jnp.float32),
        ]
        + gather_sems(FRONT_KINDS, depth)
        + [pltpu.SemaphoreType.DMA, pltpu.SemaphoreType.DMA]
        + [many, many, pltpu.SemaphoreType.DMA]
        + [many] * 4
        + [pltpu.SemaphoreType.DMA],
        compiler_params=pltpu.CompilerParams(
            collective_id=call_id, has_side_effects=True, vmem_limit_bytes=VMEM_CAP
        ),
        name="front",
    )(keys, gains, table, square, expand)


class Reduction:
    def __init__(self, kinds, depth, grads, outs, work, buffers, sems):
        self.kinds, self.depth, self.grads, self.outs, self.own_work = kinds, depth, grads, outs, work
        count = len(kinds)
        self.paired, self.step_one, self.from_x, self.from_y, self.from_z = [
            dict(zip(kinds, buffers[k * count : (k + 1) * count])) for k in range(5)
        ]
        self.load_sem, self.pair_send, self.pair_got, self.send, self.one_got = sems[:5]
        self.x_got, self.y_got, self.z_got = sems[5:8]
        self.number = {a: n for n, a in enumerate(kinds)}
        z, x, y, core = place()
        self.z, self.x, self.y, self.core = z, x, y, core
        self.sibling = device_at(z, x, y, 1 - core)
        self.x_next, self.y_next = device_at(z, 1 - x, y, core), device_at(z, x, 1 - y, core)

    def piece(self, ref, a, z_at, x_at, y_at):
        i = z_at * 2 + x_at
        if a == EXPAND:
            return ref.at[y_at, pl.ds(pl.multiple_of(i * 96, 16), 96)]
        if a == REDUCE:
            return ref.at[y_at, :, pl.ds(pl.multiple_of(i * 384, 128), 384)]
        return ref.at[i, :, :, pl.ds(pl.multiple_of(y_at * 384, 128), 384)]

    def work(self, a, z_at, x_at, y_at):
        if a in SPANS:
            return spot(self.grads, a, z_at, x_at, y_at, self.core)
        return self.piece(self.own_work[a], a, z_at, x_at, y_at)

    def half(self, a, y_at, core):
        column = y_at * 2 + core
        if a == EXPAND:
            return self.grads[a].at[:, pl.ds(pl.multiple_of(column * 768, 128), 768)]
        return self.grads[a].at[pl.ds(pl.multiple_of(column * 192, 16), 192)]

    def load(self, a, y_at):
        return pltpu.make_async_copy(
            self.half(a, y_at, self.core), self.own_work[a].at[y_at], self.load_sem.at[self.number[a], y_at]
        )

    def pair(self, a, at):
        n = self.number[a]
        if a in SPANS:
            source = self.grads[SQUARE].at[
                pl.ds(*SPANS[a]), pl.ds(pl.multiple_of(at * 96 + (1 - self.core) * 48, 16), 48)
            ]
        else:
            source = self.half(a, at, 1 - self.core)
        return remote(source, self.paired[a].at[at], self.pair_send.at[n, at], self.pair_got.at[n, at], self.sibling)

    def each_pair(self, a, act):
        if a not in SPANS:
            act(1 - self.y)
            act(self.y)
            return

        def one(i, carry):
            act(i)
            return carry

        lax.fori_loop(0, 2 * self.depth, one, 0)

    def sides(self, step, act):
        if step == 0:
            act(self.z)
            return
        for sign in (1, -1):
            z_at = self.z + sign * step

            @pl.when((z_at >= 0) & (z_at < self.depth))
            def _():
                act(z_at)

    def begin(self, kinds):
        for a in kinds:

            def start(at):
                if a not in SPANS:
                    self.load(a, at).start()
                self.pair(a, at).start()

            self.each_pair(a, start)

    def ready(self, last):
        for a in self.kinds:
            if a in SPANS:
                if not last:
                    self.each_pair(a, lambda at: self.pair(a, at).wait_recv())
            else:
                y_at = self.y if last else 1 - self.y
                self.load(a, y_at).wait()
                self.pair(a, y_at).wait_recv()

    def total(self, a, z_at, x_at, y_at, extra=()):
        here = self.work(a, z_at, x_at, y_at)
        paired = self.piece(self.paired[a], a, z_at, x_at, y_at)

        value = here[...] + paired[...]
        for buffer in extra:
            value = value + buffer[...]
        here[...] = value

    def diag_copy(self, a, z_at):
        n = self.number[a]
        return remote(
            self.work(a, z_at, 1 - self.x, 1 - self.y),
            self.step_one[a].at[z_at],
            self.send.at[0, n, z_at],
            self.one_got.at[n, z_at],
            self.y_next if a in BY_Y else self.x_next,
        )

    def diag(self, step):
        def act(z_at):
            for a in self.kinds:
                self.total(a, z_at, 1 - self.x, 1 - self.y)
                self.diag_copy(a, z_at).start()

        if step == self.depth - 1:
            self.ready(False)
        self.sides(step, act)

    def x_copy(self, a, z_at):
        n = self.number[a]
        return remote(
            self.work(a, z_at, 1 - self.x, self.y),
            self.from_x[a].at[z_at],
            self.send.at[2, n, z_at],
            self.x_got.at[n, z_at],
            self.x_next,
        )

    def y_copy(self, a, z_at):
        n = self.number[a]
        return remote(
            self.work(a, z_at, self.x, 1 - self.y),
            self.from_y[a].at[z_at],
            self.send.at[3, n, z_at],
            self.y_got.at[n, z_at],
            self.y_next,
        )

    def columns(self, step):
        x, y = self.x, self.y

        def act(z_at):
            for a in self.kinds:
                received = [self.step_one[a].at[z_at]]
                self.diag_copy(a, z_at).wait_recv()
                self.total(a, z_at, 1 - x, y, received if a in BY_Y else ())
                self.x_copy(a, z_at).start()
                self.total(a, z_at, x, 1 - y, () if a in BY_Y else received)
                self.y_copy(a, z_at).start()

        if step == self.depth - 1:
            self.ready(True)
        self.sides(step, act)

    def z_copy(self, a, z_at, side, target):
        n = self.number[a]
        return remote(
            self.work(a, z_at, self.x, self.y),
            self.from_z[a].at[side, z_at],
            self.send.at[4, n, z_at],
            self.z_got.at[n, side, z_at],
            target,
        )

    def line(self, step, keep=None):
        z, x, y, core, depth = self.z, self.x, self.y, self.core, self.depth

        def act(z_at):
            for a in self.kinds:
                self.x_copy(a, z_at).wait_recv()
                self.y_copy(a, z_at).wait_recv()
                across = [self.from_x[a].at[z_at], self.from_y[a].at[z_at]]
                if step > 0:
                    upward = z_at > z
                    before = (upward & (z > 0)) | (jnp.logical_not(upward) & (z < depth - 1))
                    side = jnp.where(upward, 0, 1)

                    @pl.when(before)
                    def _():
                        self.z_copy(a, z_at, side, self.sibling).wait_recv()
                        self.total(a, z_at, x, y, across + [self.from_z[a].at[side, z_at]])

                    @pl.when(jnp.logical_not(before))
                    def _():
                        self.total(a, z_at, x, y, across)

                    @pl.when(upward)
                    def _():
                        self.z_copy(a, z_at, 0, device_at(z + 1, x, y, core)).start()

                    @pl.when(jnp.logical_not(upward))
                    def _():
                        self.z_copy(a, z_at, 1, device_at(z - 1, x, y, core)).start()
                else:
                    for side in range(2):
                        present = (z > 0) if side == 0 else (z < depth - 1)

                        @pl.when(present)
                        def _():
                            self.z_copy(a, z, side, self.sibling).wait_recv()

                        @pl.when(jnp.logical_not(present))
                        def _():
                            self.from_z[a][side, z] = jnp.zeros(BLOCKS[a], jnp.bfloat16)

                    here, paired = self.work(a, z, x, y), self.piece(self.paired[a], a, z, x, y)

                    def finish(k, carry):
                        value = block_step(here, a, k)[...].astype(jnp.float32)
                        for buffer in [paired] + across + [self.from_z[a].at[0, z], self.from_z[a].at[1, z]]:
                            value = value + block_step(buffer, a, k)[...].astype(jnp.float32)
                        if a in SPANS:
                            spare, at = self.outs[3], k + SPANS[a][0]
                            low, high = value[:, :192], pltpu.roll(value, 192, 1)[:, :192]
                            self.outs[SQUARE][core, at] = jnp.where(core == 0, low, high)
                            spare[at] = jnp.where(core == 0, high, low)
                        else:
                            block_step(self.outs[a], a, k)[...] = value
                        return carry

                    lax.fori_loop(0, STEPS[a], finish, 0)

        self.sides(step, act)

    def groups(self):
        rounds = list(range(self.depth - 1, -1, -1))
        for k in range(self.depth + 2):
            group = []
            if k < self.depth:
                group.append((self.diag, rounds[k]))
            if 0 <= k - 1 < self.depth:
                group.append((self.columns, rounds[k - 1]))
            if 0 <= k - 2 < self.depth:
                group.append((self.line, rounds[k - 2]))
            yield group

    def finish(self):
        def wait(z_at, carry):
            for a in self.kinds:
                self.diag_copy(a, z_at).wait_send()
                self.x_copy(a, z_at).wait_send()
                self.y_copy(a, z_at).wait_send()

                @pl.when(z_at != self.z)
                def _():
                    self.z_copy(a, z_at, 0, self.sibling).wait_send()
            return carry

        lax.fori_loop(0, self.depth, wait, 0)
        for a in self.kinds:
            self.each_pair(a, lambda at: self.pair(a, at).wait_send())


def pair_shape(a, depth):
    if a == EXPAND:
        return (2, depth * 192, 768)
    if a == REDUCE:
        return (2, 192, depth * 768)
    return (2 * depth, SPANS[a][1], 48, 768)


def reduction_scratch(kinds, depth):
    def buffers(*lead):
        return [pltpu.VMEM(lead + BLOCKS[a], jnp.bfloat16) for a in kinds]

    count = len(kinds)
    spots = pltpu.SemaphoreType.DMA((count, 2 * depth))
    return (
        [pltpu.VMEM(pair_shape(a, depth), jnp.bfloat16) for a in kinds]
        + buffers(depth) + buffers(depth) + buffers(depth) + buffers(2, depth),
        [
            spots,
            spots,
            spots,
            pltpu.SemaphoreType.DMA((5, count, depth)),
            pltpu.SemaphoreType.DMA((count, depth)),
            pltpu.SemaphoreType.DMA((count, depth)),
            pltpu.SemaphoreType.DMA((count, depth)),
            pltpu.SemaphoreType.DMA((count, 2, depth)),
        ],
    )


TILE = 128
PAIRS = HEADS // 2
GELU_IN = (2.0 / np.pi) ** 0.5


def dot_nn(left, right):
    return jnp.dot(left, right, preferred_element_type=jnp.float32)


def dot_nt(left, right):
    return lax.dot_general(left, right, (((1,), (1,)), ((), ())), preferred_element_type=jnp.float32)


def dot_tn(left, right):
    return lax.dot_general(left, right, (((0,), (0,)), ((), ())), preferred_element_type=jnp.float32)


def three_parts(values):
    high = values.astype(jnp.bfloat16)
    rest = values - high.astype(jnp.float32)
    middle = rest.astype(jnp.bfloat16)
    low = (rest - middle.astype(jnp.float32)).astype(jnp.bfloat16)
    return jnp.concatenate([high, middle, low], axis=0)


def rows_at(index, size):
    return pl.ds(pl.multiple_of(index * size, size), size)


def split_heads(block):
    low = lax.broadcasted_iota(jnp.int32, block.shape, 1) < HEAD
    wide = block.astype(jnp.float32)
    first = jnp.where(low, wide, 0.0).astype(jnp.bfloat16)
    second = jnp.where(low, 0.0, wide).astype(jnp.bfloat16)
    return jnp.concatenate([first, second], axis=0)


def join_heads(stacked):
    return jnp.concatenate([stacked[:TILE], stacked[TILE:]], axis=1)


def pair_probs(query, keys_here, bias, mask):
    scores = dot_nt(split_heads(query), keys_here) * HEAD ** (-0.5) + bias
    scores = scores + mask
    raised = jnp.exp(scores - jnp.max(scores, axis=1, keepdims=True))
    return raised / jnp.sum(raised, axis=1, keepdims=True)


def pair_bias(bias_ref, pair):
    return jnp.concatenate([bias_ref[2 * pair], bias_ref[2 * pair + 1]], axis=0)


def tile_mask(mask_ref, tile):
    mask = mask_ref[tile]
    return jnp.concatenate([mask, mask], axis=0)


def hot_rows(rank_ref, rows, slots, first=0):
    place = lax.broadcasted_iota(jnp.int32, (rows.size, slots), 1) + first
    return (rank_ref[rows, :1] == place).astype(jnp.float32).astype(jnp.bfloat16)


def norm_rows(values, gain):
    scale = lax.rsqrt(jnp.mean(values * values, axis=1, keepdims=True) + NORM_EPS)
    return values * scale * gain


def gelu_parts(pre):
    inner = GELU_IN * (pre + 0.044715 * pre * pre * pre)
    return jnp.tanh(inner)


def forward_steps(
    found_ref, rank_ref, square_ref, gains_ref, bias_ref, mask_ref, pool_ref, length_ref,
    start_ref, query_ref, key_ref, value_ref, mixed_ref, middle_ref, ending_ref, low_ref, pooled_ref, embed_ref,
    inverse_ref, normed, pooled_sum, wide_found, low_found, expand_ref, reduce_ref, between, before_feed, need,
):
    between = list(between)

    def relay(count):
        for _ in range(min(count, len(between))):
            between.pop(0)()

    tokens = start_ref.shape[0]
    big = 512
    feats, half = found_ref.shape[1] // 2, found_ref.shape[2]
    need(0)

    def assemble(p, carry):
        block = found_ref[p].astype(jnp.float32)
        at = pl.ds(pl.multiple_of(p * feats, 8), feats)
        wide_found[at, :half] = block[:feats]
        wide_found[at, half:] = block[feats:]
        return carry

    lax.fori_loop(0, found_ref.shape[0], assemble, 0)
    low_found[...] = wide_found[...].astype(jnp.bfloat16)

    def begin(r, carry):
        rows = rows_at(r, 256)
        start = dot_nt(hot_rows(rank_ref, rows, tokens), low_found[...])
        start_ref[rows, :] = start.astype(jnp.bfloat16)
        normed[rows, :] = norm_rows(start, gains_ref[0:1]).astype(jnp.bfloat16)
        return carry

    lax.fori_loop(0, tokens // 256, begin, 0)
    relay(1)
    need(1)
    for k, target in enumerate((query_ref, key_ref, value_ref)):

        def project(r, carry):
            rows = rows_at(r, big)
            target[rows, :] = dot_nn(normed[rows, :], square_ref[k]).astype(jnp.bfloat16)
            return carry

        lax.fori_loop(0, tokens // big, project, 0)
        relay(1)

    def attend(t, carry):
        rows = rows_at(t, TILE)
        mask = tile_mask(mask_ref, t)
        for pair in range(PAIRS):
            lanes = pl.ds(pair * TILE, TILE)
            probs = pair_probs(query_ref[rows, lanes], key_ref[rows, lanes], pair_bias(bias_ref, pair), mask)
            mixed = dot_nn(join_heads(probs).astype(jnp.bfloat16), split_heads(value_ref[rows, lanes]))
            mixed_ref[rows, lanes] = mixed.astype(jnp.bfloat16)
        return carry

    tiles = tokens // TILE
    need(2)
    if between:
        for t in range(tiles):
            lax.fori_loop(t, t + 1, attend, 0)
            relay(1)
    else:
        lax.fori_loop(0, tiles, attend, 0)

    def merge(r, carry):
        rows = rows_at(r, big)
        middle = start_ref[rows, :].astype(jnp.float32) + dot_nn(mixed_ref[rows, :], square_ref[3])
        middle_ref[rows, :] = middle
        ending_ref[rows, :] = middle
        normed[rows, :] = norm_rows(middle, gains_ref[1:2]).astype(jnp.bfloat16)
        return carry

    lax.fori_loop(0, tokens // big, merge, 0)
    relay(len(between))
    before_feed()
    wide = expand_ref.shape[1]

    def feed(c, carry):
        lanes = rows_at(c, D)

        def rows_of(r, inner):
            rows = rows_at(r, big)
            pre = dot_nn(normed[rows, :], expand_ref[:, lanes])
            act = (0.5 * pre * (1.0 + gelu_parts(pre))).astype(jnp.bfloat16)
            ending_ref[rows, :] += dot_nt(act, reduce_ref[:, lanes])
            return inner

        return lax.fori_loop(0, tokens // big, rows_of, carry)

    lax.fori_loop(0, wide // D, feed, 0)
    pooled_sum[...] = jnp.zeros_like(pooled_sum)

    def pool(r, carry):
        rows = rows_at(r, 256)
        output = norm_rows(ending_ref[rows, :], gains_ref[2:3])
        inside = pool_ref[:, rows].astype(jnp.bfloat16)
        pooled_sum[...] += dot_nn(jnp.concatenate([inside] * 3, axis=1), three_parts(output))
        return carry

    lax.fori_loop(0, tokens // 256, pool, 0)
    pooled = (pooled_sum[...] / length_ref[:, :1]).astype(jnp.bfloat16)
    pooled_ref[...] = pooled
    projected = dot_nn(pooled, square_ref[4])
    inverse = lax.rsqrt(jnp.sum(projected * projected, axis=1, keepdims=True) + NORM_EPS)
    embeds = projected * inverse
    embed_ref[...] = embeds
    low_ref[...] = embeds.astype(jnp.bfloat16)
    inverse_ref[...] = jnp.broadcast_to(inverse, inverse_ref.shape)


def forward_kernel(*refs):
    ins, expand_ref, reduce_ref, rest = refs[:8], refs[8], refs[9], refs[10:]
    forward_steps(*ins, *rest, expand_ref, reduce_ref, [], lambda: None, lambda stage: None)


FORWARD_STAGES = ((0, 1), (2,), (4, 5), (8,))


def relayed_forward_kernel(depth, *refs):
    given, reduce_in = list(refs[:9]), refs[9]
    outs, reduce_out = refs[10:21], refs[21]
    steps, reduce_all = refs[22:26], refs[26]
    sems, save_sem = refs[27:33], refs[33]
    need = stage_loads(given, FORWARD_STAGES, refs[34:40], refs[40])
    greet_neighbours(depth)
    gather = Gather(LATER_KINDS, depth, {REDUCE: reduce_in}, {REDUCE: reduce_all}, sems)
    gather.begin(LATER_KINDS)
    save = pltpu.make_async_copy(reduce_all, reduce_out, save_sem)

    def before_feed():
        need(3)
        gather.arrive()
        save.start()

    forward_steps(*given[:8], *outs, *steps, given[8], reduce_all, gather.relays(), before_feed, need)
    gather.finish()
    save.wait()


def stage_loads(given, stages, homes, sem):
    loads, n = [], 0
    for stage in stages:
        group = []
        for at in stage:
            group.append(pltpu.make_async_copy(given[at], homes[n], sem.at[n]))
            given[at] = homes[n]
            n += 1
        loads.append(group)
    for group in loads:
        for load in group:
            load.start()

    def need(stage):
        for load in loads[stage]:
            load.wait()

    return need


def stage_specs(arrays, stages):
    whole = pl.BlockSpec(memory_space=pltpu.VMEM)
    anywhere = pl.BlockSpec(memory_space=pl.ANY)
    order = [at for stage in stages for at in stage]
    specs = [anywhere if at in order else whole for at in range(len(arrays))]
    homes = [pltpu.VMEM(arrays[at].shape, arrays[at].dtype) for at in order]
    return specs, homes, pltpu.SemaphoreType.DMA((len(order),))


def forward_outs(tokens, seqs):
    flat = jax.ShapeDtypeStruct((tokens, D), jnp.bfloat16)
    full = jax.ShapeDtypeStruct((tokens, D), jnp.float32)
    few = jax.ShapeDtypeStruct((seqs, D), jnp.bfloat16)
    return [
        flat, flat, flat, flat, flat, full, full, few, few,
        jax.ShapeDtypeStruct((seqs, D), jnp.float32),
        jax.ShapeDtypeStruct((seqs, LANES), jnp.float32),
    ]


def forward_scratch(tokens, seqs):
    return [
        pltpu.VMEM((tokens, D), jnp.bfloat16),
        pltpu.VMEM((seqs, D), jnp.float32),
        pltpu.VMEM((D, tokens), jnp.float32),
        pltpu.VMEM((D, tokens), jnp.bfloat16),
    ]


def run_forward(ins, expand, reduce_turned):
    tokens, seqs = ins[1].shape[0], ins[6].shape[0]
    return pl.pallas_call(
        forward_kernel,
        out_shape=forward_outs(tokens, seqs),
        scratch_shapes=forward_scratch(tokens, seqs),
        compiler_params=pltpu.CompilerParams(vmem_limit_bytes=VMEM_CAP),
        name="layer_forward",
    )(*ins, expand, reduce_turned)


def run_relayed_forward(ins, expand, reduce_piece, call_id):
    depth = lax.axis_size("dp") // 2
    tokens, seqs = ins[1].shape[0], ins[6].shape[0]
    weight = (768, 3072)
    outs = forward_outs(tokens, seqs)
    whole = pl.BlockSpec(memory_space=pltpu.VMEM)
    anywhere = pl.BlockSpec(memory_space=pl.ANY)
    specs, homes, load_sem = stage_specs((*ins, expand), FORWARD_STAGES)
    return pl.pallas_call(
        functools.partial(relayed_forward_kernel, depth),
        out_shape=outs + [jax.ShapeDtypeStruct(weight, jnp.bfloat16)],
        in_specs=specs + [whole],
        out_specs=[whole] * len(outs) + [anywhere],
        scratch_shapes=forward_scratch(tokens, seqs)
        + [pltpu.VMEM(weight, jnp.bfloat16)]
        + gather_sems(LATER_KINDS, depth)
        + [pltpu.SemaphoreType.DMA]
        + homes
        + [load_sem],
        compiler_params=pltpu.CompilerParams(
            collective_id=call_id, has_side_effects=True, vmem_limit_bytes=VMEM_CAP
        ),
        name="layer_forward",
    )(*ins, expand, reduce_piece)


def norm_back_rows(values, gain, grad):
    scale = lax.rsqrt(jnp.mean(values * values, axis=1, keepdims=True) + NORM_EPS)
    weighted = grad * gain
    inner = jnp.mean(weighted * values, axis=1, keepdims=True)
    through = scale * weighted - values * (scale * scale * scale * inner)
    return through, jnp.sum(grad * values * scale, axis=0, keepdims=True)


def feed_norms(middle_ref, gains_ref, normed, normed_turned):
    def step(r, carry):
        rows = rows_at(r, 256)
        middle_normed = norm_rows(middle_ref[rows, :], gains_ref[1:2])
        normed[rows, :] = middle_normed.astype(jnp.bfloat16)
        normed_turned[:, rows] = middle_normed.T.astype(jnp.bfloat16)
        return carry

    lax.fori_loop(0, middle_ref.shape[0] // 256, step, 0)


def feed_back_steps(
    grads, embed_ref, inverse_ref, pool_ref, length_ref, last_ref, middle_ref, ending_ref, expand_ref,
    reduce_ref, gains_ref,
    grad_expand_ref, grad_reduce_ref, grad_middle_ref, grad_proj_ref, grad_gains_ref,
    normed, normed_turned, end_low, end_turned, back, before_feed, saved,
):
    tokens = middle_ref.shape[0]
    embeds = embed_ref[...]
    grad_proj = inverse_ref[:, :1] * (grads - embeds * jnp.sum(grads * embeds, axis=1, keepdims=True))
    grad_proj = grad_proj.astype(jnp.bfloat16)
    grad_proj_ref[...] = grad_proj
    grad_pooled = dot_nt(grad_proj, last_ref[...]) / length_ref[:, :1]
    grad_gains_ref[...] = jnp.zeros_like(grad_gains_ref)
    grad_parts = three_parts(grad_pooled)

    def begin(r, carry):
        rows = rows_at(r, 256)
        inside = pool_ref[:, rows].astype(jnp.bfloat16)
        grad_out = dot_tn(jnp.concatenate([inside] * 3, axis=0), grad_parts)
        through, gain = norm_back_rows(ending_ref[rows, :], gains_ref[2:3], grad_out)
        grad_gains_ref[2:3] += gain
        grad_middle_ref[rows, :] = through
        end_low[rows, :] = through.astype(jnp.bfloat16)
        end_turned[:, rows] = through.T.astype(jnp.bfloat16)
        return carry

    lax.fori_loop(0, tokens // 256, begin, 0)
    before_feed()
    back[...] = jnp.zeros_like(back)
    wide = expand_ref.shape[1]
    step = FEED_STEP

    def feed(c, carry):
        lanes = rows_at(c, step)
        pre = dot_nn(normed[...], expand_ref[:, lanes])
        grad_act = dot_nn(end_low[...], reduce_ref[:, lanes])
        turn = gelu_parts(pre)
        act = (0.5 * pre * (1.0 + turn)).astype(jnp.bfloat16)
        slope = 0.5 * (1.0 + turn) + 0.5 * pre * (1.0 - turn * turn) * GELU_IN * (1.0 + 3.0 * 0.044715 * pre * pre)
        grad_pre = (grad_act * slope).astype(jnp.bfloat16)
        grad_reduce_ref[:, lanes] = dot_nn(end_turned[...], act).astype(jnp.bfloat16)
        grad_expand_ref[:, lanes] = dot_nn(normed_turned[...], grad_pre).astype(jnp.bfloat16)
        back[...] += dot_nt(grad_pre, expand_ref[:, lanes])
        saved(c)
        return carry

    lax.fori_loop(0, wide // step, feed, 0)

    def end(r, carry):
        rows = rows_at(r, 256)
        through, gain = norm_back_rows(middle_ref[rows, :], gains_ref[1:2], back[rows, :])
        grad_gains_ref[1:2] += gain
        grad_middle_ref[rows, :] += through
        return carry

    lax.fori_loop(0, tokens // 256, end, 0)


def feed_back_kernel(*refs):
    grads, (embed, inverse, pool, length, last, middle, ending, expand, reduce_turned, gains), rest = (
        refs[0], refs[1:11], refs[11:]
    )
    feed_norms(middle, gains, rest[5], rest[6])
    feed_back_steps(
        grads[...], embed, inverse, pool, length, last.at[0], middle, ending, expand, reduce_turned, gains, *rest,
        lambda: None, lambda c: None,
    )


FEED_STEP = 384


def loss_feed_kernel(query_rows, nli_rows, *refs):
    low_ref, negative_ref, scale_ref, embed_ref, inverse_ref, pool_ref, length_ref, gains_ref = refs[:8]
    square_hbm, middle_hbm, ending_hbm, expand_hbm, reduce_hbm = refs[8:13]
    grad_expand_out, grad_reduce_out, grad_middle_ref, grad_proj_ref, grad_gains_ref, stats_ref = refs[13:19]
    normed, normed_turned, end_low, end_turned, back = refs[19:24]
    last, middle, ending, expand, reduce_turned, grad_expand, grad_reduce = refs[24:31]
    everyone, grad_sims, turned_sims = refs[31:34]
    exchange_sems, load_sem, save_sem = refs[34:38], refs[38], refs[39]
    pairs = (
        (middle_hbm, middle), (ending_hbm, ending), (square_hbm.at[4], last), (expand_hbm, expand),
        (reduce_hbm, reduce_turned),
    )
    loads = [pltpu.make_async_copy(src, dst, load_sem.at[n]) for n, (src, dst) in enumerate(pairs)]
    for load in loads:
        load.start()

    def meanwhile():
        loads[0].wait()
        feed_norms(middle, gains_ref, normed, normed_turned)

    me = share_chips(low_ref, everyone, *exchange_sems, meanwhile)
    grads = loss_steps(
        query_rows, nli_rows, me, low_ref.shape[0], negative_ref, scale_ref, stats_ref, everyone, grad_sims,
        turned_sims,
    )
    loads[1].wait()
    loads[2].wait()

    def before_feed():
        loads[3].wait()
        loads[4].wait()

    def saves(c):
        lanes = rows_at(c, FEED_STEP)
        return (
            pltpu.make_async_copy(grad_expand.at[:, lanes], grad_expand_out.at[:, lanes], save_sem.at[0, c]),
            pltpu.make_async_copy(grad_reduce.at[:, lanes], grad_reduce_out.at[:, lanes], save_sem.at[1, c]),
        )

    def saved(c):
        for save in saves(c):
            save.start()

    feed_back_steps(
        grads, embed_ref, inverse_ref, pool_ref, length_ref, last, middle, ending, expand, reduce_turned, gains_ref,
        grad_expand, grad_reduce, grad_middle_ref, grad_proj_ref, grad_gains_ref,
        normed, normed_turned, end_low, end_turned, back, before_feed, saved,
    )

    def end(c, carry):
        for save in saves(c):
            save.wait()
        return carry

    lax.fori_loop(0, expand.shape[1] // FEED_STEP, end, 0)


def feed_scratch(tokens):
    low = jnp.bfloat16
    return [
        pltpu.VMEM((tokens, D), low),
        pltpu.VMEM((D, tokens), low),
        pltpu.VMEM((tokens, D), low),
        pltpu.VMEM((D, tokens), low),
        pltpu.VMEM((tokens, D), jnp.float32),
    ]


def run_loss_feed(
    embeds_low, negative, log_scale, embeds, inverse, pool, lengths, gains, square, middle, ending, expand,
    reduce_turned, query_rows, nli_rows, call_id,
):
    count = lax.axis_size("dp") * lax.axis_size("fsdp")
    tokens, seqs = middle.shape[0], pool.shape[0]
    low = jnp.bfloat16
    whole = pl.BlockSpec(memory_space=pltpu.VMEM)
    anywhere = pl.BlockSpec(memory_space=pl.ANY)
    few = pltpu.SemaphoreType.DMA((count // 2,))
    weight = pltpu.VMEM(expand.shape, low)
    pairs = pltpu.VMEM((count * seqs, count * seqs), jnp.float32)
    return pl.pallas_call(
        functools.partial(loss_feed_kernel, query_rows, nli_rows),
        out_shape=[
            jax.ShapeDtypeStruct(expand.shape, low),
            jax.ShapeDtypeStruct(reduce_turned.shape, low),
            jax.ShapeDtypeStruct((tokens, D), jnp.float32),
            jax.ShapeDtypeStruct((seqs, D), low),
            jax.ShapeDtypeStruct((8, D), jnp.float32),
            jax.ShapeDtypeStruct((8, LANES), jnp.float32),
        ],
        in_specs=[whole] * 8 + [anywhere] * 5,
        out_specs=[anywhere] * 2 + [whole] * 4,
        scratch_shapes=feed_scratch(tokens)
        + [
            pltpu.VMEM((D, D), low),
            pltpu.VMEM((tokens, D), jnp.float32),
            pltpu.VMEM((tokens, D), jnp.float32),
            weight, weight, weight, weight,
            pltpu.VMEM((count, seqs, D), low),
            pairs, pairs,
            few, few, few, few,
            pltpu.SemaphoreType.DMA((5,)),
            pltpu.SemaphoreType.DMA((2, expand.shape[1] // FEED_STEP)),
        ],
        compiler_params=pltpu.CompilerParams(
            collective_id=call_id, has_side_effects=True, vmem_limit_bytes=VMEM_CAP
        ),
        name="loss_feed",
    )(
        embeds_low, negative, log_scale, embeds, inverse, pool, lengths, gains, square, middle, ending, expand,
        reduce_turned,
    )


def run_feed_back(grad_embed, embeds, inverse, pool, lengths, square, middle, ending, expand, reduce_turned, gains):
    tokens = middle.shape[0]
    seqs = pool.shape[0]
    low = jnp.bfloat16
    whole = pl.BlockSpec(memory_space=pltpu.VMEM)
    return pl.pallas_call(
        feed_back_kernel,
        grid=(1,),
        out_shape=[
            jax.ShapeDtypeStruct(expand.shape, low),
            jax.ShapeDtypeStruct(reduce_turned.shape, low),
            jax.ShapeDtypeStruct((tokens, D), jnp.float32),
            jax.ShapeDtypeStruct((seqs, D), low),
            jax.ShapeDtypeStruct((8, D), jnp.float32),
        ],
        in_specs=[whole] * 5
        + [pl.BlockSpec((1, D, D), lambda i: (4, 0, 0))]
        + [whole] * 5,
        out_specs=[whole] * 5,
        scratch_shapes=[
            pltpu.VMEM((tokens, D), low),
            pltpu.VMEM((D, tokens), low),
            pltpu.VMEM((tokens, D), low),
            pltpu.VMEM((D, tokens), low),
            pltpu.VMEM((tokens, D), jnp.float32),
        ],
        compiler_params=pltpu.CompilerParams(vmem_limit_bytes=VMEM_CAP),
        name="feed_backward",
    )(grad_embed, embeds, inverse, pool, lengths, square, middle, ending, expand, reduce_turned, gains)


def attend_back_steps(
    grad_middle_ref, grad_proj_ref, pooled_ref, start_ref, query_ref, key_ref, value_ref, mixed_ref,
    square_ref, gains_ref, bias_ref, mask_ref, rank_ref,
    grad_square_ref, grad_score_ref, grad_gain_ref, grad_mixed, turned, grad_query, grad_key, grad_value,
    turned_half, between, early_done, squares_done, put, need,
):
    tokens = start_ref.shape[0]
    big = 512
    need(0)
    grad_square_ref[4] = dot_tn(pooled_ref[...], grad_proj_ref[...]).astype(jnp.bfloat16)

    def begin(r, carry):
        rows = rows_at(r, big)
        grad_mixed[rows, :] = dot_nt(grad_middle_ref[rows, :].astype(jnp.bfloat16), square_ref[3]).astype(
            jnp.bfloat16
        )
        turned[:, rows] = mixed_ref[rows, :].astype(jnp.float32).T.astype(jnp.bfloat16)
        return carry

    lax.fori_loop(0, tokens // big, begin, 0)

    def outer(target, right_ref):
        def part(r, carry):
            rows = rows_at(r, 384)
            grad_square_ref[target, rows, :] = dot_nn(turned[rows, :], right_ref[...].astype(jnp.bfloat16)).astype(
                jnp.bfloat16
            )
            return carry

        lax.fori_loop(0, D // 384, part, 0)

    outer(3, grad_middle_ref)
    early_done()
    grad_score_ref[...] = jnp.zeros_like(grad_score_ref)

    def attend(t, carry):
        rows = rows_at(t, TILE)
        mask = tile_mask(mask_ref, t)
        for pair in range(PAIRS):
            lanes = pl.ds(pair * TILE, TILE)
            query, keys_here = query_ref[rows, lanes], key_ref[rows, lanes]
            probs = pair_probs(query, keys_here, pair_bias(bias_ref, pair), mask)
            grads = split_heads(grad_mixed[rows, lanes])
            grad_probs = dot_nt(grads, value_ref[rows, lanes])
            grad_value[rows, lanes] = dot_tn(probs.astype(jnp.bfloat16), grads).astype(jnp.bfloat16)
            inner = jnp.sum(grad_probs * probs, axis=1, keepdims=True)
            grad_scores = (probs * (grad_probs - inner)).astype(jnp.bfloat16)
            kept = grad_scores.astype(jnp.float32)
            grad_score_ref[2 * pair] += kept[:TILE]
            grad_score_ref[2 * pair + 1] += kept[TILE:]
            grad_query[rows, lanes] = (
                dot_nn(join_heads(grad_scores), split_heads(keys_here)) * HEAD ** (-0.5)
            ).astype(jnp.bfloat16)
            grad_key[rows, lanes] = (dot_tn(grad_scores, split_heads(query)) * HEAD ** (-0.5)).astype(jnp.bfloat16)
        return carry

    tiles = tokens // TILE
    between = list(between)
    part = tokens // 2

    def relay(place, number):
        for spot_name, spot_number, act in between:
            if (spot_name, spot_number) == (place, number):
                act()

    grad_gain_ref[...] = jnp.zeros_like(grad_gain_ref)

    def attend_half(half):
        for t in range(half * tiles // 2, (half + 1) * tiles // 2):
            lax.fori_loop(t, t + 1, attend, 0)
            relay("tile", t)

    def end_half(half):
        def end(r, carry):
            rows = pl.ds(pl.multiple_of(half * part + r * 256, 256), 256)
            grad_normed = (
                dot_nt(grad_query[rows, :], square_ref[0])
                + dot_nt(grad_key[rows, :], square_ref[1])
                + dot_nt(grad_value[rows, :], square_ref[2])
            )
            through, gain = norm_back_rows(start_ref[rows, :].astype(jnp.float32), gains_ref[0:1], grad_normed)
            grad_gain_ref[0:1] += gain
            turned_half[:, rows_at(r, 256)] = (grad_middle_ref[rows, :] + through).T.astype(jnp.bfloat16)
            return carry

        lax.fori_loop(0, part // 256, end, 0)

        def merge(r, carry):
            rows = rows_at(r, 384)
            total = jnp.zeros((384, part), jnp.float32)
            for c in range(part // 256):
                hot = hot_rows(rank_ref, pl.ds(half * part + c * 256, 256), part, half * part)
                total = total + dot_nn(turned_half[rows, c * 256 : (c + 1) * 256], hot)
            put(half, r, total)
            return carry

        lax.fori_loop(0, D // 384, merge, 0)
        put(half, None, None)

    need(1)
    attend_half(0)
    need(2)
    end_half(0)
    relay("end", 0)
    attend_half(1)

    def renorm(r, carry):
        rows = rows_at(r, 256)
        normed = norm_rows(start_ref[rows, :].astype(jnp.float32), gains_ref[0:1])
        turned[:, rows] = normed.T.astype(jnp.bfloat16)
        return carry

    lax.fori_loop(0, tokens // 256, renorm, 0)
    relay("norm", 0)
    outer(0, grad_query)
    relay("outer", 0)
    outer(1, grad_key)
    relay("outer", 1)
    outer(2, grad_value)
    squares_done()
    relay("outer", 2)
    end_half(1)
    relay("end", 1)


def attend_back_kernel(*refs):
    ins, rest = refs[:13], refs[13:]
    grad_square_ref, grad_score_ref, grad_gain_ref, send_ref = rest[:4]

    def put(half, r, total):
        if r is not None:
            part = total.shape[1]
            send_ref[rows_at(r, 384), half * part : (half + 1) * part] = total.astype(jnp.bfloat16)

    nothing = lambda: None
    attend_back_steps(
        *ins, grad_square_ref, grad_score_ref, grad_gain_ref, *rest[4:], [], nothing, nothing, put, lambda stage: None
    )


def attend_scratch(tokens):
    low = jnp.bfloat16
    return [
        pltpu.VMEM((tokens, D), low),
        pltpu.VMEM((D, tokens), low),
        pltpu.VMEM((tokens, D), low),
        pltpu.VMEM((tokens, D), low),
        pltpu.VMEM((tokens, D), low),
        pltpu.VMEM((D, tokens // 2), low),
    ]


def run_attend_back(*ins):
    tokens = ins[0].shape[0]
    low = jnp.bfloat16
    return pl.pallas_call(
        attend_back_kernel,
        out_shape=[
            jax.ShapeDtypeStruct((5, D, D), low),
            jax.ShapeDtypeStruct((HEADS, TILE, TILE), jnp.float32),
            jax.ShapeDtypeStruct((8, D), jnp.float32),
            jax.ShapeDtypeStruct((D, tokens), low),
        ],
        scratch_shapes=attend_scratch(tokens),
        compiler_params=pltpu.CompilerParams(vmem_limit_bytes=VMEM_CAP),
        name="attend_backward",
    )(*ins)


BACK_CAP = 64 * 1024 * 1024 - 128 * 1024


BACK_STAGES = ((0, 8, 7), (4, 5, 6, 10, 11), (3, 12))
HIGH = 32
SEGMENTS = 8
EARLY_PLAN = (("tile", 3), ("outer", 0), ("end", 1), ("dense", 1), ("dense", 3), ("dense", 5))
LATE_PLAN = (("dense", 6), ("dense", 7), ("dense", 9), ("dense", 11), ("dense", 13), ("dense", 15))


def back_kernel(depth, *refs):
    ins, refs = list(refs[:13]), refs[13:]
    keys_ref, grad_expand, grad_reduce = refs[:3]
    square_sum, expand_sum, reduce_sum, grad_score_ref, grad_gain_ref, squares_ref, table_ref = refs[3:10]
    grad_square, *steps = refs[10:17]
    blocks, spare, work_expand, work_reduce, returned, places = refs[17:23]
    refs = refs[23:]
    turned = steps[1]
    count_first, count_last = 5 * len(FIRST_KINDS), 5 * len(LAST_KINDS)
    first_buffers, refs = refs[:count_first], refs[count_first:]
    first_sems, refs = refs[:8], refs[8:]
    last_buffers, refs = refs[:count_last], refs[count_last:]
    last_sems, refs = refs[:8], refs[8:]
    part_send, part_got, part_own, end_send, end_got = refs[:5]
    need = stage_loads(ins, BACK_STAGES, refs[5:15], refs[15])
    dp_size, fsdp_size = lax.axis_size("dp"), lax.axis_size("fsdp")
    count = dp_size * fsdp_size
    me = lax.axis_index("dp") * fsdp_size + lax.axis_index("fsdp")
    greet_all(count, fsdp_size, me)
    grads = (grad_square, grad_expand, grad_reduce)
    outs = (square_sum, expand_sum, reduce_sum, spare)
    work = {EXPAND: work_expand, REDUCE: work_reduce}
    early = Reduction(FIRST_KINDS, depth, grads, outs, work, first_buffers, first_sems)
    late = Reduction(LAST_KINDS, depth, grads, outs, work, last_buffers, last_sems)
    early.begin((EXPAND, REDUCE))
    early_groups, late_groups = list(early.groups()), list(late.groups())

    def relay(group):
        def act():
            for move, step in group:
                move(step)

        return act

    feats, quarter = blocks.shape[2] // 2, blocks.shape[3]

    def part_copy(half, k):
        target = lax.rem(me + k, count)
        device = (target // fsdp_size, lax.rem(target, fsdp_size))
        return remote(
            blocks.at[half, target], returned.at[half, me], part_send.at[half, k], part_got.at[half, k], device
        )

    def own_part(half):
        return pltpu.make_async_copy(blocks.at[half, me], returned.at[half, me], part_own.at[half])

    def put(half, r, total):
        if r is None:

            def start_part(k, carry):
                part_copy(half, k).start()
                return carry

            lax.fori_loop(1, count, start_part, 0)
            own_part(half).start()
            return
        each = 384 // feats
        for p in range(each):
            part = total[p * feats : (p + 1) * feats]
            blocks[half, r * each + p] = jnp.concatenate(
                [part[:, :quarter], part[:, quarter:]], axis=0
            ).astype(jnp.bfloat16)

    attend_back_steps(
        *ins, grad_square, grad_score_ref, grad_gain_ref, *steps,
        [(*place_at, relay(group)) for place_at, group in zip(EARLY_PLAN, early_groups)],
        lambda: early.begin((EARLY,)),
        lambda: late.begin((LATE,)),
        put,
        need,
    )

    def end_copy(number, kind, of):
        span = pl.ds(*SPANS[kind])
        return remote(
            spare.at[span], square_sum.at[of, span], end_send.at[number], end_got.at[number], early.sibling
        )

    core = early.core
    table_ref[...] = jnp.zeros_like(table_ref)
    vocab = table_ref.shape[1]
    batch = 2
    segments = 4
    slots = 2 * quarter
    lines = slots // LANES

    def add_rows(half, n, carry):
        for b in range(batch):
            k = n * batch + b

            @pl.when(k > 0)
            def _():
                part_copy(half, k).wait_recv()

            source = lax.rem(me + count - k, count)
            block = returned[half, source].astype(jnp.float32)
            keys = keys_ref[source]
            for c in range(lines):
                key = keys[half * lines + c : half * lines + c + 1]
                number = (key >> 2) + (key & 3) * fold_rows(vocab)
                at = pl.ds(b * slots + c * LANES, LANES)
                places[0:1, at] = number & 1023
                first = 0 if c < lines // 2 else feats
                low = (c % (lines // 2)) * LANES
                piece = block[first : first + feats, low : low + LANES]
                high = number >> 10
                spread = [jnp.where(high == g, piece, 0.0) for g in range(HIGH)]
                turned[:, at] = jnp.concatenate(spread, axis=0).astype(jnp.bfloat16)
        for w in range(4):
            window = 256
            row = lax.broadcasted_iota(jnp.int32, (window, batch * slots), 0) + w * window
            hot = (row == places[0:1]).astype(jnp.float32).astype(jnp.bfloat16)
            total = dot_nt(turned[...], hot)
            for g in range(HIGH):
                start = g * 1024 + w * window
                width = min(window, vocab - start)
                if width > 0:
                    table_ref[:, start : start + width] += total[g * feats : (g + 1) * feats, :width]
        return carry

    plan = list(zip(EARLY_PLAN, early_groups)) + list(zip(LATE_PLAN, late_groups))
    for half in range(2):
        own_part(half).wait()
        each = count // batch // SEGMENTS
        for segment in range(SEGMENTS):
            lax.fori_loop(segment * each, (segment + 1) * each, functools.partial(add_rows, half), 0)
            for place_at, group in plan:
                if place_at == ("dense", half * SEGMENTS + segment):
                    relay(group)()
                    if group is early_groups[-1]:
                        end_copy(0, EARLY, core).start()
    end_copy(1, LATE, core).start()
    early.finish()
    late.finish()
    for number, kind in enumerate((EARLY, LATE)):
        end_copy(number, kind, core).wait_send()
        end_copy(number, kind, 1 - core).wait_recv()
    squares = jnp.zeros((1, 1), jnp.float32)
    for sums in (square_sum, expand_sum, reduce_sum):
        value = sums[...].reshape(-1, sums.shape[-1])
        squares = squares + jnp.sum(value * value, keepdims=True)
    for g in range(HIGH):
        value = table_ref[:, g * 1024 : min(vocab, (g + 1) * 1024)]
        squares = squares + jnp.sum(value * value, keepdims=True)
    squares_ref[...] = jnp.broadcast_to(squares, squares_ref.shape)
    for half in range(2):

        def end_part(k, carry):
            part_copy(half, k).wait_send()
            return carry

        lax.fori_loop(1, count, end_part, 0)


def run_back(ins, keys, grad_expand, grad_reduce, feats, vocab, call_id):
    depth = lax.axis_size("dp") // 2
    tokens = ins[0].shape[0]
    low = jnp.bfloat16
    count = keys.shape[0]
    blocks = (2, count, 2 * feats, tokens // 4)
    whole = pl.BlockSpec(memory_space=pltpu.VMEM)
    anywhere = pl.BlockSpec(memory_space=pl.ANY)
    specs, homes, load_sem = stage_specs(ins, BACK_STAGES)
    first_buffers, first_sems = reduction_scratch(FIRST_KINDS, depth)
    last_buffers, last_sems = reduction_scratch(LAST_KINDS, depth)
    return pl.pallas_call(
        functools.partial(back_kernel, depth),
        out_shape=[
            jax.ShapeDtypeStruct((2, 5, 48, 192), jnp.float32),
            jax.ShapeDtypeStruct((96, 768), jnp.float32),
            jax.ShapeDtypeStruct((192, 384), jnp.float32),
            jax.ShapeDtypeStruct((HEADS, TILE, TILE), jnp.float32),
            jax.ShapeDtypeStruct((8, D), jnp.float32),
            jax.ShapeDtypeStruct((8, LANES), jnp.float32),
            jax.ShapeDtypeStruct((feats, vocab), jnp.float32),
        ],
        in_specs=specs + [whole] + [anywhere] * 2,
        out_specs=[whole] * 7,
        scratch_shapes=[pltpu.VMEM((5, D, D), low)]
        + attend_scratch(tokens)
        + [
            pltpu.VMEM(blocks, low),
            pltpu.VMEM((5, 48, 192), jnp.float32),
            pltpu.VMEM(pair_shape(EXPAND, depth), low),
            pltpu.VMEM(pair_shape(REDUCE, depth), low),
            pltpu.VMEM(blocks, low),
            pltpu.VMEM((8, tokens), jnp.int32),
        ]
        + first_buffers
        + first_sems
        + last_buffers
        + last_sems
        + [
            pltpu.SemaphoreType.DMA((2, count)),
            pltpu.SemaphoreType.DMA((2, count)),
            pltpu.SemaphoreType.DMA((2,)),
            pltpu.SemaphoreType.DMA((2,)),
            pltpu.SemaphoreType.DMA((2,)),
        ]
        + homes
        + [load_sem],
        compiler_params=pltpu.CompilerParams(
            collective_id=call_id, has_side_effects=True, vmem_limit_bytes=BACK_CAP
        ),
        name="back",
    )(*ins, keys, grad_expand, grad_reduce)


def share_chips(own_ref, everyone, send, got, hand_send, hand_got, meanwhile=None):
    dp_size, fsdp_size = lax.axis_size("dp"), lax.axis_size("fsdp")
    count = dp_size * fsdp_size
    chips = count // 2
    dp, fsdp = lax.axis_index("dp"), lax.axis_index("fsdp")
    me = dp * fsdp_size + fsdp
    core = lax.rem(fsdp, 2)
    chip = me // 2
    sibling = (dp, fsdp + 1 - 2 * core)
    greet_all(count, fsdp_size, me)

    def device(number):
        return (number // fsdp_size, lax.rem(number, fsdp_size))

    def across(k):
        target = lax.rem(chip + k, chips) * 2 + core
        return remote(own_ref, everyone.at[me], send.at[k], got.at[k], device(target))

    def hand(k, of):
        source = lax.rem(chip + chips - k, chips) * 2 + of
        return remote(everyone.at[source], everyone.at[source], hand_send.at[k], hand_got.at[k], sibling)

    def start(k, carry):
        across(k).start()
        return carry

    def relay(k, carry):
        across(k).wait_recv()
        hand(k, core).start()
        return carry

    def end(k, carry):
        across(k).wait_send()
        hand(k, core).wait_send()
        hand(k, 1 - core).wait_recv()
        return carry

    first = remote(own_ref, everyone.at[me], hand_send.at[0], hand_got.at[0], sibling)
    first.start()
    everyone[me] = own_ref[...]
    lax.fori_loop(1, chips, start, 0)
    if meanwhile is not None:
        meanwhile()
    lax.fori_loop(1, chips, relay, 0)
    lax.fori_loop(1, chips, end, 0)
    first.wait_send()
    hand(0, 1 - core).wait_recv()
    return me


def total_kernel(
    first_gain, late_gains, position_ref, squares_ref, stats_ref, total_ref, norm_ref, tile,
    everyone, send, got, hand_send, hand_got,
):
    gains = first_gain[...] + late_gains[...]
    rows = [squares_ref[0:1]]
    rows += [position_ref[k : k + 1] for k in range(3)]
    for k in range(3):
        rows += [gains[k : k + 1, c * LANES : (c + 1) * LANES] for c in range(D // LANES)]
    rows.append(jnp.zeros((tile.shape[0] - len(rows), LANES), jnp.float32))
    tile[...] = jnp.concatenate(rows, axis=0)
    share_chips(tile, everyone, send, got, hand_send, hand_got)

    def add(k, total):
        return total + everyone[k]

    total = lax.fori_loop(1, everyone.shape[0], add, everyone[0])
    total_ref[...] = total
    row = lax.broadcasted_iota(jnp.int32, total.shape, 0)
    lane = lax.broadcasted_iota(jnp.int32, total.shape, 1)
    squares = jnp.where(row == 0, jnp.where(lane == 0, total, 0.0), total * total)
    grad_scale = stats_ref[0:1, 2:3]
    norm = jnp.sqrt(jnp.sum(squares, keepdims=True) + grad_scale * grad_scale)
    norm_ref[...] = jnp.broadcast_to(norm, norm_ref.shape)


def run_total(first_gain, late_gains, position, squares, stats, call_id):
    count = lax.axis_size("dp") * lax.axis_size("fsdp")
    few = pltpu.SemaphoreType.DMA((count // 2,))
    return pl.pallas_call(
        total_kernel,
        out_shape=[jax.ShapeDtypeStruct((24, LANES), jnp.float32), jax.ShapeDtypeStruct((8, LANES), jnp.float32)],
        scratch_shapes=[
            pltpu.VMEM((24, LANES), jnp.float32),
            pltpu.VMEM((count, 24, LANES), jnp.float32),
            few, few, few, few,
        ],
        compiler_params=pltpu.CompilerParams(
            collective_id=call_id, has_side_effects=True, vmem_limit_bytes=VMEM_CAP
        ),
        name="total",
    )(first_gain, late_gains, position, squares, stats)


def loss_steps(query_rows, nli_rows, me, slots, negative_ref, scale_ref, stats_ref, everyone, grad_sims, turned_sims):
    count = everyone.shape[0]
    total_rows = count * slots
    embeds = everyone[...].reshape(total_rows, D)
    scale = jnp.exp(scale_ref[...])
    sims = dot_nt(embeds, embeds)
    row = lax.broadcasted_iota(jnp.int32, sims.shape, 0)
    col = lax.broadcasted_iota(jnp.int32, sims.shape, 1)
    row_slot, col_slot = row & (slots - 1), col & (slots - 1)
    hypo, answer = query_rows + nli_rows, query_rows + 2 * nli_rows
    is_query = row_slot < query_rows
    is_premise = (row_slot >= query_rows) & (row_slot < hypo)
    is_hypo = (col_slot >= hypo) & (col_slot < answer)
    is_answer = (col_slot >= answer) & (col_slot < answer + query_rows)
    allowed = (is_query & is_answer) | (is_premise & is_hypo)
    target = (is_query & (col == row + answer)) | (is_premise & (col == row + nli_rows))
    target = jnp.where(target, 1.0, 0.0)
    logits = scale * sims
    shown = jnp.where(allowed, logits, -1e30)
    row_top = jnp.max(shown, axis=1, keepdims=True)
    weight = jnp.where(negative_ref[:, :1] == col, 2.0, 1.0)
    raised = jnp.where(allowed, weight * jnp.exp(shown - row_top), 0.0)
    left = is_query | is_premise
    row_total = jnp.where(left[:, :1], jnp.sum(raised, axis=1, keepdims=True), 1.0)
    hits = jnp.sum(jnp.where(target > 0.0, logits, 0.0), axis=1, keepdims=True)
    losses = jnp.where(left[:, :1], row_top + jnp.log(row_total), 0.0) - hits
    first_loss = jnp.sum(jnp.where(is_query[:, :1], losses, 0.0), keepdims=True)
    second_loss = jnp.sum(jnp.where(is_premise[:, :1], losses, 0.0), keepdims=True)
    grad_logits = raised / row_total - target
    grad_scale = scale * jnp.sum(grad_logits * sims, keepdims=True)
    lane = lax.broadcasted_iota(jnp.int32, stats_ref.shape, 1)
    stats_ref[...] = jnp.where(lane == 0, first_loss, jnp.where(lane == 1, second_loss, grad_scale))
    grads = scale * grad_logits
    grad_sims[...] = grads
    turned_sims[...] = grads.T
    own = pl.ds(pl.multiple_of(me * slots, 8), slots)
    return dot_nn(grad_sims[own, :].astype(jnp.bfloat16), embeds) + dot_nn(
        turned_sims[own, :].astype(jnp.bfloat16), embeds
    )


def shards(
    embed_table,
    square_weights,
    expand_weight,
    reduce_weight,
    norm_gains,
    position_bias,
    log_scale,
    table_moment,
    table_second,
    square_moment,
    square_second,
    expand_moment,
    expand_second,
    reduce_moment,
    reduce_second,
    gains_moment,
    gains_second,
    position_moment,
    position_second,
    scale_moment,
    scale_second,
    query_tokens,
    answer_tokens,
    query_length,
    answer_length,
    premise_tokens,
    hypothesis_tokens,
    hard_negative,
):
    both = ("dp", "fsdp")
    dp_size, fsdp_size = lax.axis_size("dp"), lax.axis_size("fsdp")
    count = dp_size * fsdp_size
    direct = dp_size == 8 and fsdp_size == 4
    position = lax.axis_index(both)
    feats, vocab_size = embed_table.shape
    feats_pad = up8(feats)
    fold = fold_rows(vocab_size)
    query_rows = query_tokens.shape[0]
    nli_rows = premise_tokens.shape[0]
    short_length = query_tokens.shape[1]
    long_length = answer_tokens.shape[1]
    short_tokens = jnp.concatenate([query_tokens, premise_tokens, hypothesis_tokens], axis=0)
    lengths = jnp.concatenate(
        [query_length, jnp.full((2 * nli_rows,), short_length, jnp.int32), answer_length]
    )
    all_tokens = jnp.concatenate([short_tokens.reshape(-1), answer_tokens.reshape(-1)])
    token_count = all_tokens.shape[0]
    hypo_start = query_rows + nli_rows
    answer_start = query_rows + 2 * nli_rows
    seq_count = answer_start + query_rows
    seq_pad = -(-seq_count // 16) * 16
    split_at = short_tokens.shape[0] * short_length

    packed, rank = token_keys(all_tokens, fold)
    key_rows = token_count // LANES
    info = jnp.concatenate(
        [
            packed.reshape(key_rows, LANES),
            jnp.pad(hard_negative, (0, LANES - nli_rows)).reshape(1, LANES),
            jnp.zeros((7, LANES), jnp.int32),
        ],
        axis=0,
    )
    square_low = square_weights.astype(jnp.bfloat16)
    expand_low = expand_weight.astype(jnp.bfloat16)
    reduce_low = reduce_weight.astype(jnp.bfloat16).T
    half = token_count // 2
    if direct:
        found, square_all, expand_all, info_all, gains_all = run_front(
            info, norm_gains, token_count, embed_table, square_weights, expand_weight, 1
        )
    else:
        info_all = exchange(info[None], True, 0, "share_keys")
        own_gains = jnp.pad(norm_gains, ((0, 5), (0, LANES - feats)))
        gains_all = exchange(own_gains[None], True, 6, "share_gains")

        def whole(piece, row_name, column_name):
            axis = piece.ndim - 2
            wide = lax.all_gather(piece, column_name, axis=axis + 1, tiled=True)
            return lax.all_gather(wide, row_name, axis=axis, tiled=True)

        square_all = whole(square_low, "dp", "fsdp")
        expand_all = whole(expand_low, "dp", "fsdp")
        reduce_all = whole(reduce_low, "fsdp", "dp")
        padded = jnp.pad(embed_table, ((0, feats_pad - feats), (0, 0)))
        key_all = info_all[:, :key_rows].reshape(count, 1, token_count)
        found = exchange(lookup(padded, key_all >> 2, key_all & 3), False, 8, "send_features")
        found = found.reshape(count, 2, feats_pad, half)[:, :, :feats]
        found = found.transpose(1, 0, 2, 3).reshape(1, 2 * D, half)
    packed_all = info_all[:, :key_rows].reshape(count, 1, token_count)
    row_all, group_all = packed_all >> 2, packed_all & 3
    negative_all = info_all[:, key_rows, :nli_rows]
    gains = gains_all[:, :3, :feats].transpose(1, 0, 2).reshape(3, D)
    gains = jnp.pad(gains.astype(jnp.bfloat16).astype(jnp.float32), ((0, 5), (0, 0)))

    sequence = np.concatenate(
        [
            np.repeat(np.arange(answer_start), short_length),
            answer_start + np.repeat(np.arange(query_rows), long_length),
        ]
    )
    inside = np.concatenate(
        [
            np.tile(np.arange(short_length), answer_start),
            np.tile(np.arange(long_length), query_rows),
        ]
    )
    lengths_pad = jnp.pad(lengths, (0, seq_pad - seq_count), constant_values=1)
    pool = (sequence[None, :] == np.arange(seq_pad)[:, None]) & (inside[None, :] < lengths_pad[:, None])
    token_ok = jnp.any(pool, axis=0).reshape(-1, 1, TILE)
    sequence_tiles = sequence.reshape(-1, TILE)
    together = sequence_tiles[:, :, None] == sequence_tiles[:, None, :]
    mask = jnp.where(together & token_ok, 0.0, -1e30).astype(jnp.float32)
    pool = pool.astype(jnp.float32)
    length_rows = jnp.broadcast_to(lengths_pad.astype(jnp.float32)[:, None], (seq_pad, LANES))
    rank_rows = jnp.broadcast_to(rank[:, None], (token_count, LANES))
    bias, onehot = attention_bias(position_bias, TILE)

    forward_ins = (found, rank_rows, square_all, gains, bias, mask, pool, length_rows)
    if direct:
        *forward_all, reduce_all = run_relayed_forward(forward_ins, expand_all, reduce_low, 2)
    else:
        forward_all = run_forward(forward_ins, expand_all, reduce_all)
    (start, queries, keys_here, values_here, mixed, middle, ending, embeds_low, pooled, embeds, inverse) = forward_all
    if direct:
        negative_place = (negative_all // nli_rows) * seq_pad + hypo_start + negative_all % nli_rows
        negative_place = jnp.pad(
            negative_place, ((0, 0), (query_rows, seq_pad - hypo_start)), constant_values=-1
        )
        negative_place = jnp.broadcast_to(negative_place.reshape(-1, 1), (count * seq_pad, LANES))
        (grad_expand, grad_reduce, grad_middle, grad_proj, late_gains, stats) = run_loss_feed(
            embeds_low, negative_place, log_scale.reshape(1, 1), embeds, inverse, pool, length_rows, gains,
            square_all, middle, ending, expand_all, reduce_all, query_rows, nli_rows, 3,
        )
        losses, grad_scale = stats[0, :2], stats[0, 2:3]
    else:
        gathered = exchange(embeds_low[None], True, 3, "share_embeds")
        queries_all = gathered[:, :query_rows].reshape(-1, D)
        premises_all = gathered[:, query_rows:hypo_start].reshape(-1, D)
        hypotheses_all = gathered[:, hypo_start:answer_start].reshape(-1, D)
        answers_all = gathered[:, answer_start:seq_count].reshape(-1, D)
        scale = jnp.exp(log_scale[0])

        def contrast(left, right, extra, own):
            sims = product_right(left, right)
            logits = scale * sims
            row_top = jnp.max(logits, axis=1, keepdims=True)
            raised = (1.0 + extra) * jnp.exp(logits - row_top)
            row_total = jnp.sum(raised, axis=1, keepdims=True)
            spread = row_top[:, 0] + jnp.log(row_total[:, 0])
            target_hit = jnp.eye(left.shape[0], dtype=jnp.float32)
            loss_sum = jnp.sum(spread - jnp.sum(target_hit * logits, axis=1))
            grad_logits = raised / row_total - target_hit
            grad_scale = jnp.sum(grad_logits * sims)
            grad_sims = (scale * grad_logits).astype(jnp.bfloat16)
            mine_left = lax.dynamic_slice_in_dim(grad_sims, position * own, own, 0)
            mine_right = lax.dynamic_slice_in_dim(grad_sims, position * own, own, 1)
            return (loss_sum, grad_scale, product(mine_left, right), product_left(mine_right, left))

        first_loss, first_dscale, grad_queries, grad_answers = contrast(
            queries_all, answers_all, 0.0, query_rows
        )
        negatives = (jnp.arange(hypotheses_all.shape[0])[None, :] == negative_all.reshape(-1)[:, None]).astype(
            jnp.float32
        )
        second_loss, second_dscale, grad_premises, grad_hypotheses = contrast(
            premises_all, hypotheses_all, negatives, nli_rows
        )
        grad_embeds = jnp.concatenate(
            [
                grad_queries,
                grad_premises,
                grad_hypotheses,
                grad_answers,
                jnp.zeros((seq_pad - seq_count, D), jnp.float32),
            ],
            axis=0,
        )
        losses = jnp.stack([first_loss, second_loss])
        grad_scale = ((first_dscale + second_dscale) * scale).reshape(1)
        stats = jnp.broadcast_to(grad_scale, (8, LANES))
        (grad_expand, grad_reduce, grad_middle, grad_proj, late_gains) = run_feed_back(
            grad_embeds, embeds, inverse, pool, length_rows, square_all, middle, ending, expand_all, reduce_all, gains
        )
    back_ins = (
        grad_middle, grad_proj, pooled, start, queries, keys_here, values_here, mixed, square_all,
        gains, bias, mask, rank_rows,
    )
    if direct:
        (square_sum, expand_sum, reduce_sum, grad_scores, first_gain, layer_squares, grad_table) = run_back(
            back_ins, info_all, grad_expand, grad_reduce, feats, vocab_size, 5
        )

        square_sum = square_sum.transpose(1, 0, 2, 3).reshape(5, 96, 192)
    else:

        def shard(gradient, row_name, column_name):
            axis = gradient.ndim - 2
            part = lax.psum_scatter(
                gradient.astype(jnp.float32), row_name, scatter_dimension=axis, tiled=True
            )
            return lax.psum_scatter(part, column_name, scatter_dimension=axis + 1, tiled=True)

        (grad_square, grad_scores, first_gain, merged) = run_attend_back(*back_ins)
        square_sum = shard(grad_square, "dp", "fsdp")
        expand_sum = shard(grad_expand, "dp", "fsdp")
        reduce_sum = shard(grad_reduce, "fsdp", "dp")
        layer_squares = jnp.full(
            (8, LANES), sum(jnp.sum(part * part) for part in (square_sum, expand_sum, reduce_sum)), jnp.float32
        )
        merged = merged.reshape(count, feats, 2, 2, half // 2).transpose(2, 0, 3, 1, 4)
        if feats_pad > feats:
            merged = jnp.pad(merged, ((0, 0), (0, 0), (0, 0), (0, feats_pad - feats), (0, 0)))
        merged = merged.reshape(2, count, 2 * feats_pad, half // 2)
        returned = jnp.stack(
            [exchange(merged[n], False, 9 + n, ("send_early", "send_late")[n]) for n in range(2)]
        )
        grad_table, table_squares = scatter(returned, row_all, group_all, vocab_size)
        grad_table = grad_table[:feats]
        layer_squares = layer_squares + jnp.sum(table_squares)
    grad_position = lax.dot_general(
        onehot, grad_scores.reshape(HEADS, TILE * TILE), (((0,), (1,)), ((), ())), precision=HIGHEST
    )
    reduced = (square_sum, expand_sum, reduce_sum.T)
    total, norm = run_total(
        first_gain,
        late_gains,
        grad_position.reshape(-1, LANES),
        layer_squares,
        stats,
        7,
    )
    position_total = total[1:4].reshape(BUCKETS, HEADS)
    gains_total = total[4:22].reshape(3, D)
    scale_total = grad_scale
    gradient_norm = norm[0, 0]
    grad_gain_shard = lax.dynamic_slice_in_dim(gains_total, position * feats, feats, 1)
    factor = jnp.minimum(1.0, CLIP_NORM / gradient_norm)
    table_out = adam_update(embed_table, table_moment, table_second, grad_table, factor, TABLE_RATE)
    square_out = adam_update(
        square_weights, square_moment, square_second, reduced[0], factor, LEARN_RATE
    )
    expand_out = adam_update(
        expand_weight, expand_moment, expand_second, reduced[1], factor, LEARN_RATE
    )
    reduce_out = adam_update(
        reduce_weight, reduce_moment, reduce_second, reduced[2], factor, LEARN_RATE
    )
    gains_out = adam_update(
        norm_gains, gains_moment, gains_second, grad_gain_shard, factor, SMALL_RATE
    )
    position_out = adam_update(
        position_bias, position_moment, position_second, position_total, factor, SMALL_RATE
    )
    scale_out = adam_update(log_scale, scale_moment, scale_second, scale_total, factor, SMALL_RATE)
    return (
        *table_out,
        *square_out,
        *expand_out,
        *reduce_out,
        *gains_out,
        *position_out,
        *scale_out,
        losses,
        gradient_norm,
    )


def solution(mesh):
    return jax.shard_map(
        shards,
        mesh=mesh,
        in_specs=(
            P(("dp", "fsdp"), None),
            P(None, "dp", "fsdp"),
            P("dp", "fsdp"),
            P("dp", "fsdp"),
            P(None, ("dp", "fsdp")),
            P(),
            P(),
            P(("dp", "fsdp"), None),
            P(("dp", "fsdp"), None),
            P(None, "dp", "fsdp"),
            P(None, "dp", "fsdp"),
            P("dp", "fsdp"),
            P("dp", "fsdp"),
            P("dp", "fsdp"),
            P("dp", "fsdp"),
            P(None, ("dp", "fsdp")),
            P(None, ("dp", "fsdp")),
            P(),
            P(),
            P(),
            P(),
            P(("dp", "fsdp"), None),
            P(("dp", "fsdp"), None),
            P(("dp", "fsdp")),
            P(("dp", "fsdp")),
            P(("dp", "fsdp"), None),
            P(("dp", "fsdp"), None),
            P(("dp", "fsdp")),
        ),
        out_specs=(
            P(("dp", "fsdp"), None),
            P(("dp", "fsdp"), None),
            P(("dp", "fsdp"), None),
            P(None, "dp", "fsdp"),
            P(None, "dp", "fsdp"),
            P(None, "dp", "fsdp"),
            P("dp", "fsdp"),
            P("dp", "fsdp"),
            P("dp", "fsdp"),
            P("dp", "fsdp"),
            P("dp", "fsdp"),
            P("dp", "fsdp"),
            P(None, ("dp", "fsdp")),
            P(None, ("dp", "fsdp")),
            P(None, ("dp", "fsdp")),
            P(),
            P(),
            P(),
            P(),
            P(),
            P(),
            P(),
            P(),
        ),
        check_vma=False,
    )
```
